32 devices in a mesh: seq: 8 (over y, x, core), head: 4 (over z).
Axes of the slice: x: 2, y: 2, z: 4, core: 2. Of those that a mesh axis runs over, the one named last changes fastest.
Arguments:
- query_rows: bfloat16 [4096, 64, 128], P('seq', 'head'), may hold values from -3 to 3
- key_rows: bfloat16 [4096, 64, 128], P('seq', 'head'), may hold values from -0.59765625 to 0.59765625
- value_rows: bfloat16 [4096, 64, 128], P('seq', 'head'), may hold values from -18 to 18
- output_grad: bfloat16 [4096, 64, 128], P('seq', 'head'), may hold values from -1.796875 to 1.796875
- norm_gain: float32 [64, 128], P('head'), may hold values from 0.1 to 1.9
- log_decay: float32 [64, 4096], P('head', 'seq'), may hold values from -0.6932 to 0, as said below
Outputs:
- normed: bfloat16 [4096, 64, 128], P('seq', 'head')
- grad_q: bfloat16 [4096, 64, 128], P('seq', 'head')
- grad_k: bfloat16 [4096, 64, 128], P('seq', 'head')
- grad_v: bfloat16 [4096, 64, 128], P('seq', 'head')
The draws below stay inside these ranges and needn't reach their ends.
Inputs may be any that keep to these rules, and one draw needn't show every extreme that they name: `log_decay`: never positive.
All inputs are finite; a program needn't handle non-finite values.
Results may differ from the reference program's by a relative error of at most 0.0051.
Values sent between devices are 32-bit elements; how exact they have to be, the bound alone decides.
No kernel may reach another device: no remote copies, remote signals or barrier semaphores. Data moves between devices by JAX's collectives and lax.ppermute only.
A program may use at most 192 MiB of HBM per device.

```python
import jax
import jax.numpy as jnp
from jax import lax

HEAD_TOTAL = 64
HD = 128
BLOCK = 256
TOK_DEV = 512
TOKEN_TOTAL = 4096


def draw_log_decay(key, part):
    sequence_portions = jax.random.split(jax.random.fold_in(key, 11), 7)
    share = 0.5
    slow_mask = jax.random.uniform(sequence_portions[0], (HEAD_TOTAL, 1)) < share
    slow_rate = jnp.exp(jax.random.uniform(sequence_portions[1], (HEAD_TOTAL, 1), minval=jnp.log(0.02), maxval=jnp.log(0.5))) / TOKEN_TOTAL
    fast_rate = jnp.exp(jax.random.uniform(sequence_portions[2], (HEAD_TOTAL, 1), minval=jnp.log(5.0), maxval=jnp.log(8.0))) / BLOCK
    baseline_decay_rate = jnp.where(slow_mask, slow_rate, fast_rate)
    portion_decay_factor = jax.random.uniform(sequence_portions[3], (HEAD_TOTAL, TOKEN_TOTAL // TOK_DEV, 1), minval=0.5, maxval=1.5)
    portion_decay_factor = jnp.broadcast_to(portion_decay_factor, (HEAD_TOTAL, TOKEN_TOTAL // TOK_DEV, TOK_DEV)).reshape(HEAD_TOTAL, TOKEN_TOTAL)
    coarse_decay_factor = jax.random.uniform(sequence_portions[4], (HEAD_TOTAL, TOKEN_TOTAL), minval=0.6, maxval=1.4)
    sudden_decay_mask = jax.random.uniform(sequence_portions[5], (HEAD_TOTAL, TOKEN_TOTAL)) < 2.0 / TOKEN_TOTAL
    sudden_decay_drop = jnp.log(jax.random.uniform(sequence_portions[6], (HEAD_TOTAL, TOKEN_TOTAL), minval=0.5, maxval=0.8))
    return jnp.where(sudden_decay_mask, sudden_decay_drop, -baseline_decay_rate * portion_decay_factor * coarse_decay_factor).astype(jnp.float32)


def draw_query_rows(key, part):
    sequence_portions = jax.random.split(jax.random.fold_in(key, 23), 2)
    row_scale = jnp.exp(jax.random.uniform(sequence_portions[0], (TOKEN_TOTAL, 1, 1), minval=0.0, maxval=jnp.log(10.0)))
    base = jnp.clip(jax.random.normal(sequence_portions[1], (TOKEN_TOTAL, HEAD_TOTAL, HD)), -6.0, 6.0)
    return (0.05 * row_scale * base).astype(jnp.bfloat16)


def draw_value_rows(key, part):
    sequence_portions = jax.random.split(jax.random.fold_in(key, 37), 2)
    ramp = jnp.arange(HEAD_TOTAL, dtype=jnp.float32)[None, :, None] / (HEAD_TOTAL - 1)
    head_scale = 0.3 * jnp.exp(ramp * jnp.log(10.0))
    base = jnp.clip(jax.random.normal(sequence_portions[1], (TOKEN_TOTAL, HEAD_TOTAL, HD)), -6.0, 6.0)
    return (head_scale * base).astype(jnp.bfloat16)


def shard_levels(stream_key, dims, pieces, low, top_value):
    def one(axis_at, blocks):
        steps = jax.random.uniform(jax.random.fold_in(jax.random.fold_in(stream_key, 6), axis_at), (blocks,), jnp.float32, low / len(pieces), top_value / len(pieces))
        return jnp.repeat(jnp.exp(steps), dims[axis_at] // blocks).reshape((-1,) + (1,) * (len(dims) - axis_at - 1))

    loudness = one(*pieces[0])
    for cut in pieces[1:]:
        loudness = loudness * one(*cut)
    return loudness


def scatter_about(rng, dims, deviation, bound, pieces=(), kind=jnp.bfloat16):
    entries = jax.random.normal(rng, dims, jnp.float32) * deviation
    if len(pieces) > 0:
        entries = shard_levels(rng, dims, pieces, -0.22, 0.18) * entries
    return jnp.clip(entries, min=-bound, max=bound).astype(kind)


def setup_inputs(seed: int = 0) -> dict:
    streams_of = jax.random.split(jax.random.key(seed), 7)
    return {
        "query_rows": draw_query_rows(jax.random.fold_in(streams_of[6], 71), 0),
        "key_rows": scatter_about(streams_of[1], (TOKEN_TOTAL, HEAD_TOTAL, HD), 0.1, 0.59765625, ((0, 8), (1, 4))),
        "value_rows": draw_value_rows(jax.random.fold_in(streams_of[6], 71), 0),
        "output_grad": scatter_about(streams_of[3], (TOKEN_TOTAL, HEAD_TOTAL, HD), 0.3, 1.796875, ((0, 8), (1, 4))),
        "norm_gain": jnp.clip(1.0 + 0.18 * jax.random.normal(streams_of[4], (HEAD_TOTAL, HD), jnp.float32), 0.1, 1.9),
        "log_decay": draw_log_decay(jax.random.fold_in(streams_of[6], 71), 0),
    }


state_precision = lax.Precision.HIGH

def decay_table(cum_block):
    block_len = cum_block.shape[1]
    lower_mask = jnp.arange(block_len)[:, None] >= jnp.arange(block_len)[None, :]
    gap_table = jnp.where(lower_mask[None], cum_block[:, :, None] - cum_block[:, None, :], -jnp.inf)
    return jnp.exp(gap_table)

def reference(query_rows, key_rows, value_rows, output_grad, norm_gain, log_decay):
    nblocks = TOKEN_TOTAL // BLOCK
    query_blocks = query_rows.reshape(nblocks, BLOCK, HEAD_TOTAL, HD)
    key_blocks = key_rows.reshape(nblocks, BLOCK, HEAD_TOTAL, HD)
    value_blocks = value_rows.reshape(nblocks, BLOCK, HEAD_TOTAL, HD)
    grad_blocks = output_grad.reshape(nblocks, BLOCK, HEAD_TOTAL, HD)
    cum_all = jnp.cumsum(log_decay.reshape(HEAD_TOTAL, nblocks, BLOCK), axis=2).transpose(1, 0, 2)

    def forward_step(state_now, items):
        query_block, key_block, value_block, cum_block, grad_block = items
        query_f = query_block.astype(jnp.float32)
        key_f = key_block.astype(jnp.float32)
        value_f = value_block.astype(jnp.float32)
        decay = decay_table(cum_block)
        raw_scores = jnp.einsum('thd,shd->hts', query_f, key_f, precision=state_precision)
        weights = (raw_scores * decay).astype(jnp.bfloat16)
        inner_part = jnp.einsum('hts,shd->thd', weights.astype(jnp.float32), value_f, precision=state_precision)
        start_scale = jnp.exp(cum_block).T[:, :, None]
        attended = inner_part + jnp.einsum('thd,hde->the', query_f * start_scale, state_now, precision=state_precision)
        last_cum = cum_block[:, -1]
        end_scale = jnp.exp(last_cum[:, None] - cum_block).T[:, :, None]
        state_next = jnp.exp(last_cum)[:, None, None] * state_now + jnp.einsum('shd,she->hde', key_f * end_scale, value_f, precision=state_precision)
        mean_sq = lax.optimization_barrier(jnp.mean(attended * attended, axis=(1, 2)))
        inv_rms = lax.rsqrt(mean_sq + 1e-06)
        hat_rows = attended * inv_rms[:, None, None]
        normed = (hat_rows * norm_gain).astype(jnp.bfloat16)
        scaled = norm_gain * grad_block.astype(jnp.float32)
        projection = lax.optimization_barrier(jnp.mean(scaled * hat_rows, axis=(1, 2)))
        grad_attn = ((scaled - hat_rows * projection[:, None, None]) * inv_rms[:, None, None]).astype(jnp.bfloat16)
        return (state_next, (normed, grad_attn, state_now))
    zero_state = jnp.zeros((HEAD_TOTAL, HD, HD), jnp.float32)
    unused, (normed_all, grad_attn_all, states_all) = lax.scan(forward_step, zero_state, (query_blocks, key_blocks, value_blocks, cum_all, grad_blocks))

    def backward_step(grad_state, items):
        query_block, key_block, value_block, cum_block, grad_block, state_now = items
        query_f = query_block.astype(jnp.float32)
        key_f = key_block.astype(jnp.float32)
        value_f = value_block.astype(jnp.float32)
        grad_f = grad_block.astype(jnp.float32)
        decay = decay_table(cum_block)
        raw_scores = jnp.einsum('thd,shd->hts', query_f, key_f, precision=state_precision)
        weights = (raw_scores * decay).astype(jnp.bfloat16).astype(jnp.float32)
        grad_scores = (jnp.einsum('the,she->hts', grad_f, value_f, precision=state_precision) * decay).astype(jnp.bfloat16).astype(jnp.float32)
        start_scale = jnp.exp(cum_block).T[:, :, None]
        last_cum = cum_block[:, -1]
        end_scale = jnp.exp(last_cum[:, None] - cum_block).T[:, :, None]
        grad_query = jnp.einsum('hts,shd->thd', grad_scores, key_f, precision=state_precision) + jnp.einsum('the,hde->thd', grad_f * start_scale, state_now, precision=state_precision)
        grad_key = jnp.einsum('hts,thd->shd', grad_scores, query_f, precision=state_precision) + jnp.einsum('she,hde->shd', value_f * end_scale, grad_state, precision=state_precision)
        grad_value = jnp.einsum('hts,the->she', weights, grad_f, precision=state_precision) + jnp.einsum('shd,hde->she', key_f * end_scale, grad_state, precision=state_precision)
        grad_prev = jnp.exp(last_cum)[:, None, None] * grad_state + jnp.einsum('thd,the->hde', query_f * start_scale, grad_f, precision=state_precision)
        return (grad_prev, (grad_query.astype(jnp.bfloat16), grad_key.astype(jnp.bfloat16), grad_value.astype(jnp.bfloat16)))
    unused_grad, (grad_q, grad_k, grad_v) = lax.scan(backward_step, zero_state, (query_blocks, key_blocks, value_blocks, cum_all, grad_attn_all, states_all), reverse=True)
    shape_out = (TOKEN_TOTAL, HEAD_TOTAL, HD)
    return (normed_all.reshape(shape_out), grad_q.reshape(shape_out), grad_k.reshape(shape_out), grad_v.reshape(shape_out))
```

```python
import functools

import jax
import jax.numpy as jnp
from jax import lax
from jax.experimental import pallas as pl
from jax.experimental.pallas import tpu as pltpu
from jax.sharding import PartitionSpec as P

HEAD_TOTAL = 64
HD = 128
BLOCK = 256
GROUP = 4
STEP_TOK = 128
F32 = jnp.float32
BF16 = jnp.bfloat16
VMEM_LIMIT = 40 * 1024 * 1024


def params():
    return pltpu.CompilerParams(
        dimension_semantics=("arbitrary",), vmem_limit_bytes=VMEM_LIMIT
    )


def cost(flops, moved, exps=0):
    return pl.CostEstimate(flops=flops, bytes_accessed=moved, transcendentals=exps)


def block_cum(log_decay):
    size = log_decay.shape[1]
    upper = lax.broadcasted_iota(jnp.int32, (size, size), 0) <= lax.broadcasted_iota(
        jnp.int32, (size, size), 1
    )
    return jnp.dot(
        log_decay,
        jnp.where(upper, 1.0, 0.0).astype(F32),
        precision=lax.Precision.HIGHEST,
        preferred_element_type=F32,
    )


def as_columns(row):
    return jnp.broadcast_to(row, (HD, row.shape[1])).T


def dot(a, b):
    return jnp.dot(a, b, preferred_element_type=F32)


def dot_rows(a, b):
    return lax.dot_general(a, b, (((1,), (1,)), ((), ())), preferred_element_type=F32)


def two_parts(matrix):
    high = matrix.astype(BF16)
    return high, (matrix - high.astype(F32)).astype(BF16)


def decay_matrix(row, columns):
    size = row.shape[1]
    lower = lax.broadcasted_iota(jnp.int32, (size, size), 0) >= lax.broadcasted_iota(
        jnp.int32, (size, size), 1
    )
    both = jnp.concatenate([columns] * (size // HD), axis=1)
    return jnp.exp(jnp.where(lower, both - row, -jnp.inf))


def to_rows(dst, block):
    tok, heads, dim = block.shape
    dst[...] = block[...].astype(F32).reshape(tok * heads, dim)


def head_rows(ref, head, heads, tok):
    return ref[pl.ds(head, tok, stride=heads), :]


def state_kernel(core_ref, ld_ref, k_ref, v_ref, own_ref, send_ref, first_ref, kx, vx, cum, acc):
    heads = ld_ref.shape[0]
    step = pl.program_id(0)
    per_block = BLOCK // STEP_TOK
    half = heads // 2

    @pl.when(step == 0)
    def _():
        for b in range(2):
            cum[b] = block_cum(ld_ref[:, b * BLOCK : (b + 1) * BLOCK])
        acc[...] = jnp.zeros_like(acc)

    to_rows(kx, k_ref)
    to_rows(vx, v_ref)
    b = step // per_block
    at = pl.multiple_of((step % per_block) * STEP_TOK, STEP_TOK)
    ends = cum[b, :, BLOCK - 1 : BLOCK]
    scale = jnp.exp(ends - cum[b, :, pl.ds(at, STEP_TOK)])
    for h in range(heads):
        keys = head_rows(kx, h, heads, STEP_TOK).T * scale[h : h + 1]
        values = head_rows(vx, h, heads, STEP_TOK).astype(BF16)
        acc[b, h] += dot(keys.astype(BF16), values)

    @pl.when(step == 2 * per_block - 1)
    def _():
        first_ref[...] = acc[0]
        last = jnp.exp(cum[1, :, BLOCK - 1 : BLOCK])
        for h in range(heads):
            acc[1, h] += last[h : h + 1, :] * acc[0, h]
        core = core_ref[0]
        own_ref[...] = acc[1, pl.ds(core * half, half)]
        send_ref[...] = acc[1, pl.ds((1 - core) * half, half)]


def local_state(core, log_decay, key_rows, value_rows):
    tok, heads, dim = key_rows.shape
    half = heads // 2
    raw = pl.BlockSpec((STEP_TOK, heads, dim), lambda i: (i, 0, 0))
    whole = lambda *shape: pl.BlockSpec(shape, lambda i: (0,) * len(shape))
    return pl.pallas_call(
        state_kernel,
        grid=(tok // STEP_TOK,),
        in_specs=[pl.BlockSpec(memory_space=pltpu.SMEM), whole(heads, tok), raw, raw],
        out_specs=[whole(half, dim, dim), whole(half, dim, dim), whole(heads, dim, dim)],
        out_shape=[
            jax.ShapeDtypeStruct((half, dim, dim), F32),
            jax.ShapeDtypeStruct((half, dim, dim), F32),
            jax.ShapeDtypeStruct((heads, dim, dim), F32),
        ],
        scratch_shapes=[
            pltpu.VMEM((STEP_TOK * heads, dim), F32),
            pltpu.VMEM((STEP_TOK * heads, dim), F32),
            pltpu.VMEM((2, heads, BLOCK), F32),
            pltpu.VMEM((2, heads, dim, dim), F32),
        ],
        compiler_params=params(),
        cost_estimate=cost(2 * tok * heads * dim * dim, 4 * tok * heads * dim),
        name="local_state",
    )(core, log_decay, key_rows, value_rows)


def intra_kernel(
    second, ld_ref, q_ref, k_ref, v_ref, o_ref, first_ref,
    qh_ref, kh_ref, vh_ref, oh_ref, w_ref, inner_ref, qx, kx, vx, ox, cum,
):
    heads = ld_ref.shape[0]
    step = pl.program_id(0)

    @pl.when(step == 0)
    def _():
        cum[...] = block_cum(ld_ref[...])
        to_rows(qx, q_ref)
        to_rows(kx, k_ref)
        to_rows(vx, v_ref)
        to_rows(ox, o_ref)

    for i in range(GROUP):
        h = step * GROUP + i
        query = head_rows(qx, h, heads, BLOCK).astype(BF16)
        key = head_rows(kx, h, heads, BLOCK).astype(BF16)
        value = head_rows(vx, h, heads, BLOCK).astype(BF16)
        qh_ref[i] = query
        kh_ref[i] = key
        vh_ref[i] = value
        oh_ref[i] = head_rows(ox, h, heads, BLOCK).astype(BF16)
        row = cum[pl.ds(h, 1), :]
        columns = as_columns(row)
        weights = (dot_rows(query, key) * decay_matrix(row, columns)).astype(BF16)
        w_ref[i] = weights
        inner = dot(weights, value)
        if second:
            high, low = two_parts(first_ref[i])
            inner += jnp.exp(columns) * (dot(query, high) + dot(query, low))
        inner_ref[i] = inner


def intra(index, log_decay, query_rows, key_rows, value_rows, output_grad, first):
    tok, heads, dim = key_rows.shape
    raw = pl.BlockSpec((BLOCK, heads, dim), lambda i: (index, 0, 0))
    by_head = pl.BlockSpec((GROUP, BLOCK, dim), lambda i: (i, 0, 0))
    head_shape = jax.ShapeDtypeStruct((heads, BLOCK, dim), BF16)
    return pl.pallas_call(
        functools.partial(intra_kernel, index > 0),
        grid=(heads // GROUP,),
        in_specs=[
            pl.BlockSpec((heads, BLOCK), lambda i: (0, index)),
            raw, raw, raw, raw,
            pl.BlockSpec((GROUP, dim, dim), lambda i: (i, 0, 0)),
        ],
        out_specs=[by_head] * 4 + [pl.BlockSpec((GROUP, BLOCK, BLOCK), lambda i: (i, 0, 0)), by_head],
        out_shape=[head_shape] * 4 + [
            jax.ShapeDtypeStruct((heads, BLOCK, BLOCK), BF16),
            jax.ShapeDtypeStruct((heads, BLOCK, dim), F32),
        ],
        scratch_shapes=[pltpu.VMEM((BLOCK * heads, dim), F32)] * 4 + [pltpu.VMEM((heads, BLOCK), F32)],
        compiler_params=params(),
        cost_estimate=cost(
            2 * heads * BLOCK * BLOCK * dim * 4, 20 * heads * BLOCK * dim, heads * BLOCK * BLOCK
        ),
        name=f"intra_{index}",
    )(log_decay, query_rows, key_rows, value_rows, output_grad, first)


def whole_state(core, keep_ref, recv_ref, group, i):
    half = keep_ref.shape[0]
    head = group * GROUP + i
    mine = (head // half) == core
    return jnp.where(mine, keep_ref[head % half], recv_ref[head % half])


def attend_kernel(
    core_ref, ld_ref, gain_ref, keep_ref, recv_ref, q0, q1, o0, o1, inner0, inner1,
    att0, att1, sums_ref, cum, squares, products,
):
    step = pl.program_id(0)
    steps = pl.num_programs(0)

    @pl.when(step == 0)
    def _():
        cum[0] = block_cum(ld_ref[:, :BLOCK])
        cum[1] = cum[0, :, BLOCK - 1 : BLOCK] + block_cum(ld_ref[:, BLOCK:])
        squares[...] = jnp.zeros_like(squares)
        products[...] = jnp.zeros_like(products)

    for i in range(GROUP):
        h = step * GROUP + i
        high, low = two_parts(whole_state(core_ref[0], keep_ref, recv_ref, step, i))
        gain = gain_ref[pl.ds(h, 1), :]
        for b, (q, o, inner, att) in enumerate(((q0, o0, inner0, att0), (q1, o1, inner1, att1))):
            columns = jnp.exp(as_columns(cum[b, pl.ds(h, 1), :]))
            attended = inner[i] + columns * (dot(q[i], high) + dot(q[i], low))
            att[i] = attended
            squares[b] += attended * attended
            products[b] += gain * o[i].astype(F32) * attended

    @pl.when(step == steps - 1)
    def _():
        ones = jnp.ones((8, HD), F32)
        for b in range(2):
            for at, total in enumerate((squares, products)):
                line = lax.dot_general(
                    ones, total[b], (((1,), (1,)), ((), ())),
                    precision=lax.Precision.HIGHEST, preferred_element_type=F32,
                )
                sums_ref[at : at + 1, b * BLOCK : (b + 1) * BLOCK] = line[:1]


def attend(core, log_decay, gain, keep, recv, parts):
    heads, tok = log_decay.shape
    dim = HD
    whole = lambda *shape: pl.BlockSpec(shape, lambda i: (0,) * len(shape))
    by_head = pl.BlockSpec((GROUP, BLOCK, dim), lambda i: (i, 0, 0))
    head_shape = jax.ShapeDtypeStruct((heads, BLOCK, dim), F32)
    return pl.pallas_call(
        attend_kernel,
        grid=(heads // GROUP,),
        in_specs=[pl.BlockSpec(memory_space=pltpu.SMEM), whole(heads, tok), whole(heads, dim)]
        + [whole(heads // 2, dim, dim)] * 2 + [by_head] * 6,
        out_specs=[by_head, by_head, whole(2, tok)],
        out_shape=[head_shape, head_shape, jax.ShapeDtypeStruct((2, tok), F32)],
        scratch_shapes=[
            pltpu.VMEM((2, heads, BLOCK), F32),
            pltpu.VMEM((2, BLOCK, dim), F32),
            pltpu.VMEM((2, BLOCK, dim), F32),
        ],
        compiler_params=params(),
        cost_estimate=cost(4 * heads * tok * dim * dim, 16 * heads * tok * dim),
        name="attend",
    )(core, log_decay, gain, keep, recv, *parts)


def inverse_rms(sums_ref, b):
    at = slice(b * BLOCK, (b + 1) * BLOCK)
    inv = lax.rsqrt(sums_ref[0:1, at] / (HEAD_TOTAL * HD) + 1e-06)
    mean = sums_ref[1:2, at] * inv / (HEAD_TOTAL * HD)
    return inv, mean


def norm_grad_kernel(
    core_ref, ld_ref, gain_ref, sums_ref, q0, q1, o0, o1, att0, att1,
    g0, g1, own_ref, send_ref, second_ref, cum, scales, acc,
):
    heads = ld_ref.shape[0]
    half = heads // 2
    step = pl.program_id(0)

    @pl.when(step == 0)
    def _():
        for b in range(2):
            cum[b] = block_cum(ld_ref[:, b * BLOCK : (b + 1) * BLOCK])
            inv, mean = inverse_rms(sums_ref, b)
            scales[b, 0] = as_columns(inv)
            scales[b, 1] = as_columns(inv * inv * mean)

    for i in range(GROUP):
        h = step * GROUP + i
        gain = gain_ref[pl.ds(h, 1), :]
        ends = []
        for b, (q, o, att, g) in enumerate(((q0, o0, att0, g0), (q1, o1, att1, g1))):
            grad = gain * o[i].astype(F32) * scales[b, 0] - att[i] * scales[b, 1]
            grad = grad.astype(BF16)
            g[i] = grad
            queries = q[i].astype(F32).T * jnp.exp(cum[b, pl.ds(h, 1), :])
            ends.append(dot(queries.astype(BF16), grad))
        second_ref[i] = ends[1]
        first_decay = jnp.exp(cum[0, pl.ds(h, 1), :][:, BLOCK - 1 :])
        acc[h] = ends[0] + first_decay * ends[1]

    @pl.when(step == pl.num_programs(0) - 1)
    def _():
        core = core_ref[0]
        own_ref[...] = acc[pl.ds(core * half, half)]
        send_ref[...] = acc[pl.ds((1 - core) * half, half)]


def norm_grad(core, log_decay, gain, sums, parts):
    heads, tok = log_decay.shape
    dim = HD
    half = heads // 2
    whole = lambda *shape: pl.BlockSpec(shape, lambda i: (0,) * len(shape))
    by_head = pl.BlockSpec((GROUP, BLOCK, dim), lambda i: (i, 0, 0))
    head_shape = jax.ShapeDtypeStruct((heads, BLOCK, dim), BF16)
    return pl.pallas_call(
        norm_grad_kernel,
        grid=(heads // GROUP,),
        in_specs=[
            pl.BlockSpec(memory_space=pltpu.SMEM), whole(heads, tok), whole(heads, dim), whole(2, tok),
        ] + [by_head] * 6,
        out_specs=[
            by_head, by_head, whole(half, dim, dim), whole(half, dim, dim),
            pl.BlockSpec((GROUP, dim, dim), lambda i: (i, 0, 0)),
        ],
        out_shape=[
            head_shape, head_shape,
            jax.ShapeDtypeStruct((half, dim, dim), F32),
            jax.ShapeDtypeStruct((half, dim, dim), F32),
            jax.ShapeDtypeStruct((heads, dim, dim), F32),
        ],
        scratch_shapes=[
            pltpu.VMEM((2, heads, BLOCK), F32),
            pltpu.VMEM((2, 2, BLOCK, dim), F32),
            pltpu.VMEM((heads, dim, dim), F32),
        ],
        compiler_params=params(),
        cost_estimate=cost(2 * heads * tok * dim * dim, 14 * heads * tok * dim),
        name="norm_grad",
    )(core, log_decay, gain, sums, *parts)


def normed_kernel(gain_ref, sums_ref, att0, att1, out_ref, rows):
    heads = gain_ref.shape[0]
    b = pl.program_id(0)
    at = pl.multiple_of(b * BLOCK, BLOCK)
    inv = as_columns(lax.rsqrt(sums_ref[0:1, pl.ds(at, BLOCK)] / (HEAD_TOTAL * HD) + 1e-06))
    for index, att in enumerate((att0, att1)):

        @pl.when(b == index)
        def _():
            for h in range(heads):
                rows[pl.ds(h, BLOCK, stride=heads), :] = att[h] * inv * gain_ref[h : h + 1, :]

    out_ref[...] = rows[...].reshape(BLOCK, heads, HD).astype(BF16)


def normed_rows(gain, sums, att0, att1):
    heads, _, dim = att0.shape
    tok = 2 * BLOCK
    whole = lambda *shape: pl.BlockSpec(shape, lambda i: (0,) * len(shape))
    return pl.pallas_call(
        normed_kernel,
        grid=(2,),
        in_specs=[whole(heads, dim), whole(2, tok), whole(heads, BLOCK, dim), whole(heads, BLOCK, dim)],
        out_specs=pl.BlockSpec((BLOCK, heads, dim), lambda i: (i, 0, 0)),
        out_shape=jax.ShapeDtypeStruct((tok, heads, dim), BF16),
        scratch_shapes=[pltpu.VMEM((BLOCK * heads, dim), F32)],
        compiler_params=params(),
        cost_estimate=cost(3 * heads * tok * dim, 6 * heads * tok * dim),
        name="normed_rows",
    )(gain, sums, att0, att1)


def grad_q_kernel(
    core_ref, ld_ref, keep_ref, recv_ref, first_ref, k_ref0, k_ref1, v_ref0, v_ref1, g_ref0, g_ref1,
    out_ref, gs_ref, cum, rows,
):
    heads = ld_ref.shape[0]
    b, group = pl.program_id(0), pl.program_id(1)

    @pl.when((b == 0) & (group == 0))
    def _():
        for x in range(2):
            cum[x] = block_cum(ld_ref[:, x * BLOCK : (x + 1) * BLOCK])

    def work(second, k, v, g):
        for i in range(GROUP):
            h = group * GROUP + i
            row = cum[second, pl.ds(h, 1), :]
            columns = as_columns(row)
            scores = (dot_rows(g[i], v[i]) * decay_matrix(row, columns)).astype(BF16)
            gs_ref[0, i] = scores
            state = whole_state(core_ref[0], keep_ref, recv_ref, group, i)
            if second:
                state = jnp.exp(cum[0, pl.ds(h, 1), :][:, BLOCK - 1 :]) * state + first_ref[i]
            high, low = two_parts(state)
            grad = dot(scores, k[i]) + jnp.exp(columns) * (dot_rows(g[i], high) + dot_rows(g[i], low))
            rows[pl.ds(h, BLOCK, stride=heads), :] = grad

    @pl.when(b == 0)
    def _():
        work(0, k_ref0, v_ref0, g_ref0)

    @pl.when(b == 1)
    def _():
        work(1, k_ref1, v_ref1, g_ref1)

    @pl.when(group == pl.num_programs(1) - 1)
    def _():
        out_ref[...] = rows[...].reshape(BLOCK, heads, HD).astype(BF16)


def two_level():
    return pltpu.CompilerParams(
        dimension_semantics=("arbitrary", "arbitrary"), vmem_limit_bytes=VMEM_LIMIT
    )


def grad_query(core, log_decay, keep, recv, first, k0, k1, v0, v1, g0, g1):
    heads, tok = log_decay.shape
    dim = HD
    groups = heads // GROUP
    whole = lambda *shape: pl.BlockSpec(shape, lambda b, i: (0,) * len(shape))
    head0 = pl.BlockSpec((GROUP, BLOCK, dim), lambda b, i: (jnp.where(b == 0, i, groups - 1), 0, 0))
    head1 = pl.BlockSpec((GROUP, BLOCK, dim), lambda b, i: (jnp.where(b == 0, 0, i), 0, 0))
    return pl.pallas_call(
        grad_q_kernel,
        grid=(2, groups),
        in_specs=[
            pl.BlockSpec(memory_space=pltpu.SMEM), whole(heads, tok),
            whole(heads // 2, dim, dim), whole(heads // 2, dim, dim),
            pl.BlockSpec((GROUP, dim, dim), lambda b, i: (i, 0, 0)),
        ] + [head0, head1] * 3,
        out_specs=[
            pl.BlockSpec((BLOCK, heads, dim), lambda b, i: (b, 0, 0)),
            pl.BlockSpec((1, GROUP, BLOCK, BLOCK), lambda b, i: (b, i, 0, 0)),
        ],
        out_shape=[
            jax.ShapeDtypeStruct((tok, heads, dim), BF16),
            jax.ShapeDtypeStruct((2, heads, BLOCK, BLOCK), BF16),
        ],
        scratch_shapes=[pltpu.VMEM((2, heads, BLOCK), F32), pltpu.VMEM((BLOCK * heads, dim), F32)],
        compiler_params=two_level(),
        cost_estimate=cost(
            4 * heads * tok * dim * (BLOCK + dim), 12 * heads * tok * dim, heads * tok * BLOCK
        ),
        name="grad_query",
    )(core, log_decay, keep, recv, first, k0, k1, v0, v1, g0, g1)


def transposed_dot(a, b):
    return lax.dot_general(a, b, (((0,), (0,)), ((), ())), preferred_element_type=F32)


def grad_kv_kernel(
    ld_ref, gs_ref, w0, w1, q0, q1, k0, v0, g0, g1, second_ref, dk0, dv0, dk1, dv1, cum,
):
    group = pl.program_id(0)

    @pl.when(group == 0)
    def _():
        cum[...] = block_cum(ld_ref[...])

    for i in range(GROUP):
        h = group * GROUP + i
        row = cum[pl.ds(h, 1), :]
        columns = as_columns(jnp.exp(row[:, BLOCK - 1 :] - row))
        high, low = two_parts(second_ref[i])
        dk0[i] = transposed_dot(gs_ref[0, i], q0[i]) + columns * (
            dot_rows(v0[i], high) + dot_rows(v0[i], low)
        )
        dv0[i] = transposed_dot(w0[i], g0[i]) + columns * (dot(k0[i], high) + dot(k0[i], low))
        dk1[i] = transposed_dot(gs_ref[1, i], q1[i])
        dv1[i] = transposed_dot(w1[i], g1[i])


def grad_key_value(log_decay, gs, w0, w1, q0, q1, k0, v0, g0, g1, second):
    heads, tok = log_decay.shape
    dim = HD
    by_head = pl.BlockSpec((GROUP, BLOCK, dim), lambda i: (i, 0, 0))
    square = pl.BlockSpec((GROUP, BLOCK, BLOCK), lambda i: (i, 0, 0))
    return pl.pallas_call(
        grad_kv_kernel,
        grid=(heads // GROUP,),
        in_specs=[
            pl.BlockSpec((heads, BLOCK), lambda i: (0, 0)),
            pl.BlockSpec((2, GROUP, BLOCK, BLOCK), lambda i: (0, i, 0, 0)),
            square, square, by_head, by_head, by_head, by_head, by_head, by_head,
            pl.BlockSpec((GROUP, dim, dim), lambda i: (i, 0, 0)),
        ],
        out_specs=[by_head] * 4,
        out_shape=[jax.ShapeDtypeStruct((heads, BLOCK, dim), F32)] * 4,
        scratch_shapes=[pltpu.VMEM((heads, BLOCK), F32)],
        compiler_params=params(),
        cost_estimate=cost(4 * heads * tok * dim * (BLOCK + dim), 30 * heads * tok * dim),
        name="grad_key_value",
    )(log_decay, gs, w0, w1, q0, q1, k0, v0, g0, g1, second)


def finish_kernel(
    core_ref, ld_ref, keep_ref, recv_ref, k_ref0, k_ref1, v_ref0, v_ref1, dk0, dk1, dv0, dv1,
    out_k, out_v, cum, rows_k, rows_v,
):
    heads = ld_ref.shape[0]
    b, group = pl.program_id(0), pl.program_id(1)

    @pl.when((b == 0) & (group == 0))
    def _():
        for x in range(2):
            cum[x] = block_cum(ld_ref[:, x * BLOCK : (x + 1) * BLOCK])

    def work(second, k, v, dk, dv):
        for i in range(GROUP):
            h = group * GROUP + i
            row = cum[second, pl.ds(h, 1), :]
            left = row[:, BLOCK - 1 :] - row
            if not second:
                left = left + cum[1, pl.ds(h, 1), :][:, BLOCK - 1 :]
            columns = as_columns(jnp.exp(left))
            high, low = two_parts(whole_state(core_ref[0], keep_ref, recv_ref, group, i))
            rows_k[pl.ds(h, BLOCK, stride=heads), :] = dk[i] + columns * (
                dot_rows(v[i], high) + dot_rows(v[i], low)
            )
            rows_v[pl.ds(h, BLOCK, stride=heads), :] = dv[i] + columns * (
                dot(k[i], high) + dot(k[i], low)
            )

    @pl.when(b == 0)
    def _():
        work(0, k_ref0, v_ref0, dk0, dv0)

    @pl.when(b == 1)
    def _():
        work(1, k_ref1, v_ref1, dk1, dv1)

    @pl.when(group == pl.num_programs(1) - 1)
    def _():
        out_k[...] = rows_k[...].reshape(BLOCK, heads, HD).astype(BF16)
        out_v[...] = rows_v[...].reshape(BLOCK, heads, HD).astype(BF16)


def finish(core, log_decay, keep, recv, k0, k1, v0, v1, dk0, dk1, dv0, dv1):
    heads, tok = log_decay.shape
    dim = HD
    groups = heads // GROUP
    whole = lambda *shape: pl.BlockSpec(shape, lambda b, i: (0,) * len(shape))
    head0 = pl.BlockSpec((GROUP, BLOCK, dim), lambda b, i: (jnp.where(b == 0, i, groups - 1), 0, 0))
    head1 = pl.BlockSpec((GROUP, BLOCK, dim), lambda b, i: (jnp.where(b == 0, 0, i), 0, 0))
    raw = pl.BlockSpec((BLOCK, heads, dim), lambda b, i: (b, 0, 0))
    out = jax.ShapeDtypeStruct((tok, heads, dim), BF16)
    return pl.pallas_call(
        finish_kernel,
        grid=(2, groups),
        in_specs=[
            pl.BlockSpec(memory_space=pltpu.SMEM), whole(heads, tok),
            whole(heads // 2, dim, dim), whole(heads // 2, dim, dim),
        ] + [head0, head1] * 4,
        out_specs=[raw, raw],
        out_shape=[out, out],
        scratch_shapes=[
            pltpu.VMEM((2, heads, BLOCK), F32),
            pltpu.VMEM((BLOCK * heads, dim), F32),
            pltpu.VMEM((BLOCK * heads, dim), F32),
        ],
        compiler_params=two_level(),
        cost_estimate=cost(8 * heads * tok * dim * dim, 16 * heads * tok * dim),
        name="finish",
    )(core, log_decay, keep, recv, k0, k1, v0, v1, dk0, dk1, dv0, dv1)


def swap(value, axis, bit):
    count = lax.axis_size(axis)
    return lax.ppermute(value, axis, [(i, i ^ bit) for i in range(count)])


def quad_decays(log_total):
    partner, row_same, row_other = (swap(log_total, "seq", bit) for bit in (1, 2, 3))
    return (
        jnp.exp(log_total), jnp.exp(partner), jnp.exp(log_total + partner),
        jnp.exp(row_same + row_other),
    )


def entering_quad(own, send, decays, backward):
    mine = lax.axis_index("seq")
    core = mine % 2
    half = own.shape[0]
    quarter = half // 2
    bits = [(mine >> at) % 2 for at in range(3)]
    if backward:
        bits = [1 - bit for bit in bits]
    late, right, low = (bit == 1 for bit in bits)
    d_own, d_partner, d_chip, d_row = (
        lax.dynamic_slice_in_dim(part, core * half, half) for part in decays
    )
    one, zero = jnp.ones((quarter,), F32), jnp.zeros((quarter,), F32)
    wide = lambda scale: scale[:, None, None]
    whole_one = jnp.ones((half,), F32)

    got = swap(send, "seq", 1)
    total = wide(jnp.where(late, whole_one, d_partner)) * own + wide(
        jnp.where(late, d_own, whole_one)
    ) * got
    first_total, second_total = total[:quarter], total[quarter:]
    chip_a, chip_b = d_chip[:quarter], d_chip[quarter:]
    row_a, row_b = d_row[:quarter], d_row[quarter:]

    a1 = swap(first_total, "seq", 2)
    b1 = swap(wide(jnp.where(right, one, row_b)) * second_total, "seq", 4)
    a2 = swap(
        wide(jnp.where(right, one, row_a)) * first_total + wide(jnp.where(right, chip_a, one)) * a1,
        "seq", 4,
    )
    b2 = swap(
        wide(jnp.where(low & right, zero, one)) * second_total
        + wide(jnp.where(low, jnp.where(right, one, chip_b), zero)) * b1,
        "seq", 2,
    )
    enter_a = (
        wide(jnp.where(low, jnp.where(right, row_a, one), zero)) * a2
        + wide(jnp.where(right, one, zero)) * a1
    )
    enter_b = (
        wide(jnp.where(low, jnp.where(right, row_b, one), zero)) * b1
        + wide(jnp.where(low | right, one, zero)) * b2
    )
    enter = jnp.concatenate([enter_a, enter_b], axis=0)
    after = wide(jnp.where(late, d_partner, d_own)) * enter + jnp.where(late, got, own)
    kept = jnp.where(late, after, enter)
    sent = jnp.where(late, enter, after)
    return kept, swap(sent, "seq", 1)


def entering_any(own, send, log_total, backward):
    count, mine = lax.axis_size("seq"), lax.axis_index("seq")
    core = mine % 2
    half = own.shape[0]
    in_order = jnp.where(
        core == 0, jnp.concatenate([own, send], axis=0), jnp.concatenate([send, own], axis=0)
    )
    states = lax.all_gather(in_order, "seq")
    decays = jnp.exp(lax.all_gather(log_total, "seq"))
    place = mine
    if backward:
        states, decays, place = states[::-1], decays[::-1], count - 1 - mine

    def step(at, total):
        longer = decays[at][:, None, None] * total + states[at]
        return jnp.where(at < place, longer, total)

    total = lax.fori_loop(0, count - 1, step, jnp.zeros_like(in_order))
    kept = lax.dynamic_slice_in_dim(total, core * half, half)
    return kept, lax.dynamic_slice_in_dim(total, (1 - core) * half, half)


def sum_over_heads(value):
    count = lax.axis_size("head")
    total = value
    for shift in range(1, count):
        total = total + lax.ppermute(
            value, "head", [(i, (i + shift) % count) for i in range(count)]
        )
    return total


def on_device(query_rows, key_rows, value_rows, output_grad, norm_gain, log_decay):
    core = (lax.axis_index("seq") % 2).astype(jnp.int32).reshape(1)
    log_total = jnp.sum(log_decay, axis=1)
    if lax.axis_size("seq") == 8:
        decays = quad_decays(log_total)
        entering = lambda own, send, backward: entering_quad(own, send, decays, backward)
    else:
        entering = lambda own, send, backward: entering_any(own, send, log_total, backward)

    own, send, first = local_state(core, log_decay, key_rows, value_rows)
    keep, recv = entering(own, send, False)
    q0, k0, v0, o0, w0, inner0 = intra(
        0, log_decay, query_rows, key_rows, value_rows, output_grad, first
    )
    q1, k1, v1, o1, w1, inner1 = intra(
        1, log_decay, query_rows, key_rows, value_rows, output_grad, first
    )
    att0, att1, sums = attend(
        core, log_decay, norm_gain, keep, recv, (q0, q1, o0, o1, inner0, inner1)
    )
    sums = sum_over_heads(sums)
    g0, g1, grad_own, grad_send, second = norm_grad(
        core, log_decay, norm_gain, sums, (q0, q1, o0, o1, att0, att1)
    )
    grad_keep, grad_recv = entering(grad_own, grad_send, True)
    normed = normed_rows(norm_gain, sums, att0, att1)
    grad_q, scores = grad_query(core, log_decay, keep, recv, first, k0, k1, v0, v1, g0, g1)
    dk0, dv0, dk1, dv1 = grad_key_value(
        log_decay, scores, w0, w1, q0, q1, k0, v0, g0, g1, second
    )
    grad_k, grad_v = finish(
        core, log_decay, grad_keep, grad_recv, k0, k1, v0, v1, dk0, dk1, dv0, dv1
    )
    return normed, grad_q, grad_k, grad_v


def solution(mesh):
    rows = P("seq", "head", None)
    return jax.shard_map(
        on_device,
        mesh=mesh,
        in_specs=(rows, rows, rows, rows, P("head", None), P("head", "seq")),
        out_specs=(rows, rows, rows, rows),
        check_vma=False,
    )
```

```python
import functools

import jax
import jax.numpy as jnp
from jax import lax
from jax.experimental import pallas as pl
from jax.experimental.pallas import tpu as pltpu
from jax.sharding import PartitionSpec as P

HEAD_TOTAL = 64
HD = 128
BLOCK = 256
GROUP = 4
STEP_TOK = 128
F32 = jnp.float32
BF16 = jnp.bfloat16
MIB = 1024 * 1024


def params(mib):
    return pltpu.CompilerParams(dimension_semantics=("arbitrary",), vmem_limit_bytes=mib * MIB)


def cost(flops, moved, exps=0):
    return pl.CostEstimate(flops=flops, bytes_accessed=moved, transcendentals=exps)


def block_cum(log_decay):
    size = log_decay.shape[1]
    upper = lax.broadcasted_iota(jnp.int32, (size, size), 0) <= lax.broadcasted_iota(
        jnp.int32, (size, size), 1
    )
    return jnp.dot(
        log_decay,
        jnp.where(upper, 1.0, 0.0).astype(F32),
        precision=lax.Precision.HIGHEST,
        preferred_element_type=F32,
    )


def as_columns(row):
    return jnp.broadcast_to(row, (HD, row.shape[1])).T


def dot(a, b):
    return jnp.dot(a, b, preferred_element_type=F32)


def dot_rows(a, b):
    return lax.dot_general(a, b, (((1,), (1,)), ((), ())), preferred_element_type=F32)


def two_parts(matrix):
    high = matrix.astype(BF16)
    return high, (matrix - high.astype(F32)).astype(BF16)


def decay_matrix(row, columns):
    size = row.shape[1]
    lower = lax.broadcasted_iota(jnp.int32, (size, size), 0) >= lax.broadcasted_iota(
        jnp.int32, (size, size), 1
    )
    both = jnp.concatenate([columns] * (size // HD), axis=1)
    return jnp.exp(jnp.where(lower, both - row, -jnp.inf))


def to_rows(dst, block):
    tok, heads, dim = block.shape
    dst[...] = block[...].astype(F32).reshape(tok * heads, dim)


def head_rows(ref, head, heads, tok):
    return ref[pl.ds(head, tok, stride=heads), :]


def state_kernel(core_ref, ld_ref, k_ref, v_ref, own_ref, send_ref, first_ref, kx, vx, cum, acc):
    heads = ld_ref.shape[0]
    step = pl.program_id(0)
    per_block = BLOCK // STEP_TOK
    half = heads // 2

    @pl.when(step == 0)
    def _():
        for b in range(2):
            cum[b] = block_cum(ld_ref[:, b * BLOCK : (b + 1) * BLOCK])
        acc[...] = jnp.zeros_like(acc)

    to_rows(kx, k_ref)
    to_rows(vx, v_ref)
    b = step // per_block
    at = pl.multiple_of((step % per_block) * STEP_TOK, STEP_TOK)
    ends = cum[b, :, BLOCK - 1 : BLOCK]
    scale = jnp.exp(ends - cum[b, :, pl.ds(at, STEP_TOK)])
    for h in range(heads):
        keys = head_rows(kx, h, heads, STEP_TOK).T * scale[h : h + 1]
        values = head_rows(vx, h, heads, STEP_TOK).astype(BF16)
        acc[b, h] += dot(keys.astype(BF16), values)

    @pl.when(step == 2 * per_block - 1)
    def _():
        first_ref[...] = acc[0]
        last = jnp.exp(cum[1, :, BLOCK - 1 : BLOCK])
        for h in range(heads):
            acc[1, h] += last[h : h + 1, :] * acc[0, h]
        core = core_ref[0]
        own_ref[...] = acc[1, pl.ds(core * half, half)]
        send_ref[...] = acc[1, pl.ds((1 - core) * half, half)]


def local_state(core, log_decay, key_rows, value_rows):
    tok, heads, dim = key_rows.shape
    half = heads // 2
    raw = pl.BlockSpec((STEP_TOK, heads, dim), lambda i: (i, 0, 0))
    whole = lambda *shape: pl.BlockSpec(shape, lambda i: (0,) * len(shape))
    return pl.pallas_call(
        state_kernel,
        grid=(tok // STEP_TOK,),
        in_specs=[pl.BlockSpec(memory_space=pltpu.SMEM), whole(heads, tok), raw, raw],
        out_specs=[whole(half, dim, dim), whole(half, dim, dim), whole(heads, dim, dim)],
        out_shape=[
            jax.ShapeDtypeStruct((half, dim, dim), F32),
            jax.ShapeDtypeStruct((half, dim, dim), F32),
            jax.ShapeDtypeStruct((heads, dim, dim), F32),
        ],
        scratch_shapes=[
            pltpu.VMEM((STEP_TOK * heads, dim), F32),
            pltpu.VMEM((STEP_TOK * heads, dim), F32),
            pltpu.VMEM((2, heads, BLOCK), F32),
            pltpu.VMEM((2, heads, dim, dim), F32),
        ],
        compiler_params=params(16),
        cost_estimate=cost(2 * tok * heads * dim * dim, 4 * tok * heads * dim),
        name="local_state",
    )(core, log_decay, key_rows, value_rows)


def intra_kernel(
    second, ld_ref, q_ref, k_ref, v_ref, o_ref, first_ref,
    qh_ref, kh_ref, vh_ref, oh_ref, w_ref, inner_ref, qx, kx, vx, ox, cum,
):
    heads = ld_ref.shape[0]
    step = pl.program_id(0)

    @pl.when(step == 0)
    def _():
        cum[...] = block_cum(ld_ref[...])
        to_rows(qx, q_ref)
        to_rows(kx, k_ref)
        to_rows(vx, v_ref)
        to_rows(ox, o_ref)

    for i in range(GROUP):
        h = step * GROUP + i
        query = head_rows(qx, h, heads, BLOCK).astype(BF16)
        key = head_rows(kx, h, heads, BLOCK).astype(BF16)
        value = head_rows(vx, h, heads, BLOCK).astype(BF16)
        qh_ref[i] = query
        kh_ref[i] = key
        vh_ref[i] = value
        oh_ref[i] = head_rows(ox, h, heads, BLOCK).astype(BF16)
        row = cum[pl.ds(h, 1), :]
        columns = as_columns(row)
        weights = (dot_rows(query, key) * decay_matrix(row, columns)).astype(BF16)
        w_ref[i] = weights
        inner = dot(weights, value)
        if second:
            high, low = two_parts(first_ref[i])
            inner += jnp.exp(columns) * (dot(query, high) + dot(query, low))
        inner_ref[i] = inner


def intra(index, log_decay, query_rows, key_rows, value_rows, output_grad, first):
    tok, heads, dim = key_rows.shape
    raw = pl.BlockSpec((BLOCK, heads, dim), lambda i: (index, 0, 0))
    by_head = pl.BlockSpec((GROUP, BLOCK, dim), lambda i: (i, 0, 0))
    head_shape = jax.ShapeDtypeStruct((heads, BLOCK, dim), BF16)
    return pl.pallas_call(
        functools.partial(intra_kernel, index > 0),
        grid=(heads // GROUP,),
        in_specs=[
            pl.BlockSpec((heads, BLOCK), lambda i: (0, index)),
            raw, raw, raw, raw,
            pl.BlockSpec((GROUP, dim, dim), lambda i: (i, 0, 0)),
        ],
        out_specs=[by_head] * 4 + [pl.BlockSpec((GROUP, BLOCK, BLOCK), lambda i: (i, 0, 0)), by_head],
        out_shape=[head_shape] * 4 + [
            jax.ShapeDtypeStruct((heads, BLOCK, BLOCK), BF16),
            jax.ShapeDtypeStruct((heads, BLOCK, dim), F32),
        ],
        scratch_shapes=[pltpu.VMEM((BLOCK * heads, dim), F32)] * 4 + [pltpu.VMEM((heads, BLOCK), F32)],
        compiler_params=params(24),
        cost_estimate=cost(
            2 * heads * BLOCK * BLOCK * dim * 4, 20 * heads * BLOCK * dim, heads * BLOCK * BLOCK
        ),
        name=f"intra_{index}",
    )(log_decay, query_rows, key_rows, value_rows, output_grad, first)


def whole_state(core, keep_ref, recv_ref, group, i):
    half = keep_ref.shape[0]
    head = group * GROUP + i
    mine = (head // half) == core
    return jnp.where(mine, keep_ref[head % half], recv_ref[head % half])


def attend_kernel(
    core_ref, ld_ref, gain_ref, keep_ref, recv_ref, q0, q1, o0, o1, inner0, inner1,
    att0, att1, sums_ref, cum, squares, products,
):
    step = pl.program_id(0)
    steps = pl.num_programs(0)

    @pl.when(step == 0)
    def _():
        cum[0] = block_cum(ld_ref[:, :BLOCK])
        cum[1] = cum[0, :, BLOCK - 1 : BLOCK] + block_cum(ld_ref[:, BLOCK:])
        squares[...] = jnp.zeros_like(squares)
        products[...] = jnp.zeros_like(products)

    for i in range(GROUP):
        h = step * GROUP + i
        high, low = two_parts(whole_state(core_ref[0], keep_ref, recv_ref, step, i))
        gain = gain_ref[pl.ds(h, 1), :]
        for b, (q, o, inner, att) in enumerate(((q0, o0, inner0, att0), (q1, o1, inner1, att1))):
            columns = jnp.exp(as_columns(cum[b, pl.ds(h, 1), :]))
            attended = inner[i] + columns * (dot(q[i], high) + dot(q[i], low))
            att[i] = attended
            squares[b] += attended * attended
            products[b] += gain * o[i].astype(F32) * attended

    @pl.when(step == steps - 1)
    def _():
        ones = jnp.ones((8, HD), F32)
        for b in range(2):
            for at, total in enumerate((squares, products)):
                line = lax.dot_general(
                    ones, total[b], (((1,), (1,)), ((), ())),
                    precision=lax.Precision.HIGHEST, preferred_element_type=F32,
                )
                sums_ref[at : at + 1, b * BLOCK : (b + 1) * BLOCK] = line[:1]


def attend(core, log_decay, gain, keep, recv, parts):
    heads, tok = log_decay.shape
    dim = HD
    whole = lambda *shape: pl.BlockSpec(shape, lambda i: (0,) * len(shape))
    by_head = pl.BlockSpec((GROUP, BLOCK, dim), lambda i: (i, 0, 0))
    head_shape = jax.ShapeDtypeStruct((heads, BLOCK, dim), F32)
    return pl.pallas_call(
        attend_kernel,
        grid=(heads // GROUP,),
        in_specs=[pl.BlockSpec(memory_space=pltpu.SMEM), whole(heads, tok), whole(heads, dim)]
        + [whole(heads // 2, dim, dim)] * 2 + [by_head] * 6,
        out_specs=[by_head, by_head, whole(2, tok)],
        out_shape=[head_shape, head_shape, jax.ShapeDtypeStruct((2, tok), F32)],
        scratch_shapes=[
            pltpu.VMEM((2, heads, BLOCK), F32),
            pltpu.VMEM((2, BLOCK, dim), F32),
            pltpu.VMEM((2, BLOCK, dim), F32),
        ],
        compiler_params=params(16),
        cost_estimate=cost(4 * heads * tok * dim * dim, 16 * heads * tok * dim),
        name="attend",
    )(core, log_decay, gain, keep, recv, *parts)


def inverse_rms(sums_ref, b):
    at = slice(b * BLOCK, (b + 1) * BLOCK)
    inv = lax.rsqrt(sums_ref[0:1, at] / (HEAD_TOTAL * HD) + 1e-06)
    mean = sums_ref[1:2, at] * inv / (HEAD_TOTAL * HD)
    return inv, mean


def norm_grad_kernel(
    core_ref, ld_ref, gain_ref, sums_ref, q0, q1, o0, o1, att0, att1,
    g0, g1, own_ref, send_ref, second_ref, cum, scales, acc,
):
    heads = ld_ref.shape[0]
    half = heads // 2
    step = pl.program_id(0)

    @pl.when(step == 0)
    def _():
        for b in range(2):
            cum[b] = block_cum(ld_ref[:, b * BLOCK : (b + 1) * BLOCK])
            inv, mean = inverse_rms(sums_ref, b)
            scales[b, 0] = as_columns(inv)
            scales[b, 1] = as_columns(inv * inv * mean)

    for i in range(GROUP):
        h = step * GROUP + i
        gain = gain_ref[pl.ds(h, 1), :]
        ends = []
        for b, (q, o, att, g) in enumerate(((q0, o0, att0, g0), (q1, o1, att1, g1))):
            grad = gain * o[i].astype(F32) * scales[b, 0] - att[i] * scales[b, 1]
            grad = grad.astype(BF16)
            g[i] = grad
            queries = q[i].astype(F32).T * jnp.exp(cum[b, pl.ds(h, 1), :])
            ends.append(dot(queries.astype(BF16), grad))
        second_ref[i] = ends[1]
        first_decay = jnp.exp(cum[0, pl.ds(h, 1), :][:, BLOCK - 1 :])
        acc[h] = ends[0] + first_decay * ends[1]

    @pl.when(step == pl.num_programs(0) - 1)
    def _():
        core = core_ref[0]
        own_ref[...] = acc[pl.ds(core * half, half)]
        send_ref[...] = acc[pl.ds((1 - core) * half, half)]


def norm_grad(core, log_decay, gain, sums, parts):
    heads, tok = log_decay.shape
    dim = HD
    half = heads // 2
    whole = lambda *shape: pl.BlockSpec(shape, lambda i: (0,) * len(shape))
    by_head = pl.BlockSpec((GROUP, BLOCK, dim), lambda i: (i, 0, 0))
    head_shape = jax.ShapeDtypeStruct((heads, BLOCK, dim), BF16)
    return pl.pallas_call(
        norm_grad_kernel,
        grid=(heads // GROUP,),
        in_specs=[
            pl.BlockSpec(memory_space=pltpu.SMEM), whole(heads, tok), whole(heads, dim), whole(2, tok),
        ] + [by_head] * 6,
        out_specs=[
            by_head, by_head, whole(half, dim, dim), whole(half, dim, dim),
            pl.BlockSpec((GROUP, dim, dim), lambda i: (i, 0, 0)),
        ],
        out_shape=[
            head_shape, head_shape,
            jax.ShapeDtypeStruct((half, dim, dim), F32),
            jax.ShapeDtypeStruct((half, dim, dim), F32),
            jax.ShapeDtypeStruct((heads, dim, dim), F32),
        ],
        scratch_shapes=[
            pltpu.VMEM((2, heads, BLOCK), F32),
            pltpu.VMEM((2, 2, BLOCK, dim), F32),
            pltpu.VMEM((heads, dim, dim), F32),
        ],
        compiler_params=params(16),
        cost_estimate=cost(2 * heads * tok * dim * dim, 14 * heads * tok * dim),
        name="norm_grad",
    )(core, log_decay, gain, sums, *parts)


def normed_kernel(gain_ref, sums_ref, att0, att1, out_ref, rows):
    heads = gain_ref.shape[0]
    b = pl.program_id(0)
    at = pl.multiple_of(b * BLOCK, BLOCK)
    inv = as_columns(lax.rsqrt(sums_ref[0:1, pl.ds(at, BLOCK)] / (HEAD_TOTAL * HD) + 1e-06))
    for index, att in enumerate((att0, att1)):

        @pl.when(b == index)
        def _():
            for h in range(heads):
                rows[pl.ds(h, BLOCK, stride=heads), :] = att[h] * inv * gain_ref[h : h + 1, :]

    out_ref[...] = rows[...].reshape(BLOCK, heads, HD).astype(BF16)


def normed_rows(gain, sums, att0, att1):
    heads, _, dim = att0.shape
    tok = 2 * BLOCK
    whole = lambda *shape: pl.BlockSpec(shape, lambda i: (0,) * len(shape))
    return pl.pallas_call(
        normed_kernel,
        grid=(2,),
        in_specs=[whole(heads, dim), whole(2, tok), whole(heads, BLOCK, dim), whole(heads, BLOCK, dim)],
        out_specs=pl.BlockSpec((BLOCK, heads, dim), lambda i: (i, 0, 0)),
        out_shape=jax.ShapeDtypeStruct((tok, heads, dim), BF16),
        scratch_shapes=[pltpu.VMEM((BLOCK * heads, dim), F32)],
        compiler_params=params(16),
        cost_estimate=cost(3 * heads * tok * dim, 6 * heads * tok * dim),
        name="normed_rows",
    )(gain, sums, att0, att1)


def grad_q_kernel(
    core_ref, ld_ref, keep_ref, recv_ref, first_ref, k_ref0, k_ref1, v_ref0, v_ref1, g_ref0, g_ref1,
    out_ref, gs_ref, cum, rows,
):
    heads = ld_ref.shape[0]
    b, group = pl.program_id(0), pl.program_id(1)

    @pl.when((b == 0) & (group == 0))
    def _():
        for x in range(2):
            cum[x] = block_cum(ld_ref[:, x * BLOCK : (x + 1) * BLOCK])

    def work(second, k, v, g):
        for i in range(GROUP):
            h = group * GROUP + i
            row = cum[second, pl.ds(h, 1), :]
            columns = as_columns(row)
            scores = (dot_rows(g[i], v[i]) * decay_matrix(row, columns)).astype(BF16)
            gs_ref[0, i] = scores
            state = whole_state(core_ref[0], keep_ref, recv_ref, group, i)
            if second:
                state = jnp.exp(cum[0, pl.ds(h, 1), :][:, BLOCK - 1 :]) * state + first_ref[i]
            high, low = two_parts(state)
            grad = dot(scores, k[i]) + jnp.exp(columns) * (dot_rows(g[i], high) + dot_rows(g[i], low))
            rows[pl.ds(h, BLOCK, stride=heads), :] = grad

    @pl.when(b == 0)
    def _():
        work(0, k_ref0, v_ref0, g_ref0)

    @pl.when(b == 1)
    def _():
        work(1, k_ref1, v_ref1, g_ref1)

    @pl.when(group == pl.num_programs(1) - 1)
    def _():
        out_ref[...] = rows[...].reshape(BLOCK, heads, HD).astype(BF16)


def two_level(mib):
    return pltpu.CompilerParams(
        dimension_semantics=("arbitrary", "arbitrary"), vmem_limit_bytes=mib * MIB
    )


def grad_query(core, log_decay, keep, recv, first, k0, k1, v0, v1, g0, g1):
    heads, tok = log_decay.shape
    dim = HD
    groups = heads // GROUP
    whole = lambda *shape: pl.BlockSpec(shape, lambda b, i: (0,) * len(shape))
    head0 = pl.BlockSpec((GROUP, BLOCK, dim), lambda b, i: (jnp.where(b == 0, i, groups - 1), 0, 0))
    head1 = pl.BlockSpec((GROUP, BLOCK, dim), lambda b, i: (jnp.where(b == 0, 0, i), 0, 0))
    return pl.pallas_call(
        grad_q_kernel,
        grid=(2, groups),
        in_specs=[
            pl.BlockSpec(memory_space=pltpu.SMEM), whole(heads, tok),
            whole(heads // 2, dim, dim), whole(heads // 2, dim, dim),
            pl.BlockSpec((GROUP, dim, dim), lambda b, i: (i, 0, 0)),
        ] + [head0, head1] * 3,
        out_specs=[
            pl.BlockSpec((BLOCK, heads, dim), lambda b, i: (b, 0, 0)),
            pl.BlockSpec((1, GROUP, BLOCK, BLOCK), lambda b, i: (b, i, 0, 0)),
        ],
        out_shape=[
            jax.ShapeDtypeStruct((tok, heads, dim), BF16),
            jax.ShapeDtypeStruct((2, heads, BLOCK, BLOCK), BF16),
        ],
        scratch_shapes=[pltpu.VMEM((2, heads, BLOCK), F32), pltpu.VMEM((BLOCK * heads, dim), F32)],
        compiler_params=two_level(16),
        cost_estimate=cost(
            4 * heads * tok * dim * (BLOCK + dim), 12 * heads * tok * dim, heads * tok * BLOCK
        ),
        name="grad_query",
    )(core, log_decay, keep, recv, first, k0, k1, v0, v1, g0, g1)


def transposed_dot(a, b):
    return lax.dot_general(a, b, (((0,), (0,)), ((), ())), preferred_element_type=F32)


def grad_kv_kernel(
    ld_ref, gs_ref, w0, w1, q0, q1, k0, v0, g0, g1, second_ref, dk0, dv0, dk1, dv1, cum,
):
    group = pl.program_id(0)

    @pl.when(group == 0)
    def _():
        cum[...] = block_cum(ld_ref[...])

    for i in range(GROUP):
        h = group * GROUP + i
        row = cum[pl.ds(h, 1), :]
        columns = as_columns(jnp.exp(row[:, BLOCK - 1 :] - row))
        high, low = two_parts(second_ref[i])
        dk0[i] = transposed_dot(gs_ref[0, i], q0[i]) + columns * (
            dot_rows(v0[i], high) + dot_rows(v0[i], low)
        )
        dv0[i] = transposed_dot(w0[i], g0[i]) + columns * (dot(k0[i], high) + dot(k0[i], low))
        dk1[i] = transposed_dot(gs_ref[1, i], q1[i])
        dv1[i] = transposed_dot(w1[i], g1[i])


def grad_key_value(log_decay, gs, w0, w1, q0, q1, k0, v0, g0, g1, second):
    heads, tok = log_decay.shape
    dim = HD
    by_head = pl.BlockSpec((GROUP, BLOCK, dim), lambda i: (i, 0, 0))
    square = pl.BlockSpec((GROUP, BLOCK, BLOCK), lambda i: (i, 0, 0))
    return pl.pallas_call(
        grad_kv_kernel,
        grid=(heads // GROUP,),
        in_specs=[
            pl.BlockSpec((heads, BLOCK), lambda i: (0, 0)),
            pl.BlockSpec((2, GROUP, BLOCK, BLOCK), lambda i: (0, i, 0, 0)),
            square, square, by_head, by_head, by_head, by_head, by_head, by_head,
            pl.BlockSpec((GROUP, dim, dim), lambda i: (i, 0, 0)),
        ],
        out_specs=[by_head] * 4,
        out_shape=[jax.ShapeDtypeStruct((heads, BLOCK, dim), F32)] * 4,
        scratch_shapes=[pltpu.VMEM((heads, BLOCK), F32)],
        compiler_params=params(16),
        cost_estimate=cost(4 * heads * tok * dim * (BLOCK + dim), 30 * heads * tok * dim),
        name="grad_key_value",
    )(log_decay, gs, w0, w1, q0, q1, k0, v0, g0, g1, second)


def finish_kernel(
    core_ref, ld_ref, keep_ref, recv_ref, k_ref0, k_ref1, v_ref0, v_ref1, dk0, dk1, dv0, dv1,
    out_k, out_v, cum, rows_k, rows_v,
):
    heads = ld_ref.shape[0]
    b, group = pl.program_id(0), pl.program_id(1)

    @pl.when((b == 0) & (group == 0))
    def _():
        for x in range(2):
            cum[x] = block_cum(ld_ref[:, x * BLOCK : (x + 1) * BLOCK])

    def work(second, k, v, dk, dv):
        for i in range(GROUP):
            h = group * GROUP + i
            row = cum[second, pl.ds(h, 1), :]
            left = row[:, BLOCK - 1 :] - row
            if not second:
                left = left + cum[1, pl.ds(h, 1), :][:, BLOCK - 1 :]
            columns = as_columns(jnp.exp(left))
            high, low = two_parts(whole_state(core_ref[0], keep_ref, recv_ref, group, i))
            rows_k[pl.ds(h, BLOCK, stride=heads), :] = dk[i] + columns * (
                dot_rows(v[i], high) + dot_rows(v[i], low)
            )
            rows_v[pl.ds(h, BLOCK, stride=heads), :] = dv[i] + columns * (
                dot(k[i], high) + dot(k[i], low)
            )

    @pl.when(b == 0)
    def _():
        work(0, k_ref0, v_ref0, dk0, dv0)

    @pl.when(b == 1)
    def _():
        work(1, k_ref1, v_ref1, dk1, dv1)

    @pl.when(group == pl.num_programs(1) - 1)
    def _():
        out_k[...] = rows_k[...].reshape(BLOCK, heads, HD).astype(BF16)
        out_v[...] = rows_v[...].reshape(BLOCK, heads, HD).astype(BF16)


def finish(core, log_decay, keep, recv, k0, k1, v0, v1, dk0, dk1, dv0, dv1):
    heads, tok = log_decay.shape
    dim = HD
    groups = heads // GROUP
    whole = lambda *shape: pl.BlockSpec(shape, lambda b, i: (0,) * len(shape))
    head0 = pl.BlockSpec((GROUP, BLOCK, dim), lambda b, i: (jnp.where(b == 0, i, groups - 1), 0, 0))
    head1 = pl.BlockSpec((GROUP, BLOCK, dim), lambda b, i: (jnp.where(b == 0, 0, i), 0, 0))
    raw = pl.BlockSpec((BLOCK, heads, dim), lambda b, i: (b, 0, 0))
    out = jax.ShapeDtypeStruct((tok, heads, dim), BF16)
    return pl.pallas_call(
        finish_kernel,
        grid=(2, groups),
        in_specs=[
            pl.BlockSpec(memory_space=pltpu.SMEM), whole(heads, tok),
            whole(heads // 2, dim, dim), whole(heads // 2, dim, dim),
        ] + [head0, head1] * 4,
        out_specs=[raw, raw],
        out_shape=[out, out],
        scratch_shapes=[
            pltpu.VMEM((2, heads, BLOCK), F32),
            pltpu.VMEM((BLOCK * heads, dim), F32),
            pltpu.VMEM((BLOCK * heads, dim), F32),
        ],
        compiler_params=two_level(16),
        cost_estimate=cost(8 * heads * tok * dim * dim, 16 * heads * tok * dim),
        name="finish",
    )(core, log_decay, keep, recv, k0, k1, v0, v1, dk0, dk1, dv0, dv1)


def swap(value, axis, bit):
    count = lax.axis_size(axis)
    return lax.ppermute(value, axis, [(i, i ^ bit) for i in range(count)])


def quad_decays(log_total):
    partner, row_same, row_other = (swap(log_total, "seq", bit) for bit in (1, 2, 3))
    return (
        jnp.exp(log_total), jnp.exp(partner), jnp.exp(log_total + partner),
        jnp.exp(row_same + row_other),
    )


def entering_quad(own, send, decays, backward, tasks):
    def work(stage, after, before=()):
        if stage not in tasks:
            return before
        run, outputs = tasks[stage]
        outputs.extend(run(after))
        return lax.optimization_barrier((before, outputs[-1]))[0]

    mine = lax.axis_index("seq")
    core = mine % 2
    half = own.shape[0]
    quarter = half // 2
    bits = [(mine >> at) % 2 for at in range(3)]
    if backward:
        bits = [1 - bit for bit in bits]
    late, right, low = (bit == 1 for bit in bits)
    d_own, d_partner, d_chip, d_row = (
        lax.dynamic_slice_in_dim(part, core * half, half) for part in decays
    )
    one, zero = jnp.ones((quarter,), F32), jnp.zeros((quarter,), F32)
    wide = lambda scale: scale[:, None, None]
    whole_one = jnp.ones((half,), F32)

    got = swap(send, "seq", 1)
    work(0, got)
    total = wide(jnp.where(late, whole_one, d_partner)) * own + wide(
        jnp.where(late, d_own, whole_one)
    ) * got
    first_total, second_total = total[:quarter], total[quarter:]
    chip_a, chip_b = d_chip[:quarter], d_chip[quarter:]
    row_a, row_b = d_row[:quarter], d_row[quarter:]

    b0 = wide(jnp.where(right, one, row_b)) * second_total
    a0, b0, total, = lax.optimization_barrier((first_total, b0, total))
    a1 = swap(a0, "seq", 2)
    b1 = swap(b0, "seq", 4)
    a1, b1 = work(1, total, (a1, b1))
    a2 = wide(jnp.where(right, one, row_a)) * first_total + wide(jnp.where(right, chip_a, one)) * a1
    b2 = (
        wide(jnp.where(low & right, zero, one)) * second_total
        + wide(jnp.where(low, jnp.where(right, one, chip_b), zero)) * b1
    )
    a2, b2 = lax.optimization_barrier((a2, b2))
    sent = a2
    a2 = swap(a2, "seq", 4)
    b2 = swap(b2, "seq", 2)
    a2, b2 = work(2, sent, (a2, b2))
    enter_a = (
        wide(jnp.where(low, jnp.where(right, row_a, one), zero)) * a2
        + wide(jnp.where(right, one, zero)) * a1
    )
    enter_b = (
        wide(jnp.where(low, jnp.where(right, row_b, one), zero)) * b1
        + wide(jnp.where(low | right, one, zero)) * b2
    )
    enter = jnp.concatenate([enter_a, enter_b], axis=0)
    after = wide(jnp.where(late, d_partner, d_own)) * enter + jnp.where(late, got, own)
    kept = jnp.where(late, after, enter)
    sent = jnp.where(late, enter, after)
    received = swap(sent, "seq", 1)
    work(3, sent)
    return kept, received


def entering_any(own, send, log_total, backward, tasks):
    for run, outputs in tasks.values():
        outputs.extend(run(send))
    count, mine = lax.axis_size("seq"), lax.axis_index("seq")
    core = mine % 2
    half = own.shape[0]
    in_order = jnp.where(
        core == 0, jnp.concatenate([own, send], axis=0), jnp.concatenate([send, own], axis=0)
    )
    states = lax.all_gather(in_order, "seq")
    decays = jnp.exp(lax.all_gather(log_total, "seq"))
    place = mine
    if backward:
        states, decays, place = states[::-1], decays[::-1], count - 1 - mine

    def step(at, total):
        longer = decays[at][:, None, None] * total + states[at]
        return jnp.where(at < place, longer, total)

    total = lax.fori_loop(0, count - 1, step, jnp.zeros_like(in_order))
    kept = lax.dynamic_slice_in_dim(total, core * half, half)
    return kept, lax.dynamic_slice_in_dim(total, (1 - core) * half, half)


def sum_over_heads(value):
    count = lax.axis_size("head")
    reach = 1
    while 2 * reach <= count and count % (2 * reach) == 0:
        value = value + swap(value, "head", reach)
        reach *= 2
    part = value
    for shift in range(1, count // reach):
        value = value + lax.ppermute(
            part, "head", [(i, (i + shift * reach) % count) for i in range(count)]
        )
    return value


def follows(value, earlier):
    return lax.optimization_barrier((value, earlier))[0]


def on_device(query_rows, key_rows, value_rows, output_grad, norm_gain, log_decay):
    core = (lax.axis_index("seq") % 2).astype(jnp.int32).reshape(1)
    log_total = jnp.sum(log_decay, axis=1)
    if lax.axis_size("seq") == 8:
        decays = quad_decays(log_total)
        entering = lambda own, send, backward, tasks: entering_quad(
            own, send, decays, backward, tasks
        )
    else:
        entering = lambda own, send, backward, tasks: entering_any(
            own, send, log_total, backward, tasks
        )

    query_rows, key_rows, value_rows, output_grad = (
        pltpu.with_memory_space_constraint(rows, pltpu.HBM)
        for rows in (query_rows, key_rows, value_rows, output_grad)
    )
    own, send, first = local_state(
        core, pltpu.with_memory_space_constraint(log_decay, pltpu.HBM), key_rows, value_rows
    )

    def forward_task(index):
        return lambda earlier: intra(
            index, log_decay, query_rows, key_rows, value_rows, output_grad, follows(first, earlier)
        )

    in_0, in_1 = [], []
    keep, recv = entering(
        own, send, False, {1: (forward_task(0), in_0), 2: (forward_task(1), in_1)}
    )
    q0, k0, v0, o0, w0, inner0 = in_0
    q1, k1, v1, o1, w1, inner1 = in_1
    att0, att1, sums = attend(
        core, log_decay, norm_gain, keep, recv, (q0, q1, o0, o1, inner0, inner1)
    )
    sums = sum_over_heads(sums)
    g0, g1, grad_own, grad_send, second = norm_grad(
        core, log_decay, norm_gain, sums, (q0, q1, o0, o1, att0, att1)
    )
    queries, keys, norms = [], [], []

    def query_task(earlier):
        return grad_query(
            core, log_decay, keep, recv, follows(first, earlier), k0, k1, v0, v1, g0, g1
        )

    def key_task(earlier):
        return grad_key_value(
            log_decay, queries[1], w0, w1, q0, q1, k0, v0, g0, g1, follows(second, earlier)
        )

    def norm_task(earlier):
        return [normed_rows(follows(norm_gain, earlier), sums, att0, att1)]

    grad_keep, grad_recv = entering(
        grad_own, grad_send, True, {1: (query_task, queries), 2: (key_task, keys), 3: (norm_task, norms)}
    )
    dk0, dv0, dk1, dv1 = keys
    grad_k, grad_v = finish(
        core, log_decay, grad_keep, grad_recv, k0, k1, v0, v1, dk0, dk1, dv0, dv1
    )
    return norms[0], queries[0], grad_k, grad_v


def solution(mesh):
    rows = P("seq", "head", None)
    return jax.shard_map(
        on_device,
        mesh=mesh,
        in_specs=(rows, rows, rows, rows, P("head", None), P("head", "seq")),
        out_specs=(rows, rows, rows, rows),
        check_vma=False,
    )
```

```python
import functools

import jax
import jax.numpy as jnp
from jax import lax
from jax.experimental import pallas as pl
from jax.experimental.pallas import tpu as pltpu
from jax.sharding import PartitionSpec as P

HEAD_TOTAL = 64
HD = 128
BLOCK = 256
GROUP = 4
STEP_TOK = 128
F32 = jnp.float32
BF16 = jnp.bfloat16
MIB = 1024 * 1024


def params(mib):
    return pltpu.CompilerParams(dimension_semantics=("arbitrary",), vmem_limit_bytes=mib * MIB)


def in_vmem(*shape, kind=F32):
    return pltpu.VMEM(shape, kind)


def in_hbm(*shape, kind=F32):
    return pltpu.HBM(shape, kind)


def stay(*arrays):
    return [pltpu.with_memory_space_constraint(array, pltpu.HBM) for array in arrays]


def cost(flops, moved, exps=0):
    return pl.CostEstimate(flops=flops, bytes_accessed=moved, transcendentals=exps)


def block_cum(log_decay):
    size = log_decay.shape[1]
    upper = lax.broadcasted_iota(jnp.int32, (size, size), 0) <= lax.broadcasted_iota(
        jnp.int32, (size, size), 1
    )
    return jnp.dot(
        log_decay,
        jnp.where(upper, 1.0, 0.0).astype(F32),
        precision=lax.Precision.HIGHEST,
        preferred_element_type=F32,
    )


def as_columns(row):
    return jnp.broadcast_to(row, (HD, row.shape[1])).T


def dot(a, b):
    return jnp.dot(a, b, preferred_element_type=F32)


def dot_rows(a, b):
    return lax.dot_general(a, b, (((1,), (1,)), ((), ())), preferred_element_type=F32)


def two_parts(matrix):
    high = matrix.astype(BF16)
    return high, (matrix - high.astype(F32)).astype(BF16)


def times_state(rows, state):
    return dot(jnp.concatenate([rows, rows], axis=1), jnp.concatenate(two_parts(state), axis=0))


def times_state_t(rows, state):
    return dot_rows(
        jnp.concatenate([rows, rows], axis=1), jnp.concatenate(two_parts(state), axis=1)
    )


def decay_matrix(row, columns):
    size = row.shape[1]
    lower = lax.broadcasted_iota(jnp.int32, (size, size), 0) >= lax.broadcasted_iota(
        jnp.int32, (size, size), 1
    )
    both = jnp.concatenate([columns] * (size // HD), axis=1)
    return jnp.exp(jnp.where(lower, both - row, -jnp.inf))


def to_rows(dst, block):
    tok, heads, dim = block.shape
    dst[...] = block[...].astype(F32).reshape(tok * heads, dim)


def head_rows(ref, head, heads, tok):
    return ref[pl.ds(head, tok, stride=heads), :]


def state_kernel(
    core_ref, ld_ref, k_ref, v_ref, own_ref, send_ref, first_ref, log_ref, kx, vx, cum, acc
):
    heads = ld_ref.shape[0]
    step = pl.program_id(0)
    per_block = BLOCK // STEP_TOK
    half = heads // 2

    @pl.when(step == 0)
    def _():
        for b in range(2):
            cum[b] = block_cum(ld_ref[:, b * BLOCK : (b + 1) * BLOCK])
        ends = cum[0, :, BLOCK - 1 :] + cum[1, :, BLOCK - 1 :]
        log_ref[...] = jnp.broadcast_to(ends, log_ref.shape)

    at = pl.multiple_of((step % per_block) * STEP_TOK * heads, STEP_TOK * heads)
    to_rows(kx.at[pl.ds(at, STEP_TOK * heads)], k_ref)
    to_rows(vx.at[pl.ds(at, STEP_TOK * heads)], v_ref)

    def block_state(b, h):
        row = cum[b, h : h + 1, :]
        scale = jnp.exp(row[:, BLOCK - 1 :] - row)
        keys = head_rows(kx, h, heads, BLOCK).T * scale
        return dot(keys.astype(BF16), head_rows(vx, h, heads, BLOCK).astype(BF16))

    @pl.when(step == per_block - 1)
    def _():
        for h in range(heads):
            first_ref[h] = block_state(0, h)

    @pl.when(step == 2 * per_block - 1)
    def _():
        last = jnp.exp(cum[1, :, BLOCK - 1 : BLOCK])
        for h in range(heads):
            acc[h] = block_state(1, h) + last[h : h + 1, :] * first_ref[h]
        core = core_ref[0]
        own_ref[...] = acc[pl.ds(core * half, half)]
        send_ref[...] = acc[pl.ds((1 - core) * half, half)]


def local_state(core, log_decay, key_rows, value_rows):
    tok, heads, dim = key_rows.shape
    half = heads // 2
    raw = pl.BlockSpec((STEP_TOK, heads, dim), lambda i: (i, 0, 0))
    whole = lambda *shape: pl.BlockSpec(shape, lambda i: (0,) * len(shape))
    return pl.pallas_call(
        state_kernel,
        grid=(tok // STEP_TOK,),
        in_specs=[pl.BlockSpec(memory_space=pltpu.SMEM), whole(heads, tok), raw, raw],
        out_specs=[
            whole(half, dim, dim), whole(half, dim, dim), whole(heads, dim, dim), whole(heads, dim),
        ],
        out_shape=[
            in_vmem(half, dim, dim),
            in_vmem(half, dim, dim),
            in_hbm(heads, dim, dim),
            in_vmem(heads, dim),
        ],
        scratch_shapes=[
            pltpu.VMEM((BLOCK * heads, dim), F32),
            pltpu.VMEM((BLOCK * heads, dim), F32),
            pltpu.VMEM((2, heads, BLOCK), F32),
            pltpu.VMEM((heads, dim, dim), F32),
        ],
        compiler_params=params(16),
        cost_estimate=cost(2 * tok * heads * dim * dim, 4 * tok * heads * dim),
        name="local_state",
    )(core, *stay(log_decay, key_rows, value_rows))


def intra_kernel(
    second, ld_ref, q_ref, k_ref, v_ref, o_ref, first_ref,
    qh_ref, kh_ref, vh_ref, oh_ref, w_ref, inner_ref, qx, kx, vx, ox, cum,
):
    heads = ld_ref.shape[0]
    step = pl.program_id(0)

    @pl.when(step == 0)
    def _():
        cum[...] = block_cum(ld_ref[...])
        to_rows(qx, q_ref)
        to_rows(kx, k_ref)
        to_rows(vx, v_ref)
        to_rows(ox, o_ref)

    for i in range(GROUP):
        h = step * GROUP + i
        query = head_rows(qx, h, heads, BLOCK).astype(BF16)
        key = head_rows(kx, h, heads, BLOCK).astype(BF16)
        value = head_rows(vx, h, heads, BLOCK).astype(BF16)
        qh_ref[i] = query
        kh_ref[i] = key
        vh_ref[i] = value
        oh_ref[i] = head_rows(ox, h, heads, BLOCK).astype(BF16)
        row = cum[pl.ds(h, 1), :]
        columns = as_columns(row)
        weights = (dot_rows(query, key) * decay_matrix(row, columns)).astype(BF16)
        w_ref[i] = weights
        inner = dot(weights, value)
        if second:
            inner += jnp.exp(columns) * times_state(query, first_ref[i])
        inner_ref[i] = inner


def intra(index, log_decay, query_rows, key_rows, value_rows, output_grad, first):
    tok, heads, dim = key_rows.shape
    raw = pl.BlockSpec(
        (BLOCK, heads, dim), lambda i: (index, 0, 0), pipeline_mode=pl.Buffered(1)
    )
    by_head = pl.BlockSpec((GROUP, BLOCK, dim), lambda i: (i, 0, 0))
    near = in_vmem(heads, BLOCK, dim, kind=BF16)
    far = in_hbm(heads, BLOCK, dim, kind=BF16)
    return pl.pallas_call(
        functools.partial(intra_kernel, index > 0),
        grid=(heads // GROUP,),
        in_specs=[
            pl.BlockSpec((heads, BLOCK), lambda i: (0, index)),
            raw, raw, raw, raw,
            pl.BlockSpec((GROUP, dim, dim), lambda i: (i, 0, 0)),
        ],
        out_specs=[by_head] * 4 + [pl.BlockSpec((GROUP, BLOCK, BLOCK), lambda i: (i, 0, 0)), by_head],
        out_shape=[near, far, far, near] + [
            in_hbm(heads, BLOCK, BLOCK, kind=BF16),
            in_vmem(heads, BLOCK, dim),
        ],
        scratch_shapes=[pltpu.VMEM((BLOCK * heads, dim), F32)] * 4 + [pltpu.VMEM((heads, BLOCK), F32)],
        compiler_params=params(20),
        cost_estimate=cost(
            2 * heads * BLOCK * BLOCK * dim * 4, 20 * heads * BLOCK * dim, heads * BLOCK * BLOCK
        ),
        name=f"intra_{index}",
    )(log_decay, *stay(query_rows, key_rows, value_rows, output_grad, first))


def whole_state(core, keep_ref, recv_ref, group, i):
    half = keep_ref.shape[0]
    head = group * GROUP + i
    mine = (head // half) == core
    return jnp.where(mine, keep_ref[head % half], recv_ref[head % half])


def attend_kernel(
    core_ref, ld_ref, gain_ref, keep_ref, recv_ref, q0, q1, o0, o1, inner0, inner1,
    att0, att1, sums_ref, cum, squares, products,
):
    step = pl.program_id(0)
    steps = pl.num_programs(0)

    @pl.when(step == 0)
    def _():
        cum[0] = block_cum(ld_ref[:, :BLOCK])
        cum[1] = cum[0, :, BLOCK - 1 : BLOCK] + block_cum(ld_ref[:, BLOCK:])
        squares[...] = jnp.zeros_like(squares)
        products[...] = jnp.zeros_like(products)

    for i in range(GROUP):
        h = step * GROUP + i
        state = whole_state(core_ref[0], keep_ref, recv_ref, step, i)
        gain = gain_ref[pl.ds(h, 1), :]
        for b, (q, o, inner, att) in enumerate(((q0, o0, inner0, att0), (q1, o1, inner1, att1))):
            columns = jnp.exp(as_columns(cum[b, pl.ds(h, 1), :]))
            attended = inner[i] + columns * times_state(q[i], state)
            att[i] = attended
            squares[b] += attended * attended
            products[b] += gain * o[i].astype(F32) * attended

    @pl.when(step == steps - 1)
    def _():
        ones = jnp.ones((8, HD), F32)
        for b in range(2):
            for at, total in enumerate((squares, products)):
                line = lax.dot_general(
                    ones, total[b], (((1,), (1,)), ((), ())),
                    precision=lax.Precision.HIGHEST, preferred_element_type=F32,
                )
                sums_ref[at : at + 1, b * BLOCK : (b + 1) * BLOCK] = line[:1]


def attend(core, log_decay, gain, keep, recv, parts):
    heads, tok = log_decay.shape
    dim = HD
    whole = lambda *shape: pl.BlockSpec(shape, lambda i: (0,) * len(shape))
    by_head = pl.BlockSpec((GROUP, BLOCK, dim), lambda i: (i, 0, 0))
    head_shape = in_vmem(heads, BLOCK, dim)
    return pl.pallas_call(
        attend_kernel,
        grid=(heads // GROUP,),
        in_specs=[pl.BlockSpec(memory_space=pltpu.SMEM), whole(heads, tok), whole(heads, dim)]
        + [whole(heads // 2, dim, dim)] * 2 + [by_head] * 6,
        out_specs=[by_head, by_head, whole(2, tok)],
        out_shape=[head_shape, head_shape, in_vmem(2, tok)],
        scratch_shapes=[
            pltpu.VMEM((2, heads, BLOCK), F32),
            pltpu.VMEM((2, BLOCK, dim), F32),
            pltpu.VMEM((2, BLOCK, dim), F32),
        ],
        compiler_params=params(16),
        cost_estimate=cost(4 * heads * tok * dim * dim, 16 * heads * tok * dim),
        name="attend",
    )(core, log_decay, gain, keep, recv, *parts)


def inverse_rms(sums_ref, b):
    at = slice(b * BLOCK, (b + 1) * BLOCK)
    inv = lax.rsqrt(sums_ref[0:1, at] / (HEAD_TOTAL * HD) + 1e-06)
    mean = sums_ref[1:2, at] * inv / (HEAD_TOTAL * HD)
    return inv, mean


def norm_grad_kernel(
    core_ref, ld_ref, gain_ref, sums_ref, q0, q1, o0, o1, att0, att1,
    g0, g1, own_ref, send_ref, second_ref, cum, scales, acc,
):
    heads = ld_ref.shape[0]
    half = heads // 2
    step = pl.program_id(0)

    @pl.when(step == 0)
    def _():
        for b in range(2):
            cum[b] = block_cum(ld_ref[:, b * BLOCK : (b + 1) * BLOCK])
            inv, mean = inverse_rms(sums_ref, b)
            scales[b, 0] = as_columns(inv)
            scales[b, 1] = as_columns(inv * inv * mean)

    for i in range(GROUP):
        h = step * GROUP + i
        gain = gain_ref[pl.ds(h, 1), :]
        ends = []
        for b, (q, o, att, g) in enumerate(((q0, o0, att0, g0), (q1, o1, att1, g1))):
            grad = gain * o[i].astype(F32) * scales[b, 0] - att[i] * scales[b, 1]
            grad = grad.astype(BF16)
            g[i] = grad
            queries = q[i].astype(F32).T * jnp.exp(cum[b, pl.ds(h, 1), :])
            ends.append(dot(queries.astype(BF16), grad))
        second_ref[i] = ends[1]
        first_decay = jnp.exp(cum[0, pl.ds(h, 1), :][:, BLOCK - 1 :])
        acc[h] = ends[0] + first_decay * ends[1]

    @pl.when(step == pl.num_programs(0) - 1)
    def _():
        core = core_ref[0]
        own_ref[...] = acc[pl.ds(core * half, half)]
        send_ref[...] = acc[pl.ds((1 - core) * half, half)]


def norm_grad(core, log_decay, gain, sums, parts):
    heads, tok = log_decay.shape
    dim = HD
    half = heads // 2
    whole = lambda *shape: pl.BlockSpec(shape, lambda i: (0,) * len(shape))
    by_head = pl.BlockSpec((GROUP, BLOCK, dim), lambda i: (i, 0, 0))
    head_shape = in_hbm(heads, BLOCK, dim, kind=BF16)
    return pl.pallas_call(
        norm_grad_kernel,
        grid=(heads // GROUP,),
        in_specs=[
            pl.BlockSpec(memory_space=pltpu.SMEM), whole(heads, tok), whole(heads, dim), whole(2, tok),
        ] + [by_head] * 6,
        out_specs=[
            by_head, by_head, whole(half, dim, dim), whole(half, dim, dim),
            pl.BlockSpec((GROUP, dim, dim), lambda i: (i, 0, 0)),
        ],
        out_shape=[
            head_shape, head_shape,
            in_vmem(half, dim, dim),
            in_vmem(half, dim, dim),
            in_hbm(heads, dim, dim),
        ],
        scratch_shapes=[
            pltpu.VMEM((2, heads, BLOCK), F32),
            pltpu.VMEM((2, 2, BLOCK, dim), F32),
            pltpu.VMEM((heads, dim, dim), F32),
        ],
        compiler_params=params(16),
        cost_estimate=cost(2 * heads * tok * dim * dim, 14 * heads * tok * dim),
        name="norm_grad",
    )(core, log_decay, gain, sums, *parts)


def normed_kernel(gain_ref, sums_ref, att0, att1, out_ref, rows):
    heads = gain_ref.shape[0]
    b = pl.program_id(0)
    at = pl.multiple_of(b * BLOCK, BLOCK)
    inv = as_columns(lax.rsqrt(sums_ref[0:1, pl.ds(at, BLOCK)] / (HEAD_TOTAL * HD) + 1e-06))
    for index, att in enumerate((att0, att1)):

        @pl.when(b == index)
        def _():
            for h in range(heads):
                rows[pl.ds(h, BLOCK, stride=heads), :] = att[h] * inv * gain_ref[h : h + 1, :]

    out_ref[...] = rows[...].reshape(BLOCK, heads, HD).astype(BF16)


def normed_rows(gain, sums, att0, att1):
    heads, _, dim = att0.shape
    tok = 2 * BLOCK
    whole = lambda *shape: pl.BlockSpec(shape, lambda i: (0,) * len(shape))
    return pl.pallas_call(
        normed_kernel,
        grid=(2,),
        in_specs=[whole(heads, dim), whole(2, tok), whole(heads, BLOCK, dim), whole(heads, BLOCK, dim)],
        out_specs=pl.BlockSpec((BLOCK, heads, dim), lambda i: (i, 0, 0)),
        out_shape=jax.ShapeDtypeStruct((tok, heads, dim), BF16),
        scratch_shapes=[pltpu.VMEM((BLOCK * heads, dim), F32)],
        compiler_params=params(16),
        cost_estimate=cost(3 * heads * tok * dim, 6 * heads * tok * dim),
        name="normed_rows",
    )(gain, sums, att0, att1)


def grad_q_kernel(
    core_ref, ld_ref, keep_ref, recv_ref, first_ref, k_ref0, k_ref1, v_ref0, v_ref1, g_ref0, g_ref1,
    out_ref, gs_ref, cum, rows,
):
    heads = ld_ref.shape[0]
    b, group = pl.program_id(0), pl.program_id(1)

    @pl.when((b == 0) & (group == 0))
    def _():
        for x in range(2):
            cum[x] = block_cum(ld_ref[:, x * BLOCK : (x + 1) * BLOCK])

    def work(second, k, v, g):
        for i in range(GROUP):
            h = group * GROUP + i
            row = cum[second, pl.ds(h, 1), :]
            columns = as_columns(row)
            scores = (dot_rows(g[i], v[i]) * decay_matrix(row, columns)).astype(BF16)
            gs_ref[0, i] = scores
            state = whole_state(core_ref[0], keep_ref, recv_ref, group, i)
            if second:
                state = jnp.exp(cum[0, pl.ds(h, 1), :][:, BLOCK - 1 :]) * state + first_ref[i]
            grad = dot(scores, k[i]) + jnp.exp(columns) * times_state_t(g[i], state)
            rows[pl.ds(h, BLOCK, stride=heads), :] = grad

    @pl.when(b == 0)
    def _():
        work(0, k_ref0, v_ref0, g_ref0)

    @pl.when(b == 1)
    def _():
        work(1, k_ref1, v_ref1, g_ref1)

    @pl.when(group == pl.num_programs(1) - 1)
    def _():
        out_ref[...] = rows[...].reshape(BLOCK, heads, HD).astype(BF16)


def two_level(mib):
    return pltpu.CompilerParams(
        dimension_semantics=("arbitrary", "arbitrary"), vmem_limit_bytes=mib * MIB
    )


def grad_query(core, log_decay, keep, recv, first, k0, k1, v0, v1, g0, g1):
    heads, tok = log_decay.shape
    dim = HD
    groups = heads // GROUP
    whole = lambda *shape: pl.BlockSpec(shape, lambda b, i: (0,) * len(shape))
    head0 = pl.BlockSpec((GROUP, BLOCK, dim), lambda b, i: (jnp.where(b == 0, i, groups - 1), 0, 0))
    head1 = pl.BlockSpec((GROUP, BLOCK, dim), lambda b, i: (jnp.where(b == 0, 0, i), 0, 0))
    return pl.pallas_call(
        grad_q_kernel,
        grid=(2, groups),
        in_specs=[
            pl.BlockSpec(memory_space=pltpu.SMEM), whole(heads, tok),
            whole(heads // 2, dim, dim), whole(heads // 2, dim, dim),
            pl.BlockSpec((GROUP, dim, dim), lambda b, i: (i, 0, 0)),
        ] + [head0, head1] * 3,
        out_specs=[
            pl.BlockSpec((BLOCK, heads, dim), lambda b, i: (b, 0, 0)),
            pl.BlockSpec((1, GROUP, BLOCK, BLOCK), lambda b, i: (b, i, 0, 0)),
        ],
        out_shape=[
            jax.ShapeDtypeStruct((tok, heads, dim), BF16),
            in_hbm(2, heads, BLOCK, BLOCK, kind=BF16),
        ],
        scratch_shapes=[pltpu.VMEM((2, heads, BLOCK), F32), pltpu.VMEM((BLOCK * heads, dim), F32)],
        compiler_params=two_level(16),
        cost_estimate=cost(
            4 * heads * tok * dim * (BLOCK + dim), 12 * heads * tok * dim, heads * tok * BLOCK
        ),
        name="grad_query",
    )(core, log_decay, keep, recv, *stay(first, k0, k1, v0, v1, g0, g1))


def transposed_dot(a, b):
    return lax.dot_general(a, b, (((0,), (0,)), ((), ())), preferred_element_type=F32)


def grad_kv_kernel(
    ld_ref, gs_ref, w0, w1, q0, q1, k0, v0, g0, g1, second_ref, dk0, dv0, dk1, dv1, cum,
):
    group = pl.program_id(0)

    @pl.when(group == 0)
    def _():
        cum[...] = block_cum(ld_ref[...])

    for i in range(GROUP):
        h = group * GROUP + i
        row = cum[pl.ds(h, 1), :]
        columns = as_columns(jnp.exp(row[:, BLOCK - 1 :] - row))
        state = second_ref[i]
        dk0[i] = transposed_dot(gs_ref[0, i], q0[i]) + columns * times_state_t(v0[i], state)
        dv0[i] = transposed_dot(w0[i], g0[i]) + columns * times_state(k0[i], state)
        dk1[i] = transposed_dot(gs_ref[1, i], q1[i])
        dv1[i] = transposed_dot(w1[i], g1[i])


def grad_key_value(log_decay, gs, w0, w1, q0, q1, k0, v0, g0, g1, second):
    heads, tok = log_decay.shape
    dim = HD
    by_head = pl.BlockSpec((GROUP, BLOCK, dim), lambda i: (i, 0, 0))
    square = pl.BlockSpec((GROUP, BLOCK, BLOCK), lambda i: (i, 0, 0))
    return pl.pallas_call(
        grad_kv_kernel,
        grid=(heads // GROUP,),
        in_specs=[
            pl.BlockSpec((heads, BLOCK), lambda i: (0, 0)),
            pl.BlockSpec((2, GROUP, BLOCK, BLOCK), lambda i: (0, i, 0, 0)),
            square, square, by_head, by_head, by_head, by_head, by_head, by_head,
            pl.BlockSpec((GROUP, dim, dim), lambda i: (i, 0, 0)),
        ],
        out_specs=[by_head] * 4,
        out_shape=[in_hbm(heads, BLOCK, dim)] * 4,
        scratch_shapes=[pltpu.VMEM((heads, BLOCK), F32)],
        compiler_params=params(16),
        cost_estimate=cost(4 * heads * tok * dim * (BLOCK + dim), 30 * heads * tok * dim),
        name="grad_key_value",
    )(log_decay, *stay(gs, w0, w1), q0, q1, *stay(k0, v0, g0, g1, second))


def finish_kernel(
    core_ref, ld_ref, keep_ref, recv_ref, k_ref0, k_ref1, v_ref0, v_ref1, dk0, dk1, dv0, dv1,
    out_k, out_v, cum, rows_k, rows_v,
):
    heads = ld_ref.shape[0]
    b, group = pl.program_id(0), pl.program_id(1)

    @pl.when((b == 0) & (group == 0))
    def _():
        for x in range(2):
            cum[x] = block_cum(ld_ref[:, x * BLOCK : (x + 1) * BLOCK])

    def work(second, k, v, dk, dv):
        for i in range(GROUP):
            h = group * GROUP + i
            row = cum[second, pl.ds(h, 1), :]
            left = row[:, BLOCK - 1 :] - row
            if not second:
                left = left + cum[1, pl.ds(h, 1), :][:, BLOCK - 1 :]
            columns = as_columns(jnp.exp(left))
            state = whole_state(core_ref[0], keep_ref, recv_ref, group, i)
            rows_k[pl.ds(h, BLOCK, stride=heads), :] = dk[i] + columns * times_state_t(v[i], state)
            rows_v[pl.ds(h, BLOCK, stride=heads), :] = dv[i] + columns * times_state(k[i], state)

    @pl.when(b == 0)
    def _():
        work(0, k_ref0, v_ref0, dk0, dv0)

    @pl.when(b == 1)
    def _():
        work(1, k_ref1, v_ref1, dk1, dv1)

    @pl.when(group == pl.num_programs(1) - 1)
    def _():
        out_k[...] = rows_k[...].reshape(BLOCK, heads, HD).astype(BF16)
        out_v[...] = rows_v[...].reshape(BLOCK, heads, HD).astype(BF16)


def finish(core, log_decay, keep, recv, k0, k1, v0, v1, dk0, dk1, dv0, dv1):
    heads, tok = log_decay.shape
    dim = HD
    groups = heads // GROUP
    whole = lambda *shape: pl.BlockSpec(shape, lambda b, i: (0,) * len(shape))
    head0 = pl.BlockSpec((GROUP, BLOCK, dim), lambda b, i: (jnp.where(b == 0, i, groups - 1), 0, 0))
    head1 = pl.BlockSpec((GROUP, BLOCK, dim), lambda b, i: (jnp.where(b == 0, 0, i), 0, 0))
    raw = pl.BlockSpec((BLOCK, heads, dim), lambda b, i: (b, 0, 0))
    out = jax.ShapeDtypeStruct((tok, heads, dim), BF16)
    return pl.pallas_call(
        finish_kernel,
        grid=(2, groups),
        in_specs=[
            pl.BlockSpec(memory_space=pltpu.SMEM), whole(heads, tok),
            whole(heads // 2, dim, dim), whole(heads // 2, dim, dim),
        ] + [head0, head1] * 4,
        out_specs=[raw, raw],
        out_shape=[out, out],
        scratch_shapes=[
            pltpu.VMEM((2, heads, BLOCK), F32),
            pltpu.VMEM((BLOCK * heads, dim), F32),
            pltpu.VMEM((BLOCK * heads, dim), F32),
        ],
        compiler_params=two_level(16),
        cost_estimate=cost(8 * heads * tok * dim * dim, 16 * heads * tok * dim),
        name="finish",
    )(core, log_decay, keep, recv, *stay(k0, k1, v0, v1, dk0, dk1, dv0, dv1))


def swap(value, axis, bit):
    count = lax.axis_size(axis)
    return lax.ppermute(value, axis, [(i, i ^ bit) for i in range(count)])


def quad_scales(logs, backward):
    log_total, log_partner, log_row_same, log_row_other = logs
    mine = lax.axis_index("seq")
    core = mine % 2
    half = log_total.shape[0] // 2
    bits = [(mine >> at) % 2 for at in range(3)]
    if backward:
        bits = [1 - bit for bit in bits]
    late, right, low = (bit == 1 for bit in bits)
    own, partner, chip, row = (
        lax.dynamic_slice_in_dim(jnp.exp(part[:, 0]), core * half, half)
        for part in (log_total, log_partner, log_total + log_partner, log_row_same + log_row_other)
    )
    one, zero = jnp.ones((half,), F32), jnp.zeros((half,), F32)
    first = jnp.arange(half) < half // 2
    pick = jnp.where
    rows = [
        pick(late, one, partner),
        pick(late, own, one),
        pick(right, one, row),
        pick(first, pick(right, one, row), pick(low & right, zero, one)),
        pick(first, pick(right, chip, one), pick(low, pick(right, one, chip), zero)),
        pick(first, pick(right, one, zero), pick(low, pick(right, row, one), zero)),
        pick(first, pick(low, pick(right, row, one), zero), pick(low | right, one, zero)),
        pick(late, partner, one),
        pick(late, one, zero),
        pick(late, one, own),
        pick(late, zero, one),
    ]
    table = jnp.stack(rows)[:, :, None]
    return jnp.broadcast_to(table, table.shape[:2] + (HD,))


def mix(body, scales, arrays, heads_out, name):
    dim = HD

    def kernel(scales_ref, *refs):
        scale = lambda row, head: scales_ref[row, head : head + 1, :]
        body(scale, refs[: len(arrays)], refs[len(arrays) :])

    return pl.pallas_call(
        kernel,
        in_specs=[pl.BlockSpec(memory_space=pltpu.VMEM)] * (1 + len(arrays)),
        out_specs=[pl.BlockSpec(memory_space=pltpu.VMEM)] * len(heads_out),
        out_shape=[in_vmem(heads, dim, dim) for heads in heads_out],
        compiler_params=pltpu.CompilerParams(vmem_limit_bytes=8 * MIB),
        cost_estimate=cost(4 * 8 * dim * dim, 16 * 8 * dim * dim),
        name=name,
    )(scales, *arrays)


def mix_total(scale, arrays, outputs):
    own, got = arrays
    first, second, second_scaled = outputs
    quarter = first.shape[0]
    for h in range(2 * quarter):
        total = scale(0, h) * own[h] + scale(1, h) * got[h]
        if h < quarter:
            first[h] = total
        else:
            second[h - quarter] = total
            second_scaled[h - quarter] = scale(2, h) * total


def mix_next(scale, arrays, outputs):
    quarter = arrays[0].shape[0]
    for part in range(2):
        total, got, out = arrays[part], arrays[2 + part], outputs[part]
        for i in range(quarter):
            h = part * quarter + i
            out[i] = scale(3, h) * total[i] + scale(4, h) * got[i]


def mix_enter(scale, arrays, outputs):
    own, got = arrays[:2]
    kept, sent = outputs
    quarter = own.shape[0] // 2
    for part in range(2):
        one, two = arrays[2 + part], arrays[4 + part]
        for i in range(quarter):
            h = part * quarter + i
            enter = scale(5, h) * one[i] + scale(6, h) * two[i]
            kept[h] = scale(7, h) * enter + scale(8, h) * got[h]
            sent[h] = scale(9, h) * enter + scale(10, h) * own[h]


def entering_quad(own, send, scales, tasks, name):
    def work(stage, after, before=()):
        if stage not in tasks:
            return before
        run, outputs = tasks[stage]
        outputs.extend(run(after))
        return lax.optimization_barrier((before, outputs[-1]))[0]

    half = own.shape[0]
    quarter = half // 2
    got = swap(send, "seq", 1)
    scales = scales()
    first, second, scaled = mix(
        mix_total, scales, (own, got), (quarter,) * 3, name + "_total"
    )
    one_a, one_b = swap(first, "seq", 2), swap(scaled, "seq", 4)
    one_a, one_b = work(1, scaled, (one_a, one_b))
    next_a, next_b = mix(
        mix_next, scales, (first, second, one_a, one_b), (quarter,) * 2, name + "_next"
    )
    two_a, two_b = swap(next_a, "seq", 4), swap(next_b, "seq", 2)
    two_a, two_b = work(2, next_b, (two_a, two_b))
    kept, sent = mix(
        mix_enter, scales, (own, got, one_a, one_b, two_a, two_b), (half,) * 2, name + "_enter"
    )
    received = swap(sent, "seq", 1)
    work(3, sent)
    return kept, received


def entering_any(own, send, log_total, backward, tasks):
    for run, outputs in tasks.values():
        outputs.extend(run(send))
    count, mine = lax.axis_size("seq"), lax.axis_index("seq")
    core = mine % 2
    half = own.shape[0]
    in_order = jnp.where(
        core == 0, jnp.concatenate([own, send], axis=0), jnp.concatenate([send, own], axis=0)
    )
    states = lax.all_gather(in_order, "seq")
    decays = jnp.exp(lax.all_gather(log_total, "seq"))
    place = mine
    if backward:
        states, decays, place = states[::-1], decays[::-1], count - 1 - mine

    def step(at, total):
        longer = decays[at][:, None, None] * total + states[at]
        return jnp.where(at < place, longer, total)

    total = lax.fori_loop(0, count - 1, step, jnp.zeros_like(in_order))
    kept = lax.dynamic_slice_in_dim(total, core * half, half)
    return kept, lax.dynamic_slice_in_dim(total, (1 - core) * half, half)


def sum_over_heads(value):
    count = lax.axis_size("head")
    reach = 1
    while 2 * reach <= count and count % (2 * reach) == 0:
        value = value + swap(value, "head", reach)
        reach *= 2
    part = value
    for shift in range(1, count // reach):
        value = value + lax.ppermute(
            part, "head", [(i, (i + shift * reach) % count) for i in range(count)]
        )
    return value


def follows(value, earlier):
    return lax.optimization_barrier((value, earlier))[0]


def on_device(query_rows, key_rows, value_rows, output_grad, norm_gain, log_decay):
    core = (lax.axis_index("seq") % 2).astype(jnp.int32).reshape(1)
    own, send, first, log_total = local_state(core, log_decay, key_rows, value_rows)
    if lax.axis_size("seq") == 8:
        logs = []

        def scales(backward):
            if not logs:
                logs.append(log_total)
                logs.extend(swap(log_total, "seq", bit) for bit in (1, 2, 3))
            return lambda: quad_scales(logs, backward)

        entering = lambda own, send, backward, tasks: entering_quad(
            own, send, scales(backward), tasks, "later" if backward else "earlier"
        )
    else:
        entering = lambda own, send, backward, tasks: entering_any(
            own, send, log_total[:, 0], backward, tasks
        )

    def forward_task(index):
        return lambda earlier: intra(
            index, log_decay, query_rows, key_rows, value_rows, output_grad, follows(first, earlier)
        )

    in_0, in_1 = [], []
    keep, recv = entering(
        own, send, False, {1: (forward_task(0), in_0), 2: (forward_task(1), in_1)}
    )
    q0, k0, v0, o0, w0, inner0 = in_0
    q1, k1, v1, o1, w1, inner1 = in_1
    att0, att1, sums = attend(
        core, log_decay, norm_gain, keep, recv, (q0, q1, o0, o1, inner0, inner1)
    )
    sums = sum_over_heads(sums)
    g0, g1, grad_own, grad_send, second = norm_grad(
        core, log_decay, norm_gain, sums, (q0, q1, o0, o1, att0, att1)
    )
    queries, keys, norms = [], [], []

    def query_task(earlier):
        return grad_query(
            core, log_decay, keep, recv, follows(first, earlier), k0, k1, v0, v1, g0, g1
        )

    def key_task(earlier):
        return grad_key_value(
            log_decay, queries[1], w0, w1, q0, q1, k0, v0, g0, g1, follows(second, earlier)
        )

    def norm_task(earlier):
        return [normed_rows(follows(norm_gain, earlier), sums, att0, att1)]

    grad_keep, grad_recv = entering(
        grad_own, grad_send, True, {1: (query_task, queries), 2: (key_task, keys), 3: (norm_task, norms)}
    )
    dk0, dv0, dk1, dv1 = keys
    grad_k, grad_v = finish(
        core, log_decay, grad_keep, grad_recv, k0, k1, v0, v1, dk0, dk1, dv0, dv1
    )
    return norms[0], queries[0], grad_k, grad_v


def solution(mesh):
    rows = P("seq", "head", None)
    return jax.shard_map(
        on_device,
        mesh=mesh,
        in_specs=(rows, rows, rows, rows, P("head", None), P("head", "seq")),
        out_specs=(rows, rows, rows, rows),
        check_vma=False,
    )
```

```python
import jax
import jax.numpy as jnp
from jax import lax
from jax.experimental import pallas as pl
from jax.experimental.pallas import tpu as pltpu
from jax.sharding import PartitionSpec as P

HEAD_TOTAL = 64
HD = 128
BLOCK = 256
CHUNK = 128
TILE = 8
F32 = jnp.float32
BF16 = jnp.bfloat16
MIB = 1024 * 1024
NEAR = pl.BlockSpec(memory_space=pltpu.VMEM)
FAR = pl.BlockSpec(memory_space=pl.ANY)
SCALARS = pl.BlockSpec(memory_space=pltpu.SMEM)


def in_vmem(*shape, kind=F32):
    return pltpu.VMEM(shape, kind)


def near(*arrays):
    return [pltpu.with_memory_space_constraint(array, pltpu.VMEM) for array in arrays]


def far(*arrays):
    return [pltpu.with_memory_space_constraint(array, pltpu.HBM) for array in arrays]


def params(mib):
    return pltpu.CompilerParams(vmem_limit_bytes=mib * MIB)


def cost(flops, moved, exps=0):
    return pl.CostEstimate(flops=flops, bytes_accessed=moved, transcendentals=exps)


def block_cum(log_decay):
    size = log_decay.shape[1]
    upper = lax.broadcasted_iota(jnp.int32, (size, size), 0) <= lax.broadcasted_iota(
        jnp.int32, (size, size), 1
    )
    return jnp.dot(
        log_decay,
        jnp.where(upper, 1.0, 0.0).astype(F32),
        precision=lax.Precision.HIGHEST,
        preferred_element_type=F32,
    )


def as_columns(row):
    return jnp.broadcast_to(row, (HD, row.shape[1])).T


def dot(a, b):
    return jnp.dot(a, b, preferred_element_type=F32)


def dot_rows(a, b):
    return lax.dot_general(a, b, (((1,), (1,)), ((), ())), preferred_element_type=F32)


def two_parts(matrix):
    high = matrix.astype(BF16)
    return high, (matrix - high.astype(F32)).astype(BF16)


def times_state(rows, state):
    return dot(jnp.concatenate([rows, rows], axis=1), jnp.concatenate(two_parts(state), axis=0))


def times_state_t(rows, state):
    return dot_rows(
        jnp.concatenate([rows, rows], axis=1), jnp.concatenate(two_parts(state), axis=1)
    )


def decay_matrix(row, columns):
    size = row.shape[1]
    lower = lax.broadcasted_iota(jnp.int32, (size, size), 0) >= lax.broadcasted_iota(
        jnp.int32, (size, size), 1
    )
    both = jnp.concatenate([columns] * (size // HD), axis=1)
    return jnp.exp(jnp.where(lower, both - row, -jnp.inf))


def to_rows(dst, block):
    tok, heads, dim = block.shape
    dst[...] = block[...].astype(F32).reshape(tok * heads, dim)


def from_rows(rows, block):
    tok, heads, dim = block.shape
    block[...] = rows[...].reshape(tok, heads, dim).astype(BF16)


def transposed_dot(a, b):
    return lax.dot_general(a, b, (((0,), (0,)), ((), ())), preferred_element_type=F32)


def each_head(heads, unroll, body):
    def step(h, carry):
        body(h)
        return carry

    lax.fori_loop(0, heads, step, 0, unroll=unroll)


def head_rows(ref, head, heads, tok):
    return ref[pl.ds(head, tok, stride=heads), :]


def state_kernel(
    place_ref, ld_hbm, k_hbm, v_hbm, own_ref, send_ref, first_ref, kh, vh,
    ld_ref, k_raw, v_raw, kx, vx, cum, acc, decay, sems,
):
    heads, tok = ld_ref.shape
    half = heads // 2
    per_block = BLOCK // CHUNK
    copies = [pltpu.make_async_copy(ld_hbm, ld_ref, sems.at[0])]
    for c in range(tok // CHUNK):
        at = pl.ds(c * CHUNK, CHUNK)
        copies.append(pltpu.make_async_copy(k_hbm.at[at], k_raw.at[at], sems.at[2 * c + 1]))
        copies.append(pltpu.make_async_copy(v_hbm.at[at], v_raw.at[at], sems.at[2 * c + 2]))
    for copy in copies:
        copy.start()
    copies[0].wait()
    for b in range(2):
        cum[b] = block_cum(ld_ref[:, b * BLOCK : (b + 1) * BLOCK])
    ends = cum[0, :, BLOCK - 1 :] + cum[1, :, BLOCK - 1 :]
    decay[...] = jnp.broadcast_to(jnp.exp(ends), decay.shape)

    for b in range(2):
        for c in range(per_block):
            at = pl.ds((b * per_block + c) * CHUNK, CHUNK)
            rows = pl.ds(c * CHUNK * heads, CHUNK * heads)
            which = 2 * (b * per_block + c) + 1
            copies[which].wait()
            to_rows(kx.at[rows], k_raw.at[at])
            copies[which + 1].wait()
            to_rows(vx.at[rows], v_raw.at[at])

        def one(h, b=b):
            row = cum[b, pl.ds(h, 1), :]
            scale = jnp.exp(row[:, BLOCK - 1 :] - row)
            key = head_rows(kx, h, heads, BLOCK)
            value = head_rows(vx, h, heads, BLOCK).astype(BF16)
            kh[b, h] = key.astype(BF16)
            vh[b, h] = value
            state = dot((key.T * scale).astype(BF16), value)
            if b == 0:
                first_ref[h] = state
            else:
                acc[h] = state + jnp.exp(row[:, BLOCK - 1 :]) * first_ref[h]

        each_head(heads, 4, one)

    core = place_ref[0]
    own_ref[:, :HD] = acc[pl.ds(core * half, half)]
    send_ref[:, :HD] = acc[pl.ds((1 - core) * half, half)]
    for i in range(half):
        for ref, base in ((own_ref, core * half), (send_ref, (1 - core) * half)):
            ref[i, HD:] = jnp.broadcast_to(decay[pl.ds(base + i, 1), :], (TILE, HD))


def local_state(place, log_decay, key_rows, value_rows):
    tok, heads, dim = key_rows.shape
    half = heads // 2
    by_head = in_vmem(2, heads, BLOCK, dim, kind=BF16)
    return pl.pallas_call(
        state_kernel,
        in_specs=[SCALARS, FAR, FAR, FAR],
        out_specs=[NEAR] * 5,
        out_shape=[
            in_vmem(half, dim + TILE, dim), in_vmem(half, dim + TILE, dim),
            in_vmem(heads, dim, dim), by_head, by_head,
        ],
        scratch_shapes=[
            pltpu.VMEM((heads, tok), F32),
            pltpu.VMEM((tok, heads, dim), BF16),
            pltpu.VMEM((tok, heads, dim), BF16),
            pltpu.VMEM((BLOCK * heads, dim), F32),
            pltpu.VMEM((BLOCK * heads, dim), F32),
            pltpu.VMEM((2, heads, BLOCK), F32),
            pltpu.VMEM((heads, dim, dim), F32),
            pltpu.VMEM((heads, dim), F32),
            pltpu.SemaphoreType.DMA((2 * (tok // CHUNK) + 1,)),
        ],
        compiler_params=params(16),
        cost_estimate=cost(2 * tok * heads * dim * dim, 8 * tok * heads * dim),
        name="local_state",
    )(place, *far(log_decay, key_rows, value_rows))


def intra(index, log_decay, kh, vh, first, query_rows, output_grad):
    tok, heads, dim = query_rows.shape

    def kernel(ld_ref, kh, vh, first_ref, q_hbm, o_hbm, qh, oh, w_ref, inner_ref,
               q_raw, o_raw, qx, ox, cum, sems):
        at = pl.ds(index * BLOCK, BLOCK)
        copy_q = pltpu.make_async_copy(q_hbm.at[at], q_raw, sems.at[0])
        copy_o = pltpu.make_async_copy(o_hbm.at[at], o_raw, sems.at[1])
        copy_q.start()
        copy_o.start()
        cum[...] = block_cum(ld_ref[:, index * BLOCK : (index + 1) * BLOCK])
        copy_q.wait()
        to_rows(qx, q_raw)
        copy_o.wait()
        to_rows(ox, o_raw)

        def one(h):
            query = head_rows(qx, h, heads, BLOCK).astype(BF16)
            qh[h] = query
            oh[h] = head_rows(ox, h, heads, BLOCK).astype(BF16)
            row = cum[pl.ds(h, 1), :]
            columns = as_columns(row)
            weights = (dot_rows(query, kh[index, h]) * decay_matrix(row, columns)).astype(BF16)
            w_ref[h] = weights
            inner = dot(weights, vh[index, h])
            if index:
                inner += jnp.exp(columns) * times_state(query, first_ref[h])
            inner_ref[h] = inner

        each_head(heads, 2, one)

    by_head = in_vmem(heads, BLOCK, dim, kind=BF16)
    return pl.pallas_call(
        kernel,
        in_specs=[NEAR] * 4 + [FAR, FAR],
        out_specs=[NEAR] * 4,
        out_shape=[
            by_head, by_head, in_vmem(heads, BLOCK, BLOCK, kind=BF16), in_vmem(heads, BLOCK, dim),
        ],
        scratch_shapes=[
            pltpu.VMEM((BLOCK, heads, dim), BF16),
            pltpu.VMEM((BLOCK, heads, dim), BF16),
            pltpu.VMEM((BLOCK * heads, dim), F32),
            pltpu.VMEM((BLOCK * heads, dim), F32),
            pltpu.VMEM((heads, BLOCK), F32),
            pltpu.SemaphoreType.DMA((2,)),
        ],
        compiler_params=params(10),
        cost_estimate=cost(
            2 * heads * BLOCK * BLOCK * dim * 4, 20 * heads * BLOCK * dim, heads * BLOCK * BLOCK
        ),
        name=f"intra_{index}",
    )(log_decay, *near(kh, vh, first), *far(query_rows, output_grad))


def whole_state(core, keep_ref, recv_ref, head):
    half = keep_ref.shape[0]
    mine = (head // half) == core
    return jnp.where(mine, keep_ref[head % half], recv_ref[head % half])


def attend_kernel(
    place_ref, ld_ref, gain_ref, keep_ref, recv_ref, q0, q1, o0, o1, inner0, inner1,
    att0, att1, sums_ref, cum, squares, products,
):
    cum[0] = block_cum(ld_ref[:, :BLOCK])
    cum[1] = cum[0, :, BLOCK - 1 :] + block_cum(ld_ref[:, BLOCK:])
    squares[...] = jnp.zeros_like(squares)
    products[...] = jnp.zeros_like(products)

    def one(h):
        state = whole_state(place_ref[0], keep_ref, recv_ref, h)
        gain = gain_ref[pl.ds(h, 1), :]
        for b, (q, o, inner, att) in enumerate(((q0, o0, inner0, att0), (q1, o1, inner1, att1))):
            columns = jnp.exp(as_columns(cum[b, pl.ds(h, 1), :]))
            attended = inner[h] + columns * times_state(q[h], state)
            att[h] = attended
            squares[b] += attended * attended
            products[b] += gain * o[h].astype(F32) * attended

    each_head(ld_ref.shape[0], 2, one)
    ones = jnp.ones((8, HD), F32)
    for b in range(2):
        for at, total in enumerate((squares, products)):
            line = lax.dot_general(
                ones, total[b], (((1,), (1,)), ((), ())),
                precision=lax.Precision.HIGHEST, preferred_element_type=F32,
            )
            sums_ref[at : at + 1, b * BLOCK : (b + 1) * BLOCK] = line[:1]


def attend(place, log_decay, gain, keep, recv, parts):
    heads, tok = log_decay.shape
    dim = HD
    by_head = in_vmem(heads, BLOCK, dim)
    return pl.pallas_call(
        attend_kernel,
        in_specs=[SCALARS] + [NEAR] * 10,
        out_specs=[NEAR] * 3,
        out_shape=[by_head, by_head, in_vmem(2, tok)],
        scratch_shapes=[
            pltpu.VMEM((2, heads, BLOCK), F32),
            pltpu.VMEM((2, BLOCK, dim), F32),
            pltpu.VMEM((2, BLOCK, dim), F32),
        ],
        compiler_params=params(6),
        cost_estimate=cost(4 * heads * tok * dim * dim, 16 * heads * tok * dim),
        name="attend",
    )(place, log_decay, gain, *near(keep, recv, *parts))


def inverse_rms(sums_ref, b):
    at = slice(b * BLOCK, (b + 1) * BLOCK)
    inv = lax.rsqrt(sums_ref[0:1, at] / (HEAD_TOTAL * HD) + 1e-06)
    mean = sums_ref[1:2, at] * inv / (HEAD_TOTAL * HD)
    return inv, mean


def norm_grad_kernel(
    place_ref, ld_ref, gain_ref, sums_ref, q0, q1, o0, o1, att0, att1,
    g0, g1, own_ref, send_ref, second_ref, cum, scales, acc,
):
    heads = ld_ref.shape[0]
    half = heads // 2
    for b in range(2):
        cum[b] = block_cum(ld_ref[:, b * BLOCK : (b + 1) * BLOCK])
        inv, mean = inverse_rms(sums_ref, b)
        scales[b, 0] = as_columns(inv)
        scales[b, 1] = as_columns(inv * inv * mean)

    def one(h):
        gain = gain_ref[pl.ds(h, 1), :]
        ends = []
        for b, (q, o, att, g) in enumerate(((q0, o0, att0, g0), (q1, o1, att1, g1))):
            grad = gain * o[h].astype(F32) * scales[b, 0] - att[h] * scales[b, 1]
            grad = grad.astype(BF16)
            g[h] = grad
            queries = q[h].astype(F32).T * jnp.exp(cum[b, pl.ds(h, 1), :])
            ends.append(dot(queries.astype(BF16), grad))
        second_ref[h] = ends[1]
        first_decay = jnp.exp(cum[0, pl.ds(h, 1), :][:, BLOCK - 1 :])
        acc[h] = ends[0] + first_decay * ends[1]

    each_head(heads, 2, one)
    core = place_ref[0]
    own_ref[...] = acc[pl.ds(core * half, half)]
    send_ref[...] = acc[pl.ds((1 - core) * half, half)]


def norm_grad(place, log_decay, gain, sums, parts):
    heads, tok = log_decay.shape
    dim = HD
    half = heads // 2
    by_head = in_vmem(heads, BLOCK, dim, kind=BF16)
    return pl.pallas_call(
        norm_grad_kernel,
        in_specs=[SCALARS] + [NEAR] * 9,
        out_specs=[NEAR] * 5,
        out_shape=[
            by_head, by_head, in_vmem(half, dim, dim), in_vmem(half, dim, dim),
            in_vmem(heads, dim, dim),
        ],
        scratch_shapes=[
            pltpu.VMEM((2, heads, BLOCK), F32),
            pltpu.VMEM((2, 2, BLOCK, dim), F32),
            pltpu.VMEM((heads, dim, dim), F32),
        ],
        compiler_params=params(6),
        cost_estimate=cost(2 * heads * tok * dim * dim, 14 * heads * tok * dim),
        name="norm_grad",
    )(place, log_decay, gain, sums, *near(*parts))


def on_block(work):
    for index in range(2):
        pl.when(pl.program_id(0) == index)(lambda index=index: work(index))


def raw_output(heads, tok):
    spec = pl.BlockSpec((BLOCK, heads, HD), lambda i: (i, 0, 0))
    return spec, jax.ShapeDtypeStruct((tok, heads, HD), BF16)


def normed_kernel(gain_ref, sums_ref, att0, att1, out_ref, rows):
    heads = gain_ref.shape[0]

    def work(b):
        inv = as_columns(inverse_rms(sums_ref, b)[0])
        att = (att0, att1)[b]

        def one(h):
            rows[pl.ds(h, BLOCK, stride=heads), :] = att[h] * inv * gain_ref[pl.ds(h, 1), :]

        each_head(heads, 2, one)

    on_block(work)
    from_rows(rows, out_ref)


def normed_rows(gain, sums, att0, att1):
    heads, _, dim = att0.shape
    tok = 2 * BLOCK
    spec, shape = raw_output(heads, tok)
    return pl.pallas_call(
        normed_kernel,
        grid=(2,),
        in_specs=[NEAR] * 4,
        out_specs=spec,
        out_shape=shape,
        scratch_shapes=[pltpu.VMEM((BLOCK * heads, dim), F32)],
        compiler_params=params(7),
        cost_estimate=cost(3 * heads * tok * dim, 6 * heads * tok * dim),
        name="normed_rows",
    )(gain, sums, *near(att0, att1))


def grad_q_kernel(
    place_ref, ld_ref, keep_ref, recv_ref, first_ref, kh, vh, g0, g1, out_ref, gs_ref, cum, rows,
):
    heads = ld_ref.shape[0]

    def work(b):
        g = (g0, g1)[b]
        for x in range(2):
            cum[x] = block_cum(ld_ref[:, x * BLOCK : (x + 1) * BLOCK])

        def one(h):
            row = cum[b, pl.ds(h, 1), :]
            columns = as_columns(row)
            scores = (dot_rows(g[h], vh[b, h]) * decay_matrix(row, columns)).astype(BF16)
            gs_ref[b, h] = scores
            state = whole_state(place_ref[0], keep_ref, recv_ref, h)
            if b:
                state = jnp.exp(cum[0, pl.ds(h, 1), :][:, BLOCK - 1 :]) * state + first_ref[h]
            grad = dot(scores, kh[b, h]) + jnp.exp(columns) * times_state_t(g[h], state)
            rows[pl.ds(h, BLOCK, stride=heads), :] = grad

        each_head(heads, 2, one)

    on_block(work)
    from_rows(rows, out_ref)


def grad_query(place, log_decay, keep, recv, first, kh, vh, g0, g1):
    heads, tok = log_decay.shape
    dim = HD
    spec, shape = raw_output(heads, tok)
    return pl.pallas_call(
        grad_q_kernel,
        grid=(2,),
        in_specs=[SCALARS] + [NEAR] * 8,
        out_specs=[spec, NEAR],
        out_shape=[shape, in_vmem(2, heads, BLOCK, BLOCK, kind=BF16)],
        scratch_shapes=[pltpu.VMEM((2, heads, BLOCK), F32), pltpu.VMEM((BLOCK * heads, dim), F32)],
        compiler_params=params(8),
        cost_estimate=cost(
            4 * heads * tok * dim * (BLOCK + dim), 12 * heads * tok * dim, heads * tok * BLOCK
        ),
        name="grad_query",
    )(place, log_decay, *near(keep, recv, first, kh, vh, g0, g1))


def grad_kv_kernel(
    ld_ref, gs_ref, w0, w1, q0, q1, kh, vh, g0, g1, second_ref, dk, dv, cum,
):
    cum[...] = block_cum(ld_ref[:, :BLOCK])

    def one(h):
        row = cum[pl.ds(h, 1), :]
        columns = as_columns(jnp.exp(row[:, BLOCK - 1 :] - row))
        state = second_ref[h]
        dk[0, h] = transposed_dot(gs_ref[0, h], q0[h]) + columns * times_state_t(vh[0, h], state)
        dv[0, h] = transposed_dot(w0[h], g0[h]) + columns * times_state(kh[0, h], state)
        dk[1, h] = transposed_dot(gs_ref[1, h], q1[h])
        dv[1, h] = transposed_dot(w1[h], g1[h])

    each_head(ld_ref.shape[0], 2, one)


def grad_key_value(log_decay, gs, w0, w1, q0, q1, kh, vh, g0, g1, second):
    heads, tok = log_decay.shape
    dim = HD
    return pl.pallas_call(
        grad_kv_kernel,
        in_specs=[NEAR] * 11,
        out_specs=[NEAR] * 2,
        out_shape=[in_vmem(2, heads, BLOCK, dim)] * 2,
        scratch_shapes=[pltpu.VMEM((heads, BLOCK), F32)],
        compiler_params=params(4),
        cost_estimate=cost(4 * heads * tok * dim * (BLOCK + dim), 30 * heads * tok * dim),
        name="grad_key_value",
    )(log_decay, *near(gs, w0, w1, q0, q1, kh, vh, g0, g1, second))


def finish_kernel(
    place_ref, ld_ref, keep_ref, recv_ref, kh, vh, dk, dv, out_k, out_v, cum, rows_k, rows_v,
):
    heads = ld_ref.shape[0]

    def work(b):
        for x in range(2):
            cum[x] = block_cum(ld_ref[:, x * BLOCK : (x + 1) * BLOCK])

        def one(h):
            row = cum[b, pl.ds(h, 1), :]
            left = row[:, BLOCK - 1 :] - row
            if b == 0:
                left = left + cum[1, pl.ds(h, 1), :][:, BLOCK - 1 :]
            columns = as_columns(jnp.exp(left))
            state = whole_state(place_ref[0], keep_ref, recv_ref, h)
            at = pl.ds(h, BLOCK, stride=heads)
            rows_k[at, :] = dk[b, h] + columns * times_state_t(vh[b, h], state)
            rows_v[at, :] = dv[b, h] + columns * times_state(kh[b, h], state)

        each_head(heads, 2, one)

    on_block(work)
    from_rows(rows_k, out_k)
    from_rows(rows_v, out_v)


def finish(place, log_decay, keep, recv, kh, vh, dk, dv):
    heads, tok = log_decay.shape
    dim = HD
    spec, shape = raw_output(heads, tok)
    return pl.pallas_call(
        finish_kernel,
        grid=(2,),
        in_specs=[SCALARS] + [NEAR] * 7,
        out_specs=[spec, spec],
        out_shape=[shape, shape],
        scratch_shapes=[
            pltpu.VMEM((2, heads, BLOCK), F32),
            pltpu.VMEM((BLOCK * heads, dim), F32),
            pltpu.VMEM((BLOCK * heads, dim), F32),
        ],
        compiler_params=params(12),
        cost_estimate=cost(8 * heads * tok * dim * dim, 16 * heads * tok * dim),
        name="finish",
    )(place, log_decay, *near(keep, recv, kh, vh, dk, dv))


def swap(value, axis, bit):
    count = lax.axis_size(axis)
    return lax.ppermute(value, axis, [(i, i ^ bit) for i in range(count)])


def mix(body, place, arrays, shapes, name):
    def kernel(place_ref, *refs):
        bits = [place_ref[at] == 1 for at in range(1, 4)]
        body(bits, refs[: len(arrays)], refs[len(arrays) :])

    return pl.pallas_call(
        kernel,
        in_specs=[SCALARS] + [NEAR] * len(arrays),
        out_specs=[NEAR] * len(shapes),
        out_shape=[in_vmem(*shape) for shape in shapes],
        compiler_params=params(4),
        cost_estimate=cost(4 * 8 * HD * HD, 16 * 8 * HD * HD),
        name=name,
    )(place, *arrays)


OWN, PARTNER, CHIP, ROW, CORNER = range(5)


def mix_total(bits, own, got, d_own, d_got, first, second):
    late = bits[0]
    quarter = first.shape[0]
    for h in range(2 * quarter):
        total = jnp.where(late, 1.0, d_got(h)) * own[h, :HD] + jnp.where(late, d_own(h), 1.0) * got[h, :HD]
        if h < quarter:
            first[h, :HD] = total
        else:
            second[h - quarter] = total


def mix_total_first(bits, arrays, outputs):
    own, got = arrays
    first, second, chip = outputs
    quarter = first.shape[0]
    d_own = lambda h: own[h, HD : HD + 1]
    d_got = lambda h: got[h, HD : HD + 1]
    mix_total(bits, own, got, d_own, d_got, first, second)
    for h in range(2 * quarter):
        whole = d_own(h) * d_got(h)
        chip[h : h + 1] = whole
        place = HD + (TILE // 2) * (h // quarter)
        first[h % quarter, place : place + TILE // 2] = jnp.broadcast_to(whole, (TILE // 2, HD))


def mix_total_again(bits, arrays, outputs):
    table, own, got = arrays
    decay = lambda which: lambda h: table[which, h : h + 1]
    mix_total(bits, own, got, decay(OWN), decay(PARTNER), *outputs)


def mix_next(bits, decay, totals, gots, outputs):
    _, right, low = bits
    quarter = totals[1].shape[0]
    for i in range(quarter):
        h = i
        scale_total = jnp.where(right, 1.0, decay(ROW, h))
        scale_got = jnp.where(right, decay(CHIP, h), 1.0)
        outputs[0][i] = scale_total * totals[0][i, :HD] + scale_got * gots[0][i, :HD]
        h = quarter + i
        scale_total = jnp.where(low & right, 0.0, 1.0)
        corner = jnp.where(right, 1.0, decay(CHIP, h) * decay(CORNER, h))
        scale_got = jnp.where(low, corner, 0.0)
        outputs[1][i] = scale_total * totals[1][i] + scale_got * gots[1][i]


def mix_next_first(bits, arrays, outputs):
    own, got, chip, corner, first, second, one_a, one_b = arrays
    table = outputs[2]
    quarter = second.shape[0]
    for h in range(2 * quarter):
        place = HD + (TILE // 2) * (h // quarter)
        table[OWN, h : h + 1] = own[h, HD : HD + 1]
        table[PARTNER, h : h + 1] = got[h, HD : HD + 1]
        table[ROW, h : h + 1] = one_a[h % quarter, place : place + 1]
    table[CHIP] = chip[...]
    table[CORNER] = corner[...]
    decay = lambda which, h: table[which, h : h + 1]
    mix_next(bits, decay, (first, second), (one_a, one_b), outputs[:2])


def mix_next_again(bits, arrays, outputs):
    table, first, second, one_a, one_b = arrays
    decay = lambda which, h: table[which, h : h + 1]
    mix_next(bits, decay, (first, second), (one_a, one_b), outputs)


def mix_enter(bits, arrays, outputs):
    table, own, got, one_a, one_b, two_a, two_b = arrays
    kept, sent = outputs
    late, right, low = bits
    quarter = one_b.shape[0]
    decay = lambda which, h: table[which, h : h + 1]
    for h in range(2 * quarter):
        i = h % quarter
        row = jnp.where(right, decay(ROW, h), 1.0)
        if h < quarter:
            one, two = one_a[i, :HD], two_a[i]
            scale_one = jnp.where(right, 1.0, 0.0)
            scale_two = jnp.where(low, row, 0.0)
        else:
            one, two = one_b[i], two_b[i]
            scale_one = jnp.where(low, jnp.where(right, row, decay(CORNER, h)), 0.0)
            scale_two = jnp.where(low | right, 1.0, 0.0)
        enter = scale_one * one + scale_two * two
        after = jnp.where(late, decay(PARTNER, h), decay(OWN, h)) * enter
        after += jnp.where(late, got[h, :HD], own[h, :HD])
        kept[h] = jnp.where(late, after, enter)
        sent[h] = jnp.where(late, enter, after)


def entering_quad(own, send, table, place, tasks, name):
    def work(stage, after, before=()):
        if stage not in tasks:
            return before
        run, outputs = tasks[stage]
        outputs.extend(run(after))
        return lax.optimization_barrier((before, outputs[-1]))[0]

    half = own.shape[0]
    quarter = half // 2
    states, wide = (quarter, HD, HD), (quarter, HD + TILE, HD)
    got = swap(send, "seq", 1)
    if table is None:
        first, second, chip = mix(
            mix_total_first, place, (own, got), (wide, states, (half, HD)), name + "_total"
        )
    else:
        first, second = mix(
            mix_total_again, place, (table, own, got), (states, states), name + "_total"
        )
    one_a, one_b = swap(first, "seq", 2), swap(second, "seq", 4)
    if table is None:
        corner = swap(chip, "seq", 6)
        one_a, one_b, corner = work(1, second, (one_a, one_b, corner))
        next_a, next_b, table = mix(
            mix_next_first, place, (own, got, chip, corner, first, second, one_a, one_b),
            (states, states, (5, half, HD)), name + "_next",
        )
    else:
        one_a, one_b = work(1, second, (one_a, one_b))
        next_a, next_b = mix(
            mix_next_again, place, (table, first, second, one_a, one_b), (states, states),
            name + "_next",
        )
    two_a, two_b = swap(next_a, "seq", 4), swap(next_b, "seq", 2)
    two_a, two_b = work(2, next_b, (two_a, two_b))
    kept, sent = mix(
        mix_enter, place, (table, own, got, one_a, one_b, two_a, two_b),
        ((half, HD, HD), (half, HD, HD)), name + "_enter",
    )
    received = swap(sent, "seq", 1)
    work(3, sent)
    return kept, received, table


def entering_any(own, send, log_total, backward, tasks):
    for run, outputs in tasks.values():
        outputs.extend(run(send))
    count, mine = lax.axis_size("seq"), lax.axis_index("seq")
    core = mine % 2
    own, send = own[:, :HD], send[:, :HD]
    half = own.shape[0]
    in_order = jnp.where(
        core == 0, jnp.concatenate([own, send], axis=0), jnp.concatenate([send, own], axis=0)
    )
    states = lax.all_gather(in_order, "seq")
    decays = jnp.exp(lax.all_gather(log_total, "seq"))
    place = mine
    if backward:
        states, decays, place = states[::-1], decays[::-1], count - 1 - mine

    def step(at, total):
        longer = decays[at][:, None, None] * total + states[at]
        return jnp.where(at < place, longer, total)

    total = lax.fori_loop(0, count - 1, step, jnp.zeros_like(in_order))
    kept = lax.dynamic_slice_in_dim(total, core * half, half)
    return kept, lax.dynamic_slice_in_dim(total, (1 - core) * half, half)


def sum_over_heads(value):
    count = lax.axis_size("head")
    reach = 1
    while 2 * reach <= count and count % (2 * reach) == 0:
        value = value + swap(value, "head", reach)
        reach *= 2
    part = value
    for shift in range(1, count // reach):
        value = value + lax.ppermute(
            part, "head", [(i, (i + shift * reach) % count) for i in range(count)]
        )
    return value


def follows(value, earlier):
    return lax.optimization_barrier((value, earlier))[0]


def on_device(query_rows, key_rows, value_rows, output_grad, norm_gain, log_decay):
    mine = lax.axis_index("seq")
    bits = jnp.stack([(mine >> at) % 2 for at in range(3)])
    core = bits[:1]
    ahead = jnp.concatenate([core, bits]).astype(jnp.int32)
    behind = jnp.concatenate([core, 1 - bits]).astype(jnp.int32)
    table = [None]

    def entering(own, send, backward, tasks):
        if lax.axis_size("seq") != 8:
            return entering_any(own, send, jnp.sum(log_decay, axis=1), backward, tasks)
        kept, received, table[0] = entering_quad(
            own, send, table[0], behind if backward else ahead, tasks,
            "later" if backward else "earlier",
        )
        return kept, received

    own, send, first, kh, vh = local_state(ahead, log_decay, key_rows, value_rows)

    def forward_task(index):
        return lambda earlier: intra(
            index, log_decay, kh, vh, follows(first, earlier), query_rows, output_grad
        )

    in_0, in_1 = [], []
    keep, recv = entering(
        own, send, False, {1: (forward_task(0), in_0), 2: (forward_task(1), in_1)}
    )
    q0, o0, w0, inner0 = in_0
    q1, o1, w1, inner1 = in_1
    att0, att1, sums = attend(
        ahead, log_decay, norm_gain, keep, recv, (q0, q1, o0, o1, inner0, inner1)
    )
    sums = sum_over_heads(sums)
    g0, g1, grad_own, grad_send, second = norm_grad(
        ahead, log_decay, norm_gain, sums, (q0, q1, o0, o1, att0, att1)
    )
    queries, pairs, norms = [], [], []

    def query_task(earlier):
        return grad_query(
            ahead, log_decay, keep, recv, follows(first, earlier), kh, vh, g0, g1
        )

    def pair_task(earlier):
        return grad_key_value(
            log_decay, queries[1], w0, w1, q0, q1, kh, vh, g0, g1, follows(second, earlier)
        )

    def norm_task(earlier):
        return [normed_rows(follows(norm_gain, earlier), sums, att0, att1)]

    grad_keep, grad_recv = entering(
        grad_own, grad_send, True, {1: (query_task, queries), 2: (pair_task, pairs), 3: (norm_task, norms)}
    )
    grad_k, grad_v = finish(ahead, log_decay, grad_keep, grad_recv, kh, vh, *pairs)
    return norms[0], queries[0], grad_k, grad_v


def solution(mesh):
    rows = P("seq", "head", None)
    return jax.shard_map(
        on_device,
        mesh=mesh,
        in_specs=(rows, rows, rows, rows, P("head", None), P("head", "seq")),
        out_specs=(rows, rows, rows, rows),
        check_vma=False,
    )
```

```python
import jax
import jax.numpy as jnp
from jax import lax
from jax.experimental import pallas as pl
from jax.experimental.pallas import tpu as pltpu
from jax.sharding import PartitionSpec as P

HEAD_TOTAL = 64
HD = 128
BLOCK = 256
CHUNK = 128
TILE = 8
F32 = jnp.float32
BF16 = jnp.bfloat16
MIB = 1024 * 1024
NEAR = pl.BlockSpec(memory_space=pltpu.VMEM)
FAR = pl.BlockSpec(memory_space=pl.ANY)
LOWER, UPPER, LATE, RIGHT, LOW = range(5)


def in_vmem(*shape, kind=F32):
    return pltpu.VMEM(shape, kind)


def near(*arrays):
    return [pltpu.with_memory_space_constraint(array, pltpu.VMEM) for array in arrays]


def far(*arrays):
    return [pltpu.with_memory_space_constraint(array, pltpu.HBM) for array in arrays]


def params(mib):
    return pltpu.CompilerParams(vmem_limit_bytes=mib * MIB)


def cost(flops, moved, exps=0):
    return pl.CostEstimate(flops=flops, bytes_accessed=moved, transcendentals=exps)


def block_cum(log_decay):
    size = log_decay.shape[1]
    upper = lax.broadcasted_iota(jnp.int32, (size, size), 0) <= lax.broadcasted_iota(
        jnp.int32, (size, size), 1
    )
    return jnp.dot(
        log_decay,
        jnp.where(upper, 1.0, 0.0).astype(F32),
        precision=lax.Precision.HIGHEST,
        preferred_element_type=F32,
    )


def as_columns(row):
    return jnp.broadcast_to(row, (HD, row.shape[1])).T


def dot(a, b):
    return jnp.dot(a, b, preferred_element_type=F32)


def dot_rows(a, b):
    return lax.dot_general(a, b, (((1,), (1,)), ((), ())), preferred_element_type=F32)


def two_parts(matrix):
    high = matrix.astype(BF16)
    return high, (matrix - high.astype(F32)).astype(BF16)


def times_state(rows, state):
    return dot(jnp.concatenate([rows, rows], axis=1), jnp.concatenate(two_parts(state), axis=0))


def times_state_t(rows, state):
    return dot_rows(
        jnp.concatenate([rows, rows], axis=1), jnp.concatenate(two_parts(state), axis=1)
    )


def causal(table, row, columns):
    half = row.shape[1] // 2
    lower = lax.broadcasted_iota(jnp.int32, (half, half), 0) >= lax.broadcasted_iota(
        jnp.int32, (half, half), 1
    )
    quarters = []
    for t in range(2):
        for s in range(t + 1):
            gap = columns[t * half : (t + 1) * half] - row[:, s * half : (s + 1) * half]
            if t == s:
                gap = jnp.where(lower, gap, -jnp.inf)
            part = table[t * half : (t + 1) * half, s * half : (s + 1) * half]
            quarters.append((part * jnp.exp(gap)).astype(BF16))
    top = jnp.concatenate([quarters[0], jnp.zeros_like(quarters[0])], axis=1)
    return jnp.concatenate([top, jnp.concatenate(quarters[1:], axis=1)], axis=0)


def transposed_dot(a, b):
    return lax.dot_general(a, b, (((0,), (0,)), ((), ())), preferred_element_type=F32)


def each_head(heads, unroll, body):
    def step(h, carry):
        body(h)
        return carry

    lax.fori_loop(0, heads, step, 0, unroll=unroll)


def turn_tiles(tiles):
    count = len(tiles)
    at = lax.broadcasted_iota(jnp.int32, tiles[0].shape, 0)
    turned = [tile if i == 0 else pltpu.roll(tile, i, 0) for i, tile in enumerate(tiles)]
    reach = 1
    while reach < count:
        odd = (at & reach) != 0
        turned = [
            jnp.where(odd, turned[(n + reach) % count], turned[n]) for n in range(count)
        ]
        reach *= 2
    picked = [turned[-j % count] for j in range(count)]
    return [tile if j == 0 else pltpu.roll(tile, count - j, 0) for j, tile in enumerate(picked)]


def to_heads(dst, block):
    tok, heads, _ = block.shape

    def step(group, carry):
        at = pl.multiple_of(group * 2 * TILE, 2 * TILE)
        tokens = block[pl.ds(at, 2 * TILE)].astype(F32)
        for first in range(0, heads, TILE):
            halves = [
                turn_tiles([tokens[base + i, first : first + TILE] for i in range(TILE)])
                for base in (0, TILE)
            ]
            for j in range(TILE):
                both = jnp.concatenate([halves[0][j], halves[1][j]], axis=0)
                dst[first + j, pl.ds(at, 2 * TILE)] = both.astype(BF16)
        return carry

    lax.fori_loop(0, tok // (2 * TILE), step, 0, unroll=2)


def from_heads(block, src, start, tok):
    heads = src.shape[0]

    def step(group, carry):
        at = pl.multiple_of(group * TILE, TILE)
        parts = [
            turn_tiles([src[first + i, pl.ds(start + at, TILE)] for i in range(TILE)])
            for first in range(0, heads, TILE)
        ]
        for j in range(TILE):
            block[at + j] = jnp.concatenate([part[j] for part in parts], axis=0).astype(BF16)
        return carry

    lax.fori_loop(0, tok // TILE, step, 0, unroll=2)


def is_set(place_ref, which):
    return place_ref[which : which + 1] > 0.5


def split_halves(place_ref, whole, own_ref, send_ref):
    half = own_ref.shape[0]
    mine = is_set(place_ref, LOWER)
    for i in range(half):
        own_ref[i, :HD] = jnp.where(mine, whole[i], whole[half + i])
        send_ref[i, :HD] = jnp.where(mine, whole[half + i], whole[i])


def state_kernel(
    place_ref, ld_hbm, k_hbm, v_hbm, own_ref, send_ref, first_ref, kh, vh,
    ld_ref, k_raw, v_raw, cum, acc, decay, sems,
):
    heads, tok = ld_ref.shape
    half = heads // 2
    per_block = BLOCK // CHUNK
    copies = [pltpu.make_async_copy(ld_hbm, ld_ref, sems.at[0])]
    for c in range(tok // CHUNK):
        at = pl.ds(c * CHUNK, CHUNK)
        copies.append(pltpu.make_async_copy(k_hbm.at[at], k_raw.at[at], sems.at[2 * c + 1]))
        copies.append(pltpu.make_async_copy(v_hbm.at[at], v_raw.at[at], sems.at[2 * c + 2]))
    for copy in copies:
        copy.start()
    copies[0].wait()
    for b in range(2):
        cum[b] = block_cum(ld_ref[:, b * BLOCK : (b + 1) * BLOCK])
    ends = cum[0, :, BLOCK - 1 :] + cum[1, :, BLOCK - 1 :]
    decay[...] = jnp.broadcast_to(jnp.exp(ends), decay.shape)

    for b in range(2):
        for c in range(per_block):
            at = pl.ds((b * per_block + c) * CHUNK, CHUNK)
            here = pl.ds(c * CHUNK, CHUNK)
            which = 2 * (b * per_block + c) + 1
            copies[which].wait()
            to_heads(kh.at[b, :, here], k_raw.at[at])
            copies[which + 1].wait()
            to_heads(vh.at[b, :, here], v_raw.at[at])

        def one(h, b=b):
            row = cum[b, pl.ds(h, 1), :]
            scale = jnp.exp(row[:, BLOCK - 1 :] - row)
            state = dot((kh[b, h].astype(F32).T * scale).astype(BF16), vh[b, h])
            if b == 0:
                first_ref[h] = state
            else:
                acc[h] = state + jnp.exp(row[:, BLOCK - 1 :]) * first_ref[h]

        each_head(heads, 4, one)

    split_halves(place_ref, acc, own_ref, send_ref)
    mine = is_set(place_ref, LOWER)
    for i in range(half):
        lower, upper = decay[i : i + 1], decay[half + i : half + i + 1]
        for ref, row in (
            (own_ref, jnp.where(mine, lower, upper)), (send_ref, jnp.where(mine, upper, lower)),
        ):
            ref[i, HD:] = jnp.broadcast_to(row, (TILE, HD))


def local_state(place, log_decay, key_rows, value_rows):
    tok, heads, dim = key_rows.shape
    half = heads // 2
    by_head = in_vmem(2, heads, BLOCK, dim, kind=BF16)
    return pl.pallas_call(
        state_kernel,
        in_specs=[NEAR, FAR, FAR, FAR],
        out_specs=[NEAR] * 5,
        out_shape=[
            in_vmem(half, dim + TILE, dim), in_vmem(half, dim + TILE, dim),
            in_vmem(heads, dim, dim), by_head, by_head,
        ],
        scratch_shapes=[
            pltpu.VMEM((heads, tok), F32),
            pltpu.VMEM((tok, heads, dim), BF16),
            pltpu.VMEM((tok, heads, dim), BF16),
            pltpu.VMEM((2, heads, BLOCK), F32),
            pltpu.VMEM((heads, dim, dim), F32),
            pltpu.VMEM((heads, dim), F32),
            pltpu.SemaphoreType.DMA((2 * (tok // CHUNK) + 1,)),
        ],
        compiler_params=params(8),
        cost_estimate=cost(2 * tok * heads * dim * dim, 8 * tok * heads * dim),
        name="local_state",
    )(place, *far(log_decay, key_rows, value_rows))


def intra(index, log_decay, kh, vh, first, query_rows, output_grad):
    tok, heads, dim = query_rows.shape

    def kernel(ld_ref, kh, vh, first_ref, q_hbm, o_hbm, qh, oh, w_ref, inner_ref,
               q_raw, o_raw, cum, sems):
        at = pl.ds(index * BLOCK, BLOCK)
        copy_q = pltpu.make_async_copy(q_hbm.at[at], q_raw, sems.at[0])
        copy_o = pltpu.make_async_copy(o_hbm.at[at], o_raw, sems.at[1])
        copy_q.start()
        copy_o.start()
        cum[...] = block_cum(ld_ref[:, index * BLOCK : (index + 1) * BLOCK])
        copy_q.wait()
        to_heads(qh, q_raw)
        copy_o.wait()
        to_heads(oh, o_raw)

        def one(h):
            query = qh[h]
            row = cum[pl.ds(h, 1), :]
            columns = as_columns(row)
            weights = causal(dot_rows(query, kh[index, h]), row, columns)
            w_ref[h] = weights
            inner = dot(weights, vh[index, h])
            if index:
                inner += jnp.exp(columns) * times_state(query, first_ref[h])
            inner_ref[h] = inner

        each_head(heads, 2, one)

    by_head = in_vmem(heads, BLOCK, dim, kind=BF16)
    return pl.pallas_call(
        kernel,
        in_specs=[NEAR] * 4 + [FAR, FAR],
        out_specs=[NEAR] * 4,
        out_shape=[
            by_head, by_head, in_vmem(heads, BLOCK, BLOCK, kind=BF16), in_vmem(heads, BLOCK, dim),
        ],
        scratch_shapes=[
            pltpu.VMEM((BLOCK, heads, dim), BF16),
            pltpu.VMEM((BLOCK, heads, dim), BF16),
            pltpu.VMEM((heads, BLOCK), F32),
            pltpu.SemaphoreType.DMA((2,)),
        ],
        compiler_params=params(6),
        cost_estimate=cost(
            2 * heads * BLOCK * BLOCK * dim * 4, 20 * heads * BLOCK * dim, heads * BLOCK * BLOCK
        ),
        name=f"intra_{index}",
    )(log_decay, *near(kh, vh, first), *far(query_rows, output_grad))


def whole_state(place_ref, keep_ref, recv_ref, head):
    half = keep_ref.shape[0]
    mine = place_ref[pl.ds(head // half, 1)] > 0.5
    return jnp.where(mine, keep_ref[head % half], recv_ref[head % half])


def attend_kernel(
    place_ref, ld_ref, gain_ref, keep_ref, recv_ref, q0, q1, o0, o1, inner0, inner1,
    att0, att1, sums_ref, cum, squares, products,
):
    cum[0] = block_cum(ld_ref[:, :BLOCK])
    cum[1] = cum[0, :, BLOCK - 1 :] + block_cum(ld_ref[:, BLOCK:])
    squares[...] = jnp.zeros_like(squares)
    products[...] = jnp.zeros_like(products)

    def one(h):
        state = whole_state(place_ref, keep_ref, recv_ref, h)
        gain = gain_ref[pl.ds(h, 1), :]
        for b, (q, o, inner, att) in enumerate(((q0, o0, inner0, att0), (q1, o1, inner1, att1))):
            columns = as_columns(jnp.exp(cum[b, pl.ds(h, 1), :]))
            attended = inner[h] + columns * times_state(q[h], state)
            att[h] = attended
            squares[b] += attended * attended
            products[b] += gain * o[h].astype(F32) * attended

    each_head(ld_ref.shape[0], 2, one)
    ones = jnp.ones((8, HD), F32)
    for b in range(2):
        for at, total in enumerate((squares, products)):
            line = lax.dot_general(
                ones, total[b], (((1,), (1,)), ((), ())),
                precision=lax.Precision.HIGHEST, preferred_element_type=F32,
            )
            sums_ref[at : at + 1, b * BLOCK : (b + 1) * BLOCK] = line[:1]


def attend(place, log_decay, gain, keep, recv, parts):
    heads, tok = log_decay.shape
    dim = HD
    by_head = in_vmem(heads, BLOCK, dim)
    return pl.pallas_call(
        attend_kernel,
        in_specs=[NEAR] + [NEAR] * 10,
        out_specs=[NEAR] * 3,
        out_shape=[by_head, by_head, in_vmem(2, tok)],
        scratch_shapes=[
            pltpu.VMEM((2, heads, BLOCK), F32),
            pltpu.VMEM((2, BLOCK, dim), F32),
            pltpu.VMEM((2, BLOCK, dim), F32),
        ],
        compiler_params=params(6),
        cost_estimate=cost(4 * heads * tok * dim * dim, 16 * heads * tok * dim),
        name="attend",
    )(place, log_decay, gain, *near(keep, recv, *parts))


def inverse_rms(sums_ref, b):
    at = slice(b * BLOCK, (b + 1) * BLOCK)
    inv = lax.rsqrt(sums_ref[0:1, at] / (HEAD_TOTAL * HD) + 1e-06)
    mean = sums_ref[1:2, at] * inv / (HEAD_TOTAL * HD)
    return inv, mean


def norm_grad_kernel(
    place_ref, ld_ref, gain_ref, sums_ref, q0, q1, o0, o1, att0, att1,
    g0, g1, own_ref, send_ref, second_ref, cum, scales, acc,
):
    heads = ld_ref.shape[0]
    for b in range(2):
        cum[b] = block_cum(ld_ref[:, b * BLOCK : (b + 1) * BLOCK])
        inv, mean = inverse_rms(sums_ref, b)
        scales[b, 0] = as_columns(inv)
        scales[b, 1] = as_columns(inv * inv * mean)

    def one(h):
        gain = gain_ref[pl.ds(h, 1), :]
        ends = []
        for b, (q, o, att, g) in enumerate(((q0, o0, att0, g0), (q1, o1, att1, g1))):
            grad = gain * o[h].astype(F32) * scales[b, 0] - att[h] * scales[b, 1]
            grad = grad.astype(BF16)
            g[h] = grad
            queries = q[h].astype(F32).T * jnp.exp(cum[b, pl.ds(h, 1), :])
            ends.append(dot(queries.astype(BF16), grad))
        second_ref[h] = ends[1]
        first_decay = jnp.exp(cum[0, pl.ds(h, 1), :][:, BLOCK - 1 :])
        acc[h] = ends[0] + first_decay * ends[1]

    each_head(heads, 2, one)
    split_halves(place_ref, acc, own_ref, send_ref)


def norm_grad(place, log_decay, gain, sums, parts):
    heads, tok = log_decay.shape
    dim = HD
    half = heads // 2
    by_head = in_vmem(heads, BLOCK, dim, kind=BF16)
    return pl.pallas_call(
        norm_grad_kernel,
        in_specs=[NEAR] + [NEAR] * 9,
        out_specs=[NEAR] * 5,
        out_shape=[
            by_head, by_head, in_vmem(half, dim, dim), in_vmem(half, dim, dim),
            in_vmem(heads, dim, dim),
        ],
        scratch_shapes=[
            pltpu.VMEM((2, heads, BLOCK), F32),
            pltpu.VMEM((2, 2, BLOCK, dim), F32),
            pltpu.VMEM((heads, dim, dim), F32),
        ],
        compiler_params=params(6),
        cost_estimate=cost(2 * heads * tok * dim * dim, 14 * heads * tok * dim),
        name="norm_grad",
    )(place, log_decay, gain, sums, *near(*parts))


def on_block(work):
    for index in range(2):
        pl.when(pl.program_id(0) == index)(lambda index=index: work(index))


def raw_output(heads, tok):
    spec = pl.BlockSpec((BLOCK, heads, HD), lambda i: (i, 0, 0))
    return spec, jax.ShapeDtypeStruct((tok, heads, HD), BF16)


def normed_kernel(gain_ref, sums_ref, att0, att1, out_ref, rows):
    heads = gain_ref.shape[0]

    def work(b):
        inv = as_columns(inverse_rms(sums_ref, b)[0])
        att = (att0, att1)[b]

        def one(h):
            rows[h] = att[h] * inv * gain_ref[pl.ds(h, 1), :]

        each_head(heads, 2, one)

    on_block(work)
    from_heads(out_ref, rows, 0, BLOCK)


def normed_rows(gain, sums, att0, att1):
    heads, _, dim = att0.shape
    tok = 2 * BLOCK
    spec, shape = raw_output(heads, tok)
    return pl.pallas_call(
        normed_kernel,
        grid=(2,),
        in_specs=[NEAR] * 4,
        out_specs=spec,
        out_shape=shape,
        scratch_shapes=[pltpu.VMEM((heads, BLOCK, dim), F32)],
        compiler_params=params(7),
        cost_estimate=cost(3 * heads * tok * dim, 6 * heads * tok * dim),
        name="normed_rows",
    )(gain, sums, *near(att0, att1))


def grad_q_kernel(
    place_ref, ld_ref, keep_ref, recv_ref, first_ref, kh, vh, g0, g1, out_ref, gs_ref, cum, rows,
):
    heads = ld_ref.shape[0]

    def work(b):
        g = (g0, g1)[b]
        for x in range(2):
            cum[x] = block_cum(ld_ref[:, x * BLOCK : (x + 1) * BLOCK])

        def one(h):
            row = cum[b, pl.ds(h, 1), :]
            columns = as_columns(row)
            scores = causal(dot_rows(g[h], vh[b, h]), row, columns)
            gs_ref[b, h] = scores
            state = whole_state(place_ref, keep_ref, recv_ref, h)
            if b:
                state = jnp.exp(cum[0, pl.ds(h, 1), :][:, BLOCK - 1 :]) * state + first_ref[h]
            grad = dot(scores, kh[b, h]) + jnp.exp(columns) * times_state_t(g[h], state)
            rows[h] = grad

        each_head(heads, 2, one)

    on_block(work)
    from_heads(out_ref, rows, 0, BLOCK)


def grad_query(place, log_decay, keep, recv, first, kh, vh, g0, g1):
    heads, tok = log_decay.shape
    dim = HD
    spec, shape = raw_output(heads, tok)
    return pl.pallas_call(
        grad_q_kernel,
        grid=(2,),
        in_specs=[NEAR] + [NEAR] * 8,
        out_specs=[spec, NEAR],
        out_shape=[shape, in_vmem(2, heads, BLOCK, BLOCK, kind=BF16)],
        scratch_shapes=[pltpu.VMEM((2, heads, BLOCK), F32), pltpu.VMEM((heads, BLOCK, dim), F32)],
        compiler_params=params(8),
        cost_estimate=cost(
            4 * heads * tok * dim * (BLOCK + dim), 12 * heads * tok * dim, heads * tok * BLOCK
        ),
        name="grad_query",
    )(place, log_decay, *near(keep, recv, first, kh, vh, g0, g1))


def grad_kv_kernel(
    ld_ref, gs_ref, w0, w1, q0, q1, kh, vh, g0, g1, second_ref, dk, dv, cum,
):
    cum[...] = block_cum(ld_ref[:, :BLOCK])

    def one(h):
        row = cum[pl.ds(h, 1), :]
        columns = as_columns(jnp.exp(row[:, BLOCK - 1 :] - row))
        state = second_ref[h]
        dk[0, h] = transposed_dot(gs_ref[0, h], q0[h]) + columns * times_state_t(vh[0, h], state)
        dv[0, h] = transposed_dot(w0[h], g0[h]) + columns * times_state(kh[0, h], state)
        dk[1, h] = transposed_dot(gs_ref[1, h], q1[h])
        dv[1, h] = transposed_dot(w1[h], g1[h])

    each_head(ld_ref.shape[0], 2, one)


def grad_key_value(log_decay, gs, w0, w1, q0, q1, kh, vh, g0, g1, second):
    heads, tok = log_decay.shape
    dim = HD
    return pl.pallas_call(
        grad_kv_kernel,
        in_specs=[NEAR] * 11,
        out_specs=[NEAR] * 2,
        out_shape=[in_vmem(2, heads, BLOCK, dim)] * 2,
        scratch_shapes=[pltpu.VMEM((heads, BLOCK), F32)],
        compiler_params=params(4),
        cost_estimate=cost(4 * heads * tok * dim * (BLOCK + dim), 30 * heads * tok * dim),
        name="grad_key_value",
    )(log_decay, *near(gs, w0, w1, q0, q1, kh, vh, g0, g1, second))


def finish_kernel(
    place_ref, ld_ref, keep_ref, recv_ref, kh, vh, dk, dv, out_k, out_v, cum, rows_k, rows_v,
    raw_k, raw_v, sems,
):
    heads = ld_ref.shape[0]
    for x in range(2):
        cum[x] = block_cum(ld_ref[:, x * BLOCK : (x + 1) * BLOCK])
    copies = []
    for b in range(2):

        def one(h, b=b):
            row = cum[b, pl.ds(h, 1), :]
            left = row[:, BLOCK - 1 :] - row
            if b == 0:
                left = left + cum[1, pl.ds(h, 1), :][:, BLOCK - 1 :]
            columns = as_columns(jnp.exp(left))
            state = whole_state(place_ref, keep_ref, recv_ref, h)
            rows_k[h] = dk[b, h] + columns * times_state_t(vh[b, h], state)
            rows_v[h] = dv[b, h] + columns * times_state(kh[b, h], state)

        each_head(heads, 2, one)
        for start in range(0, BLOCK, CHUNK):
            at = pl.ds(b * BLOCK + start, CHUNK)
            for rows, raw, out in ((rows_k, raw_k, out_k), (rows_v, raw_v, out_v)):
                from_heads(raw.at[at], rows, start, CHUNK)
                copies.append(pltpu.make_async_copy(raw.at[at], out.at[at], sems.at[len(copies)]))
                copies[-1].start()
    for copy in copies:
        copy.wait()


def finish(place, log_decay, keep, recv, kh, vh, dk, dv):
    heads, tok = log_decay.shape
    dim = HD
    shape = jax.ShapeDtypeStruct((tok, heads, dim), BF16)
    return pl.pallas_call(
        finish_kernel,
        in_specs=[NEAR] * 8,
        out_specs=[FAR, FAR],
        out_shape=[shape, shape],
        scratch_shapes=[
            pltpu.VMEM((2, heads, BLOCK), F32),
            pltpu.VMEM((heads, BLOCK, dim), F32),
            pltpu.VMEM((heads, BLOCK, dim), F32),
            pltpu.VMEM((tok, heads, dim), BF16),
            pltpu.VMEM((tok, heads, dim), BF16),
            pltpu.SemaphoreType.DMA((2 * (tok // CHUNK),)),
        ],
        compiler_params=params(12),
        cost_estimate=cost(8 * heads * tok * dim * dim, 16 * heads * tok * dim),
        name="finish",
    )(place, log_decay, *near(keep, recv, kh, vh, dk, dv))


def swap(value, axis, bit):
    count = lax.axis_size(axis)
    return lax.ppermute(value, axis, [(i, i ^ bit) for i in range(count)])


def mix(body, place, arrays, shapes, name):
    def kernel(place_ref, *refs):
        bits = [is_set(place_ref, which) for which in (LATE, RIGHT, LOW)]
        body(bits, refs[: len(arrays)], refs[len(arrays) :])

    return pl.pallas_call(
        kernel,
        in_specs=[NEAR] + [NEAR] * len(arrays),
        out_specs=[NEAR] * len(shapes),
        out_shape=[in_vmem(*shape) for shape in shapes],
        compiler_params=params(4),
        cost_estimate=cost(4 * 8 * HD * HD, 16 * 8 * HD * HD),
        name=name,
    )(place, *arrays)


OWN, PARTNER, CHIP, ROW, CORNER = range(5)


def mix_total(bits, own, got, d_own, d_got, first, second):
    late = bits[0]
    quarter = first.shape[0]
    for h in range(2 * quarter):
        total = jnp.where(late, 1.0, d_got(h)) * own[h, :HD] + jnp.where(late, d_own(h), 1.0) * got[h, :HD]
        if h < quarter:
            first[h, :HD] = total
        else:
            second[h - quarter] = total


def mix_total_first(bits, arrays, outputs):
    own, got = arrays
    first, second, chip = outputs
    quarter = first.shape[0]
    d_own = lambda h: own[h, HD : HD + 1]
    d_got = lambda h: got[h, HD : HD + 1]
    mix_total(bits, own, got, d_own, d_got, first, second)
    for h in range(2 * quarter):
        whole = d_own(h) * d_got(h)
        chip[h : h + 1] = whole
        place = HD + (TILE // 2) * (h // quarter)
        first[h % quarter, place : place + TILE // 2] = jnp.broadcast_to(whole, (TILE // 2, HD))


def mix_total_again(bits, arrays, outputs):
    table, own, got = arrays
    decay = lambda which: lambda h: table[which, h : h + 1]
    mix_total(bits, own, got, decay(OWN), decay(PARTNER), *outputs)


def mix_next(bits, decay, totals, gots, outputs):
    _, right, low = bits
    quarter = totals[1].shape[0]
    for i in range(quarter):
        h = i
        scale_total = jnp.where(right, 1.0, decay(ROW, h))
        scale_got = jnp.where(right, decay(CHIP, h), 1.0)
        outputs[0][i] = scale_total * totals[0][i, :HD] + scale_got * gots[0][i, :HD]
        h = quarter + i
        scale_total = jnp.where(low & right, 0.0, 1.0)
        corner = jnp.where(right, 1.0, decay(CHIP, h) * decay(CORNER, h))
        scale_got = jnp.where(low, corner, 0.0)
        outputs[1][i] = scale_total * totals[1][i] + scale_got * gots[1][i]


def mix_next_first(bits, arrays, outputs):
    own, got, chip, corner, first, second, one_a, one_b = arrays
    table = outputs[2]
    quarter = second.shape[0]
    for h in range(2 * quarter):
        place = HD + (TILE // 2) * (h // quarter)
        table[OWN, h : h + 1] = own[h, HD : HD + 1]
        table[PARTNER, h : h + 1] = got[h, HD : HD + 1]
        table[ROW, h : h + 1] = one_a[h % quarter, place : place + 1]
    table[CHIP] = chip[...]
    table[CORNER] = corner[...]
    decay = lambda which, h: table[which, h : h + 1]
    mix_next(bits, decay, (first, second), (one_a, one_b), outputs[:2])


def mix_next_again(bits, arrays, outputs):
    table, first, second, one_a, one_b = arrays
    decay = lambda which, h: table[which, h : h + 1]
    mix_next(bits, decay, (first, second), (one_a, one_b), outputs)


def mix_enter(bits, arrays, outputs):
    table, own, got, one_a, one_b, two_a, two_b = arrays
    kept, sent = outputs
    late, right, low = bits
    quarter = one_b.shape[0]
    decay = lambda which, h: table[which, h : h + 1]
    for h in range(2 * quarter):
        i = h % quarter
        row = jnp.where(right, decay(ROW, h), 1.0)
        if h < quarter:
            one, two = one_a[i, :HD], two_a[i]
            scale_one = jnp.where(right, 1.0, 0.0)
            scale_two = jnp.where(low, row, 0.0)
        else:
            one, two = one_b[i], two_b[i]
            scale_one = jnp.where(low, jnp.where(right, row, decay(CORNER, h)), 0.0)
            scale_two = jnp.where(low | right, 1.0, 0.0)
        enter = scale_one * one + scale_two * two
        after = jnp.where(late, decay(PARTNER, h), decay(OWN, h)) * enter
        after += jnp.where(late, got[h, :HD], own[h, :HD])
        kept[h] = jnp.where(late, after, enter)
        sent[h] = jnp.where(late, enter, after)


def entering_quad(own, send, table, place, tasks, name):
    def work(stage, after, before=()):
        if stage not in tasks:
            return before
        run, outputs = tasks[stage]
        outputs.extend(run(after))
        return lax.optimization_barrier((before, outputs[-1]))[0]

    half = own.shape[0]
    quarter = half // 2
    states, wide = (quarter, HD, HD), (quarter, HD + TILE, HD)
    got = swap(send, "seq", 1)
    if table is None:
        first, second, chip = mix(
            mix_total_first, place, (own, got), (wide, states, (half, HD)), name + "_total"
        )
    else:
        first, second = mix(
            mix_total_again, place, (table, own, got), (states, states), name + "_total"
        )
    one_a, one_b = swap(first, "seq", 2), swap(second, "seq", 4)
    if table is None:
        corner = swap(chip, "seq", 6)
        one_a, one_b, corner = work(1, second, (one_a, one_b, corner))
        next_a, next_b, table = mix(
            mix_next_first, place, (own, got, chip, corner, first, second, one_a, one_b),
            (states, states, (5, half, HD)), name + "_next",
        )
    else:
        one_a, one_b = work(1, second, (one_a, one_b))
        next_a, next_b = mix(
            mix_next_again, place, (table, first, second, one_a, one_b), (states, states),
            name + "_next",
        )
    two_a, two_b = swap(next_a, "seq", 4), swap(next_b, "seq", 2)
    two_a, two_b = work(2, next_b, (two_a, two_b))
    kept, sent = mix(
        mix_enter, place, (table, own, got, one_a, one_b, two_a, two_b),
        ((half, HD, HD), (half, HD, HD)), name + "_enter",
    )
    received = swap(sent, "seq", 1)
    work(3, sent)
    return kept, received, table


def entering_any(own, send, log_total, backward, tasks):
    for run, outputs in tasks.values():
        outputs.extend(run(send))
    count, mine = lax.axis_size("seq"), lax.axis_index("seq")
    core = mine % 2
    own, send = own[:, :HD], send[:, :HD]
    half = own.shape[0]
    in_order = jnp.where(
        core == 0, jnp.concatenate([own, send], axis=0), jnp.concatenate([send, own], axis=0)
    )
    states = lax.all_gather(in_order, "seq")
    decays = jnp.exp(lax.all_gather(log_total, "seq"))
    place = mine
    if backward:
        states, decays, place = states[::-1], decays[::-1], count - 1 - mine

    def step(at, total):
        longer = decays[at][:, None, None] * total + states[at]
        return jnp.where(at < place, longer, total)

    total = lax.fori_loop(0, count - 1, step, jnp.zeros_like(in_order))
    kept = lax.dynamic_slice_in_dim(total, core * half, half)
    return kept, lax.dynamic_slice_in_dim(total, (1 - core) * half, half)


def sum_over_heads(value):
    count = lax.axis_size("head")
    reach = 1
    while 2 * reach <= count and count % (2 * reach) == 0:
        value = value + swap(value, "head", reach)
        reach *= 2
    part = value
    for shift in range(1, count // reach):
        value = value + lax.ppermute(
            part, "head", [(i, (i + shift * reach) % count) for i in range(count)]
        )
    return value


def follows(value, earlier):
    return lax.optimization_barrier((value, earlier))[0]


def on_device(query_rows, key_rows, value_rows, output_grad, norm_gain, log_decay):
    mine = lax.axis_index("seq")
    core, *chip = ((mine >> at) % 2 for at in range(3))
    no = jnp.zeros_like(core)
    ahead, behind = (
        jnp.broadcast_to(jnp.stack(marks).astype(F32)[:, None], (TILE, HD))
        for marks in (
            (1 - core, core, core, *chip, no, no, no),
            (1 - core, core, 1 - core, *(1 - bit for bit in chip), no, no, no),
        )
    )
    table = [None]

    def entering(own, send, backward, tasks):
        if lax.axis_size("seq") != 8:
            return entering_any(own, send, jnp.sum(log_decay, axis=1), backward, tasks)
        kept, received, table[0] = entering_quad(
            own, send, table[0], behind if backward else ahead, tasks,
            "later" if backward else "earlier",
        )
        return kept, received

    own, send, first, kh, vh = local_state(ahead, log_decay, key_rows, value_rows)

    def forward_task(index):
        return lambda earlier: intra(
            index, log_decay, kh, vh, follows(first, earlier), query_rows, output_grad
        )

    in_0, in_1 = [], []
    keep, recv = entering(
        own, send, False, {1: (forward_task(0), in_0), 2: (forward_task(1), in_1)}
    )
    q0, o0, w0, inner0 = in_0
    q1, o1, w1, inner1 = in_1
    att0, att1, sums = attend(
        ahead, log_decay, norm_gain, keep, recv, (q0, q1, o0, o1, inner0, inner1)
    )
    sums = sum_over_heads(sums)
    g0, g1, grad_own, grad_send, second = norm_grad(
        ahead, log_decay, norm_gain, sums, (q0, q1, o0, o1, att0, att1)
    )
    queries, pairs, norms = [], [], []

    def query_task(earlier):
        return grad_query(
            ahead, log_decay, keep, recv, follows(first, earlier), kh, vh, g0, g1
        )

    def pair_task(earlier):
        return grad_key_value(
            log_decay, queries[1], w0, w1, q0, q1, kh, vh, g0, g1, follows(second, earlier)
        )

    def norm_task(earlier):
        return [normed_rows(follows(norm_gain, earlier), sums, att0, att1)]

    grad_keep, grad_recv = entering(
        grad_own, grad_send, True, {1: (query_task, queries), 2: (pair_task, pairs), 3: (norm_task, norms)}
    )
    grad_k, grad_v = finish(ahead, log_decay, grad_keep, grad_recv, kh, vh, *pairs)
    return norms[0], queries[0], grad_k, grad_v


def solution(mesh):
    rows = P("seq", "head", None)
    return jax.shard_map(
        on_device,
        mesh=mesh,
        in_specs=(rows, rows, rows, rows, P("head", None), P("head", "seq")),
        out_specs=(rows, rows, rows, rows),
        check_vma=False,
    )
```

```python
import jax
import jax.numpy as jnp
from jax import lax
from jax.experimental import pallas as pl
from jax.experimental.pallas import tpu as pltpu
from jax.sharding import PartitionSpec as P

HEAD_TOTAL = 64
HD = 128
BLOCK = 256
CHUNK = 128
TILE = 8
F32 = jnp.float32
BF16 = jnp.bfloat16
MIB = 1024 * 1024
NEAR = pl.BlockSpec(memory_space=pltpu.VMEM)
FAR = pl.BlockSpec(memory_space=pl.ANY)
LOWER, UPPER, LATE, RIGHT, LOW = range(5)


def in_vmem(*shape, kind=F32):
    return pltpu.VMEM(shape, kind)


def near(*arrays):
    return [pltpu.with_memory_space_constraint(array, pltpu.VMEM) for array in arrays]


def far(*arrays):
    return [pltpu.with_memory_space_constraint(array, pltpu.HBM) for array in arrays]


def params(mib):
    return pltpu.CompilerParams(vmem_limit_bytes=mib * MIB)


def cost(flops, moved, exps=0):
    return pl.CostEstimate(flops=flops, bytes_accessed=moved, transcendentals=exps)


def block_cum(log_decay):
    size = log_decay.shape[1]
    upper = lax.broadcasted_iota(jnp.int32, (size, size), 0) <= lax.broadcasted_iota(
        jnp.int32, (size, size), 1
    )
    return jnp.dot(
        log_decay,
        jnp.where(upper, 1.0, 0.0).astype(F32),
        precision=lax.Precision.HIGHEST,
        preferred_element_type=F32,
    )


def as_columns(row):
    return jnp.broadcast_to(row, (HD, row.shape[1])).T


def dot(a, b):
    return jnp.dot(a, b, preferred_element_type=F32)


def dot_rows(a, b):
    return lax.dot_general(a, b, (((1,), (1,)), ((), ())), preferred_element_type=F32)


def two_parts(matrix):
    high = matrix.astype(BF16)
    return high, (matrix - high.astype(F32)).astype(BF16)


def times_state(rows, state):
    return dot(jnp.concatenate([rows, rows], axis=1), jnp.concatenate(two_parts(state), axis=0))


def times_state_t(rows, state):
    return dot_rows(
        jnp.concatenate([rows, rows], axis=1), jnp.concatenate(two_parts(state), axis=1)
    )


def causal(table, row, columns):
    half = row.shape[1] // 2
    lower = lax.broadcasted_iota(jnp.int32, (half, half), 0) >= lax.broadcasted_iota(
        jnp.int32, (half, half), 1
    )
    quarters = []
    for t in range(2):
        for s in range(t + 1):
            gap = columns[t * half : (t + 1) * half] - row[:, s * half : (s + 1) * half]
            if t == s:
                gap = jnp.where(lower, gap, -jnp.inf)
            part = table[t * half : (t + 1) * half, s * half : (s + 1) * half]
            quarters.append((part * jnp.exp(gap)).astype(BF16))
    top = jnp.concatenate([quarters[0], jnp.zeros_like(quarters[0])], axis=1)
    return jnp.concatenate([top, jnp.concatenate(quarters[1:], axis=1)], axis=0)


def transposed_dot(a, b):
    return lax.dot_general(a, b, (((0,), (0,)), ((), ())), preferred_element_type=F32)


def each_head(heads, unroll, body):
    def step(h, carry):
        body(h)
        return carry

    lax.fori_loop(0, heads, step, 0, unroll=unroll)


def turn_tiles(tiles):
    count = len(tiles)
    at = lax.broadcasted_iota(jnp.int32, tiles[0].shape, 0)
    turned = [tile if i == 0 else pltpu.roll(tile, i, 0) for i, tile in enumerate(tiles)]
    reach = 1
    while reach < count:
        odd = (at & reach) != 0
        turned = [
            jnp.where(odd, turned[(n + reach) % count], turned[n]) for n in range(count)
        ]
        reach *= 2
    picked = [turned[-j % count] for j in range(count)]
    return [tile if j == 0 else pltpu.roll(tile, count - j, 0) for j, tile in enumerate(picked)]


def to_heads(dst, block):
    tok, heads, _ = block.shape

    def step(group, carry):
        at = pl.multiple_of(group * 2 * TILE, 2 * TILE)
        tokens = block[pl.ds(at, 2 * TILE)].astype(F32)
        for first in range(0, heads, TILE):
            halves = [
                turn_tiles([tokens[base + i, first : first + TILE] for i in range(TILE)])
                for base in (0, TILE)
            ]
            for j in range(TILE):
                both = jnp.concatenate([halves[0][j], halves[1][j]], axis=0)
                dst[first + j, pl.ds(at, 2 * TILE)] = both.astype(BF16)
        return carry

    lax.fori_loop(0, tok // (2 * TILE), step, 0, unroll=2)


def from_heads(block, src, start, tok):
    heads = src.shape[0]

    def step(group, carry):
        at = pl.multiple_of(group * TILE, TILE)
        parts = [
            turn_tiles([src[first + i, pl.ds(start + at, TILE)] for i in range(TILE)])
            for first in range(0, heads, TILE)
        ]
        for j in range(TILE):
            block[at + j] = jnp.concatenate([part[j] for part in parts], axis=0).astype(BF16)
        return carry

    lax.fori_loop(0, tok // TILE, step, 0, unroll=2)


def is_set(place_ref, which):
    return place_ref[which : which + 1] > 0.5


def split_halves(place_ref, whole, own_ref, send_ref):
    half = own_ref.shape[0]
    mine = is_set(place_ref, LOWER)
    for i in range(half):
        own_ref[i, :HD] = jnp.where(mine, whole[i], whole[half + i])
        send_ref[i, :HD] = jnp.where(mine, whole[half + i], whole[i])


def state_kernel(
    place_ref, ld_hbm, k_hbm, v_hbm, own_ref, send_ref, first_ref, kh, vh,
    ld_ref, k_raw, v_raw, cum, acc, decay, sems,
):
    heads, tok = ld_ref.shape
    half = heads // 2
    per_block = BLOCK // CHUNK
    copies = [pltpu.make_async_copy(ld_hbm, ld_ref, sems.at[0])]
    for c in range(tok // CHUNK):
        at = pl.ds(c * CHUNK, CHUNK)
        copies.append(pltpu.make_async_copy(k_hbm.at[at], k_raw.at[at], sems.at[2 * c + 1]))
        copies.append(pltpu.make_async_copy(v_hbm.at[at], v_raw.at[at], sems.at[2 * c + 2]))
    for copy in copies:
        copy.start()
    copies[0].wait()
    for b in range(2):
        cum[b] = block_cum(ld_ref[:, b * BLOCK : (b + 1) * BLOCK])
    ends = cum[0, :, BLOCK - 1 :] + cum[1, :, BLOCK - 1 :]
    decay[...] = jnp.broadcast_to(jnp.exp(ends), decay.shape)

    for b in range(2):
        for c in range(per_block):
            at = pl.ds((b * per_block + c) * CHUNK, CHUNK)
            here = pl.ds(c * CHUNK, CHUNK)
            which = 2 * (b * per_block + c) + 1
            copies[which].wait()
            to_heads(kh.at[b, :, here], k_raw.at[at])
            copies[which + 1].wait()
            to_heads(vh.at[b, :, here], v_raw.at[at])

        def one(h, b=b):
            row = cum[b, pl.ds(h, 1), :]
            scale = jnp.exp(row[:, BLOCK - 1 :] - row)
            state = dot((kh[b, h].astype(F32).T * scale).astype(BF16), vh[b, h])
            if b == 0:
                first_ref[h] = state
            else:
                acc[h] = state + jnp.exp(row[:, BLOCK - 1 :]) * first_ref[h]

        each_head(heads, 4, one)

    split_halves(place_ref, acc, own_ref, send_ref)
    mine = is_set(place_ref, LOWER)
    for i in range(half):
        lower, upper = decay[i : i + 1], decay[half + i : half + i + 1]
        for ref, row in (
            (own_ref, jnp.where(mine, lower, upper)), (send_ref, jnp.where(mine, upper, lower)),
        ):
            ref[i, HD:] = jnp.broadcast_to(row, (TILE, HD))


def local_state(place, log_decay, key_rows, value_rows):
    tok, heads, dim = key_rows.shape
    half = heads // 2
    by_head = in_vmem(2, heads, BLOCK, dim, kind=BF16)
    return pl.pallas_call(
        state_kernel,
        in_specs=[NEAR, FAR, FAR, FAR],
        out_specs=[NEAR] * 5,
        out_shape=[
            in_vmem(half, dim + TILE, dim), in_vmem(half, dim + TILE, dim),
            in_vmem(heads, dim, dim), by_head, by_head,
        ],
        scratch_shapes=[
            pltpu.VMEM((heads, tok), F32),
            pltpu.VMEM((tok, heads, dim), BF16),
            pltpu.VMEM((tok, heads, dim), BF16),
            pltpu.VMEM((2, heads, BLOCK), F32),
            pltpu.VMEM((heads, dim, dim), F32),
            pltpu.VMEM((heads, dim), F32),
            pltpu.SemaphoreType.DMA((2 * (tok // CHUNK) + 1,)),
        ],
        compiler_params=params(8),
        cost_estimate=cost(2 * tok * heads * dim * dim, 8 * tok * heads * dim),
        name="local_state",
    )(place, *far(log_decay, key_rows, value_rows))


def intra(index, log_decay, kh, vh, first, query_rows, output_grad):
    tok, heads, dim = query_rows.shape

    def kernel(ld_ref, kh, vh, first_ref, q_hbm, o_hbm, qh, oh, w_ref, inner_ref,
               q_raw, o_raw, cum, sems):
        at = pl.ds(index * BLOCK, BLOCK)
        copy_q = pltpu.make_async_copy(q_hbm.at[at], q_raw, sems.at[0])
        copy_o = pltpu.make_async_copy(o_hbm.at[at], o_raw, sems.at[1])
        copy_q.start()
        copy_o.start()
        cum[...] = block_cum(ld_ref[:, index * BLOCK : (index + 1) * BLOCK])
        copy_q.wait()
        to_heads(qh, q_raw)
        copy_o.wait()
        to_heads(oh, o_raw)

        def one(h):
            query = qh[h]
            row = cum[pl.ds(h, 1), :]
            columns = as_columns(row)
            weights = causal(dot_rows(query, kh[index, h]), row, columns)
            w_ref[h] = weights
            inner = dot(weights, vh[index, h])
            if index:
                inner += jnp.exp(columns) * times_state(query, first_ref[h])
            inner_ref[h] = inner

        each_head(heads, 2, one)

    by_head = in_vmem(heads, BLOCK, dim, kind=BF16)
    return pl.pallas_call(
        kernel,
        in_specs=[NEAR] * 4 + [FAR, FAR],
        out_specs=[NEAR] * 4,
        out_shape=[
            by_head, by_head, in_vmem(heads, BLOCK, BLOCK, kind=BF16), in_vmem(heads, BLOCK, dim),
        ],
        scratch_shapes=[
            pltpu.VMEM((BLOCK, heads, dim), BF16),
            pltpu.VMEM((BLOCK, heads, dim), BF16),
            pltpu.VMEM((heads, BLOCK), F32),
            pltpu.SemaphoreType.DMA((2,)),
        ],
        compiler_params=params(6),
        cost_estimate=cost(
            2 * heads * BLOCK * BLOCK * dim * 4, 20 * heads * BLOCK * dim, heads * BLOCK * BLOCK
        ),
        name=f"intra_{index}",
    )(log_decay, *near(kh, vh, first), *far(query_rows, output_grad))


def whole_state(place_ref, keep_ref, recv_ref, head):
    half = keep_ref.shape[0]
    mine = place_ref[pl.ds(head // half, 1)] > 0.5
    return jnp.where(mine, keep_ref[head % half], recv_ref[head % half])


def attend_kernel(
    place_ref, ld_ref, gain_ref, keep_ref, recv_ref, q0, q1, o0, o1, inner0, inner1,
    att0, att1, sums_ref, cum, squares, products,
):
    cum[0] = block_cum(ld_ref[:, :BLOCK])
    cum[1] = cum[0, :, BLOCK - 1 :] + block_cum(ld_ref[:, BLOCK:])
    squares[...] = jnp.zeros_like(squares)
    products[...] = jnp.zeros_like(products)

    def one(h):
        state = whole_state(place_ref, keep_ref, recv_ref, h)
        gain = gain_ref[pl.ds(h, 1), :]
        for b, (q, o, inner, att) in enumerate(((q0, o0, inner0, att0), (q1, o1, inner1, att1))):
            columns = as_columns(jnp.exp(cum[b, pl.ds(h, 1), :]))
            attended = inner[h] + columns * times_state(q[h], state)
            att[h] = attended
            squares[b] += attended * attended
            products[b] += gain * o[h].astype(F32) * attended

    each_head(ld_ref.shape[0], 2, one)
    ones = jnp.ones((8, HD), F32)
    for b in range(2):
        for at, total in enumerate((squares, products)):
            line = lax.dot_general(
                ones, total[b], (((1,), (1,)), ((), ())),
                precision=lax.Precision.HIGHEST, preferred_element_type=F32,
            )
            sums_ref[at : at + 1, b * BLOCK : (b + 1) * BLOCK] = line[:1]


def attend(place, log_decay, gain, keep, recv, parts):
    heads, tok = log_decay.shape
    dim = HD
    by_head = in_vmem(heads, BLOCK, dim)
    return pl.pallas_call(
        attend_kernel,
        in_specs=[NEAR] + [NEAR] * 10,
        out_specs=[NEAR] * 3,
        out_shape=[by_head, by_head, in_vmem(2, tok)],
        scratch_shapes=[
            pltpu.VMEM((2, heads, BLOCK), F32),
            pltpu.VMEM((2, BLOCK, dim), F32),
            pltpu.VMEM((2, BLOCK, dim), F32),
        ],
        compiler_params=params(6),
        cost_estimate=cost(4 * heads * tok * dim * dim, 16 * heads * tok * dim),
        name="attend",
    )(place, log_decay, gain, *near(keep, recv, *parts))


def inverse_rms(sums_ref, b):
    at = slice(b * BLOCK, (b + 1) * BLOCK)
    inv = lax.rsqrt(sums_ref[0:1, at] / (HEAD_TOTAL * HD) + 1e-06)
    mean = sums_ref[1:2, at] * inv / (HEAD_TOTAL * HD)
    return inv, mean


def norm_grad_kernel(
    place_ref, ld_ref, gain_ref, sums_ref, q0, q1, o0, o1, att0, att1,
    g0, g1, own_ref, send_ref, second_ref, cum, scales, acc,
):
    heads = ld_ref.shape[0]
    for b in range(2):
        cum[b] = block_cum(ld_ref[:, b * BLOCK : (b + 1) * BLOCK])
        inv, mean = inverse_rms(sums_ref, b)
        scales[b, 0] = as_columns(inv)
        scales[b, 1] = as_columns(inv * inv * mean)

    def one(h):
        gain = gain_ref[pl.ds(h, 1), :]
        ends = []
        for b, (q, o, att, g) in enumerate(((q0, o0, att0, g0), (q1, o1, att1, g1))):
            grad = gain * o[h].astype(F32) * scales[b, 0] - att[h] * scales[b, 1]
            grad = grad.astype(BF16)
            g[h] = grad
            queries = q[h].astype(F32).T * jnp.exp(cum[b, pl.ds(h, 1), :])
            ends.append(dot(queries.astype(BF16), grad))
        second_ref[h] = ends[1]
        first_decay = jnp.exp(cum[0, pl.ds(h, 1), :][:, BLOCK - 1 :])
        acc[h] = ends[0] + first_decay * ends[1]

    each_head(heads, 2, one)
    split_halves(place_ref, acc, own_ref, send_ref)


def norm_grad(place, log_decay, gain, sums, parts):
    heads, tok = log_decay.shape
    dim = HD
    half = heads // 2
    by_head = in_vmem(heads, BLOCK, dim, kind=BF16)
    return pl.pallas_call(
        norm_grad_kernel,
        in_specs=[NEAR] + [NEAR] * 9,
        out_specs=[NEAR] * 5,
        out_shape=[
            by_head, by_head, in_vmem(half, dim, dim), in_vmem(half, dim, dim),
            in_vmem(heads, dim, dim),
        ],
        scratch_shapes=[
            pltpu.VMEM((2, heads, BLOCK), F32),
            pltpu.VMEM((2, 2, BLOCK, dim), F32),
            pltpu.VMEM((heads, dim, dim), F32),
        ],
        compiler_params=params(6),
        cost_estimate=cost(2 * heads * tok * dim * dim, 14 * heads * tok * dim),
        name="norm_grad",
    )(place, log_decay, gain, sums, *near(*parts))


def on_block(work):
    for index in range(2):
        pl.when(pl.program_id(0) == index)(lambda index=index: work(index))


def raw_output(heads, tok):
    spec = pl.BlockSpec((BLOCK, heads, HD), lambda i: (i, 0, 0))
    return spec, jax.ShapeDtypeStruct((tok, heads, HD), BF16)


def normed_kernel(gain_ref, sums_ref, att0, att1, out_ref, rows):
    heads = gain_ref.shape[0]

    def work(b):
        inv = as_columns(inverse_rms(sums_ref, b)[0])
        att = (att0, att1)[b]

        def one(h):
            rows[h] = att[h] * inv * gain_ref[pl.ds(h, 1), :]

        each_head(heads, 2, one)

    on_block(work)
    from_heads(out_ref, rows, 0, BLOCK)


def normed_rows(gain, sums, att0, att1):
    heads, _, dim = att0.shape
    tok = 2 * BLOCK
    spec, shape = raw_output(heads, tok)
    return pl.pallas_call(
        normed_kernel,
        grid=(2,),
        in_specs=[NEAR] * 4,
        out_specs=spec,
        out_shape=shape,
        scratch_shapes=[pltpu.VMEM((heads, BLOCK, dim), F32)],
        compiler_params=params(7),
        cost_estimate=cost(3 * heads * tok * dim, 6 * heads * tok * dim),
        name="normed_rows",
    )(gain, sums, *near(att0, att1))


def grad_q_kernel(
    place_ref, ld_ref, keep_ref, recv_ref, first_ref, kh, vh, g0, g1, out_ref, gs_ref, cum, rows,
):
    heads = ld_ref.shape[0]

    def work(b):
        g = (g0, g1)[b]
        for x in range(2):
            cum[x] = block_cum(ld_ref[:, x * BLOCK : (x + 1) * BLOCK])

        def one(h):
            row = cum[b, pl.ds(h, 1), :]
            columns = as_columns(row)
            scores = causal(dot_rows(g[h], vh[b, h]), row, columns)
            gs_ref[b, h] = scores
            state = whole_state(place_ref, keep_ref, recv_ref, h)
            if b:
                state = jnp.exp(cum[0, pl.ds(h, 1), :][:, BLOCK - 1 :]) * state + first_ref[h]
            grad = dot(scores, kh[b, h]) + jnp.exp(columns) * times_state_t(g[h], state)
            rows[h] = grad

        each_head(heads, 2, one)

    on_block(work)
    from_heads(out_ref, rows, 0, BLOCK)


def grad_query(place, log_decay, keep, recv, first, kh, vh, g0, g1):
    heads, tok = log_decay.shape
    dim = HD
    spec, shape = raw_output(heads, tok)
    return pl.pallas_call(
        grad_q_kernel,
        grid=(2,),
        in_specs=[NEAR] + [NEAR] * 8,
        out_specs=[spec, NEAR],
        out_shape=[shape, in_vmem(2, heads, BLOCK, BLOCK, kind=BF16)],
        scratch_shapes=[pltpu.VMEM((2, heads, BLOCK), F32), pltpu.VMEM((heads, BLOCK, dim), F32)],
        compiler_params=params(8),
        cost_estimate=cost(
            4 * heads * tok * dim * (BLOCK + dim), 12 * heads * tok * dim, heads * tok * BLOCK
        ),
        name="grad_query",
    )(place, log_decay, *near(keep, recv, first, kh, vh, g0, g1))


def grad_kv_kernel(
    ld_ref, gs_ref, w0, w1, q0, q1, kh, vh, g0, g1, second_ref, dk, dv, cum,
):
    cum[...] = block_cum(ld_ref[:, :BLOCK])

    def one(h):
        row = cum[pl.ds(h, 1), :]
        columns = as_columns(jnp.exp(row[:, BLOCK - 1 :] - row))
        state = second_ref[h]
        dk[0, h] = transposed_dot(gs_ref[0, h], q0[h]) + columns * times_state_t(vh[0, h], state)
        dv[0, h] = transposed_dot(w0[h], g0[h]) + columns * times_state(kh[0, h], state)
        dk[1, h] = transposed_dot(gs_ref[1, h], q1[h])
        dv[1, h] = transposed_dot(w1[h], g1[h])

    each_head(ld_ref.shape[0], 2, one)


def grad_key_value(log_decay, gs, w0, w1, q0, q1, kh, vh, g0, g1, second):
    heads, tok = log_decay.shape
    dim = HD
    return pl.pallas_call(
        grad_kv_kernel,
        in_specs=[NEAR] * 11,
        out_specs=[NEAR] * 2,
        out_shape=[in_vmem(2, heads, BLOCK, dim)] * 2,
        scratch_shapes=[pltpu.VMEM((heads, BLOCK), F32)],
        compiler_params=params(4),
        cost_estimate=cost(4 * heads * tok * dim * (BLOCK + dim), 30 * heads * tok * dim),
        name="grad_key_value",
    )(log_decay, *near(gs, w0, w1, q0, q1, kh, vh, g0, g1, second))


def finish_kernel(
    place_ref, ld_ref, keep_ref, recv_ref, kh, vh, dk, dv, out_k, out_v, cum, rows_k, rows_v,
    raw_k, raw_v, sems,
):
    heads = ld_ref.shape[0]
    for x in range(2):
        cum[x] = block_cum(ld_ref[:, x * BLOCK : (x + 1) * BLOCK])
    copies = []
    for b in range(2):

        def one(h, b=b):
            row = cum[b, pl.ds(h, 1), :]
            left = row[:, BLOCK - 1 :] - row
            if b == 0:
                left = left + cum[1, pl.ds(h, 1), :][:, BLOCK - 1 :]
            columns = as_columns(jnp.exp(left))
            state = whole_state(place_ref, keep_ref, recv_ref, h)
            rows_k[h] = dk[b, h] + columns * times_state_t(vh[b, h], state)
            rows_v[h] = dv[b, h] + columns * times_state(kh[b, h], state)

        each_head(heads, 2, one)
        for start in range(0, BLOCK, CHUNK):
            at = pl.ds(b * BLOCK + start, CHUNK)
            for rows, raw, out in ((rows_k, raw_k, out_k), (rows_v, raw_v, out_v)):
                from_heads(raw.at[at], rows, start, CHUNK)
                copies.append(pltpu.make_async_copy(raw.at[at], out.at[at], sems.at[len(copies)]))
                copies[-1].start()
    for copy in copies:
        copy.wait()


def finish(place, log_decay, keep, recv, kh, vh, dk, dv):
    heads, tok = log_decay.shape
    dim = HD
    shape = jax.ShapeDtypeStruct((tok, heads, dim), BF16)
    return pl.pallas_call(
        finish_kernel,
        in_specs=[NEAR] * 8,
        out_specs=[FAR, FAR],
        out_shape=[shape, shape],
        scratch_shapes=[
            pltpu.VMEM((2, heads, BLOCK), F32),
            pltpu.VMEM((heads, BLOCK, dim), F32),
            pltpu.VMEM((heads, BLOCK, dim), F32),
            pltpu.VMEM((tok, heads, dim), BF16),
            pltpu.VMEM((tok, heads, dim), BF16),
            pltpu.SemaphoreType.DMA((2 * (tok // CHUNK),)),
        ],
        compiler_params=params(12),
        cost_estimate=cost(8 * heads * tok * dim * dim, 16 * heads * tok * dim),
        name="finish",
    )(place, log_decay, *near(keep, recv, kh, vh, dk, dv))


def swap(value, axis, bit):
    count = lax.axis_size(axis)
    return lax.ppermute(value, axis, [(i, i ^ bit) for i in range(count)])


def mix(body, backward, place, arrays, shapes, name):
    def kernel(place_ref, *refs):
        bits = [is_set(place_ref, which) != backward for which in (LATE, RIGHT, LOW)]
        body(bits, refs[: len(arrays)], refs[len(arrays) :])

    return pl.pallas_call(
        kernel,
        in_specs=[NEAR] + [NEAR] * len(arrays),
        out_specs=[NEAR] * len(shapes),
        out_shape=[in_vmem(*shape) for shape in shapes],
        compiler_params=params(4),
        cost_estimate=cost(4 * 8 * HD * HD, 16 * 8 * HD * HD),
        name=name,
    )(place, *near(*arrays))


OWN, PARTNER, CHIP, ROW, CORNER = range(5)


def mix_total(bits, own, got, d_own, d_got, first, second):
    late = bits[0]
    quarter = first.shape[0]
    for h in range(2 * quarter):
        total = jnp.where(late, 1.0, d_got(h)) * own[h, :HD] + jnp.where(late, d_own(h), 1.0) * got[h, :HD]
        if h < quarter:
            first[h, :HD] = total
        else:
            second[h - quarter] = total


def mix_total_first(bits, arrays, outputs):
    own, got = arrays
    first, second, chip = outputs
    quarter = first.shape[0]
    d_own = lambda h: own[h, HD : HD + 1]
    d_got = lambda h: got[h, HD : HD + 1]
    mix_total(bits, own, got, d_own, d_got, first, second)
    for h in range(2 * quarter):
        whole = d_own(h) * d_got(h)
        chip[h : h + 1] = whole
        place = HD + (TILE // 2) * (h // quarter)
        first[h % quarter, place : place + TILE // 2] = jnp.broadcast_to(whole, (TILE // 2, HD))


def mix_total_again(bits, arrays, outputs):
    table, own, got = arrays
    decay = lambda which: lambda h: table[which, h : h + 1]
    mix_total(bits, own, got, decay(OWN), decay(PARTNER), *outputs)


def mix_next(bits, decay, totals, gots, outputs):
    _, right, low = bits
    quarter = totals[1].shape[0]
    for i in range(quarter):
        h = i
        scale_total = jnp.where(right, 1.0, decay(ROW, h))
        scale_got = jnp.where(right, decay(CHIP, h), 1.0)
        outputs[0][i] = scale_total * totals[0][i, :HD] + scale_got * gots[0][i, :HD]
        h = quarter + i
        scale_total = jnp.where(low & right, 0.0, 1.0)
        corner = jnp.where(right, 1.0, decay(CHIP, h) * decay(CORNER, h))
        scale_got = jnp.where(low, corner, 0.0)
        outputs[1][i] = scale_total * totals[1][i] + scale_got * gots[1][i]


def mix_next_first(bits, arrays, outputs):
    own, got, chip, corner, first, second, one_a, one_b = arrays
    table = outputs[2]
    quarter = second.shape[0]
    for h in range(2 * quarter):
        place = HD + (TILE // 2) * (h // quarter)
        table[OWN, h : h + 1] = own[h, HD : HD + 1]
        table[PARTNER, h : h + 1] = got[h, HD : HD + 1]
        table[ROW, h : h + 1] = one_a[h % quarter, place : place + 1]
    table[CHIP] = chip[...]
    table[CORNER] = corner[...]
    decay = lambda which, h: table[which, h : h + 1]
    mix_next(bits, decay, (first, second), (one_a, one_b), outputs[:2])


def mix_next_again(bits, arrays, outputs):
    table, first, second, one_a, one_b = arrays
    decay = lambda which, h: table[which, h : h + 1]
    mix_next(bits, decay, (first, second), (one_a, one_b), outputs)


def mix_enter(bits, arrays, outputs):
    table, own, got, one_a, one_b, two_a, two_b = arrays
    kept, sent = outputs
    late, right, low = bits
    quarter = one_b.shape[0]
    decay = lambda which, h: table[which, h : h + 1]
    for h in range(2 * quarter):
        i = h % quarter
        row = jnp.where(right, decay(ROW, h), 1.0)
        if h < quarter:
            one, two = one_a[i, :HD], two_a[i]
            scale_one = jnp.where(right, 1.0, 0.0)
            scale_two = jnp.where(low, row, 0.0)
        else:
            one, two = one_b[i], two_b[i]
            scale_one = jnp.where(low, jnp.where(right, row, decay(CORNER, h)), 0.0)
            scale_two = jnp.where(low | right, 1.0, 0.0)
        enter = scale_one * one + scale_two * two
        after = jnp.where(late, decay(PARTNER, h), decay(OWN, h)) * enter
        after += jnp.where(late, got[h, :HD], own[h, :HD])
        kept[h] = jnp.where(late, after, enter)
        sent[h] = jnp.where(late, enter, after)


def entering_quad(own, send, table, place, backward, tasks):
    def work(stage, after, before=()):
        if stage not in tasks:
            return before
        run, outputs = tasks[stage]
        outputs.extend(run(after))
        return lax.optimization_barrier((before, outputs[-1]))[0]

    name = "later" if backward else "earlier"
    half = own.shape[0]
    quarter = half // 2
    states, wide = (quarter, HD, HD), (quarter, HD + TILE, HD)
    got = swap(send, "seq", 1)
    if table is None:
        first, second, chip = mix(
            mix_total_first, backward, place, (own, got), (wide, states, (half, HD)), name + "_total"
        )
    else:
        first, second = mix(
            mix_total_again, backward, place, (table, own, got), (states, states), name + "_total"
        )
    one_a, one_b = swap(first, "seq", 2), swap(second, "seq", 4)
    if table is None:
        corner = swap(chip, "seq", 6)
        one_a, one_b, corner = work(1, second, (one_a, one_b, corner))
        next_a, next_b, table = mix(
            mix_next_first, backward, place, (own, got, chip, corner, first, second, one_a, one_b),
            (states, states, (5, half, HD)), name + "_next",
        )
    else:
        one_a, one_b = work(1, second, (one_a, one_b))
        next_a, next_b = mix(
            mix_next_again, backward, place, (table, first, second, one_a, one_b), (states, states),
            name + "_next",
        )
    two_a, two_b = swap(next_a, "seq", 4), swap(next_b, "seq", 2)
    two_a, two_b = work(2, next_b, (two_a, two_b))
    kept, sent = mix(
        mix_enter, backward, place, (table, own, got, one_a, one_b, two_a, two_b),
        ((half, HD, HD), (half, HD, HD)), name + "_enter",
    )
    received = swap(sent, "seq", 1)
    work(3, sent)
    return kept, received, table


def entering_any(own, send, log_total, backward, tasks):
    for run, outputs in tasks.values():
        outputs.extend(run(send))
    count, mine = lax.axis_size("seq"), lax.axis_index("seq")
    core = mine % 2
    own, send = own[:, :HD], send[:, :HD]
    half = own.shape[0]
    in_order = jnp.where(
        core == 0, jnp.concatenate([own, send], axis=0), jnp.concatenate([send, own], axis=0)
    )
    states = lax.all_gather(in_order, "seq")
    decays = jnp.exp(lax.all_gather(log_total, "seq"))
    place = mine
    if backward:
        states, decays, place = states[::-1], decays[::-1], count - 1 - mine

    def step(at, total):
        longer = decays[at][:, None, None] * total + states[at]
        return jnp.where(at < place, longer, total)

    total = lax.fori_loop(0, count - 1, step, jnp.zeros_like(in_order))
    kept = lax.dynamic_slice_in_dim(total, core * half, half)
    return kept, lax.dynamic_slice_in_dim(total, (1 - core) * half, half)


def add(first, second):
    def kernel(first_ref, second_ref, out_ref):
        out_ref[...] = first_ref[...] + second_ref[...]

    return pl.pallas_call(
        kernel,
        in_specs=[NEAR, NEAR],
        out_specs=NEAR,
        out_shape=in_vmem(*first.shape),
        compiler_params=params(2),
        name="add",
    )(*near(first, second))


def sum_over_heads(value):
    count = lax.axis_size("head")
    reach = 1
    while 2 * reach <= count and count % (2 * reach) == 0:
        value = add(value, swap(value, "head", reach))
        reach *= 2
    part = value
    for shift in range(1, count // reach):
        value = add(
            value,
            lax.ppermute(part, "head", [(i, (i + shift * reach) % count) for i in range(count)]),
        )
    return value


def follows(value, earlier):
    return lax.optimization_barrier((value, earlier))[0]


def on_device(query_rows, key_rows, value_rows, output_grad, norm_gain, log_decay):
    mine = lax.axis_index("seq")
    bits = [(mine >> at) % 2 for at in range(3)]
    marks = [1 - bits[0], bits[0], *bits] + [jnp.zeros_like(mine)] * (TILE - 5)
    place = jnp.broadcast_to(jnp.stack(marks).astype(F32)[:, None], (TILE, HD))
    table = [None]

    def entering(own, send, backward, tasks):
        if lax.axis_size("seq") != 8:
            return entering_any(own, send, jnp.sum(log_decay, axis=1), backward, tasks)
        kept, received, table[0] = entering_quad(
            own, send, table[0], place, backward, tasks
        )
        return kept, received

    own, send, first, kh, vh = local_state(place, log_decay, key_rows, value_rows)

    def forward_task(index):
        return lambda earlier: intra(
            index, log_decay, kh, vh, follows(first, earlier), query_rows, output_grad
        )

    in_0, in_1 = [], []
    keep, recv = entering(
        own, send, False, {1: (forward_task(0), in_0), 2: (forward_task(1), in_1)}
    )
    q0, o0, w0, inner0 = in_0
    q1, o1, w1, inner1 = in_1
    att0, att1, sums = attend(
        place, log_decay, norm_gain, keep, recv, (q0, q1, o0, o1, inner0, inner1)
    )
    sums = sum_over_heads(sums)
    g0, g1, grad_own, grad_send, second = norm_grad(
        place, log_decay, norm_gain, sums, (q0, q1, o0, o1, att0, att1)
    )
    queries, pairs, norms = [], [], []

    def query_task(earlier):
        return grad_query(
            place, log_decay, keep, recv, follows(first, earlier), kh, vh, g0, g1
        )

    def pair_task(earlier):
        return grad_key_value(
            log_decay, queries[1], w0, w1, q0, q1, kh, vh, g0, g1, follows(second, earlier)
        )

    def norm_task(earlier):
        return [normed_rows(follows(norm_gain, earlier), sums, att0, att1)]

    grad_keep, grad_recv = entering(
        grad_own, grad_send, True, {1: (query_task, queries), 2: (pair_task, pairs), 3: (norm_task, norms)}
    )
    grad_k, grad_v = finish(place, log_decay, grad_keep, grad_recv, kh, vh, *pairs)
    return norms[0], queries[0], grad_k, grad_v


def solution(mesh):
    rows = P("seq", "head", None)
    return jax.shard_map(
        on_device,
        mesh=mesh,
        in_specs=(rows, rows, rows, rows, P("head", None), P("head", "seq")),
        out_specs=(rows, rows, rows, rows),
        check_vma=False,
    )
```

```python
import jax
import jax.numpy as jnp
from jax import lax
from jax.experimental import pallas as pl
from jax.experimental.pallas import tpu as pltpu
from jax.sharding import PartitionSpec as P

HEAD_TOTAL = 64
HD = 128
BLOCK = 256
CHUNK = 128
TILE = 8
F32 = jnp.float32
BF16 = jnp.bfloat16
MIB = 1024 * 1024
NEAR = pl.BlockSpec(memory_space=pltpu.VMEM)
FAR = pl.BlockSpec(memory_space=pl.ANY)
LOWER, UPPER, LATE, RIGHT, LOW = range(5)


def in_vmem(*shape, kind=F32):
    return pltpu.VMEM(shape, kind)


def near(*arrays):
    return [pltpu.with_memory_space_constraint(array, pltpu.VMEM) for array in arrays]


def far(*arrays):
    return [pltpu.with_memory_space_constraint(array, pltpu.HBM) for array in arrays]


def params(mib):
    return pltpu.CompilerParams(vmem_limit_bytes=mib * MIB)


def cost(flops, moved, exps=0):
    return pl.CostEstimate(flops=flops, bytes_accessed=moved, transcendentals=exps)


def block_cum(log_decay):
    size = log_decay.shape[1]
    upper = lax.broadcasted_iota(jnp.int32, (size, size), 0) <= lax.broadcasted_iota(
        jnp.int32, (size, size), 1
    )
    return jnp.dot(
        log_decay,
        jnp.where(upper, 1.0, 0.0).astype(F32),
        precision=lax.Precision.HIGHEST,
        preferred_element_type=F32,
    )


def as_columns(row):
    return jnp.broadcast_to(row, (HD, row.shape[1])).T


def dot(a, b):
    return jnp.dot(a, b, preferred_element_type=F32)


def dot_rows(a, b):
    return lax.dot_general(a, b, (((1,), (1,)), ((), ())), preferred_element_type=F32)


def two_parts(matrix):
    high = matrix.astype(BF16)
    return high, (matrix - high.astype(F32)).astype(BF16)


def times_state(rows, state):
    return dot(jnp.concatenate([rows, rows], axis=1), jnp.concatenate(two_parts(state), axis=0))


def times_state_t(rows, state):
    return dot_rows(
        jnp.concatenate([rows, rows], axis=1), jnp.concatenate(two_parts(state), axis=1)
    )


def decay_quarters(row, columns):
    half = row.shape[1] // 2
    lower = lax.broadcasted_iota(jnp.int32, (half, half), 0) >= lax.broadcasted_iota(
        jnp.int32, (half, half), 1
    )
    quarters = []
    for t, s in ((0, 0), (1, 0), (1, 1)):
        gap = columns[t * half : (t + 1) * half] - row[:, s * half : (s + 1) * half]
        quarters.append(jnp.exp(jnp.where(lower, gap, -jnp.inf) if t == s else gap))
    return quarters


def causal(table, quarters):
    half = table.shape[0] // 2
    first, second, third = (
        (table[t * half : (t + 1) * half, s * half : (s + 1) * half] * quarter).astype(BF16)
        for (t, s), quarter in zip(((0, 0), (1, 0), (1, 1)), quarters)
    )
    top = jnp.concatenate([first, jnp.zeros_like(first)], axis=1)
    return jnp.concatenate([top, jnp.concatenate([second, third], axis=1)], axis=0)


def transposed_dot(a, b):
    return lax.dot_general(a, b, (((0,), (0,)), ((), ())), preferred_element_type=F32)


def each_head(heads, unroll, body):
    def step(h, carry):
        body(h)
        return carry

    lax.fori_loop(0, heads, step, 0, unroll=unroll)


def turn_tiles(tiles):
    count = len(tiles)
    at = lax.broadcasted_iota(jnp.int32, tiles[0].shape, 0)
    turned = [tile if i == 0 else pltpu.roll(tile, i, 0) for i, tile in enumerate(tiles)]
    reach = 1
    while reach < count:
        odd = (at & reach) != 0
        turned = [
            jnp.where(odd, turned[(n + reach) % count], turned[n]) for n in range(count)
        ]
        reach *= 2
    picked = [turned[-j % count] for j in range(count)]
    return [tile if j == 0 else pltpu.roll(tile, count - j, 0) for j, tile in enumerate(picked)]


def to_heads(dst, block):
    tok, heads, _ = block.shape

    def step(group, carry):
        at = pl.multiple_of(group * 2 * TILE, 2 * TILE)
        tokens = block[pl.ds(at, 2 * TILE)].astype(F32)
        for first in range(0, heads, TILE):
            halves = [
                turn_tiles([tokens[base + i, first : first + TILE] for i in range(TILE)])
                for base in (0, TILE)
            ]
            for j in range(TILE):
                both = jnp.concatenate([halves[0][j], halves[1][j]], axis=0)
                dst[first + j, pl.ds(at, 2 * TILE)] = both.astype(BF16)
        return carry

    lax.fori_loop(0, tok // (2 * TILE), step, 0, unroll=2)


def from_heads(block, src, start, tok):
    heads = src.shape[0]

    def step(group, carry):
        at = pl.multiple_of(group * TILE, TILE)
        parts = [
            turn_tiles([src[first + i, pl.ds(start + at, TILE)] for i in range(TILE)])
            for first in range(0, heads, TILE)
        ]
        for j in range(TILE):
            block[at + j] = jnp.concatenate([part[j] for part in parts], axis=0).astype(BF16)
        return carry

    lax.fori_loop(0, tok // TILE, step, 0, unroll=2)


def is_set(place_ref, which):
    return place_ref[which : which + 1] > 0.5


def split_halves(place_ref, whole, own_ref, send_ref):
    half = own_ref.shape[0]
    mine = is_set(place_ref, LOWER)
    for i in range(half):
        own_ref[i, :HD] = jnp.where(mine, whole[i], whole[half + i])
        send_ref[i, :HD] = jnp.where(mine, whole[half + i], whole[i])


def state_kernel(
    place_ref, ld_hbm, k_hbm, v_hbm, own_ref, send_ref, first_ref, kh, vh,
    ld_ref, k_raw, v_raw, cum, acc, decay, sems,
):
    heads, tok = ld_ref.shape
    half = heads // 2
    per_block = BLOCK // CHUNK
    copies = [pltpu.make_async_copy(ld_hbm, ld_ref, sems.at[0])]
    for c in range(tok // CHUNK):
        at = pl.ds(c * CHUNK, CHUNK)
        copies.append(pltpu.make_async_copy(k_hbm.at[at], k_raw.at[at], sems.at[2 * c + 1]))
        copies.append(pltpu.make_async_copy(v_hbm.at[at], v_raw.at[at], sems.at[2 * c + 2]))
    for copy in copies:
        copy.start()
    copies[0].wait()
    for b in range(2):
        cum[b] = block_cum(ld_ref[:, b * BLOCK : (b + 1) * BLOCK])
    ends = cum[0, :, BLOCK - 1 :] + cum[1, :, BLOCK - 1 :]
    decay[...] = jnp.broadcast_to(jnp.exp(ends), decay.shape)

    for b in range(2):
        for c in range(per_block):
            at = pl.ds((b * per_block + c) * CHUNK, CHUNK)
            here = pl.ds(c * CHUNK, CHUNK)
            which = 2 * (b * per_block + c) + 1
            copies[which].wait()
            to_heads(kh.at[b, :, here], k_raw.at[at])
            copies[which + 1].wait()
            to_heads(vh.at[b, :, here], v_raw.at[at])

        def one(h, b=b):
            row = cum[b, pl.ds(h, 1), :]
            scale = jnp.exp(row[:, BLOCK - 1 :] - row)
            state = dot((kh[b, h].astype(F32).T * scale).astype(BF16), vh[b, h])
            if b == 0:
                first_ref[h] = state
            else:
                acc[h] = state + jnp.exp(row[:, BLOCK - 1 :]) * first_ref[h]

        each_head(heads, 4, one)

    split_halves(place_ref, acc, own_ref, send_ref)
    mine = is_set(place_ref, LOWER)
    for i in range(half):
        lower, upper = decay[i : i + 1], decay[half + i : half + i + 1]
        for ref, row in (
            (own_ref, jnp.where(mine, lower, upper)), (send_ref, jnp.where(mine, upper, lower)),
        ):
            ref[i, HD:] = jnp.broadcast_to(row, (TILE, HD))


def local_state(place, log_decay, key_rows, value_rows):
    tok, heads, dim = key_rows.shape
    half = heads // 2
    by_head = in_vmem(2, heads, BLOCK, dim, kind=BF16)
    return pl.pallas_call(
        state_kernel,
        in_specs=[NEAR, FAR, FAR, FAR],
        out_specs=[NEAR] * 5,
        out_shape=[
            in_vmem(half, dim + TILE, dim), in_vmem(half, dim + TILE, dim),
            in_vmem(heads, dim, dim), by_head, by_head,
        ],
        scratch_shapes=[
            pltpu.VMEM((heads, tok), F32),
            pltpu.VMEM((tok, heads, dim), BF16),
            pltpu.VMEM((tok, heads, dim), BF16),
            pltpu.VMEM((2, heads, BLOCK), F32),
            pltpu.VMEM((heads, dim, dim), F32),
            pltpu.VMEM((heads, dim), F32),
            pltpu.SemaphoreType.DMA((2 * (tok // CHUNK) + 1,)),
        ],
        compiler_params=params(8),
        cost_estimate=cost(2 * tok * heads * dim * dim, 8 * tok * heads * dim),
        name="local_state",
    )(place, *far(log_decay, key_rows, value_rows))


def intra(index, log_decay, kh, vh, first, query_rows, output_grad):
    tok, heads, dim = query_rows.shape

    def kernel(ld_ref, kh, vh, first_ref, q_hbm, o_hbm,
               qh, oh, w_ref, decays_ref, columns_ref, inner_ref,
               q_raw, o_raw, cum, sems):
        at = pl.ds(index * BLOCK, BLOCK)
        copy_q = pltpu.make_async_copy(q_hbm.at[at], q_raw, sems.at[0])
        copy_o = pltpu.make_async_copy(o_hbm.at[at], o_raw, sems.at[1])
        copy_q.start()
        copy_o.start()
        cum[...] = block_cum(ld_ref[:, index * BLOCK : (index + 1) * BLOCK])
        copy_q.wait()
        to_heads(qh, q_raw)
        copy_o.wait()
        to_heads(oh, o_raw)

        def one(h):
            query = qh[h]
            row = cum[pl.ds(h, 1), :]
            columns = as_columns(row)
            quarters = decay_quarters(row, columns)
            for at, quarter in enumerate(quarters):
                decays_ref[h, at] = quarter
            weights = causal(dot_rows(query, kh[index, h]), quarters)
            w_ref[h] = weights
            inner = dot(weights, vh[index, h])
            columns = jnp.exp(columns)
            columns_ref[h] = columns
            if index:
                inner += columns * times_state(query, first_ref[h])
            inner_ref[h] = inner

        each_head(heads, 2, one)

    by_head = in_vmem(heads, BLOCK, dim, kind=BF16)
    return pl.pallas_call(
        kernel,
        in_specs=[NEAR] * 4 + [FAR, FAR],
        out_specs=[NEAR] * 6,
        out_shape=[
            by_head, by_head, in_vmem(heads, BLOCK, BLOCK, kind=BF16),
            in_vmem(heads, 3, BLOCK // 2, BLOCK // 2), in_vmem(heads, BLOCK, dim),
            in_vmem(heads, BLOCK, dim),
        ],
        scratch_shapes=[
            pltpu.VMEM((BLOCK, heads, dim), BF16),
            pltpu.VMEM((BLOCK, heads, dim), BF16),
            pltpu.VMEM((heads, BLOCK), F32),
            pltpu.SemaphoreType.DMA((2,)),
        ],
        compiler_params=params(6),
        cost_estimate=cost(
            2 * heads * BLOCK * BLOCK * dim * 4, 20 * heads * BLOCK * dim, heads * BLOCK * BLOCK
        ),
        name=f"intra_{index}",
    )(log_decay, *near(kh, vh, first), *far(query_rows, output_grad))


def whole_state(place_ref, keep_ref, recv_ref, head):
    half = keep_ref.shape[0]
    mine = place_ref[pl.ds(head // half, 1)] > 0.5
    return jnp.where(mine, keep_ref[head % half], recv_ref[head % half])


def attend_kernel(
    place_ref, gain_ref, keep_ref, recv_ref, q0, q1, o0, o1, columns0, columns1, inner0, inner1,
    att0, att1, sums_ref, squares, products,
):
    heads = gain_ref.shape[0]
    squares[...] = jnp.zeros_like(squares)
    products[...] = jnp.zeros_like(products)

    def one(h):
        state = whole_state(place_ref, keep_ref, recv_ref, h)
        gain = gain_ref[pl.ds(h, 1), :]
        blocks = ((q0, o0, columns0, inner0, att0), (q1, o1, columns1, inner1, att1))
        for b, (q, o, columns, inner, att) in enumerate(blocks):
            attended = inner[h] + columns[h] * times_state(q[h], state)
            att[h] = attended
            squares[b] += attended * attended
            products[b] += gain * o[h].astype(F32) * attended
            state = columns[h, BLOCK - 1 :] * state

    each_head(heads, 2, one)
    ones = jnp.ones((8, HD), F32)
    for b in range(2):
        for at, total in enumerate((squares, products)):
            line = lax.dot_general(
                ones, total[b], (((1,), (1,)), ((), ())),
                precision=lax.Precision.HIGHEST, preferred_element_type=F32,
            )
            sums_ref[at : at + 1, b * BLOCK : (b + 1) * BLOCK] = line[:1]


def attend(place, gain, keep, recv, parts):
    heads, dim = gain.shape
    tok = 2 * BLOCK
    by_head = in_vmem(heads, BLOCK, dim)
    return pl.pallas_call(
        attend_kernel,
        in_specs=[NEAR] * 12,
        out_specs=[NEAR] * 3,
        out_shape=[by_head, by_head, in_vmem(2, tok)],
        scratch_shapes=[pltpu.VMEM((2, BLOCK, dim), F32), pltpu.VMEM((2, BLOCK, dim), F32)],
        compiler_params=params(6),
        cost_estimate=cost(4 * heads * tok * dim * dim, 16 * heads * tok * dim),
        name="attend",
    )(place, gain, *near(keep, recv, *parts))


def queries_kernel(ld_ref, q0, q1, out_ref, ends_ref, cum):
    heads = ld_ref.shape[0]
    for b in range(2):
        cum[b] = jnp.exp(block_cum(ld_ref[:, b * BLOCK : (b + 1) * BLOCK]))
        ends_ref[b] = jnp.broadcast_to(cum[b, :, BLOCK - 1 :], (heads, HD))

    def one(h):
        for b, q in enumerate((q0, q1)):
            out_ref[b, h] = (q[h].astype(F32).T * cum[b, pl.ds(h, 1), :]).astype(BF16)

    each_head(heads, 2, one)


def scaled_queries(log_decay, q0, q1):
    heads, tok = log_decay.shape
    return pl.pallas_call(
        queries_kernel,
        in_specs=[NEAR] * 3,
        out_specs=[NEAR] * 2,
        out_shape=[in_vmem(2, heads, HD, BLOCK, kind=BF16), in_vmem(2, heads, HD)],
        scratch_shapes=[pltpu.VMEM((2, heads, BLOCK), F32)],
        compiler_params=params(4),
        cost_estimate=cost(2 * heads * tok * HD, 4 * heads * tok * HD),
        name="scaled_queries",
    )(log_decay, *near(q0, q1))


def remaining_kernel(ld_ref, out_ref, cum):
    heads = ld_ref.shape[0]
    for b in range(2):
        total = block_cum(ld_ref[:, b * BLOCK : (b + 1) * BLOCK])
        cum[b] = jnp.exp(total[:, BLOCK - 1 :] - total)

    def one(h):
        for b in range(2):
            out_ref[b, h] = as_columns(cum[b, pl.ds(h, 1), :])

    each_head(heads, 2, one)


def remaining_decay(log_decay):
    heads, tok = log_decay.shape
    return pl.pallas_call(
        remaining_kernel,
        in_specs=[NEAR],
        out_specs=NEAR,
        out_shape=in_vmem(2, heads, BLOCK, HD),
        scratch_shapes=[pltpu.VMEM((2, heads, BLOCK), F32)],
        compiler_params=params(4),
        cost_estimate=cost(heads * tok * HD, 4 * heads * tok * HD),
        name="remaining_decay",
    )(log_decay)


def inverse_rms(sums_ref, b):
    at = slice(b * BLOCK, (b + 1) * BLOCK)
    inv = lax.rsqrt(sums_ref[0:1, at] / (HEAD_TOTAL * HD) + 1e-06)
    mean = sums_ref[1:2, at] * inv / (HEAD_TOTAL * HD)
    return inv, mean


def norm_grad_kernel(
    place_ref, ends_ref, gain_ref, sums_ref, queries_ref, o0, o1, att0, att1,
    g0, g1, own_ref, send_ref, second_ref, scales, acc,
):
    for b in range(2):
        inv, mean = inverse_rms(sums_ref, b)
        scales[b, 0] = as_columns(inv)
        scales[b, 1] = as_columns(inv * inv * mean)

    def one(h):
        gain = gain_ref[pl.ds(h, 1), :]
        starts = []
        for b, (o, att, g) in enumerate(((o0, att0, g0), (o1, att1, g1))):
            grad = gain * o[h].astype(F32) * scales[b, 0] - att[h] * scales[b, 1]
            grad = grad.astype(BF16)
            g[h] = grad
            starts.append(dot(queries_ref[b, h], grad))
        second_ref[h] = starts[1]
        acc[h] = starts[0] + ends_ref[0, pl.ds(h, 1)] * starts[1]

    each_head(gain_ref.shape[0], 2, one)
    split_halves(place_ref, acc, own_ref, send_ref)


def norm_grad(place, ends, gain, sums, parts):
    heads, dim = gain.shape
    tok = 2 * BLOCK
    half = heads // 2
    by_head = in_vmem(heads, BLOCK, dim, kind=BF16)
    return pl.pallas_call(
        norm_grad_kernel,
        in_specs=[NEAR] * 9,
        out_specs=[NEAR] * 5,
        out_shape=[
            by_head, by_head, in_vmem(half, dim, dim), in_vmem(half, dim, dim),
            in_vmem(heads, dim, dim),
        ],
        scratch_shapes=[
            pltpu.VMEM((2, 2, BLOCK, dim), F32),
            pltpu.VMEM((heads, dim, dim), F32),
        ],
        compiler_params=params(6),
        cost_estimate=cost(2 * heads * tok * dim * dim, 14 * heads * tok * dim),
        name="norm_grad",
    )(place, ends, gain, sums, *near(*parts))


def on_block(work):
    for index in range(2):
        pl.when(pl.program_id(0) == index)(lambda index=index: work(index))


def raw_output(heads, tok):
    spec = pl.BlockSpec((BLOCK, heads, HD), lambda i: (i, 0, 0))
    return spec, jax.ShapeDtypeStruct((tok, heads, HD), BF16)


def normed_kernel(gain_ref, sums_ref, att0, att1, out_ref, rows):
    heads = gain_ref.shape[0]

    def work(b):
        inv = as_columns(inverse_rms(sums_ref, b)[0])
        att = (att0, att1)[b]

        def one(h):
            rows[h] = att[h] * inv * gain_ref[pl.ds(h, 1), :]

        each_head(heads, 2, one)

    on_block(work)
    from_heads(out_ref, rows, 0, BLOCK)


def normed_rows(gain, sums, att0, att1):
    heads, _, dim = att0.shape
    tok = 2 * BLOCK
    spec, shape = raw_output(heads, tok)
    return pl.pallas_call(
        normed_kernel,
        grid=(2,),
        in_specs=[NEAR] * 4,
        out_specs=spec,
        out_shape=shape,
        scratch_shapes=[pltpu.VMEM((heads, BLOCK, dim), F32)],
        compiler_params=params(7),
        cost_estimate=cost(3 * heads * tok * dim, 6 * heads * tok * dim),
        name="normed_rows",
    )(gain, sums, *near(att0, att1))


def grad_q_kernel(
    place_ref, ends_ref, keep_ref, recv_ref, first_ref, kh, vh, g0, g1, decays0, decays1,
    columns0, columns1, out_ref, gs_ref, rows,
):
    heads = ends_ref.shape[1]

    def work(b):
        g, decays, columns = ((g0, decays0, columns0), (g1, decays1, columns1))[b]

        def one(h):
            quarters = [decays[h, at] for at in range(3)]
            scores = causal(dot_rows(g[h], vh[b, h]), quarters)
            gs_ref[b, h] = scores
            state = whole_state(place_ref, keep_ref, recv_ref, h)
            if b:
                state = ends_ref[0, pl.ds(h, 1)] * state + first_ref[h]
            rows[h] = dot(scores, kh[b, h]) + columns[h] * times_state_t(g[h], state)

        each_head(heads, 2, one)

    on_block(work)
    from_heads(out_ref, rows, 0, BLOCK)


def grad_query(place, ends, keep, recv, first, parts):
    _, heads, dim = ends.shape
    tok = 2 * BLOCK
    spec, shape = raw_output(heads, tok)
    return pl.pallas_call(
        grad_q_kernel,
        grid=(2,),
        in_specs=[NEAR] * 13,
        out_specs=[spec, NEAR],
        out_shape=[shape, in_vmem(2, heads, BLOCK, BLOCK, kind=BF16)],
        scratch_shapes=[pltpu.VMEM((heads, BLOCK, dim), F32)],
        compiler_params=params(8),
        cost_estimate=cost(
            4 * heads * tok * dim * (BLOCK + dim), 12 * heads * tok * dim, heads * tok * BLOCK
        ),
        name="grad_query",
    )(place, ends, *near(keep, recv, first, *parts))


def grad_kv_kernel(
    gs_ref, w0, w1, q0, q1, kh, vh, g0, g1, remaining_ref, second_ref, dk, dv,
):
    def one(h):
        columns = remaining_ref[0, h]
        state = second_ref[h]
        dk[0, h] = transposed_dot(gs_ref[0, h], q0[h]) + columns * times_state_t(vh[0, h], state)
        dv[0, h] = transposed_dot(w0[h], g0[h]) + columns * times_state(kh[0, h], state)
        dk[1, h] = transposed_dot(gs_ref[1, h], q1[h])
        dv[1, h] = transposed_dot(w1[h], g1[h])

    each_head(gs_ref.shape[1], 2, one)


def grad_key_value(*arrays):
    _, heads, _, dim = arrays[5].shape
    tok = 2 * BLOCK
    return pl.pallas_call(
        grad_kv_kernel,
        in_specs=[NEAR] * 11,
        out_specs=[NEAR] * 2,
        out_shape=[in_vmem(2, heads, BLOCK, dim)] * 2,
        compiler_params=params(4),
        cost_estimate=cost(4 * heads * tok * dim * (BLOCK + dim), 30 * heads * tok * dim),
        name="grad_key_value",
    )(*near(*arrays))


def finish_kernel(
    place_ref, ends_ref, keep_ref, recv_ref, kh, vh, remaining_ref, dk, dv, out_k, out_v,
    rows_k, rows_v, raw_k, raw_v, sems,
):
    heads = ends_ref.shape[1]
    copies = []
    for b in range(2):

        def one(h, b=b):
            columns = remaining_ref[b, h]
            state = whole_state(place_ref, keep_ref, recv_ref, h)
            if b == 0:
                state = ends_ref[1, pl.ds(h, 1)] * state
            rows_k[h] = dk[b, h] + columns * times_state_t(vh[b, h], state)
            rows_v[h] = dv[b, h] + columns * times_state(kh[b, h], state)

        each_head(heads, 2, one)
        for start in range(0, BLOCK, CHUNK):
            at = pl.ds(b * BLOCK + start, CHUNK)
            for rows, raw, out in ((rows_k, raw_k, out_k), (rows_v, raw_v, out_v)):
                from_heads(raw.at[at], rows, start, CHUNK)
                copies.append(pltpu.make_async_copy(raw.at[at], out.at[at], sems.at[len(copies)]))
                copies[-1].start()
    for copy in copies:
        copy.wait()


def finish(place, ends, keep, recv, kh, vh, remaining, dk, dv):
    _, heads, dim = ends.shape
    tok = 2 * BLOCK
    shape = jax.ShapeDtypeStruct((tok, heads, dim), BF16)
    return pl.pallas_call(
        finish_kernel,
        in_specs=[NEAR] * 9,
        out_specs=[FAR, FAR],
        out_shape=[shape, shape],
        scratch_shapes=[
            pltpu.VMEM((heads, BLOCK, dim), F32),
            pltpu.VMEM((heads, BLOCK, dim), F32),
            pltpu.VMEM((tok, heads, dim), BF16),
            pltpu.VMEM((tok, heads, dim), BF16),
            pltpu.SemaphoreType.DMA((2 * (tok // CHUNK),)),
        ],
        compiler_params=params(12),
        cost_estimate=cost(8 * heads * tok * dim * dim, 16 * heads * tok * dim),
        name="finish",
    )(place, ends, *near(keep, recv, kh, vh, remaining, dk, dv))


def swap(value, axis, bit):
    count = lax.axis_size(axis)
    return lax.ppermute(value, axis, [(i, i ^ bit) for i in range(count)])


def mix(body, backward, place, arrays, shapes, name):
    def kernel(place_ref, *refs):
        bits = [is_set(place_ref, which) != backward for which in (LATE, RIGHT, LOW)]
        body(bits, refs[: len(arrays)], refs[len(arrays) :])

    return pl.pallas_call(
        kernel,
        in_specs=[NEAR] + [NEAR] * len(arrays),
        out_specs=[NEAR] * len(shapes),
        out_shape=[in_vmem(*shape) for shape in shapes],
        compiler_params=params(4),
        cost_estimate=cost(4 * 8 * HD * HD, 16 * 8 * HD * HD),
        name=name,
    )(place, *near(*arrays))


OWN, PARTNER, CHIP, ROW, CORNER = range(5)


def mix_total(bits, own, got, d_own, d_got, first, second):
    late = bits[0]
    quarter = first.shape[0]
    for h in range(2 * quarter):
        total = jnp.where(late, 1.0, d_got(h)) * own[h, :HD] + jnp.where(late, d_own(h), 1.0) * got[h, :HD]
        if h < quarter:
            first[h, :HD] = total
        else:
            second[h - quarter] = total


def mix_total_first(bits, arrays, outputs):
    own, got = arrays
    first, second, chip = outputs
    quarter = first.shape[0]
    d_own = lambda h: own[h, HD : HD + 1]
    d_got = lambda h: got[h, HD : HD + 1]
    mix_total(bits, own, got, d_own, d_got, first, second)
    for h in range(2 * quarter):
        whole = d_own(h) * d_got(h)
        chip[h : h + 1] = whole
        place = HD + (TILE // 2) * (h // quarter)
        first[h % quarter, place : place + TILE // 2] = jnp.broadcast_to(whole, (TILE // 2, HD))


def mix_total_again(bits, arrays, outputs):
    table, own, got = arrays
    decay = lambda which: lambda h: table[which, h : h + 1]
    mix_total(bits, own, got, decay(OWN), decay(PARTNER), *outputs)


def mix_next(bits, decay, totals, gots, outputs):
    _, right, low = bits
    quarter = totals[1].shape[0]
    for i in range(quarter):
        h = i
        scale_total = jnp.where(right, 1.0, decay(ROW, h))
        scale_got = jnp.where(right, decay(CHIP, h), 1.0)
        outputs[0][i] = scale_total * totals[0][i, :HD] + scale_got * gots[0][i, :HD]
        h = quarter + i
        scale_total = jnp.where(low & right, 0.0, 1.0)
        corner = jnp.where(right, 1.0, decay(CHIP, h) * decay(CORNER, h))
        scale_got = jnp.where(low, corner, 0.0)
        outputs[1][i] = scale_total * totals[1][i] + scale_got * gots[1][i]


def mix_next_first(bits, arrays, outputs):
    own, got, chip, corner, first, second, one_a, one_b = arrays
    table = outputs[2]
    quarter = second.shape[0]
    for h in range(2 * quarter):
        place = HD + (TILE // 2) * (h // quarter)
        table[OWN, h : h + 1] = own[h, HD : HD + 1]
        table[PARTNER, h : h + 1] = got[h, HD : HD + 1]
        table[ROW, h : h + 1] = one_a[h % quarter, place : place + 1]
    table[CHIP] = chip[...]
    table[CORNER] = corner[...]
    decay = lambda which, h: table[which, h : h + 1]
    mix_next(bits, decay, (first, second), (one_a, one_b), outputs[:2])


def mix_next_again(bits, arrays, outputs):
    table, first, second, one_a, one_b = arrays
    decay = lambda which, h: table[which, h : h + 1]
    mix_next(bits, decay, (first, second), (one_a, one_b), outputs)


def mix_enter(bits, arrays, outputs):
    table, own, got, one_a, one_b, two_a, two_b = arrays
    kept, sent = outputs
    late, right, low = bits
    quarter = one_b.shape[0]
    decay = lambda which, h: table[which, h : h + 1]
    for h in range(2 * quarter):
        i = h % quarter
        row = jnp.where(right, decay(ROW, h), 1.0)
        if h < quarter:
            one, two = one_a[i, :HD], two_a[i]
            scale_one = jnp.where(right, 1.0, 0.0)
            scale_two = jnp.where(low, row, 0.0)
        else:
            one, two = one_b[i], two_b[i]
            scale_one = jnp.where(low, jnp.where(right, row, decay(CORNER, h)), 0.0)
            scale_two = jnp.where(low | right, 1.0, 0.0)
        enter = scale_one * one + scale_two * two
        after = jnp.where(late, decay(PARTNER, h), decay(OWN, h)) * enter
        after += jnp.where(late, got[h, :HD], own[h, :HD])
        kept[h] = jnp.where(late, after, enter)
        sent[h] = jnp.where(late, enter, after)


def entering_quad(own, send, table, place, backward, tasks):
    def work(stage, after, before=()):
        if stage not in tasks:
            return before
        run, outputs = tasks[stage]
        outputs.extend(run(after))
        return lax.optimization_barrier((before, outputs[-1]))[0]

    name = "later" if backward else "earlier"
    half = own.shape[0]
    quarter = half // 2
    states, wide = (quarter, HD, HD), (quarter, HD + TILE, HD)
    got = swap(send, "seq", 1)
    if table is None:
        first, second, chip = mix(
            mix_total_first, backward, place, (own, got), (wide, states, (half, HD)), name + "_total"
        )
    else:
        first, second = mix(
            mix_total_again, backward, place, (table, own, got), (states, states), name + "_total"
        )
    one_a, one_b = swap(first, "seq", 2), swap(second, "seq", 4)
    if table is None:
        corner = swap(chip, "seq", 6)
        one_a, one_b, corner = work(1, second, (one_a, one_b, corner))
        next_a, next_b, table = mix(
            mix_next_first, backward, place, (own, got, chip, corner, first, second, one_a, one_b),
            (states, states, (5, half, HD)), name + "_next",
        )
    else:
        one_a, one_b = work(1, second, (one_a, one_b))
        next_a, next_b = mix(
            mix_next_again, backward, place, (table, first, second, one_a, one_b), (states, states),
            name + "_next",
        )
    two_a, two_b = swap(next_a, "seq", 4), swap(next_b, "seq", 2)
    two_a, two_b = work(2, next_b, (two_a, two_b))
    kept, sent = mix(
        mix_enter, backward, place, (table, own, got, one_a, one_b, two_a, two_b),
        ((half, HD, HD), (half, HD, HD)), name + "_enter",
    )
    received = swap(sent, "seq", 1)
    work(3, sent)
    return kept, received, table


def entering_any(own, send, log_total, backward, tasks):
    for run, outputs in tasks.values():
        outputs.extend(run(send))
    count, mine = lax.axis_size("seq"), lax.axis_index("seq")
    core = mine % 2
    own, send = own[:, :HD], send[:, :HD]
    half = own.shape[0]
    in_order = jnp.where(
        core == 0, jnp.concatenate([own, send], axis=0), jnp.concatenate([send, own], axis=0)
    )
    states = lax.all_gather(in_order, "seq")
    decays = jnp.exp(lax.all_gather(log_total, "seq"))
    place = mine
    if backward:
        states, decays, place = states[::-1], decays[::-1], count - 1 - mine

    def step(at, total):
        longer = decays[at][:, None, None] * total + states[at]
        return jnp.where(at < place, longer, total)

    total = lax.fori_loop(0, count - 1, step, jnp.zeros_like(in_order))
    kept = lax.dynamic_slice_in_dim(total, core * half, half)
    return kept, lax.dynamic_slice_in_dim(total, (1 - core) * half, half)


def add(first, second):
    def kernel(first_ref, second_ref, out_ref):
        out_ref[...] = first_ref[...] + second_ref[...]

    return pl.pallas_call(
        kernel,
        in_specs=[NEAR, NEAR],
        out_specs=NEAR,
        out_shape=in_vmem(*first.shape),
        compiler_params=params(2),
        name="add",
    )(*near(first, second))


def sum_over_heads(value, tasks):
    tasks = list(tasks)
    results = []
    count = lax.axis_size("head")
    reach = 1
    while 2 * reach <= count and count % (2 * reach) == 0:
        got = swap(value, "head", reach)
        if tasks:
            results.append(tasks.pop(0)(value))
            got = follows(got, results[-1])
        value = add(value, got)
        reach *= 2
    results += [task(value) for task in tasks]
    part = value
    for shift in range(1, count // reach):
        value = add(
            value,
            lax.ppermute(part, "head", [(i, (i + shift * reach) % count) for i in range(count)]),
        )
    return value, results


def follows(value, earlier):
    return lax.optimization_barrier((value, earlier))[0]


def on_device(query_rows, key_rows, value_rows, output_grad, norm_gain, log_decay):
    mine = lax.axis_index("seq")
    bits = [(mine >> at) % 2 for at in range(3)]
    marks = [1 - bits[0], bits[0], *bits] + [jnp.zeros_like(mine)] * (TILE - 5)
    place = jnp.broadcast_to(jnp.stack(marks).astype(F32)[:, None], (TILE, HD))
    table = [None]

    def entering(own, send, backward, tasks):
        if lax.axis_size("seq") != 8:
            return entering_any(own, send, jnp.sum(log_decay, axis=1), backward, tasks)
        kept, received, table[0] = entering_quad(
            own, send, table[0], place, backward, tasks
        )
        return kept, received

    own, send, first, kh, vh = local_state(place, log_decay, key_rows, value_rows)

    def forward_task(index):
        return lambda earlier: intra(
            index, log_decay, kh, vh, follows(first, earlier), query_rows, output_grad
        )

    in_0, in_1 = [], []
    keep, recv = entering(
        own, send, False, {1: (forward_task(0), in_0), 2: (forward_task(1), in_1)}
    )
    q0, o0, w0, decays0, columns0, inner0 = in_0
    q1, o1, w1, decays1, columns1, inner1 = in_1
    att0, att1, sums = attend(
        place, norm_gain, keep, recv, (q0, q1, o0, o1, columns0, columns1, inner0, inner1)
    )
    sums, ((scaled, ends), remaining) = sum_over_heads(
        sums,
        (
            lambda earlier: scaled_queries(log_decay, follows(q0, earlier), q1),
            lambda earlier: remaining_decay(follows(log_decay, earlier)),
        ),
    )
    g0, g1, grad_own, grad_send, second = norm_grad(
        place, ends, norm_gain, sums, (scaled, o0, o1, att0, att1)
    )
    queries, pairs, norms = [], [], []

    def query_task(earlier):
        return grad_query(
            place, ends, keep, recv, follows(first, earlier),
            (kh, vh, g0, g1, decays0, decays1, columns0, columns1),
        )

    def pair_task(earlier):
        return grad_key_value(
            queries[1], w0, w1, q0, q1, kh, vh, g0, g1, remaining, follows(second, earlier)
        )

    def norm_task(earlier):
        return [normed_rows(follows(norm_gain, earlier), sums, att0, att1)]

    grad_keep, grad_recv = entering(
        grad_own, grad_send, True, {1: (query_task, queries), 2: (pair_task, pairs), 3: (norm_task, norms)}
    )
    grad_k, grad_v = finish(place, ends, grad_keep, grad_recv, kh, vh, remaining, *pairs)
    return norms[0], queries[0], grad_k, grad_v


def solution(mesh):
    rows = P("seq", "head", None)
    return jax.shard_map(
        on_device,
        mesh=mesh,
        in_specs=(rows, rows, rows, rows, P("head", None), P("head", "seq")),
        out_specs=(rows, rows, rows, rows),
        check_vma=False,
    )
```

```python
import jax
import jax.numpy as jnp
from jax import lax
from jax.experimental import pallas as pl
from jax.experimental.pallas import tpu as pltpu
from jax.sharding import PartitionSpec as P

HEAD_TOTAL = 64
HD = 128
BLOCK = 256
CHUNK = 128
TILE = 8
F32 = jnp.float32
BF16 = jnp.bfloat16
MIB = 1024 * 1024
NEAR = pl.BlockSpec(memory_space=pltpu.VMEM)
FAR = pl.BlockSpec(memory_space=pl.ANY)
LOWER, UPPER, LATE, RIGHT, LOW = range(5)


def in_vmem(*shape, kind=F32):
    return pltpu.VMEM(shape, kind)


def near(*arrays):
    return [pltpu.with_memory_space_constraint(array, pltpu.VMEM) for array in arrays]


def far(*arrays):
    return [pltpu.with_memory_space_constraint(array, pltpu.HBM) for array in arrays]


def params(mib):
    return pltpu.CompilerParams(vmem_limit_bytes=mib * MIB)


def cost(flops, moved, exps=0):
    return pl.CostEstimate(flops=flops, bytes_accessed=moved, transcendentals=exps)


def block_cum(log_decay):
    size = log_decay.shape[1]
    upper = lax.broadcasted_iota(jnp.int32, (size, size), 0) <= lax.broadcasted_iota(
        jnp.int32, (size, size), 1
    )
    return jnp.dot(
        log_decay,
        jnp.where(upper, 1.0, 0.0).astype(F32),
        precision=lax.Precision.HIGHEST,
        preferred_element_type=F32,
    )


def as_columns(row):
    return jnp.broadcast_to(row, (HD, row.shape[1])).T


def dot(a, b):
    return jnp.dot(a, b, preferred_element_type=F32)


def dot_rows(a, b):
    return lax.dot_general(a, b, (((1,), (1,)), ((), ())), preferred_element_type=F32)


def two_parts(matrix):
    high = matrix.astype(BF16)
    return high, (matrix - high.astype(F32)).astype(BF16)


def times_state(rows, state):
    return dot(jnp.concatenate([rows, rows], axis=1), jnp.concatenate(two_parts(state), axis=0))


def times_state_t(rows, state):
    return dot_rows(
        jnp.concatenate([rows, rows], axis=1), jnp.concatenate(two_parts(state), axis=1)
    )


def decay_quarters(row, columns):
    half = row.shape[1] // 2
    lower = lax.broadcasted_iota(jnp.int32, (half, half), 0) >= lax.broadcasted_iota(
        jnp.int32, (half, half), 1
    )
    quarters = []
    for t, s in ((0, 0), (1, 0), (1, 1)):
        gap = columns[t * half : (t + 1) * half] - row[:, s * half : (s + 1) * half]
        quarters.append(jnp.exp(jnp.where(lower, gap, -jnp.inf) if t == s else gap))
    return quarters


def causal(table, quarters):
    half = table.shape[0] // 2
    first, second, third = (
        (table[t * half : (t + 1) * half, s * half : (s + 1) * half] * quarter).astype(BF16)
        for (t, s), quarter in zip(((0, 0), (1, 0), (1, 1)), quarters)
    )
    top = jnp.concatenate([first, jnp.zeros_like(first)], axis=1)
    return jnp.concatenate([top, jnp.concatenate([second, third], axis=1)], axis=0)


def transposed_dot(a, b):
    return lax.dot_general(a, b, (((0,), (0,)), ((), ())), preferred_element_type=F32)


def each_head(heads, unroll, body):
    def step(h, carry):
        body(h)
        return carry

    lax.fori_loop(0, heads, step, 0, unroll=unroll)


def turn_tiles(tiles):
    count = len(tiles)
    at = lax.broadcasted_iota(jnp.int32, tiles[0].shape, 0)
    turned = [tile if i == 0 else pltpu.roll(tile, i, 0) for i, tile in enumerate(tiles)]
    reach = 1
    while reach < count:
        odd = (at & reach) != 0
        turned = [
            jnp.where(odd, turned[(n + reach) % count], turned[n]) for n in range(count)
        ]
        reach *= 2
    picked = [turned[-j % count] for j in range(count)]
    return [tile if j == 0 else pltpu.roll(tile, count - j, 0) for j, tile in enumerate(picked)]


def to_heads(dst, block):
    tok, heads, _ = block.shape

    def step(group, carry):
        at = pl.multiple_of(group * 2 * TILE, 2 * TILE)
        tokens = block[pl.ds(at, 2 * TILE)].astype(F32)
        for first in range(0, heads, TILE):
            halves = [
                turn_tiles([tokens[base + i, first : first + TILE] for i in range(TILE)])
                for base in (0, TILE)
            ]
            for j in range(TILE):
                both = jnp.concatenate([halves[0][j], halves[1][j]], axis=0)
                dst[first + j, pl.ds(at, 2 * TILE)] = both.astype(BF16)
        return carry

    lax.fori_loop(0, tok // (2 * TILE), step, 0, unroll=2)


def from_heads(block, src, start, tok):
    heads = src.shape[0]

    def step(group, carry):
        at = pl.multiple_of(group * TILE, TILE)
        parts = [
            turn_tiles([src[first + i, pl.ds(start + at, TILE)] for i in range(TILE)])
            for first in range(0, heads, TILE)
        ]
        for j in range(TILE):
            block[at + j] = jnp.concatenate([part[j] for part in parts], axis=0).astype(BF16)
        return carry

    lax.fori_loop(0, tok // TILE, step, 0, unroll=2)


def is_set(place_ref, which):
    return place_ref[which : which + 1] > 0.5


def split_halves(place_ref, whole, own_ref, send_ref):
    half = own_ref.shape[0]
    mine = is_set(place_ref, LOWER)
    for i in range(half):
        own_ref[i, :HD] = jnp.where(mine, whole[i], whole[half + i])
        send_ref[i, :HD] = jnp.where(mine, whole[half + i], whole[i])


def state_kernel(
    place_ref, ld_hbm, k_hbm, v_hbm, own_ref, send_ref, first_ref, kh, vh,
    ld_ref, k_raw, v_raw, cum, acc, decay, sems,
):
    heads, tok = ld_ref.shape
    half = heads // 2
    per_block = BLOCK // CHUNK
    copies = [pltpu.make_async_copy(ld_hbm, ld_ref, sems.at[0])]
    for c in range(tok // CHUNK):
        at = pl.ds(c * CHUNK, CHUNK)
        copies.append(pltpu.make_async_copy(k_hbm.at[at], k_raw.at[at], sems.at[2 * c + 1]))
        copies.append(pltpu.make_async_copy(v_hbm.at[at], v_raw.at[at], sems.at[2 * c + 2]))
    for copy in copies:
        copy.start()
    copies[0].wait()
    for b in range(2):
        cum[b] = block_cum(ld_ref[:, b * BLOCK : (b + 1) * BLOCK])
    ends = cum[0, :, BLOCK - 1 :] + cum[1, :, BLOCK - 1 :]
    decay[...] = jnp.broadcast_to(jnp.exp(ends), decay.shape)

    for b in range(2):
        for c in range(per_block):
            at = pl.ds((b * per_block + c) * CHUNK, CHUNK)
            here = pl.ds(c * CHUNK, CHUNK)
            which = 2 * (b * per_block + c) + 1
            copies[which].wait()
            to_heads(kh.at[b, :, here], k_raw.at[at])
            copies[which + 1].wait()
            to_heads(vh.at[b, :, here], v_raw.at[at])

        def one(h, b=b):
            row = cum[b, pl.ds(h, 1), :]
            scale = jnp.exp(row[:, BLOCK - 1 :] - row)
            state = dot((kh[b, h].astype(F32).T * scale).astype(BF16), vh[b, h])
            if b == 0:
                first_ref[h] = state
            else:
                acc[h] = state + jnp.exp(row[:, BLOCK - 1 :]) * first_ref[h]

        each_head(heads, 4, one)

    split_halves(place_ref, acc, own_ref, send_ref)
    mine = is_set(place_ref, LOWER)
    for i in range(half):
        lower, upper = decay[i : i + 1], decay[half + i : half + i + 1]
        for ref, row in (
            (own_ref, jnp.where(mine, lower, upper)), (send_ref, jnp.where(mine, upper, lower)),
        ):
            ref[i, HD:] = jnp.broadcast_to(row, (TILE, HD))


def local_state(place, log_decay, key_rows, value_rows):
    tok, heads, dim = key_rows.shape
    half = heads // 2
    by_head = in_vmem(2, heads, BLOCK, dim, kind=BF16)
    return pl.pallas_call(
        state_kernel,
        in_specs=[NEAR, FAR, FAR, FAR],
        out_specs=[NEAR] * 5,
        out_shape=[
            in_vmem(half, dim + TILE, dim), in_vmem(half, dim + TILE, dim),
            in_vmem(heads, dim, dim), by_head, by_head,
        ],
        scratch_shapes=[
            pltpu.VMEM((heads, tok), F32),
            pltpu.VMEM((tok, heads, dim), BF16),
            pltpu.VMEM((tok, heads, dim), BF16),
            pltpu.VMEM((2, heads, BLOCK), F32),
            pltpu.VMEM((heads, dim, dim), F32),
            pltpu.VMEM((heads, dim), F32),
            pltpu.SemaphoreType.DMA((2 * (tok // CHUNK) + 1,)),
        ],
        compiler_params=params(8),
        cost_estimate=cost(2 * tok * heads * dim * dim, 8 * tok * heads * dim),
        name="local_state",
    )(place, *far(log_decay, key_rows, value_rows))


def intra(index, log_decay, kh, vh, first, query_rows, output_grad):
    tok, heads, dim = query_rows.shape

    def kernel(ld_ref, kh, vh, first_ref, q_hbm, o_hbm,
               qh, oh, w_ref, decays_ref, columns_ref, inner_ref,
               q_raw, o_raw, cum, sems):
        at = pl.ds(index * BLOCK, BLOCK)
        copy_q = pltpu.make_async_copy(q_hbm.at[at], q_raw, sems.at[0])
        copy_o = pltpu.make_async_copy(o_hbm.at[at], o_raw, sems.at[1])
        copy_q.start()
        copy_o.start()
        cum[...] = block_cum(ld_ref[:, index * BLOCK : (index + 1) * BLOCK])
        copy_q.wait()
        to_heads(qh, q_raw)
        copy_o.wait()
        to_heads(oh, o_raw)

        def one(h):
            query = qh[h]
            row = cum[pl.ds(h, 1), :]
            columns = as_columns(row)
            quarters = decay_quarters(row, columns)
            for at, quarter in enumerate(quarters):
                decays_ref[h, at] = quarter
            weights = causal(dot_rows(query, kh[index, h]), quarters)
            w_ref[h] = weights
            inner = dot(weights, vh[index, h])
            columns = jnp.exp(columns)
            columns_ref[h] = columns
            if index:
                inner += columns * times_state(query, first_ref[h])
            inner_ref[h] = inner

        each_head(heads, 2, one)

    by_head = in_vmem(heads, BLOCK, dim, kind=BF16)
    return pl.pallas_call(
        kernel,
        in_specs=[NEAR] * 4 + [FAR, FAR],
        out_specs=[NEAR] * 6,
        out_shape=[
            by_head, by_head, in_vmem(heads, BLOCK, BLOCK, kind=BF16),
            in_vmem(heads, 3, BLOCK // 2, BLOCK // 2), in_vmem(heads, BLOCK, dim),
            in_vmem(heads, BLOCK, dim),
        ],
        scratch_shapes=[
            pltpu.VMEM((BLOCK, heads, dim), BF16),
            pltpu.VMEM((BLOCK, heads, dim), BF16),
            pltpu.VMEM((heads, BLOCK), F32),
            pltpu.SemaphoreType.DMA((2,)),
        ],
        compiler_params=params(6),
        cost_estimate=cost(
            2 * heads * BLOCK * BLOCK * dim * 4, 20 * heads * BLOCK * dim, heads * BLOCK * BLOCK
        ),
        name=f"intra_{index}",
    )(log_decay, *near(kh, vh, first), *far(query_rows, output_grad))


def whole_state(place_ref, keep_ref, recv_ref, head):
    half = keep_ref.shape[0]
    mine = place_ref[pl.ds(head // half, 1)] > 0.5
    return jnp.where(mine, keep_ref[head % half], recv_ref[head % half])


def attend_kernel(
    place_ref, gain_ref, keep_ref, recv_ref, q0, q1, o0, o1, columns0, columns1, inner0, inner1,
    att0, att1, sums_ref, squares, products,
):
    heads = gain_ref.shape[0]
    squares[...] = jnp.zeros_like(squares)
    products[...] = jnp.zeros_like(products)

    def one(h):
        state = whole_state(place_ref, keep_ref, recv_ref, h)
        gain = gain_ref[pl.ds(h, 1), :]
        blocks = ((q0, o0, columns0, inner0, att0), (q1, o1, columns1, inner1, att1))
        for b, (q, o, columns, inner, att) in enumerate(blocks):
            attended = inner[h] + columns[h] * times_state(q[h], state)
            att[h] = attended
            squares[b] += attended * attended
            products[b] += gain * o[h].astype(F32) * attended
            state = columns[h, BLOCK - 1 :] * state

    each_head(heads, 4, one)
    ones = jnp.ones((8, HD), F32)
    for b in range(2):
        for at, total in enumerate((squares, products)):
            line = lax.dot_general(
                ones, total[b], (((1,), (1,)), ((), ())),
                precision=lax.Precision.HIGHEST, preferred_element_type=F32,
            )
            sums_ref[at : at + 1, b * BLOCK : (b + 1) * BLOCK] = line[:1]


def attend(place, gain, keep, recv, parts):
    heads, dim = gain.shape
    tok = 2 * BLOCK
    by_head = in_vmem(heads, BLOCK, dim)
    return pl.pallas_call(
        attend_kernel,
        in_specs=[NEAR] * 12,
        out_specs=[NEAR] * 3,
        out_shape=[by_head, by_head, in_vmem(2, tok)],
        scratch_shapes=[pltpu.VMEM((2, BLOCK, dim), F32), pltpu.VMEM((2, BLOCK, dim), F32)],
        compiler_params=params(6),
        cost_estimate=cost(4 * heads * tok * dim * dim, 16 * heads * tok * dim),
        name="attend",
    )(place, gain, *near(keep, recv, *parts))


def queries_kernel(ld_ref, q0, q1, out_ref, ends_ref, cum):
    heads = ld_ref.shape[0]
    for b in range(2):
        cum[b] = jnp.exp(block_cum(ld_ref[:, b * BLOCK : (b + 1) * BLOCK]))
        ends_ref[b] = jnp.broadcast_to(cum[b, :, BLOCK - 1 :], (heads, HD))

    def one(h):
        for b, q in enumerate((q0, q1)):
            out_ref[b, h] = (q[h].astype(F32).T * cum[b, pl.ds(h, 1), :]).astype(BF16)

    each_head(heads, 2, one)


def scaled_queries(log_decay, q0, q1):
    heads, tok = log_decay.shape
    return pl.pallas_call(
        queries_kernel,
        in_specs=[NEAR] * 3,
        out_specs=[NEAR] * 2,
        out_shape=[in_vmem(2, heads, HD, BLOCK, kind=BF16), in_vmem(2, heads, HD)],
        scratch_shapes=[pltpu.VMEM((2, heads, BLOCK), F32)],
        compiler_params=params(4),
        cost_estimate=cost(2 * heads * tok * HD, 4 * heads * tok * HD),
        name="scaled_queries",
    )(log_decay, *near(q0, q1))


def remaining_kernel(ld_ref, out_ref, cum):
    heads = ld_ref.shape[0]
    for b in range(2):
        total = block_cum(ld_ref[:, b * BLOCK : (b + 1) * BLOCK])
        cum[b] = jnp.exp(total[:, BLOCK - 1 :] - total)

    def one(h):
        for b in range(2):
            out_ref[b, h] = as_columns(cum[b, pl.ds(h, 1), :])

    each_head(heads, 2, one)


def remaining_decay(log_decay):
    heads, tok = log_decay.shape
    return pl.pallas_call(
        remaining_kernel,
        in_specs=[NEAR],
        out_specs=NEAR,
        out_shape=in_vmem(2, heads, BLOCK, HD),
        scratch_shapes=[pltpu.VMEM((2, heads, BLOCK), F32)],
        compiler_params=params(4),
        cost_estimate=cost(heads * tok * HD, 4 * heads * tok * HD),
        name="remaining_decay",
    )(log_decay)


def inverse_rms(sums_ref, b):
    at = slice(b * BLOCK, (b + 1) * BLOCK)
    inv = lax.rsqrt(sums_ref[0:1, at] / (HEAD_TOTAL * HD) + 1e-06)
    mean = sums_ref[1:2, at] * inv / (HEAD_TOTAL * HD)
    return inv, mean


def norm_grad_kernel(
    place_ref, ends_ref, gain_ref, sums_ref, queries_ref, o0, o1, att0, att1,
    g0, g1, own_ref, send_ref, second_ref, scales, acc,
):
    for b in range(2):
        inv, mean = inverse_rms(sums_ref, b)
        scales[b, 0] = as_columns(inv)
        scales[b, 1] = as_columns(inv * inv * mean)

    def one(h):
        gain = gain_ref[pl.ds(h, 1), :]
        starts = []
        for b, (o, att, g) in enumerate(((o0, att0, g0), (o1, att1, g1))):
            grad = gain * o[h].astype(F32) * scales[b, 0] - att[h] * scales[b, 1]
            grad = grad.astype(BF16)
            g[h] = grad
            starts.append(dot(queries_ref[b, h], grad))
        second_ref[h] = starts[1]
        acc[h] = starts[0] + ends_ref[0, pl.ds(h, 1)] * starts[1]

    each_head(gain_ref.shape[0], 2, one)
    split_halves(place_ref, acc, own_ref, send_ref)


def norm_grad(place, ends, gain, sums, parts):
    heads, dim = gain.shape
    tok = 2 * BLOCK
    half = heads // 2
    by_head = in_vmem(heads, BLOCK, dim, kind=BF16)
    return pl.pallas_call(
        norm_grad_kernel,
        in_specs=[NEAR] * 9,
        out_specs=[NEAR] * 5,
        out_shape=[
            by_head, by_head, in_vmem(half, dim, dim), in_vmem(half, dim, dim),
            in_vmem(heads, dim, dim),
        ],
        scratch_shapes=[
            pltpu.VMEM((2, 2, BLOCK, dim), F32),
            pltpu.VMEM((heads, dim, dim), F32),
        ],
        compiler_params=params(6),
        cost_estimate=cost(2 * heads * tok * dim * dim, 14 * heads * tok * dim),
        name="norm_grad",
    )(place, ends, gain, sums, *near(*parts))


def on_block(work):
    for index in range(2):
        pl.when(pl.program_id(0) == index)(lambda index=index: work(index))


def raw_output(heads, tok):
    spec = pl.BlockSpec((BLOCK, heads, HD), lambda i: (i, 0, 0))
    return spec, jax.ShapeDtypeStruct((tok, heads, HD), BF16)


def normed_kernel(gain_ref, sums_ref, att0, att1, out_ref, rows):
    heads = gain_ref.shape[0]

    def work(b):
        inv = as_columns(inverse_rms(sums_ref, b)[0])
        att = (att0, att1)[b]

        def one(h):
            rows[h] = att[h] * inv * gain_ref[pl.ds(h, 1), :]

        each_head(heads, 2, one)

    on_block(work)
    from_heads(out_ref, rows, 0, BLOCK)


def normed_rows(gain, sums, att0, att1):
    heads, _, dim = att0.shape
    tok = 2 * BLOCK
    spec, shape = raw_output(heads, tok)
    return pl.pallas_call(
        normed_kernel,
        grid=(2,),
        in_specs=[NEAR] * 4,
        out_specs=spec,
        out_shape=shape,
        scratch_shapes=[pltpu.VMEM((heads, BLOCK, dim), F32)],
        compiler_params=params(7),
        cost_estimate=cost(3 * heads * tok * dim, 6 * heads * tok * dim),
        name="normed_rows",
    )(gain, sums, *near(att0, att1))


def grad_q_kernel(
    place_ref, ends_ref, keep_ref, recv_ref, first_ref, kh, vh, g0, g1, decays0, decays1,
    columns0, columns1, rows, gs_ref,
):
    heads = ends_ref.shape[1]
    for b, (g, decays, columns) in enumerate(((g0, decays0, columns0), (g1, decays1, columns1))):

        def one(h, b=b, g=g, decays=decays, columns=columns):
            quarters = [decays[h, at] for at in range(3)]
            scores = causal(dot_rows(g[h], vh[b, h]), quarters)
            gs_ref[b, h] = scores
            state = whole_state(place_ref, keep_ref, recv_ref, h)
            if b:
                state = ends_ref[0, pl.ds(h, 1)] * state + first_ref[h]
            rows[b, h] = dot(scores, kh[b, h]) + columns[h] * times_state_t(g[h], state)

        each_head(heads, 4, one)


def grad_query(place, ends, keep, recv, first, parts):
    _, heads, dim = ends.shape
    tok = 2 * BLOCK
    return pl.pallas_call(
        grad_q_kernel,
        in_specs=[NEAR] * 13,
        out_specs=[NEAR, NEAR],
        out_shape=[
            in_vmem(2, heads, BLOCK, dim), in_vmem(2, heads, BLOCK, BLOCK, kind=BF16),
        ],
        compiler_params=params(4),
        cost_estimate=cost(
            4 * heads * tok * dim * (BLOCK + dim), 12 * heads * tok * dim, heads * tok * BLOCK
        ),
        name="grad_query",
    )(place, ends, *near(keep, recv, first, *parts))


def grad_kv_kernel(
    gs_ref, w0, w1, q0, q1, kh, vh, g0, g1, remaining_ref, second_ref, rows, dk, dv, out_q,
    raw, sems,
):
    heads = gs_ref.shape[1]
    copies = []
    for b in range(2):
        for start in range(0, BLOCK, CHUNK):
            at = pl.ds(b * BLOCK + start, CHUNK)
            from_heads(raw.at[at], rows.at[b], start, CHUNK)
            copies.append(pltpu.make_async_copy(raw.at[at], out_q.at[at], sems.at[len(copies)]))
            copies[-1].start()

    def one(h):
        columns = remaining_ref[0, h]
        state = second_ref[h]
        dk[0, h] = transposed_dot(gs_ref[0, h], q0[h]) + columns * times_state_t(vh[0, h], state)
        dv[0, h] = transposed_dot(w0[h], g0[h]) + columns * times_state(kh[0, h], state)
        dk[1, h] = transposed_dot(gs_ref[1, h], q1[h])
        dv[1, h] = transposed_dot(w1[h], g1[h])

    each_head(heads, 2, one)
    for copy in copies:
        copy.wait()


def grad_key_value(*arrays):
    _, heads, _, dim = arrays[5].shape
    tok = 2 * BLOCK
    return pl.pallas_call(
        grad_kv_kernel,
        in_specs=[NEAR] * 12,
        out_specs=[NEAR, NEAR, FAR],
        out_shape=[in_vmem(2, heads, BLOCK, dim)] * 2
        + [jax.ShapeDtypeStruct((tok, heads, dim), BF16)],
        scratch_shapes=[
            pltpu.VMEM((tok, heads, dim), BF16),
            pltpu.SemaphoreType.DMA((tok // CHUNK,)),
        ],
        compiler_params=params(6),
        cost_estimate=cost(4 * heads * tok * dim * (BLOCK + dim), 30 * heads * tok * dim),
        name="grad_key_value",
    )(*near(*arrays))


def finish_kernel(
    place_ref, ends_ref, keep_ref, recv_ref, kh, vh, remaining_ref, dk, dv, out_k, out_v,
    rows_k, rows_v, raw_k, raw_v, sems,
):
    heads = ends_ref.shape[1]
    copies = []
    for b in range(2):

        def one(h, b=b):
            columns = remaining_ref[b, h]
            state = whole_state(place_ref, keep_ref, recv_ref, h)
            if b == 0:
                state = ends_ref[1, pl.ds(h, 1)] * state
            state = state.astype(BF16)
            none = jnp.zeros_like(state)
            both = jnp.concatenate(
                [jnp.concatenate([state.T, none], axis=1), jnp.concatenate([none, state], axis=1)],
                axis=0,
            )
            carried = dot(jnp.concatenate([vh[b, h], kh[b, h]], axis=1), both)
            rows_k[h] = dk[b, h] + columns * carried[:, :HD]
            rows_v[h] = dv[b, h] + columns * carried[:, HD:]

        each_head(heads, 4, one)
        for start in range(0, BLOCK, CHUNK):
            at = pl.ds(b * BLOCK + start, CHUNK)
            for rows, raw, out in ((rows_k, raw_k, out_k), (rows_v, raw_v, out_v)):
                from_heads(raw.at[at], rows, start, CHUNK)
                copies.append(pltpu.make_async_copy(raw.at[at], out.at[at], sems.at[len(copies)]))
                copies[-1].start()
    for copy in copies:
        copy.wait()


def finish(place, ends, keep, recv, kh, vh, remaining, dk, dv):
    _, heads, dim = ends.shape
    tok = 2 * BLOCK
    shape = jax.ShapeDtypeStruct((tok, heads, dim), BF16)
    return pl.pallas_call(
        finish_kernel,
        in_specs=[NEAR] * 9,
        out_specs=[FAR, FAR],
        out_shape=[shape, shape],
        scratch_shapes=[
            pltpu.VMEM((heads, BLOCK, dim), F32),
            pltpu.VMEM((heads, BLOCK, dim), F32),
            pltpu.VMEM((tok, heads, dim), BF16),
            pltpu.VMEM((tok, heads, dim), BF16),
            pltpu.SemaphoreType.DMA((2 * (tok // CHUNK),)),
        ],
        compiler_params=params(12),
        cost_estimate=cost(8 * heads * tok * dim * dim, 16 * heads * tok * dim),
        name="finish",
    )(place, ends, *near(keep, recv, kh, vh, remaining, dk, dv))


def swap(value, axis, bit):
    count = lax.axis_size(axis)
    return lax.ppermute(value, axis, [(i, i ^ bit) for i in range(count)])


def mix(body, backward, place, arrays, shapes, name):
    def kernel(place_ref, *refs):
        bits = [is_set(place_ref, which) != backward for which in (LATE, RIGHT, LOW)]
        body(bits, refs[: len(arrays)], refs[len(arrays) :])

    return pl.pallas_call(
        kernel,
        in_specs=[NEAR] + [NEAR] * len(arrays),
        out_specs=[NEAR] * len(shapes),
        out_shape=[in_vmem(*shape) for shape in shapes],
        compiler_params=params(4),
        cost_estimate=cost(4 * 8 * HD * HD, 16 * 8 * HD * HD),
        name=name,
    )(place, *near(*arrays))


OWN, PARTNER, CHIP, ROW, CORNER = range(5)


def mix_total(bits, own, got, d_own, d_got, first, second):
    late = bits[0]
    quarter = first.shape[0]
    for h in range(2 * quarter):
        total = jnp.where(late, 1.0, d_got(h)) * own[h, :HD] + jnp.where(late, d_own(h), 1.0) * got[h, :HD]
        if h < quarter:
            first[h, :HD] = total
        else:
            second[h - quarter] = total


def mix_total_first(bits, arrays, outputs):
    own, got = arrays
    first, second, chip = outputs
    quarter = first.shape[0]
    d_own = lambda h: own[h, HD : HD + 1]
    d_got = lambda h: got[h, HD : HD + 1]
    mix_total(bits, own, got, d_own, d_got, first, second)
    for h in range(2 * quarter):
        whole = d_own(h) * d_got(h)
        chip[h : h + 1] = whole
        place = HD + (TILE // 2) * (h // quarter)
        first[h % quarter, place : place + TILE // 2] = jnp.broadcast_to(whole, (TILE // 2, HD))


def mix_total_again(bits, arrays, outputs):
    table, own, got = arrays
    decay = lambda which: lambda h: table[which, h : h + 1]
    mix_total(bits, own, got, decay(OWN), decay(PARTNER), *outputs)


def mix_next(bits, decay, totals, gots, outputs):
    _, right, low = bits
    quarter = totals[1].shape[0]
    for i in range(quarter):
        h = i
        scale_total = jnp.where(right, 1.0, decay(ROW, h))
        scale_got = jnp.where(right, decay(CHIP, h), 1.0)
        outputs[0][i] = scale_total * totals[0][i, :HD] + scale_got * gots[0][i, :HD]
        h = quarter + i
        scale_total = jnp.where(low & right, 0.0, 1.0)
        corner = jnp.where(right, 1.0, decay(CHIP, h) * decay(CORNER, h))
        scale_got = jnp.where(low, corner, 0.0)
        outputs[1][i] = scale_total * totals[1][i] + scale_got * gots[1][i]


def mix_next_first(bits, arrays, outputs):
    own, got, chip, corner, first, second, one_a, one_b = arrays
    table = outputs[2]
    quarter = second.shape[0]
    for h in range(2 * quarter):
        place = HD + (TILE // 2) * (h // quarter)
        table[OWN, h : h + 1] = own[h, HD : HD + 1]
        table[PARTNER, h : h + 1] = got[h, HD : HD + 1]
        table[ROW, h : h + 1] = one_a[h % quarter, place : place + 1]
    table[CHIP] = chip[...]
    table[CORNER] = corner[...]
    decay = lambda which, h: table[which, h : h + 1]
    mix_next(bits, decay, (first, second), (one_a, one_b), outputs[:2])


def mix_next_again(bits, arrays, outputs):
    table, first, second, one_a, one_b = arrays
    decay = lambda which, h: table[which, h : h + 1]
    mix_next(bits, decay, (first, second), (one_a, one_b), outputs)


def mix_enter(bits, arrays, outputs):
    table, own, got, one_a, one_b, two_a, two_b = arrays
    kept, sent = outputs
    late, right, low = bits
    quarter = one_b.shape[0]
    decay = lambda which, h: table[which, h : h + 1]
    for h in range(2 * quarter):
        i = h % quarter
        row = jnp.where(right, decay(ROW, h), 1.0)
        if h < quarter:
            one, two = one_a[i, :HD], two_a[i]
            scale_one = jnp.where(right, 1.0, 0.0)
            scale_two = jnp.where(low, row, 0.0)
        else:
            one, two = one_b[i], two_b[i]
            scale_one = jnp.where(low, jnp.where(right, row, decay(CORNER, h)), 0.0)
            scale_two = jnp.where(low | right, 1.0, 0.0)
        enter = scale_one * one + scale_two * two
        after = jnp.where(late, decay(PARTNER, h), decay(OWN, h)) * enter
        after += jnp.where(late, got[h, :HD], own[h, :HD])
        kept[h] = jnp.where(late, after, enter)
        sent[h] = jnp.where(late, enter, after)


def entering_quad(own, send, table, place, backward, tasks):
    def work(stage, after, before=()):
        if stage not in tasks:
            return before
        run, outputs = tasks[stage]
        outputs.extend(run(after))
        return lax.optimization_barrier((before, outputs[-1]))[0]

    name = "later" if backward else "earlier"
    half = own.shape[0]
    quarter = half // 2
    states, wide = (quarter, HD, HD), (quarter, HD + TILE, HD)
    got = swap(send, "seq", 1)
    if table is None:
        first, second, chip = mix(
            mix_total_first, backward, place, (own, got), (wide, states, (half, HD)), name + "_total"
        )
    else:
        first, second = mix(
            mix_total_again, backward, place, (table, own, got), (states, states), name + "_total"
        )
    one_a, one_b = swap(first, "seq", 2), swap(second, "seq", 4)
    if table is None:
        corner = swap(chip, "seq", 6)
        one_a, one_b, corner = work(1, second, (one_a, one_b, corner))
        next_a, next_b, table = mix(
            mix_next_first, backward, place, (own, got, chip, corner, first, second, one_a, one_b),
            (states, states, (5, half, HD)), name + "_next",
        )
    else:
        one_a, one_b = work(1, second, (one_a, one_b))
        next_a, next_b = mix(
            mix_next_again, backward, place, (table, first, second, one_a, one_b), (states, states),
            name + "_next",
        )
    two_a, two_b = swap(next_a, "seq", 4), swap(next_b, "seq", 2)
    two_a, two_b = work(2, next_b, (two_a, two_b))
    kept, sent = mix(
        mix_enter, backward, place, (table, own, got, one_a, one_b, two_a, two_b),
        ((half, HD, HD), (half, HD, HD)), name + "_enter",
    )
    received = swap(sent, "seq", 1)
    work(3, sent)
    return kept, received, table


def entering_any(own, send, log_total, backward, tasks):
    for run, outputs in tasks.values():
        outputs.extend(run(send))
    count, mine = lax.axis_size("seq"), lax.axis_index("seq")
    core = mine % 2
    own, send = own[:, :HD], send[:, :HD]
    half = own.shape[0]
    in_order = jnp.where(
        core == 0, jnp.concatenate([own, send], axis=0), jnp.concatenate([send, own], axis=0)
    )
    states = lax.all_gather(in_order, "seq")
    decays = jnp.exp(lax.all_gather(log_total, "seq"))
    place = mine
    if backward:
        states, decays, place = states[::-1], decays[::-1], count - 1 - mine

    def step(at, total):
        longer = decays[at][:, None, None] * total + states[at]
        return jnp.where(at < place, longer, total)

    total = lax.fori_loop(0, count - 1, step, jnp.zeros_like(in_order))
    kept = lax.dynamic_slice_in_dim(total, core * half, half)
    return kept, lax.dynamic_slice_in_dim(total, (1 - core) * half, half)


def add(first, second):
    def kernel(first_ref, second_ref, out_ref):
        out_ref[...] = first_ref[...] + second_ref[...]

    return pl.pallas_call(
        kernel,
        in_specs=[NEAR, NEAR],
        out_specs=NEAR,
        out_shape=in_vmem(*first.shape),
        compiler_params=params(2),
        name="add",
    )(*near(first, second))


def sum_over_heads(value, tasks):
    tasks = list(tasks)
    results = []
    count = lax.axis_size("head")
    reach = 1
    while 2 * reach <= count and count % (2 * reach) == 0:
        got = swap(value, "head", reach)
        if tasks:
            results.append(tasks.pop(0)(value))
            got = follows(got, results[-1])
        value = add(value, got)
        reach *= 2
    results += [task(value) for task in tasks]
    part = value
    for shift in range(1, count // reach):
        value = add(
            value,
            lax.ppermute(part, "head", [(i, (i + shift * reach) % count) for i in range(count)]),
        )
    return value, results


def follows(value, earlier):
    return lax.optimization_barrier((value, earlier))[0]


def on_device(query_rows, key_rows, value_rows, output_grad, norm_gain, log_decay):
    mine = lax.axis_index("seq")
    bits = [(mine >> at) % 2 for at in range(3)]
    marks = [1 - bits[0], bits[0], *bits] + [jnp.zeros_like(mine)] * (TILE - 5)
    place = jnp.broadcast_to(jnp.stack(marks).astype(F32)[:, None], (TILE, HD))
    table = [None]

    def entering(own, send, backward, tasks):
        if lax.axis_size("seq") != 8:
            return entering_any(own, send, jnp.sum(log_decay, axis=1), backward, tasks)
        kept, received, table[0] = entering_quad(
            own, send, table[0], place, backward, tasks
        )
        return kept, received

    own, send, first, kh, vh = local_state(place, log_decay, key_rows, value_rows)

    def forward_task(index):
        return lambda earlier: intra(
            index, log_decay, kh, vh, follows(first, earlier), query_rows, output_grad
        )

    in_0, in_1 = [], []
    keep, recv = entering(
        own, send, False, {1: (forward_task(0), in_0), 2: (forward_task(1), in_1)}
    )
    q0, o0, w0, decays0, columns0, inner0 = in_0
    q1, o1, w1, decays1, columns1, inner1 = in_1
    att0, att1, sums = attend(
        place, norm_gain, keep, recv, (q0, q1, o0, o1, columns0, columns1, inner0, inner1)
    )
    sums, ((scaled, ends), remaining) = sum_over_heads(
        sums,
        (
            lambda earlier: scaled_queries(log_decay, follows(q0, earlier), q1),
            lambda earlier: remaining_decay(follows(log_decay, earlier)),
        ),
    )
    g0, g1, grad_own, grad_send, second = norm_grad(
        place, ends, norm_gain, sums, (scaled, o0, o1, att0, att1)
    )
    queries, pairs, norms = [], [], []

    def query_task(earlier):
        return grad_query(
            place, ends, keep, recv, follows(first, earlier),
            (kh, vh, g0, g1, decays0, decays1, columns0, columns1),
        )

    def pair_task(earlier):
        return grad_key_value(
            queries[1], w0, w1, q0, q1, kh, vh, g0, g1, remaining, follows(second, earlier),
            queries[0],
        )

    def norm_task(earlier):
        return [normed_rows(follows(norm_gain, earlier), sums, att0, att1)]

    grad_keep, grad_recv = entering(
        grad_own, grad_send, True, {1: (query_task, queries), 2: (pair_task, pairs), 3: (norm_task, norms)}
    )
    dk, dv, grad_q = pairs
    grad_k, grad_v = finish(place, ends, grad_keep, grad_recv, kh, vh, remaining, dk, dv)
    return norms[0], grad_q, grad_k, grad_v


def solution(mesh):
    rows = P("seq", "head", None)
    return jax.shard_map(
        on_device,
        mesh=mesh,
        in_specs=(rows, rows, rows, rows, P("head", None), P("head", "seq")),
        out_specs=(rows, rows, rows, rows),
        check_vma=False,
    )
```

```python
import jax
import jax.numpy as jnp
from jax import lax
from jax.experimental import pallas as pl
from jax.experimental.pallas import tpu as pltpu
from jax.sharding import PartitionSpec as P

HEAD_TOTAL = 64
HD = 128
BLOCK = 256
CHUNK = 128
TILE = 8
F32 = jnp.float32
BF16 = jnp.bfloat16
MIB = 1024 * 1024
NEAR = pl.BlockSpec(memory_space=pltpu.VMEM)
FAR = pl.BlockSpec(memory_space=pl.ANY)
LOWER, UPPER, LATE, RIGHT, LOW = range(5)


def in_vmem(*shape, kind=F32):
    return pltpu.VMEM(shape, kind)


def near(*arrays):
    return [pltpu.with_memory_space_constraint(array, pltpu.VMEM) for array in arrays]


def far(*arrays):
    return [pltpu.with_memory_space_constraint(array, pltpu.HBM) for array in arrays]


def params(mib):
    return pltpu.CompilerParams(vmem_limit_bytes=mib * MIB)


def cost(flops, moved, exps=0):
    return pl.CostEstimate(flops=flops, bytes_accessed=moved, transcendentals=exps)


def block_cum(log_decay):
    size = log_decay.shape[1]
    upper = lax.broadcasted_iota(jnp.int32, (size, size), 0) <= lax.broadcasted_iota(
        jnp.int32, (size, size), 1
    )
    return jnp.dot(
        log_decay,
        jnp.where(upper, 1.0, 0.0).astype(F32),
        precision=lax.Precision.HIGHEST,
        preferred_element_type=F32,
    )


def as_columns(row):
    return jnp.broadcast_to(row, (HD, row.shape[1])).T


def dot(a, b):
    return jnp.dot(a, b, preferred_element_type=F32)


def dot_rows(a, b):
    return lax.dot_general(a, b, (((1,), (1,)), ((), ())), preferred_element_type=F32)


def two_parts(matrix):
    high = matrix.astype(BF16)
    return high, (matrix - high.astype(F32)).astype(BF16)


def times_state(rows, state):
    return dot(jnp.concatenate([rows, rows], axis=1), jnp.concatenate(two_parts(state), axis=0))


def times_state_t(rows, state):
    return dot_rows(
        jnp.concatenate([rows, rows], axis=1), jnp.concatenate(two_parts(state), axis=1)
    )


def decay_quarters(row, columns):
    half = row.shape[1] // 2
    lower = lax.broadcasted_iota(jnp.int32, (half, half), 0) >= lax.broadcasted_iota(
        jnp.int32, (half, half), 1
    )
    quarters = []
    for t, s in ((0, 0), (1, 0), (1, 1)):
        gap = columns[t * half : (t + 1) * half] - row[:, s * half : (s + 1) * half]
        quarters.append(jnp.exp(jnp.where(lower, gap, -jnp.inf) if t == s else gap))
    return quarters


def causal(table, quarters):
    half = table.shape[0] // 2
    first, second, third = (
        (table[t * half : (t + 1) * half, s * half : (s + 1) * half] * quarter).astype(BF16)
        for (t, s), quarter in zip(((0, 0), (1, 0), (1, 1)), quarters)
    )
    top = jnp.concatenate([first, jnp.zeros_like(first)], axis=1)
    return jnp.concatenate([top, jnp.concatenate([second, third], axis=1)], axis=0)


def transposed_dot(a, b):
    return lax.dot_general(a, b, (((0,), (0,)), ((), ())), preferred_element_type=F32)


def each_head(heads, unroll, body):
    def step(h, carry):
        body(h)
        return carry

    lax.fori_loop(0, heads, step, 0, unroll=unroll)


def turn_tiles(tiles):
    count = len(tiles)
    at = lax.broadcasted_iota(jnp.int32, tiles[0].shape, 0)
    turned = [tile if i == 0 else pltpu.roll(tile, i, 0) for i, tile in enumerate(tiles)]
    reach = 1
    while reach < count:
        odd = (at & reach) != 0
        turned = [
            jnp.where(odd, turned[(n + reach) % count], turned[n]) for n in range(count)
        ]
        reach *= 2
    picked = [turned[-j % count] for j in range(count)]
    return [tile if j == 0 else pltpu.roll(tile, count - j, 0) for j, tile in enumerate(picked)]


def to_heads(dst, block):
    tok, heads, _ = block.shape

    def step(group, carry):
        at = pl.multiple_of(group * 2 * TILE, 2 * TILE)
        tokens = block[pl.ds(at, 2 * TILE)].astype(F32)
        for first in range(0, heads, TILE):
            halves = [
                turn_tiles([tokens[base + i, first : first + TILE] for i in range(TILE)])
                for base in (0, TILE)
            ]
            for j in range(TILE):
                both = jnp.concatenate([halves[0][j], halves[1][j]], axis=0)
                dst[first + j, pl.ds(at, 2 * TILE)] = both.astype(BF16)
        return carry

    lax.fori_loop(0, tok // (2 * TILE), step, 0, unroll=2)


def from_heads(block, src, start, tok):
    heads = src.shape[0]

    def step(group, carry):
        at = pl.multiple_of(group * TILE, TILE)
        parts = [
            turn_tiles([src[first + i, pl.ds(start + at, TILE)] for i in range(TILE)])
            for first in range(0, heads, TILE)
        ]
        for j in range(TILE):
            block[at + j] = jnp.concatenate([part[j] for part in parts], axis=0).astype(BF16)
        return carry

    lax.fori_loop(0, tok // TILE, step, 0, unroll=2)


def is_set(place_ref, which):
    return place_ref[which : which + 1] > 0.5


def split_halves(place_ref, whole, own_ref, send_ref):
    half = own_ref.shape[0]
    mine = is_set(place_ref, LOWER)
    for i in range(half):
        own_ref[i, :HD] = jnp.where(mine, whole[i], whole[half + i])
        send_ref[i, :HD] = jnp.where(mine, whole[half + i], whole[i])


def state_kernel(
    place_ref, ld_hbm, k_hbm, v_hbm, own_ref, send_ref, first_ref, kh, vh,
    ld_ref, k_raw, v_raw, cum, acc, decay, sems,
):
    heads, tok = ld_ref.shape
    half = heads // 2
    per_block = BLOCK // CHUNK
    copies = [pltpu.make_async_copy(ld_hbm, ld_ref, sems.at[0])]
    for c in range(tok // CHUNK):
        at = pl.ds(c * CHUNK, CHUNK)
        copies.append(pltpu.make_async_copy(k_hbm.at[at], k_raw.at[at], sems.at[2 * c + 1]))
        copies.append(pltpu.make_async_copy(v_hbm.at[at], v_raw.at[at], sems.at[2 * c + 2]))
    for copy in copies:
        copy.start()
    copies[0].wait()
    for b in range(2):
        cum[b] = block_cum(ld_ref[:, b * BLOCK : (b + 1) * BLOCK])
    ends = cum[0, :, BLOCK - 1 :] + cum[1, :, BLOCK - 1 :]
    decay[...] = jnp.broadcast_to(jnp.exp(ends), decay.shape)

    for b in range(2):
        for c in range(per_block):
            at = pl.ds((b * per_block + c) * CHUNK, CHUNK)
            here = pl.ds(c * CHUNK, CHUNK)
            which = 2 * (b * per_block + c) + 1
            copies[which].wait()
            to_heads(kh.at[b, :, here], k_raw.at[at])
            copies[which + 1].wait()
            to_heads(vh.at[b, :, here], v_raw.at[at])

        def one(h, b=b):
            row = cum[b, pl.ds(h, 1), :]
            scale = jnp.exp(row[:, BLOCK - 1 :] - row)
            state = dot((kh[b, h].astype(F32).T * scale).astype(BF16), vh[b, h])
            if b == 0:
                first_ref[h] = state
            else:
                acc[h] = state + jnp.exp(row[:, BLOCK - 1 :]) * first_ref[h]

        each_head(heads, 4, one)

    split_halves(place_ref, acc, own_ref, send_ref)
    mine = is_set(place_ref, LOWER)
    for i in range(half):
        lower, upper = decay[i : i + 1], decay[half + i : half + i + 1]
        for ref, row in (
            (own_ref, jnp.where(mine, lower, upper)), (send_ref, jnp.where(mine, upper, lower)),
        ):
            ref[i, HD:] = jnp.broadcast_to(row, (TILE, HD))


def local_state(place, log_decay, key_rows, value_rows):
    tok, heads, dim = key_rows.shape
    half = heads // 2
    by_head = in_vmem(2, heads, BLOCK, dim, kind=BF16)
    return pl.pallas_call(
        state_kernel,
        in_specs=[NEAR, FAR, FAR, FAR],
        out_specs=[NEAR] * 5,
        out_shape=[
            in_vmem(half, dim + TILE, dim), in_vmem(half, dim + TILE, dim),
            in_vmem(heads, dim, dim), by_head, by_head,
        ],
        scratch_shapes=[
            pltpu.VMEM((heads, tok), F32),
            pltpu.VMEM((tok, heads, dim), BF16),
            pltpu.VMEM((tok, heads, dim), BF16),
            pltpu.VMEM((2, heads, BLOCK), F32),
            pltpu.VMEM((heads, dim, dim), F32),
            pltpu.VMEM((heads, dim), F32),
            pltpu.SemaphoreType.DMA((2 * (tok // CHUNK) + 1,)),
        ],
        compiler_params=params(8),
        cost_estimate=cost(2 * tok * heads * dim * dim, 8 * tok * heads * dim),
        name="local_state",
    )(place, *far(log_decay, key_rows, value_rows))


def intra(index, log_decay, kh, vh, first, query_rows, output_grad):
    tok, heads, dim = query_rows.shape

    def kernel(ld_ref, kh, vh, first_ref, q_hbm, o_hbm,
               qh, oh, w_ref, decays_ref, columns_ref, inner_ref,
               q_raw, o_raw, cum, sems):
        at = pl.ds(index * BLOCK, BLOCK)
        copy_q = pltpu.make_async_copy(q_hbm.at[at], q_raw, sems.at[0])
        copy_o = pltpu.make_async_copy(o_hbm.at[at], o_raw, sems.at[1])
        copy_q.start()
        copy_o.start()
        cum[...] = block_cum(ld_ref[:, index * BLOCK : (index + 1) * BLOCK])
        copy_q.wait()
        to_heads(qh, q_raw)
        copy_o.wait()
        to_heads(oh, o_raw)

        def one(h):
            query = qh[h]
            row = cum[pl.ds(h, 1), :]
            columns = as_columns(row)
            quarters = decay_quarters(row, columns)
            for at, quarter in enumerate(quarters):
                decays_ref[h, at] = quarter
            weights = causal(dot_rows(query, kh[index, h]), quarters)
            w_ref[h] = weights
            inner = dot(weights, vh[index, h])
            columns = jnp.exp(columns)
            columns_ref[h] = columns
            if index:
                inner += columns * times_state(query, first_ref[h])
            inner_ref[h] = inner

        each_head(heads, 2, one)

    by_head = in_vmem(heads, BLOCK, dim, kind=BF16)
    return pl.pallas_call(
        kernel,
        in_specs=[NEAR] * 4 + [FAR, FAR],
        out_specs=[NEAR] * 6,
        out_shape=[
            by_head, by_head, in_vmem(heads, BLOCK, BLOCK, kind=BF16),
            in_vmem(heads, 3, BLOCK // 2, BLOCK // 2), in_vmem(heads, BLOCK, dim),
            in_vmem(heads, BLOCK, dim),
        ],
        scratch_shapes=[
            pltpu.VMEM((BLOCK, heads, dim), BF16),
            pltpu.VMEM((BLOCK, heads, dim), BF16),
            pltpu.VMEM((heads, BLOCK), F32),
            pltpu.SemaphoreType.DMA((2,)),
        ],
        compiler_params=params(6),
        cost_estimate=cost(
            2 * heads * BLOCK * BLOCK * dim * 4, 20 * heads * BLOCK * dim, heads * BLOCK * BLOCK
        ),
        name=f"intra_{index}",
    )(log_decay, *near(kh, vh, first), *far(query_rows, output_grad))


def whole_state(place_ref, keep_ref, recv_ref, head):
    half = keep_ref.shape[0]
    mine = place_ref[pl.ds(head // half, 1)] > 0.5
    return jnp.where(mine, keep_ref[head % half], recv_ref[head % half])


def attend_kernel(
    place_ref, gain_ref, keep_ref, recv_ref, q0, q1, o0, o1, columns0, columns1, inner0, inner1,
    att0, att1, sums_ref, squares, products,
):
    heads = gain_ref.shape[0]
    squares[...] = jnp.zeros_like(squares)
    products[...] = jnp.zeros_like(products)

    def one(h):
        state = whole_state(place_ref, keep_ref, recv_ref, h)
        gain = gain_ref[pl.ds(h, 1), :]
        blocks = ((q0, o0, columns0, inner0, att0), (q1, o1, columns1, inner1, att1))
        for b, (q, o, columns, inner, att) in enumerate(blocks):
            attended = inner[h] + columns[h] * times_state(q[h], state)
            att[h] = attended
            squares[b] += attended * attended
            products[b] += gain * o[h].astype(F32) * attended
            state = columns[h, BLOCK - 1 :] * state

    each_head(heads, 4, one)
    ones = jnp.ones((8, HD), F32)
    for b in range(2):
        for at, total in enumerate((squares, products)):
            line = lax.dot_general(
                ones, total[b], (((1,), (1,)), ((), ())),
                precision=lax.Precision.HIGHEST, preferred_element_type=F32,
            )
            sums_ref[at : at + 1, b * BLOCK : (b + 1) * BLOCK] = line[:1]


def attend(place, gain, keep, recv, parts):
    heads, dim = gain.shape
    tok = 2 * BLOCK
    by_head = in_vmem(heads, BLOCK, dim)
    return pl.pallas_call(
        attend_kernel,
        in_specs=[NEAR] * 12,
        out_specs=[NEAR] * 3,
        out_shape=[by_head, by_head, in_vmem(2, tok)],
        scratch_shapes=[pltpu.VMEM((2, BLOCK, dim), F32), pltpu.VMEM((2, BLOCK, dim), F32)],
        compiler_params=params(6),
        cost_estimate=cost(4 * heads * tok * dim * dim, 16 * heads * tok * dim),
        name="attend",
    )(place, gain, *near(keep, recv, *parts))


def queries_kernel(ld_ref, q0, q1, out_ref, ends_ref, cum):
    heads = ld_ref.shape[0]
    for b in range(2):
        cum[b] = jnp.exp(block_cum(ld_ref[:, b * BLOCK : (b + 1) * BLOCK]))
        ends_ref[b] = jnp.broadcast_to(cum[b, :, BLOCK - 1 :], (heads, HD))

    def one(h):
        for b, q in enumerate((q0, q1)):
            out_ref[b, h] = (q[h].astype(F32).T * cum[b, pl.ds(h, 1), :]).astype(BF16)

    each_head(heads, 2, one)


def scaled_queries(log_decay, q0, q1):
    heads, tok = log_decay.shape
    return pl.pallas_call(
        queries_kernel,
        in_specs=[NEAR] * 3,
        out_specs=[NEAR] * 2,
        out_shape=[in_vmem(2, heads, HD, BLOCK, kind=BF16), in_vmem(2, heads, HD)],
        scratch_shapes=[pltpu.VMEM((2, heads, BLOCK), F32)],
        compiler_params=params(4),
        cost_estimate=cost(2 * heads * tok * HD, 4 * heads * tok * HD),
        name="scaled_queries",
    )(log_decay, *near(q0, q1))


def remaining_kernel(ld_ref, out_ref, cum):
    heads = ld_ref.shape[0]
    for b in range(2):
        total = block_cum(ld_ref[:, b * BLOCK : (b + 1) * BLOCK])
        cum[b] = jnp.exp(total[:, BLOCK - 1 :] - total)

    def one(h):
        for b in range(2):
            out_ref[b, h] = as_columns(cum[b, pl.ds(h, 1), :])

    each_head(heads, 2, one)


def remaining_decay(log_decay):
    heads, tok = log_decay.shape
    return pl.pallas_call(
        remaining_kernel,
        in_specs=[NEAR],
        out_specs=NEAR,
        out_shape=in_vmem(2, heads, BLOCK, HD),
        scratch_shapes=[pltpu.VMEM((2, heads, BLOCK), F32)],
        compiler_params=params(4),
        cost_estimate=cost(heads * tok * HD, 4 * heads * tok * HD),
        name="remaining_decay",
    )(log_decay)


def inverse_rms(sums_ref, b):
    at = slice(b * BLOCK, (b + 1) * BLOCK)
    inv = lax.rsqrt(sums_ref[0:1, at] / (HEAD_TOTAL * HD) + 1e-06)
    mean = sums_ref[1:2, at] * inv / (HEAD_TOTAL * HD)
    return inv, mean


def norm_grad_kernel(
    place_ref, ends_ref, gain_ref, sums_ref, queries_ref, o0, o1, att0, att1,
    g0, g1, own_ref, send_ref, second_ref, scales, acc,
):
    for b in range(2):
        inv, mean = inverse_rms(sums_ref, b)
        scales[b, 0] = as_columns(inv)
        scales[b, 1] = as_columns(inv * inv * mean)

    def one(h):
        gain = gain_ref[pl.ds(h, 1), :]
        starts = []
        for b, (o, att, g) in enumerate(((o0, att0, g0), (o1, att1, g1))):
            grad = gain * o[h].astype(F32) * scales[b, 0] - att[h] * scales[b, 1]
            grad = grad.astype(BF16)
            g[h] = grad
            starts.append(dot(queries_ref[b, h], grad))
        second_ref[h] = starts[1]
        acc[h] = starts[0] + ends_ref[0, pl.ds(h, 1)] * starts[1]

    each_head(gain_ref.shape[0], 2, one)
    split_halves(place_ref, acc, own_ref, send_ref)


def norm_grad(place, ends, gain, sums, parts):
    heads, dim = gain.shape
    tok = 2 * BLOCK
    half = heads // 2
    by_head = in_vmem(heads, BLOCK, dim, kind=BF16)
    return pl.pallas_call(
        norm_grad_kernel,
        in_specs=[NEAR] * 9,
        out_specs=[NEAR] * 5,
        out_shape=[
            by_head, by_head, in_vmem(half, dim, dim), in_vmem(half, dim, dim),
            in_vmem(heads, dim, dim),
        ],
        scratch_shapes=[
            pltpu.VMEM((2, 2, BLOCK, dim), F32),
            pltpu.VMEM((heads, dim, dim), F32),
        ],
        compiler_params=params(6),
        cost_estimate=cost(2 * heads * tok * dim * dim, 14 * heads * tok * dim),
        name="norm_grad",
    )(place, ends, gain, sums, *near(*parts))


def on_block(work):
    for index in range(2):
        pl.when(pl.program_id(0) == index)(lambda index=index: work(index))


def raw_output(heads, tok):
    spec = pl.BlockSpec((BLOCK, heads, HD), lambda i: (i, 0, 0))
    return spec, jax.ShapeDtypeStruct((tok, heads, HD), BF16)


def normed_kernel(gain_ref, sums_ref, att0, att1, out_ref, rows):
    heads = gain_ref.shape[0]

    def work(b):
        inv = as_columns(inverse_rms(sums_ref, b)[0])
        att = (att0, att1)[b]

        def one(h):
            rows[h] = att[h] * inv * gain_ref[pl.ds(h, 1), :]

        each_head(heads, 2, one)

    on_block(work)
    from_heads(out_ref, rows, 0, BLOCK)


def normed_rows(gain, sums, att0, att1):
    heads, _, dim = att0.shape
    tok = 2 * BLOCK
    spec, shape = raw_output(heads, tok)
    return pl.pallas_call(
        normed_kernel,
        grid=(2,),
        in_specs=[NEAR] * 4,
        out_specs=spec,
        out_shape=shape,
        scratch_shapes=[pltpu.VMEM((heads, BLOCK, dim), F32)],
        compiler_params=params(7),
        cost_estimate=cost(3 * heads * tok * dim, 6 * heads * tok * dim),
        name="normed_rows",
    )(gain, sums, *near(att0, att1))


def grad_q_kernel(
    place_ref, ends_ref, keep_ref, recv_ref, first_ref, kh, vh, g0, g1, decays0, decays1,
    columns0, columns1, rows, gs_ref,
):
    heads = ends_ref.shape[1]
    for b, (g, decays, columns) in enumerate(((g0, decays0, columns0), (g1, decays1, columns1))):

        def one(h, b=b, g=g, decays=decays, columns=columns):
            quarters = [decays[h, at] for at in range(3)]
            scores = causal(dot_rows(g[h], vh[b, h]), quarters)
            gs_ref[b, h] = scores
            state = whole_state(place_ref, keep_ref, recv_ref, h)
            if b:
                state = ends_ref[0, pl.ds(h, 1)] * state + first_ref[h]
            rows[b, h] = dot(scores, kh[b, h]) + columns[h] * times_state_t(g[h], state)

        each_head(heads, 4, one)


def grad_query(place, ends, keep, recv, first, parts):
    _, heads, dim = ends.shape
    tok = 2 * BLOCK
    return pl.pallas_call(
        grad_q_kernel,
        in_specs=[NEAR] * 13,
        out_specs=[NEAR, NEAR],
        out_shape=[
            in_vmem(2, heads, BLOCK, dim), in_vmem(2, heads, BLOCK, BLOCK, kind=BF16),
        ],
        compiler_params=params(4),
        cost_estimate=cost(
            4 * heads * tok * dim * (BLOCK + dim), 12 * heads * tok * dim, heads * tok * BLOCK
        ),
        name="grad_query",
    )(place, ends, *near(keep, recv, first, *parts))


def grad_kv_kernel(
    gs_ref, w0, w1, q0, q1, kh, vh, g0, g1, remaining_ref, second_ref, rows, dk, dv, out_q,
    raw, sems,
):
    heads = gs_ref.shape[1]
    copies = []
    for b in range(2):
        for start in range(0, BLOCK, CHUNK):
            at = pl.ds(b * BLOCK + start, CHUNK)
            from_heads(raw.at[at], rows.at[b], start, CHUNK)
            copies.append(pltpu.make_async_copy(raw.at[at], out_q.at[at], sems.at[len(copies)]))
            copies[-1].start()

    def one(h):
        columns = remaining_ref[0, h]
        state = second_ref[h]
        dk[0, h] = transposed_dot(gs_ref[0, h], q0[h]) + columns * times_state_t(vh[0, h], state)
        dv[0, h] = transposed_dot(w0[h], g0[h]) + columns * times_state(kh[0, h], state)
        dk[1, h] = transposed_dot(gs_ref[1, h], q1[h])
        dv[1, h] = transposed_dot(w1[h], g1[h])

    each_head(heads, 2, one)
    for copy in copies:
        copy.wait()


def grad_key_value(*arrays):
    _, heads, _, dim = arrays[5].shape
    tok = 2 * BLOCK
    return pl.pallas_call(
        grad_kv_kernel,
        in_specs=[NEAR] * 12,
        out_specs=[NEAR, NEAR, FAR],
        out_shape=[in_vmem(2, heads, BLOCK, dim)] * 2
        + [jax.ShapeDtypeStruct((tok, heads, dim), BF16)],
        scratch_shapes=[
            pltpu.VMEM((tok, heads, dim), BF16),
            pltpu.SemaphoreType.DMA((tok // CHUNK,)),
        ],
        compiler_params=params(6),
        cost_estimate=cost(4 * heads * tok * dim * (BLOCK + dim), 30 * heads * tok * dim),
        name="grad_key_value",
    )(*near(*arrays))


def finish_kernel(
    place_ref, ends_ref, keep_ref, recv_ref, kh, vh, remaining_ref, dk, dv, out_k, out_v,
    rows_k, rows_v, raw_k, raw_v, sems,
):
    heads = ends_ref.shape[1]
    copies = []
    for b in range(2):

        def one(h, b=b):
            columns = remaining_ref[b, h]
            state = whole_state(place_ref, keep_ref, recv_ref, h)
            if b == 0:
                state = ends_ref[1, pl.ds(h, 1)] * state
            state = state.astype(BF16)
            none = jnp.zeros_like(state)
            both = jnp.concatenate(
                [jnp.concatenate([state.T, none], axis=1), jnp.concatenate([none, state], axis=1)],
                axis=0,
            )
            carried = dot(jnp.concatenate([vh[b, h], kh[b, h]], axis=1), both)
            rows_k[h] = dk[b, h] + columns * carried[:, :HD]
            rows_v[h] = dv[b, h] + columns * carried[:, HD:]

        each_head(heads, 4, one)
        for start in range(0, BLOCK, CHUNK):
            at = pl.ds(b * BLOCK + start, CHUNK)
            for rows, raw, out in ((rows_k, raw_k, out_k), (rows_v, raw_v, out_v)):
                from_heads(raw.at[at], rows, start, CHUNK)
                copies.append(pltpu.make_async_copy(raw.at[at], out.at[at], sems.at[len(copies)]))
                copies[-1].start()
    for copy in copies:
        copy.wait()


def finish(place, ends, keep, recv, kh, vh, remaining, dk, dv):
    _, heads, dim = ends.shape
    tok = 2 * BLOCK
    shape = jax.ShapeDtypeStruct((tok, heads, dim), BF16)
    return pl.pallas_call(
        finish_kernel,
        in_specs=[NEAR] * 9,
        out_specs=[FAR, FAR],
        out_shape=[shape, shape],
        scratch_shapes=[
            pltpu.VMEM((heads, BLOCK, dim), F32),
            pltpu.VMEM((heads, BLOCK, dim), F32),
            pltpu.VMEM((tok, heads, dim), BF16),
            pltpu.VMEM((tok, heads, dim), BF16),
            pltpu.SemaphoreType.DMA((2 * (tok // CHUNK),)),
        ],
        compiler_params=params(12),
        cost_estimate=cost(8 * heads * tok * dim * dim, 16 * heads * tok * dim),
        name="finish",
    )(place, ends, *near(keep, recv, kh, vh, remaining, dk, dv))


def swap(value, axis, bit):
    count = lax.axis_size(axis)
    bits = bit if isinstance(bit, tuple) else (bit, bit)
    return lax.ppermute(value, axis, [(i, i ^ bits[i % 2]) for i in range(count)])


def mix(body, backward, place, arrays, shapes, name):
    def kernel(place_ref, *refs):
        bits = [is_set(place_ref, which) != backward for which in (LATE, RIGHT, LOW)]
        bits.append(is_set(place_ref, UPPER))
        body(bits, refs[: len(arrays)], refs[len(arrays) :])

    return pl.pallas_call(
        kernel,
        in_specs=[NEAR] + [NEAR] * len(arrays),
        out_specs=[NEAR] * len(shapes),
        out_shape=[in_vmem(*shape) for shape in shapes],
        compiler_params=params(4),
        cost_estimate=cost(4 * 8 * HD * HD, 16 * 8 * HD * HD),
        name=name,
    )(place, *near(*arrays))


OWN, PARTNER, CHIP, ROW, CORNER = range(5)


def mix_total(bits, own, got, d_own, d_got, out):
    late = bits[0]
    for h in range(out.shape[0]):
        scale_own, scale_got = jnp.where(late, 1.0, d_got(h)), jnp.where(late, d_own(h), 1.0)
        out[h, :HD] = scale_own * own[h, :HD] + scale_got * got[h, :HD]


def mix_total_first(bits, arrays, outputs):
    own, got = arrays
    total, chip = outputs
    d_own = lambda h: own[h, HD : HD + 1]
    d_got = lambda h: got[h, HD : HD + 1]
    mix_total(bits, own, got, d_own, d_got, total)
    for h in range(total.shape[0]):
        both = d_own(h) * d_got(h)
        chip[h : h + 1] = both
        total[h, HD:] = jnp.broadcast_to(both, (TILE, HD))


def mix_total_again(bits, arrays, outputs):
    table, own, got = arrays
    decay = lambda which: lambda h: table[which, h : h + 1]
    mix_total(bits, own, got, decay(OWN), decay(PARTNER), *outputs)


def mix_next(bits, chip, corner, row, total, one, out):
    _, right, low, by_column = bits
    for h in range(out.shape[0]):
        scale_total = jnp.where(
            by_column, jnp.where(low & right, 0.0, 1.0), jnp.where(right, 1.0, row(h))
        )
        scale_one = jnp.where(
            by_column,
            jnp.where(low, jnp.where(right, 1.0, chip(h) * corner(h)), 0.0),
            jnp.where(right, chip(h), 1.0),
        )
        out[h, :HD] = scale_total * total[h, :HD] + scale_one * one[h, :HD]


def mix_next_first(bits, arrays, outputs):
    chip, corner, total, one = arrays
    (out,) = outputs
    lines = lambda ref: lambda h: ref[h : h + 1]
    mix_next(bits, lines(chip), lines(corner), lambda h: one[h, HD : HD + 1], total, one, out)
    out[:, HD:] = total[:, HD:]


def mix_next_again(bits, arrays, outputs):
    table, total, one = arrays
    decay = lambda which: lambda h: table[which, h : h + 1]
    mix_next(bits, decay(CHIP), decay(CORNER), decay(ROW), total, one, *outputs)


def mix_enter(bits, table, own, got, one, two, kept, sent):
    late, right, low, by_column = bits
    for h in range(kept.shape[0]):
        decay = lambda which: table[which, h : h + 1]
        row = jnp.where(right, decay(ROW), 1.0)
        scale_one = jnp.where(
            by_column,
            jnp.where(low, jnp.where(right, row, decay(CORNER)), 0.0),
            jnp.where(right, 1.0, 0.0),
        )
        scale_two = jnp.where(
            by_column, jnp.where(low | right, 1.0, 0.0), jnp.where(low, row, 0.0)
        )
        enter = scale_one * one[h, :HD] + scale_two * two[h, :HD]
        after = jnp.where(late, decay(PARTNER), decay(OWN)) * enter
        after += jnp.where(late, got[h, :HD], own[h, :HD])
        kept[h] = jnp.where(late, after, enter)
        sent[h] = jnp.where(late, enter, after)


def mix_enter_first(bits, arrays, outputs):
    own, got, chip, corner, one, two = arrays
    kept, sent, table = outputs
    for h in range(kept.shape[0]):
        at, line = slice(h, h + 1), slice(HD, HD + 1)
        table[OWN, at], table[PARTNER, at] = own[h, line], got[h, line]
        table[ROW, at] = jnp.where(bits[3], two[h, line], one[h, line])
    table[CHIP], table[CORNER] = chip[...], corner[...]
    mix_enter(bits, table, own, got, one, two, kept, sent)


def mix_enter_again(bits, arrays, outputs):
    mix_enter(bits, *arrays, *outputs)


def entering_quad(own, send, table, place, backward, tasks):
    def work(stage, after, before=()):
        if stage not in tasks:
            return before
        run, outputs = tasks[stage]
        outputs.extend(run(after))
        return lax.optimization_barrier((before, outputs[-1]))[0]

    name = "later" if backward else "earlier"
    half = own.shape[0]
    states, wide = (half, HD, HD), (half, HD + TILE, HD)
    got = swap(send, "seq", 1)
    if table is None:
        total, chip = mix(
            mix_total_first, backward, place, (own, got), (wide, (half, HD)), name + "_total"
        )
        one, corner = swap(total, "seq", (2, 4)), swap(chip, "seq", 6)
        one, corner = work(1, total, (one, corner))
        (after,) = mix(
            mix_next_first, backward, place, (chip, corner, total, one), (wide,), name + "_next"
        )
    else:
        (total,) = mix(
            mix_total_again, backward, place, (table, own, got), (states,), name + "_total"
        )
        one = work(1, total, swap(total, "seq", (2, 4)))
        (after,) = mix(
            mix_next_again, backward, place, (table, total, one), (states,), name + "_next"
        )
    two = work(2, after, swap(after, "seq", (4, 2)))
    if table is None:
        kept, sent, table = mix(
            mix_enter_first, backward, place, (own, got, chip, corner, one, two),
            (states, states, (5, half, HD)), name + "_enter",
        )
    else:
        kept, sent = mix(
            mix_enter_again, backward, place, (table, own, got, one, two), (states, states),
            name + "_enter",
        )
    received = swap(sent, "seq", 1)
    work(3, sent)
    return kept, received, table


def entering_any(own, send, log_total, backward, tasks):
    for run, outputs in tasks.values():
        outputs.extend(run(send))
    count, mine = lax.axis_size("seq"), lax.axis_index("seq")
    core = mine % 2
    own, send = own[:, :HD], send[:, :HD]
    half = own.shape[0]
    in_order = jnp.where(
        core == 0, jnp.concatenate([own, send], axis=0), jnp.concatenate([send, own], axis=0)
    )
    states = lax.all_gather(in_order, "seq")
    decays = jnp.exp(lax.all_gather(log_total, "seq"))
    place = mine
    if backward:
        states, decays, place = states[::-1], decays[::-1], count - 1 - mine

    def step(at, total):
        longer = decays[at][:, None, None] * total + states[at]
        return jnp.where(at < place, longer, total)

    total = lax.fori_loop(0, count - 1, step, jnp.zeros_like(in_order))
    kept = lax.dynamic_slice_in_dim(total, core * half, half)
    return kept, lax.dynamic_slice_in_dim(total, (1 - core) * half, half)


def add(first, second):
    def kernel(first_ref, second_ref, out_ref):
        out_ref[...] = first_ref[...] + second_ref[...]

    return pl.pallas_call(
        kernel,
        in_specs=[NEAR, NEAR],
        out_specs=NEAR,
        out_shape=in_vmem(*first.shape),
        compiler_params=params(2),
        name="add",
    )(*near(first, second))


def sum_over_heads(value, tasks):
    tasks = list(tasks)
    results = []
    count = lax.axis_size("head")
    reach = 1
    while 2 * reach <= count and count % (2 * reach) == 0:
        got = swap(value, "head", reach)
        if tasks:
            results.append(tasks.pop(0)(value))
            got = follows(got, results[-1])
        value = add(value, got)
        reach *= 2
    results += [task(value) for task in tasks]
    part = value
    for shift in range(1, count // reach):
        value = add(
            value,
            lax.ppermute(part, "head", [(i, (i + shift * reach) % count) for i in range(count)]),
        )
    return value, results


def follows(value, earlier):
    return lax.optimization_barrier((value, earlier))[0]


def on_device(query_rows, key_rows, value_rows, output_grad, norm_gain, log_decay):
    mine = lax.axis_index("seq")
    bits = [(mine >> at) % 2 for at in range(3)]
    marks = [1 - bits[0], bits[0], *bits] + [jnp.zeros_like(mine)] * (TILE - 5)
    place = jnp.broadcast_to(jnp.stack(marks).astype(F32)[:, None], (TILE, HD))
    table = [None]

    def entering(own, send, backward, tasks):
        if lax.axis_size("seq") != 8:
            return entering_any(own, send, jnp.sum(log_decay, axis=1), backward, tasks)
        kept, received, table[0] = entering_quad(
            own, send, table[0], place, backward, tasks
        )
        return kept, received

    own, send, first, kh, vh = local_state(place, log_decay, key_rows, value_rows)

    def forward_task(index):
        return lambda earlier: intra(
            index, log_decay, kh, vh, follows(first, earlier), query_rows, output_grad
        )

    in_0, in_1 = [], []
    keep, recv = entering(
        own, send, False, {1: (forward_task(0), in_0), 2: (forward_task(1), in_1)}
    )
    q0, o0, w0, decays0, columns0, inner0 = in_0
    q1, o1, w1, decays1, columns1, inner1 = in_1
    att0, att1, sums = attend(
        place, norm_gain, keep, recv, (q0, q1, o0, o1, columns0, columns1, inner0, inner1)
    )
    sums, ((scaled, ends), remaining) = sum_over_heads(
        sums,
        (
            lambda earlier: scaled_queries(log_decay, follows(q0, earlier), q1),
            lambda earlier: remaining_decay(follows(log_decay, earlier)),
        ),
    )
    g0, g1, grad_own, grad_send, second = norm_grad(
        place, ends, norm_gain, sums, (scaled, o0, o1, att0, att1)
    )
    queries, pairs, norms = [], [], []

    def query_task(earlier):
        return grad_query(
            place, ends, keep, recv, follows(first, earlier),
            (kh, vh, g0, g1, decays0, decays1, columns0, columns1),
        )

    def pair_task(earlier):
        return grad_key_value(
            queries[1], w0, w1, q0, q1, kh, vh, g0, g1, remaining, follows(second, earlier),
            queries[0],
        )

    def norm_task(earlier):
        return [normed_rows(follows(norm_gain, earlier), sums, att0, att1)]

    grad_keep, grad_recv = entering(
        grad_own, grad_send, True, {1: (query_task, queries), 2: (pair_task, pairs), 3: (norm_task, norms)}
    )
    dk, dv, grad_q = pairs
    grad_k, grad_v = finish(place, ends, grad_keep, grad_recv, kh, vh, remaining, dk, dv)
    return norms[0], grad_q, grad_k, grad_v


def solution(mesh):
    rows = P("seq", "head", None)
    return jax.shard_map(
        on_device,
        mesh=mesh,
        in_specs=(rows, rows, rows, rows, P("head", None), P("head", "seq")),
        out_specs=(rows, rows, rows, rows),
        check_vma=False,
    )
```

```python
import functools

import jax
import jax.numpy as jnp
from jax import lax
from jax.experimental import pallas as pl
from jax.experimental.pallas import tpu as pltpu
from jax.sharding import PartitionSpec as P

HEAD_TOTAL = 64
HD = 128
BLOCK = 256
CHUNK = 128
TILE = 8
F32 = jnp.float32
BF16 = jnp.bfloat16
MIB = 1024 * 1024
NEAR = pl.BlockSpec(memory_space=pltpu.VMEM)
FAR = pl.BlockSpec(memory_space=pl.ANY)
LOWER, UPPER, LATE, RIGHT, LOW = range(5)


def in_vmem(*shape, kind=F32):
    return pltpu.VMEM(shape, kind)


def near(*arrays):
    return [pltpu.with_memory_space_constraint(array, pltpu.VMEM) for array in arrays]


def far(*arrays):
    return [pltpu.with_memory_space_constraint(array, pltpu.HBM) for array in arrays]


def params(mib):
    return pltpu.CompilerParams(vmem_limit_bytes=mib * MIB)


def cost(flops, moved, exps=0):
    return pl.CostEstimate(flops=flops, bytes_accessed=moved, transcendentals=exps)


def block_cum(log_decay):
    size = log_decay.shape[1]
    upper = lax.broadcasted_iota(jnp.int32, (size, size), 0) <= lax.broadcasted_iota(
        jnp.int32, (size, size), 1
    )
    return jnp.dot(
        log_decay,
        jnp.where(upper, 1.0, 0.0).astype(F32),
        precision=lax.Precision.HIGHEST,
        preferred_element_type=F32,
    )


def as_columns(row):
    return jnp.broadcast_to(row, (HD, row.shape[1])).T


def dot(a, b):
    return jnp.dot(a, b, preferred_element_type=F32)


def dot_rows(a, b):
    return lax.dot_general(a, b, (((1,), (1,)), ((), ())), preferred_element_type=F32)


def two_parts(matrix):
    high = matrix.astype(BF16)
    return high, (matrix - high.astype(F32)).astype(BF16)


def times_state(rows, state):
    return dot(jnp.concatenate([rows, rows], axis=1), jnp.concatenate(two_parts(state), axis=0))


def times_state_t(rows, state):
    return dot_rows(
        jnp.concatenate([rows, rows], axis=1), jnp.concatenate(two_parts(state), axis=1)
    )


def decay_quarters(row, columns):
    half = row.shape[1] // 2
    lower = lax.broadcasted_iota(jnp.int32, (half, half), 0) >= lax.broadcasted_iota(
        jnp.int32, (half, half), 1
    )
    quarters = []
    for t, s in ((0, 0), (1, 0), (1, 1)):
        gap = columns[t * half : (t + 1) * half] - row[:, s * half : (s + 1) * half]
        quarters.append(jnp.exp(jnp.where(lower, gap, -jnp.inf) if t == s else gap))
    return quarters


def causal(table, quarters):
    half = table.shape[0] // 2
    first, second, third = (
        (table[t * half : (t + 1) * half, s * half : (s + 1) * half] * quarter).astype(BF16)
        for (t, s), quarter in zip(((0, 0), (1, 0), (1, 1)), quarters)
    )
    top = jnp.concatenate([first, jnp.zeros_like(first)], axis=1)
    return jnp.concatenate([top, jnp.concatenate([second, third], axis=1)], axis=0)


def transposed_dot(a, b):
    return lax.dot_general(a, b, (((0,), (0,)), ((), ())), preferred_element_type=F32)


def each_head(heads, unroll, body):
    def step(h, carry):
        body(h)
        return carry

    lax.fori_loop(0, heads, step, 0, unroll=unroll)


def each_half(half, unroll, body):
    for part in range(2):
        each_head(half, unroll, lambda i, part=part: body(part, i, part * half + i))


def turn_tiles(tiles):
    count = len(tiles)
    at = lax.broadcasted_iota(jnp.int32, tiles[0].shape, 0)
    turned = [tile if i == 0 else pltpu.roll(tile, i, 0) for i, tile in enumerate(tiles)]
    reach = 1
    while reach < count:
        odd = (at & reach) != 0
        turned = [
            jnp.where(odd, turned[(n + reach) % count], turned[n]) for n in range(count)
        ]
        reach *= 2
    picked = [turned[-j % count] for j in range(count)]
    return [tile if j == 0 else pltpu.roll(tile, count - j, 0) for j, tile in enumerate(picked)]


def is_upper(place_ref):
    return jnp.max(place_ref[UPPER : UPPER + 1]) > 0.5


def to_heads(dst, block, upper):
    tok, heads, _ = block.shape

    def step(group, carry):
        at = pl.multiple_of(group * 2 * TILE, 2 * TILE)
        tokens = block[pl.ds(at, 2 * TILE)].astype(F32)
        for first in range(0, heads, TILE):
            halves = [
                turn_tiles([tokens[base + i, first : first + TILE] for i in range(TILE)])
                for base in (0, TILE)
            ]
            local = jnp.where(upper, heads - TILE - first, first)
            for j in range(TILE):
                both = jnp.concatenate([halves[0][j], halves[1][j]], axis=0)
                dst[local + j, pl.ds(at, 2 * TILE)] = both.astype(BF16)
        return carry

    lax.fori_loop(0, tok // (2 * TILE), step, 0, unroll=2)


def from_heads(block, src, start, tok, upper):
    heads = src.shape[0]

    def step(group, carry):
        at = pl.multiple_of(group * TILE, TILE)
        parts = []
        for first in range(0, heads, TILE):
            local = jnp.where(upper, heads - TILE - first, first)
            parts.append(turn_tiles([src[local + i, pl.ds(start + at, TILE)] for i in range(TILE)]))
        for j in range(TILE):
            block[at + j] = jnp.concatenate([part[j] for part in parts], axis=0).astype(BF16)
        return carry

    lax.fori_loop(0, tok // TILE, step, 0, unroll=2)


def is_set(place_ref, which):
    return place_ref[which : which + 1] > 0.5


def in_local_order(place_ref, rows):
    half = rows.shape[0] // 2
    lower, upper = rows[:half], rows[half:]
    mine = jnp.broadcast_to(place_ref[LOWER : LOWER + 1, :1], lower.shape) > 0.5
    return jnp.concatenate(
        [jnp.where(mine, lower, upper), jnp.where(mine, upper, lower)], axis=0
    )


def half_states(part, kh, vh, cum, b, out, first=None):
    half = kh.shape[1] // 2

    def one(i):
        h = part * half + i
        row = cum[b, pl.ds(h, 1), :]
        scale = jnp.exp(row[:, BLOCK - 1 :] - row)
        state = dot((kh[b, h].astype(F32).T * scale).astype(BF16), vh[b, h])
        if first is not None:
            state += jnp.exp(row[:, BLOCK - 1 :]) * first[i]
        out[i, :HD] = state

    each_head(half, 4, one)


def add_decays(out, decay, part):
    half = out.shape[0]
    for i in range(half):
        out[i, HD:] = jnp.broadcast_to(decay[part * half + i : part * half + i + 1], (TILE, HD))


def state_kernel(
    place_ref, gain_hbm, ld_hbm, k_hbm, v_hbm, send_ref, first_ref, kh, vh, cum, ld_ref, decay,
    gain_ref, gain_raw, ld_raw, k_raw, v_raw, sems,
):
    heads, tok = ld_ref.shape
    per_block = BLOCK // CHUNK
    copies = [pltpu.make_async_copy(ld_hbm, ld_raw, sems.at[0])]
    for c in range(tok // CHUNK):
        at = pl.ds(c * CHUNK, CHUNK)
        copies.append(pltpu.make_async_copy(k_hbm.at[at], k_raw.at[at], sems.at[2 * c + 1]))
        copies.append(pltpu.make_async_copy(v_hbm.at[at], v_raw.at[at], sems.at[2 * c + 2]))
    copies.append(pltpu.make_async_copy(gain_hbm, gain_raw, sems.at[len(copies)]))
    for copy in copies:
        copy.start()
    upper = is_upper(place_ref)
    copies[0].wait()
    ld_ref[...] = in_local_order(place_ref, ld_raw[...])
    for b in range(2):
        cum[b] = block_cum(ld_ref[:, b * BLOCK : (b + 1) * BLOCK])
    ends = cum[0, :, BLOCK - 1 :] + cum[1, :, BLOCK - 1 :]
    decay[...] = jnp.broadcast_to(jnp.exp(ends), decay.shape)

    for b in range(2):
        for c in range(per_block):
            at = pl.ds((b * per_block + c) * CHUNK, CHUNK)
            here = pl.ds(c * CHUNK, CHUNK)
            which = 2 * (b * per_block + c) + 1
            copies[which].wait()
            to_heads(kh.at[b, :, here], k_raw.at[at], upper)
            copies[which + 1].wait()
            to_heads(vh.at[b, :, here], v_raw.at[at], upper)
        if b == 0:
            half_states(1, kh, vh, cum, 0, first_ref)
        else:
            half_states(1, kh, vh, cum, 1, send_ref, first_ref)
    add_decays(send_ref, decay, 1)
    copies[-1].wait()
    gain_ref[...] = in_local_order(place_ref, gain_raw[...])


def state_to_send(place, gain, log_decay, key_rows, value_rows):
    tok, heads, dim = key_rows.shape
    half = heads // 2
    by_head = in_vmem(2, heads, BLOCK, dim, kind=BF16)
    return pl.pallas_call(
        state_kernel,
        in_specs=[NEAR, FAR, FAR, FAR, FAR],
        out_specs=[NEAR] * 8,
        out_shape=[
            in_vmem(half, dim + TILE, dim), in_vmem(half, dim, dim), by_head, by_head,
            in_vmem(2, heads, BLOCK), in_vmem(heads, tok), in_vmem(heads, dim), in_vmem(heads, dim),
        ],
        scratch_shapes=[
            pltpu.VMEM((heads, dim), F32),
            pltpu.VMEM((heads, tok), F32),
            pltpu.VMEM((tok, heads, dim), BF16),
            pltpu.VMEM((tok, heads, dim), BF16),
            pltpu.SemaphoreType.DMA((2 * (tok // CHUNK) + 2,)),
        ],
        compiler_params=params(8),
        cost_estimate=cost(tok * heads * dim * dim, 8 * tok * heads * dim),
        name="state_to_send",
    )(place, *far(gain, log_decay, key_rows, value_rows))


def own_state_kernel(kh, vh, cum, decay, own_ref, first_ref):
    half_states(0, kh, vh, cum, 0, first_ref)
    half_states(0, kh, vh, cum, 1, own_ref, first_ref)
    add_decays(own_ref, decay, 0)


def own_state(kh, vh, cum, decay):
    _, heads, tok, dim = kh.shape
    half = heads // 2
    return pl.pallas_call(
        own_state_kernel,
        in_specs=[NEAR] * 4,
        out_specs=[NEAR] * 2,
        out_shape=[in_vmem(half, dim + TILE, dim), in_vmem(half, dim, dim)],
        compiler_params=params(4),
        cost_estimate=cost(2 * tok * heads * dim * dim, 4 * tok * heads * dim),
        name="own_state",
    )(*near(kh, vh, cum, decay))


def intra(index, place, cum, kh, vh, first_own, first_send, query_rows, output_grad):
    tok, heads, dim = query_rows.shape

    def kernel(place_ref, cum, kh, vh, first_own, first_send, q_hbm, o_hbm,
               qh, oh, w_ref, decays_ref, columns_ref, inner_ref,
               q_raw, o_raw, sems):
        at = pl.ds(index * BLOCK, BLOCK)
        copy_q = pltpu.make_async_copy(q_hbm.at[at], q_raw, sems.at[0])
        copy_o = pltpu.make_async_copy(o_hbm.at[at], o_raw, sems.at[1])
        copy_q.start()
        copy_o.start()
        upper = is_upper(place_ref)
        copy_q.wait()
        to_heads(qh, q_raw, upper)
        copy_o.wait()
        to_heads(oh, o_raw, upper)

        def one(part, i, h):
            query = qh[h]
            row = cum[index, pl.ds(h, 1), :]
            columns = as_columns(row)
            quarters = decay_quarters(row, columns)
            for at, quarter in enumerate(quarters):
                decays_ref[h, at] = quarter
            weights = causal(dot_rows(query, kh[index, h]), quarters)
            w_ref[h] = weights
            inner = dot(weights, vh[index, h])
            columns = jnp.exp(columns)
            columns_ref[h] = columns
            if index:
                inner += columns * times_state(query, (first_own, first_send)[part][i])
            inner_ref[h] = inner

        each_half(heads // 2, 2, one)

    by_head = in_vmem(heads, BLOCK, dim, kind=BF16)
    return pl.pallas_call(
        kernel,
        in_specs=[NEAR] * 6 + [FAR, FAR],
        out_specs=[NEAR] * 6,
        out_shape=[
            by_head, by_head, in_vmem(heads, BLOCK, BLOCK, kind=BF16),
            in_vmem(heads, 3, BLOCK // 2, BLOCK // 2), in_vmem(heads, BLOCK, dim),
            in_vmem(heads, BLOCK, dim),
        ],
        scratch_shapes=[
            pltpu.VMEM((BLOCK, heads, dim), BF16),
            pltpu.VMEM((BLOCK, heads, dim), BF16),
            pltpu.SemaphoreType.DMA((2,)),
        ],
        compiler_params=params(6),
        cost_estimate=cost(
            2 * heads * BLOCK * BLOCK * dim * 4, 20 * heads * BLOCK * dim, heads * BLOCK * BLOCK
        ),
        name=f"intra_{index}",
    )(place, *near(cum, kh, vh, first_own, first_send), *far(query_rows, output_grad))


def attend_kernel(part, *refs):
    gain_ref, state_ref, q0, q1, o0, o1, columns0, columns1, inner0, inner1 = refs[:10]
    half = state_ref.shape[0]
    if part:
        before, att0, att1, sums_ref, partial = refs[10:]
        partial[...] = before[...]
    else:
        att0, att1, partial = refs[10:]
        partial[...] = jnp.zeros_like(partial)

    def one(i):
        h = part * half + i
        state = state_ref[i]
        gain = gain_ref[pl.ds(h, 1), :]
        blocks = ((q0, o0, columns0, inner0, att0), (q1, o1, columns1, inner1, att1))
        for b, (q, o, columns, inner, att) in enumerate(blocks):
            attended = inner[h] + columns[h] * times_state(q[h], state)
            att[i] = attended
            partial[0, b] += attended * attended
            partial[1, b] += gain * o[h].astype(F32) * attended
            state = columns[h, BLOCK - 1 :] * state

    each_head(half, 4, one)
    if part:
        ones = jnp.ones((8, HD), F32)
        for b in range(2):
            for at in range(2):
                line = lax.dot_general(
                    ones, partial[at, b], (((1,), (1,)), ((), ())),
                    precision=lax.Precision.HIGHEST, preferred_element_type=F32,
                )
                sums_ref[at : at + 1, b * BLOCK : (b + 1) * BLOCK] = line[:1]


def attend(part, gain, state, arrays, before=()):
    heads, dim = gain.shape
    tok = 2 * BLOCK
    half = heads // 2
    by_head = in_vmem(half, BLOCK, dim)
    partial = (2, 2, BLOCK, dim)
    return pl.pallas_call(
        functools.partial(attend_kernel, part),
        in_specs=[NEAR] * (10 + part),
        out_specs=[NEAR] * 3,
        out_shape=[by_head, by_head, in_vmem(2, tok) if part else in_vmem(*partial)],
        scratch_shapes=[pltpu.VMEM(partial, F32)] * part,
        compiler_params=params(6),
        cost_estimate=cost(2 * heads * tok * dim * dim, 8 * heads * tok * dim),
        name=f"attend_{part}",
    )(*near(gain, state, *arrays, *before))


def scaled_queries(cum, q0, q1):
    _, heads, _ = cum.shape

    def kernel(cum_ref, q0, q1, out_ref, ends_ref):
        for b in range(2):
            ends_ref[b] = jnp.broadcast_to(jnp.exp(cum_ref[b, :, BLOCK - 1 :]), (heads, HD))

        def one(h):
            for b, q in enumerate((q0, q1)):
                scale = jnp.exp(cum_ref[b, pl.ds(h, 1), :])
                out_ref[b, h] = (q[h].astype(F32).T * scale).astype(BF16)

        each_head(heads, 2, one)

    return pl.pallas_call(
        kernel,
        in_specs=[NEAR] * 3,
        out_specs=[NEAR] * 2,
        out_shape=[in_vmem(2, heads, HD, BLOCK, kind=BF16), in_vmem(2, heads, HD)],
        compiler_params=params(4),
        cost_estimate=cost(4 * heads * BLOCK * HD, 8 * heads * BLOCK * HD),
        name="scaled_queries",
    )(*near(cum, q0, q1))


def remaining_decay(cum):
    _, heads, _ = cum.shape

    def kernel(cum_ref, out_ref):
        def one(h):
            for b in range(2):
                row = cum_ref[b, pl.ds(h, 1), :]
                out_ref[b, h] = as_columns(jnp.exp(row[:, BLOCK - 1 :] - row))

        each_head(heads, 2, one)

    return pl.pallas_call(
        kernel,
        in_specs=[NEAR],
        out_specs=NEAR,
        out_shape=in_vmem(2, heads, BLOCK, HD),
        compiler_params=params(4),
        cost_estimate=cost(2 * heads * BLOCK * HD, 8 * heads * BLOCK * HD),
        name="remaining_decay",
    )(*near(cum))


def inverse_rms(sums_ref, b):
    at = slice(b * BLOCK, (b + 1) * BLOCK)
    inv = lax.rsqrt(sums_ref[0:1, at] / (HEAD_TOTAL * HD) + 1e-06)
    mean = sums_ref[1:2, at] * inv / (HEAD_TOTAL * HD)
    return inv, mean


def norm_grad(part, ends, gain, sums, scaled, arrays):
    heads, dim = gain.shape
    tok = 2 * BLOCK
    half = heads // 2

    def kernel(ends_ref, gain_ref, sums_ref, queries_ref, o0, o1, att0, att1,
               out_ref, second_ref, g0, g1, scales):
        for b in range(2):
            inv, mean = inverse_rms(sums_ref, b)
            scales[b, 0] = as_columns(inv)
            scales[b, 1] = as_columns(inv * inv * mean)

        def one(i):
            h = part * half + i
            line = gain_ref[pl.ds(h, 1), :]
            starts = []
            for b, (o, att, g) in enumerate(((o0, att0, g0), (o1, att1, g1))):
                grad = line * o[h].astype(F32) * scales[b, 0] - att[i] * scales[b, 1]
                grad = grad.astype(BF16)
                g[i] = grad
                starts.append(dot(queries_ref[b, h], grad))
            second_ref[i] = starts[1]
            out_ref[i] = starts[0] + ends_ref[0, pl.ds(h, 1)] * starts[1]

        each_head(half, 4, one)

    by_head = in_vmem(half, BLOCK, dim, kind=BF16)
    return pl.pallas_call(
        kernel,
        in_specs=[NEAR] * 8,
        out_specs=[NEAR] * 4,
        out_shape=[in_vmem(half, dim, dim), in_vmem(half, dim, dim), by_head, by_head],
        scratch_shapes=[pltpu.VMEM((2, 2, BLOCK, dim), F32)],
        compiler_params=params(4),
        cost_estimate=cost(heads * tok * dim * dim, 7 * heads * tok * dim),
        name=f"norm_grad_{part}",
    )(*near(ends, gain, sums, scaled, *arrays))


def on_block(work):
    for index in range(2):
        pl.when(pl.program_id(0) == index)(lambda index=index: work(index))


def raw_output(heads, tok):
    spec = pl.BlockSpec((BLOCK, heads, HD), lambda i: (i, 0, 0))
    return spec, jax.ShapeDtypeStruct((tok, heads, HD), BF16)


def normed_kernel(place_ref, gain_ref, sums_ref, own0, own1, other0, other1, out_ref, rows):
    upper = is_upper(place_ref)

    def work(b):
        inv = as_columns(inverse_rms(sums_ref, b)[0])
        halves = ((own0, other0), (own1, other1))[b]

        def one(part, i, h):
            rows[h] = halves[part][i] * inv * gain_ref[pl.ds(h, 1), :]

        each_half(own0.shape[0], 4, one)

    on_block(work)
    from_heads(out_ref, rows, 0, BLOCK, upper)


def normed_rows(place, gain, sums, arrays):
    heads, dim = gain.shape
    tok = 2 * BLOCK
    spec, shape = raw_output(heads, tok)
    return pl.pallas_call(
        normed_kernel,
        grid=(2,),
        in_specs=[NEAR] * 7,
        out_specs=spec,
        out_shape=shape,
        scratch_shapes=[pltpu.VMEM((heads, BLOCK, dim), F32)],
        compiler_params=params(7),
        cost_estimate=cost(3 * heads * tok * dim, 6 * heads * tok * dim),
        name="normed_rows",
    )(place, *near(gain, sums, *arrays))


def grad_q_kernel(
    ends_ref, keep_ref, recv_ref, first_own, first_send, kh, vh, own0, own1, other0, other1,
    decays0, decays1, columns0, columns1, rows, gs_ref,
):
    blocks = (((own0, other0), decays0, columns0), ((own1, other1), decays1, columns1))
    for b, (g, decays, columns) in enumerate(blocks):

        def one(part, i, h, b=b, g=g, decays=decays, columns=columns):
            grad = g[part][i]
            scores = causal(dot_rows(grad, vh[b, h]), [decays[h, at] for at in range(3)])
            gs_ref[b, h] = scores
            state = (keep_ref, recv_ref)[part][i]
            if b:
                state = ends_ref[0, pl.ds(h, 1)] * state + (first_own, first_send)[part][i]
            rows[b, h] = dot(scores, kh[b, h]) + columns[h] * times_state_t(grad, state)

        each_half(keep_ref.shape[0], 4, one)


def grad_query(ends, arrays):
    _, heads, dim = ends.shape
    tok = 2 * BLOCK
    return pl.pallas_call(
        grad_q_kernel,
        in_specs=[NEAR] * 15,
        out_specs=[NEAR, NEAR],
        out_shape=[
            in_vmem(2, heads, BLOCK, dim), in_vmem(2, heads, BLOCK, BLOCK, kind=BF16),
        ],
        compiler_params=params(4),
        cost_estimate=cost(
            4 * heads * tok * dim * (BLOCK + dim), 12 * heads * tok * dim, heads * tok * BLOCK
        ),
        name="grad_query",
    )(*near(ends, *arrays))


def grad_kv_kernel(
    place_ref, gs_ref, w0, w1, q0, q1, kh, vh, own0, own1, other0, other1, remaining_ref,
    second_own, second_send, rows, dk, dv, out_q, raw, sems,
):
    upper = is_upper(place_ref)
    copies = []
    for b in range(2):
        for start in range(0, BLOCK, CHUNK):
            at = pl.ds(b * BLOCK + start, CHUNK)
            from_heads(raw.at[at], rows.at[b], start, CHUNK, upper)
            copies.append(pltpu.make_async_copy(raw.at[at], out_q.at[at], sems.at[len(copies)]))
            copies[-1].start()

    def one(part, i, h):
        columns = remaining_ref[0, h]
        state = (second_own, second_send)[part][i]
        g0, g1 = ((own0, own1), (other0, other1))[part]
        dk[0, h] = transposed_dot(gs_ref[0, h], q0[h]) + columns * times_state_t(vh[0, h], state)
        dv[0, h] = transposed_dot(w0[h], g0[i]) + columns * times_state(kh[0, h], state)
        dk[1, h] = transposed_dot(gs_ref[1, h], q1[h])
        dv[1, h] = transposed_dot(w1[h], g1[i])

    each_half(second_own.shape[0], 2, one)
    for copy in copies:
        copy.wait()


def grad_key_value(*arrays):
    _, heads, _, dim = arrays[6].shape
    tok = 2 * BLOCK
    return pl.pallas_call(
        grad_kv_kernel,
        in_specs=[NEAR] * 16,
        out_specs=[NEAR, NEAR, FAR],
        out_shape=[in_vmem(2, heads, BLOCK, dim)] * 2
        + [jax.ShapeDtypeStruct((tok, heads, dim), BF16)],
        scratch_shapes=[
            pltpu.VMEM((tok, heads, dim), BF16),
            pltpu.SemaphoreType.DMA((tok // CHUNK,)),
        ],
        compiler_params=params(6),
        cost_estimate=cost(4 * heads * tok * dim * (BLOCK + dim), 30 * heads * tok * dim),
        name="grad_key_value",
    )(*near(*arrays))


def finish_rows(part, b, ends_ref, state_ref, kh, vh, remaining_ref, dk, dv, rows_k, rows_v):
    half = state_ref.shape[0]

    def one(i):
        h = part * half + i
        columns = remaining_ref[b, h]
        state = state_ref[i]
        if b == 0:
            state = ends_ref[1, pl.ds(h, 1)] * state
        state = state.astype(BF16)
        none = jnp.zeros_like(state)
        both = jnp.concatenate(
            [jnp.concatenate([state.T, none], axis=1), jnp.concatenate([none, state], axis=1)],
            axis=0,
        )
        carried = dot(jnp.concatenate([vh[b, h], kh[b, h]], axis=1), both)
        rows_k[b, h] = dk[b, h] + columns * carried[:, :HD]
        rows_v[b, h] = dv[b, h] + columns * carried[:, HD:]

    each_head(half, 4, one)


def finish_own_kernel(*refs):
    for b in range(2):
        finish_rows(0, b, *refs)


def finish_other_kernel(
    place_ref, old_k, old_v, ends_ref, state_ref, kh, vh, remaining_ref, dk, dv,
    out_k, out_v, rows_k, rows_v, raw_k, raw_v, sems,
):
    upper = is_upper(place_ref)
    copies = []
    for b in range(2):
        finish_rows(1, b, ends_ref, state_ref, kh, vh, remaining_ref, dk, dv, rows_k, rows_v)
        for start in range(0, BLOCK, CHUNK):
            at = pl.ds(b * BLOCK + start, CHUNK)
            for rows, raw, out in ((rows_k, raw_k, out_k), (rows_v, raw_v, out_v)):
                from_heads(raw.at[at], rows.at[b], start, CHUNK, upper)
                copies.append(pltpu.make_async_copy(raw.at[at], out.at[at], sems.at[len(copies)]))
                copies[-1].start()
    for copy in copies:
        copy.wait()


def finish_own(ends, keep, arrays):
    _, heads, dim = ends.shape
    tok = 2 * BLOCK
    return pl.pallas_call(
        finish_own_kernel,
        in_specs=[NEAR] * 7,
        out_specs=[NEAR, NEAR],
        out_shape=[in_vmem(2, heads, BLOCK, dim)] * 2,
        compiler_params=params(4),
        cost_estimate=cost(4 * heads * tok * dim * dim, 8 * heads * tok * dim),
        name="finish_own",
    )(*near(ends, keep, *arrays))


def finish_other(place, rows, ends, recv, arrays):
    _, heads, dim = ends.shape
    tok = 2 * BLOCK
    shape = jax.ShapeDtypeStruct((tok, heads, dim), BF16)
    return pl.pallas_call(
        finish_other_kernel,
        in_specs=[NEAR] * 10,
        out_specs=[FAR, FAR, NEAR, NEAR],
        out_shape=[shape, shape] + [in_vmem(2, heads, BLOCK, dim)] * 2,
        input_output_aliases={1: 2, 2: 3},
        scratch_shapes=[
            pltpu.VMEM((tok, heads, dim), BF16),
            pltpu.VMEM((tok, heads, dim), BF16),
            pltpu.SemaphoreType.DMA((2 * (tok // CHUNK),)),
        ],
        compiler_params=params(8),
        cost_estimate=cost(4 * heads * tok * dim * dim, 8 * heads * tok * dim),
        name="finish_other",
    )(*near(place, *rows, ends, recv, *arrays))[:2]


def follows(value, earlier):
    return lax.optimization_barrier((value, earlier))[0]


def swap(value, axis, bit):
    count = lax.axis_size(axis)
    return lax.ppermute(value, axis, [(i, i ^ bit) for i in range(count)])


def mix(body, backward, place, arrays, shapes, name):
    def kernel(place_ref, *refs):
        bits = [is_set(place_ref, which) != backward for which in (LATE, RIGHT, LOW)]
        body(bits, refs[: len(arrays)], refs[len(arrays) :])

    return pl.pallas_call(
        kernel,
        in_specs=[NEAR] + [NEAR] * len(arrays),
        out_specs=[NEAR] * len(shapes),
        out_shape=[in_vmem(*shape) for shape in shapes],
        compiler_params=params(4),
        cost_estimate=cost(4 * 8 * HD * HD, 16 * 8 * HD * HD),
        name=name,
    )(place, *near(*arrays))


OWN, PARTNER, CHIP, ROW, CORNER = range(5)


def mix_total(bits, own, got, d_own, d_got, first, second):
    late = bits[0]
    quarter = first.shape[0]
    for h in range(2 * quarter):
        total = jnp.where(late, 1.0, d_got(h)) * own[h, :HD] + jnp.where(late, d_own(h), 1.0) * got[h, :HD]
        if h < quarter:
            first[h, :HD] = total
        else:
            second[h - quarter] = total


def mix_total_first(bits, arrays, outputs):
    own, got = arrays
    first, second, chip = outputs
    quarter = first.shape[0]
    d_own = lambda h: own[h, HD : HD + 1]
    d_got = lambda h: got[h, HD : HD + 1]
    mix_total(bits, own, got, d_own, d_got, first, second)
    for h in range(2 * quarter):
        whole = d_own(h) * d_got(h)
        chip[h : h + 1] = whole
        place = HD + (TILE // 2) * (h // quarter)
        first[h % quarter, place : place + TILE // 2] = jnp.broadcast_to(whole, (TILE // 2, HD))


def mix_total_again(bits, arrays, outputs):
    table, own, got = arrays
    decay = lambda which: lambda h: table[which, h : h + 1]
    mix_total(bits, own, got, decay(OWN), decay(PARTNER), *outputs)


def mix_next(bits, decay, totals, gots, outputs):
    _, right, low = bits
    quarter = totals[1].shape[0]
    for i in range(quarter):
        h = i
        scale_total = jnp.where(right, 1.0, decay(ROW, h))
        scale_got = jnp.where(right, decay(CHIP, h), 1.0)
        outputs[0][i] = scale_total * totals[0][i, :HD] + scale_got * gots[0][i, :HD]
        h = quarter + i
        scale_total = jnp.where(low & right, 0.0, 1.0)
        corner = jnp.where(right, 1.0, decay(CHIP, h) * decay(CORNER, h))
        scale_got = jnp.where(low, corner, 0.0)
        outputs[1][i] = scale_total * totals[1][i] + scale_got * gots[1][i]


def mix_next_first(bits, arrays, outputs):
    own, got, chip, corner, first, second, one_a, one_b = arrays
    table = outputs[2]
    quarter = second.shape[0]
    for h in range(2 * quarter):
        place = HD + (TILE // 2) * (h // quarter)
        table[OWN, h : h + 1] = own[h, HD : HD + 1]
        table[PARTNER, h : h + 1] = got[h, HD : HD + 1]
        table[ROW, h : h + 1] = one_a[h % quarter, place : place + 1]
    table[CHIP] = chip[...]
    table[CORNER] = corner[...]
    decay = lambda which, h: table[which, h : h + 1]
    mix_next(bits, decay, (first, second), (one_a, one_b), outputs[:2])


def mix_next_again(bits, arrays, outputs):
    table, first, second, one_a, one_b = arrays
    decay = lambda which, h: table[which, h : h + 1]
    mix_next(bits, decay, (first, second), (one_a, one_b), outputs)


def mix_enter(bits, arrays, outputs):
    table, own, got, one_a, one_b, two_a, two_b = arrays
    kept, sent = outputs
    late, right, low = bits
    quarter = one_b.shape[0]
    decay = lambda which, h: table[which, h : h + 1]
    for h in range(2 * quarter):
        i = h % quarter
        row = jnp.where(right, decay(ROW, h), 1.0)
        if h < quarter:
            one, two = one_a[i, :HD], two_a[i]
            scale_one = jnp.where(right, 1.0, 0.0)
            scale_two = jnp.where(low, row, 0.0)
        else:
            one, two = one_b[i], two_b[i]
            scale_one = jnp.where(low, jnp.where(right, row, decay(CORNER, h)), 0.0)
            scale_two = jnp.where(low | right, 1.0, 0.0)
        enter = scale_one * one + scale_two * two
        after = jnp.where(late, decay(PARTNER, h), decay(OWN, h)) * enter
        after += jnp.where(late, got[h, :HD], own[h, :HD])
        kept[h] = jnp.where(late, after, enter)
        sent[h] = jnp.where(late, enter, after)


def entering_quad(send, own_task, table, place, backward, tasks):
    def work(stage, after, before=()):
        if stage not in tasks:
            return before
        run, outputs = tasks[stage]
        outputs.extend(run(after))
        return lax.optimization_barrier((before, outputs[-1]))[0]

    name = "later" if backward else "earlier"
    half = send.shape[0]
    quarter = half // 2
    states, wide = (quarter, HD, HD), (quarter, HD + TILE, HD)
    got = swap(send, "seq", 1)
    own = own_task(send)
    if table is None:
        first, second, chip = mix(
            mix_total_first, backward, place, (own, got), (wide, states, (half, HD)), name + "_total"
        )
    else:
        first, second = mix(
            mix_total_again, backward, place, (table, own, got), (states, states), name + "_total"
        )
    one_a, one_b = swap(first, "seq", 2), swap(second, "seq", 4)
    if table is None:
        corner = swap(chip, "seq", 6)
        one_a, one_b, corner = work(1, second, (one_a, one_b, corner))
        next_a, next_b, table = mix(
            mix_next_first, backward, place, (own, got, chip, corner, first, second, one_a, one_b),
            (states, states, (5, half, HD)), name + "_next",
        )
    else:
        one_a, one_b = work(1, second, (one_a, one_b))
        next_a, next_b = mix(
            mix_next_again, backward, place, (table, first, second, one_a, one_b), (states, states),
            name + "_next",
        )
    two_a, two_b = swap(next_a, "seq", 4), swap(next_b, "seq", 2)
    two_a, two_b = work(2, next_b, (two_a, two_b))
    kept, sent = mix(
        mix_enter, backward, place, (table, own, got, one_a, one_b, two_a, two_b),
        ((half, HD, HD), (half, HD, HD)), name + "_enter",
    )
    received = swap(sent, "seq", 1)
    received = follows(received, tasks[3](follows(kept, sent)))
    return kept, received, table


def entering_any(send, own_task, log_total, backward, tasks):
    own = own_task(send)
    for stage in (1, 2):
        run, outputs = tasks[stage]
        outputs.extend(run(send))
    count, mine = lax.axis_size("seq"), lax.axis_index("seq")
    core = mine % 2
    own, send = own[:, :HD], send[:, :HD]
    half = own.shape[0]
    in_order = jnp.where(
        core == 0, jnp.concatenate([own, send], axis=0), jnp.concatenate([send, own], axis=0)
    )
    states = lax.all_gather(in_order, "seq")
    decays = jnp.exp(lax.all_gather(log_total, "seq"))
    place = mine
    if backward:
        states, decays, place = states[::-1], decays[::-1], count - 1 - mine

    def step(at, total):
        longer = decays[at][:, None, None] * total + states[at]
        return jnp.where(at < place, longer, total)

    total = lax.fori_loop(0, count - 1, step, jnp.zeros_like(in_order))
    kept = lax.dynamic_slice_in_dim(total, core * half, half)
    tasks[3](kept)
    return kept, lax.dynamic_slice_in_dim(total, (1 - core) * half, half)


def add(first, second):
    def kernel(first_ref, second_ref, out_ref):
        out_ref[...] = first_ref[...] + second_ref[...]

    return pl.pallas_call(
        kernel,
        in_specs=[NEAR, NEAR],
        out_specs=NEAR,
        out_shape=in_vmem(*first.shape),
        compiler_params=params(2),
        name="add",
    )(*near(first, second))


def sum_over_heads(value, tasks):
    tasks = list(tasks)
    results = []
    count = lax.axis_size("head")
    reach = 1
    while 2 * reach <= count and count % (2 * reach) == 0:
        got = swap(value, "head", reach)
        if tasks:
            results.append(tasks.pop(0)(value))
            got = follows(got, results[-1])
        value = add(value, got)
        reach *= 2
    results += [task(value) for task in tasks]
    part = value
    for shift in range(1, count // reach):
        value = add(
            value,
            lax.ppermute(part, "head", [(i, (i + shift * reach) % count) for i in range(count)]),
        )
    return value, results


def on_device(query_rows, key_rows, value_rows, output_grad, norm_gain, log_decay):
    mine = lax.axis_index("seq")
    bits = [(mine >> at) % 2 for at in range(3)]
    marks = [1 - bits[0], bits[0], *bits] + [jnp.zeros_like(mine)] * (TILE - 5)
    place = jnp.broadcast_to(jnp.stack(marks).astype(F32)[:, None], (TILE, HD))
    table = [None]

    def entering(send, own_task, backward, tasks):
        if lax.axis_size("seq") != 8:
            log_total = jnp.sum(log_decay, axis=1)
            return entering_any(send, own_task, log_total, backward, tasks)
        kept, received, table[0] = entering_quad(
            send, own_task, table[0], place, backward, tasks
        )
        return kept, received

    send, first_send, kh, vh, cum, _, decay, gain = state_to_send(
        place, norm_gain, log_decay, key_rows, value_rows
    )
    firsts, in_0, in_1, begun = [], [], [], []

    def own_task(earlier):
        own, first = own_state(follows(kh, earlier), vh, cum, decay)
        firsts.extend((first, first_send))
        return own

    def forward_task(index):
        return lambda earlier: intra(
            index, place, follows(cum, earlier), kh, vh, *firsts, query_rows, output_grad
        )

    def parts():
        q0, o0, _, _, columns0, inner0 = in_0
        q1, o1, _, _, columns1, inner1 = in_1
        return q0, q1, o0, o1, columns0, columns1, inner0, inner1

    def attend_task(kept):
        begun.extend(attend(0, gain, kept, parts()))
        return begun[-1]

    keep, recv = entering(
        send, own_task, False, {1: (forward_task(0), in_0), 2: (forward_task(1), in_1), 3: attend_task}
    )
    q0, o0, w0, decays0, columns0, _ = in_0
    q1, o1, w1, decays1, columns1, _ = in_1
    own_att = begun[:2]
    *other_att, sums = attend(1, gain, recv, parts(), begun[2:])
    sums, ((scaled, ends), remaining) = sum_over_heads(
        sums,
        (
            lambda earlier: scaled_queries(cum, follows(q0, earlier), q1),
            lambda earlier: remaining_decay(follows(cum, earlier)),
        ),
    )
    grad_send, second_send, *other_g = norm_grad(1, ends, gain, sums, scaled, (o0, o1, *other_att))
    own_g, seconds, queries, pairs, norms, rows = [], [], [], [], [], []

    def own_grad_task(earlier):
        own, second, *grads = norm_grad(
            0, ends, gain, follows(sums, earlier), scaled, (o0, o1, *own_att)
        )
        own_g.extend(grads)
        seconds.extend((second, second_send))
        return own

    def query_task(earlier):
        made = grad_query(
            follows(ends, earlier),
            (keep, recv, *firsts, kh, vh, *own_g, *other_g, decays0, decays1, columns0, columns1),
        )
        norms.append(
            normed_rows(place, gain, follows(sums, made[-1]), (*own_att, *other_att))
        )
        return *made, norms[0]

    def pair_task(earlier):
        return grad_key_value(
            place, queries[1], w0, w1, q0, q1, kh, vh, *own_g, *other_g, remaining,
            follows(seconds[0], earlier), seconds[1], queries[0],
        )

    def finish_task(kept):
        rows.extend(finish_own(ends, kept, (kh, vh, remaining, *pairs[:2])))
        return rows[-1]

    _, grad_recv = entering(
        grad_send, own_grad_task, True,
        {1: (query_task, queries), 2: (pair_task, pairs), 3: finish_task},
    )
    grad_k, grad_v = finish_other(
        place, rows, ends, grad_recv, (kh, vh, remaining, *pairs[:2])
    )
    return norms[0], pairs[2], grad_k, grad_v


def solution(mesh):
    rows = P("seq", "head", None)
    return jax.shard_map(
        on_device,
        mesh=mesh,
        in_specs=(rows, rows, rows, rows, P("head", None), P("head", "seq")),
        out_specs=(rows, rows, rows, rows),
        check_vma=False,
    )
```

```python
import functools

import jax
import jax.numpy as jnp
from jax import lax
from jax.experimental import pallas as pl
from jax.experimental.pallas import tpu as pltpu
from jax.sharding import PartitionSpec as P

HEAD_TOTAL = 64
HD = 128
BLOCK = 256
CHUNK = 128
TILE = 8
F32 = jnp.float32
BF16 = jnp.bfloat16
MIB = 1024 * 1024
NEAR = pl.BlockSpec(memory_space=pltpu.VMEM)
FAR = pl.BlockSpec(memory_space=pl.ANY)
LOWER, UPPER, LATE, RIGHT, LOW = range(5)


def in_vmem(*shape, kind=F32):
    return pltpu.VMEM(shape, kind)


def near(*arrays):
    return [pltpu.with_memory_space_constraint(array, pltpu.VMEM) for array in arrays]


def far(*arrays):
    return [pltpu.with_memory_space_constraint(array, pltpu.HBM) for array in arrays]


def params(mib):
    return pltpu.CompilerParams(vmem_limit_bytes=mib * MIB)


def cost(flops, moved, exps=0):
    return pl.CostEstimate(flops=flops, bytes_accessed=moved, transcendentals=exps)


def block_cum(log_decay):
    size = log_decay.shape[1]
    upper = lax.broadcasted_iota(jnp.int32, (size, size), 0) <= lax.broadcasted_iota(
        jnp.int32, (size, size), 1
    )
    return jnp.dot(
        log_decay,
        jnp.where(upper, 1.0, 0.0).astype(F32),
        precision=lax.Precision.HIGHEST,
        preferred_element_type=F32,
    )


def as_columns(row):
    return jnp.broadcast_to(row, (HD, row.shape[1])).T


def dot(a, b):
    return jnp.dot(a, b, preferred_element_type=F32)


def dot_rows(a, b):
    return lax.dot_general(a, b, (((1,), (1,)), ((), ())), preferred_element_type=F32)


def two_parts(matrix):
    high = matrix.astype(BF16)
    return high, (matrix - high.astype(F32)).astype(BF16)


def times_state(rows, state):
    return dot(jnp.concatenate([rows, rows], axis=1), jnp.concatenate(two_parts(state), axis=0))


def times_state_t(rows, state):
    return dot_rows(
        jnp.concatenate([rows, rows], axis=1), jnp.concatenate(two_parts(state), axis=1)
    )


def decay_quarters(row, columns):
    half = row.shape[1] // 2
    lower = lax.broadcasted_iota(jnp.int32, (half, half), 0) >= lax.broadcasted_iota(
        jnp.int32, (half, half), 1
    )
    quarters = []
    for t, s in ((0, 0), (1, 0), (1, 1)):
        gap = columns[t * half : (t + 1) * half] - row[:, s * half : (s + 1) * half]
        quarters.append(jnp.exp(jnp.where(lower, gap, -jnp.inf) if t == s else gap))
    return quarters


def causal(table, quarters):
    half = table.shape[0] // 2
    first, second, third = (
        (table[t * half : (t + 1) * half, s * half : (s + 1) * half] * quarter).astype(BF16)
        for (t, s), quarter in zip(((0, 0), (1, 0), (1, 1)), quarters)
    )
    top = jnp.concatenate([first, jnp.zeros_like(first)], axis=1)
    return jnp.concatenate([top, jnp.concatenate([second, third], axis=1)], axis=0)


def transposed_dot(a, b):
    return lax.dot_general(a, b, (((0,), (0,)), ((), ())), preferred_element_type=F32)


def each_head(heads, unroll, body):
    def step(h, carry):
        body(h)
        return carry

    lax.fori_loop(0, heads, step, 0, unroll=unroll)


def each_half(half, unroll, body):
    for part in range(2):
        each_head(half, unroll, lambda i, part=part: body(part, i, part * half + i))


def turn_tiles(tiles):
    count = len(tiles)
    at = lax.broadcasted_iota(jnp.int32, tiles[0].shape, 0)
    turned = [tile if i == 0 else pltpu.roll(tile, i, 0) for i, tile in enumerate(tiles)]
    reach = 1
    while reach < count:
        odd = (at & reach) != 0
        turned = [
            jnp.where(odd, turned[(n + reach) % count], turned[n]) for n in range(count)
        ]
        reach *= 2
    picked = [turned[-j % count] for j in range(count)]
    return [tile if j == 0 else pltpu.roll(tile, count - j, 0) for j, tile in enumerate(picked)]


def is_upper(place_ref):
    return jnp.max(place_ref[UPPER : UPPER + 1]) > 0.5


def to_heads(dst, block, upper):
    tok, heads, _ = block.shape

    def step(group, carry):
        at = pl.multiple_of(group * 2 * TILE, 2 * TILE)
        tokens = block[pl.ds(at, 2 * TILE)].astype(F32)
        for first in range(0, heads, TILE):
            halves = [
                turn_tiles([tokens[base + i, first : first + TILE] for i in range(TILE)])
                for base in (0, TILE)
            ]
            local = jnp.where(upper, heads - TILE - first, first)
            for j in range(TILE):
                both = jnp.concatenate([halves[0][j], halves[1][j]], axis=0)
                dst[local + j, pl.ds(at, 2 * TILE)] = both.astype(BF16)
        return carry

    lax.fori_loop(0, tok // (2 * TILE), step, 0, unroll=2)


def from_heads(block, src, start, tok, upper):
    heads = src.shape[0]

    def step(group, carry):
        at = pl.multiple_of(group * TILE, TILE)
        parts = []
        for first in range(0, heads, TILE):
            local = jnp.where(upper, heads - TILE - first, first)
            parts.append(turn_tiles([src[local + i, pl.ds(start + at, TILE)] for i in range(TILE)]))
        for j in range(TILE):
            block[at + j] = jnp.concatenate([part[j] for part in parts], axis=0).astype(BF16)
        return carry

    lax.fori_loop(0, tok // TILE, step, 0, unroll=2)


def is_set(place_ref, which):
    return place_ref[which : which + 1] > 0.5


def in_local_order(place_ref, rows):
    half = rows.shape[0] // 2
    lower, upper = rows[:half], rows[half:]
    mine = jnp.broadcast_to(place_ref[LOWER : LOWER + 1, :1], lower.shape) > 0.5
    return jnp.concatenate(
        [jnp.where(mine, lower, upper), jnp.where(mine, upper, lower)], axis=0
    )


def half_states(part, kh, vh, cum, b, out, first=None):
    half = kh.shape[1] // 2

    def one(i):
        h = part * half + i
        row = cum[b, pl.ds(h, 1), :]
        scale = jnp.exp(row[:, BLOCK - 1 :] - row)
        state = dot((kh[b, h].astype(F32).T * scale).astype(BF16), vh[b, h])
        if first is not None:
            state += jnp.exp(row[:, BLOCK - 1 :]) * first[i]
        out[i, :HD] = state

    each_head(half, 4, one)


def add_decays(out, decay, part):
    half = out.shape[0]
    for i in range(half):
        out[i, HD:] = jnp.broadcast_to(decay[part * half + i : part * half + i + 1], (TILE, HD))


def state_kernel(
    place_ref, gain_hbm, ld_hbm, k_hbm, v_hbm, send_ref, first_ref, kh, vh, cum, ld_ref, decay,
    gain_ref, gain_raw, ld_raw, k_raw, v_raw, sems,
):
    heads, tok = ld_ref.shape
    per_block = BLOCK // CHUNK
    copies = [pltpu.make_async_copy(ld_hbm, ld_raw, sems.at[0])]
    for c in range(tok // CHUNK):
        at = pl.ds(c * CHUNK, CHUNK)
        copies.append(pltpu.make_async_copy(k_hbm.at[at], k_raw.at[at], sems.at[2 * c + 1]))
        copies.append(pltpu.make_async_copy(v_hbm.at[at], v_raw.at[at], sems.at[2 * c + 2]))
    copies.append(pltpu.make_async_copy(gain_hbm, gain_raw, sems.at[len(copies)]))
    for copy in copies:
        copy.start()
    upper = is_upper(place_ref)
    copies[0].wait()
    ld_ref[...] = in_local_order(place_ref, ld_raw[...])
    for b in range(2):
        cum[b] = block_cum(ld_ref[:, b * BLOCK : (b + 1) * BLOCK])
    ends = cum[0, :, BLOCK - 1 :] + cum[1, :, BLOCK - 1 :]
    decay[...] = jnp.broadcast_to(jnp.exp(ends), decay.shape)

    for b in range(2):
        for c in range(per_block):
            at = pl.ds((b * per_block + c) * CHUNK, CHUNK)
            here = pl.ds(c * CHUNK, CHUNK)
            which = 2 * (b * per_block + c) + 1
            copies[which].wait()
            to_heads(kh.at[b, :, here], k_raw.at[at], upper)
            copies[which + 1].wait()
            to_heads(vh.at[b, :, here], v_raw.at[at], upper)
        if b == 0:
            half_states(1, kh, vh, cum, 0, first_ref)
        else:
            half_states(1, kh, vh, cum, 1, send_ref, first_ref)
    add_decays(send_ref, decay, 1)
    copies[-1].wait()
    gain_ref[...] = in_local_order(place_ref, gain_raw[...])


def state_to_send(place, gain, log_decay, key_rows, value_rows):
    tok, heads, dim = key_rows.shape
    half = heads // 2
    by_head = in_vmem(2, heads, BLOCK, dim, kind=BF16)
    return pl.pallas_call(
        state_kernel,
        in_specs=[NEAR, FAR, FAR, FAR, FAR],
        out_specs=[NEAR] * 8,
        out_shape=[
            in_vmem(half, dim + TILE, dim), in_vmem(half, dim, dim), by_head, by_head,
            in_vmem(2, heads, BLOCK), in_vmem(heads, tok), in_vmem(heads, dim), in_vmem(heads, dim),
        ],
        scratch_shapes=[
            pltpu.VMEM((heads, dim), F32),
            pltpu.VMEM((heads, tok), F32),
            pltpu.VMEM((tok, heads, dim), BF16),
            pltpu.VMEM((tok, heads, dim), BF16),
            pltpu.SemaphoreType.DMA((2 * (tok // CHUNK) + 2,)),
        ],
        compiler_params=params(8),
        cost_estimate=cost(tok * heads * dim * dim, 8 * tok * heads * dim),
        name="state_to_send",
    )(place, *far(gain, log_decay, key_rows, value_rows))


def fetch_block(index, arrays, blocks, sems):
    copies = [
        pltpu.make_async_copy(array.at[pl.ds(index * BLOCK, BLOCK)], block, sems.at[at])
        for at, (array, block) in enumerate(zip(arrays, blocks))
    ]
    for copy in copies:
        copy.start()
    return copies


def own_state_kernel(
    kh, vh, cum, decay, q_hbm, o_hbm, own_ref, first_ref, q_raw, o_raw, sems
):
    copies = fetch_block(0, (q_hbm, o_hbm), (q_raw, o_raw), sems)
    half_states(0, kh, vh, cum, 0, first_ref)
    half_states(0, kh, vh, cum, 1, own_ref, first_ref)
    add_decays(own_ref, decay, 0)
    for copy in copies:
        copy.wait()


def own_state(kh, vh, cum, decay, query_rows, output_grad):
    _, heads, tok, dim = kh.shape
    half = heads // 2
    raw = in_vmem(BLOCK, heads, dim, kind=BF16)
    return pl.pallas_call(
        own_state_kernel,
        in_specs=[NEAR] * 4 + [FAR, FAR],
        out_specs=[NEAR] * 4,
        out_shape=[in_vmem(half, dim + TILE, dim), in_vmem(half, dim, dim), raw, raw],
        scratch_shapes=[pltpu.SemaphoreType.DMA((2,))],
        compiler_params=params(4),
        cost_estimate=cost(2 * tok * heads * dim * dim, 4 * tok * heads * dim),
        name="own_state",
    )(*near(kh, vh, cum, decay), *far(query_rows, output_grad))


def intra(index, place, cum, kh, vh, first_own, first_send, raw, query_rows, output_grad):
    tok, heads, dim = query_rows.shape
    ahead = index == 0

    def kernel(place_ref, cum, kh, vh, first_own, first_send, q_raw, o_raw, *refs):
        if ahead:
            q_hbm, o_hbm, *refs = refs
            *refs, q_next, o_next, sems = refs
            copies = fetch_block(1, (q_hbm, o_hbm), (q_next, o_next), sems)
        qh, oh, w_ref, decays_ref, columns_ref, inner_ref = refs
        upper = is_upper(place_ref)
        to_heads(qh, q_raw, upper)
        to_heads(oh, o_raw, upper)

        def one(part, i, h):
            query = qh[h]
            row = cum[index, pl.ds(h, 1), :]
            columns = as_columns(row)
            quarters = decay_quarters(row, columns)
            for at, quarter in enumerate(quarters):
                decays_ref[h, at] = quarter
            weights = causal(dot_rows(query, kh[index, h]), quarters)
            w_ref[h] = weights
            inner = dot(weights, vh[index, h])
            columns = jnp.exp(columns)
            columns_ref[h] = columns
            if index:
                inner += columns * times_state(query, (first_own, first_send)[part][i])
            inner_ref[h] = inner

        each_half(heads // 2, 4, one)
        if ahead:
            for copy in copies:
                copy.wait()

    by_head = in_vmem(heads, BLOCK, dim, kind=BF16)
    return pl.pallas_call(
        kernel,
        in_specs=[NEAR] * 8 + [FAR, FAR] * ahead,
        out_specs=[NEAR] * (6 + 2 * ahead),
        out_shape=[
            by_head, by_head, in_vmem(heads, BLOCK, BLOCK, kind=BF16),
            in_vmem(heads, 3, BLOCK // 2, BLOCK // 2), in_vmem(heads, BLOCK, dim),
            in_vmem(heads, BLOCK, dim),
        ]
        + [in_vmem(BLOCK, heads, dim, kind=BF16)] * (2 * ahead),
        scratch_shapes=[pltpu.SemaphoreType.DMA((2,))] * ahead,
        compiler_params=params(4),
        cost_estimate=cost(
            2 * heads * BLOCK * BLOCK * dim * 4, 20 * heads * BLOCK * dim, heads * BLOCK * BLOCK
        ),
        name=f"intra_{index}",
    )(
        *near(place, cum, kh, vh, first_own, first_send, *raw),
        *(far(query_rows, output_grad) if ahead else ()),
    )


def attend_kernel(part, *refs):
    gain_ref, state_ref, q0, q1, o0, o1, columns0, columns1, inner0, inner1 = refs[:10]
    half = state_ref.shape[0]
    if part:
        before, att0, att1, sums_ref, partial = refs[10:]
        partial[...] = before[...]
    else:
        att0, att1, partial = refs[10:]
        partial[...] = jnp.zeros_like(partial)

    def one(i):
        h = part * half + i
        state = state_ref[i]
        gain = gain_ref[pl.ds(h, 1), :]
        blocks = ((q0, o0, columns0, inner0, att0), (q1, o1, columns1, inner1, att1))
        for b, (q, o, columns, inner, att) in enumerate(blocks):
            attended = inner[h] + columns[h] * times_state(q[h], state)
            att[i] = attended
            partial[0, b] += attended * attended
            partial[1, b] += gain * o[h].astype(F32) * attended
            state = columns[h, BLOCK - 1 :] * state

    each_head(half, 4, one)
    if part:
        ones = jnp.ones((8, HD), F32)
        for b in range(2):
            for at in range(2):
                line = lax.dot_general(
                    ones, partial[at, b], (((1,), (1,)), ((), ())),
                    precision=lax.Precision.HIGHEST, preferred_element_type=F32,
                )
                sums_ref[at : at + 1, b * BLOCK : (b + 1) * BLOCK] = line[:1]


def attend(part, gain, state, arrays, before=()):
    heads, dim = gain.shape
    tok = 2 * BLOCK
    half = heads // 2
    by_head = in_vmem(half, BLOCK, dim)
    partial = (2, 2, BLOCK, dim)
    return pl.pallas_call(
        functools.partial(attend_kernel, part),
        in_specs=[NEAR] * (10 + part),
        out_specs=[NEAR] * 3,
        out_shape=[by_head, by_head, in_vmem(2, tok) if part else in_vmem(*partial)],
        scratch_shapes=[pltpu.VMEM(partial, F32)] * part,
        compiler_params=params(6),
        cost_estimate=cost(2 * heads * tok * dim * dim, 8 * heads * tok * dim),
        name=f"attend_{part}",
    )(*near(gain, state, *arrays, *before))


def scaled_queries(cum, q0, q1):
    _, heads, _ = cum.shape

    def kernel(cum_ref, q0, q1, out_ref, ends_ref):
        for b in range(2):
            ends_ref[b] = jnp.broadcast_to(jnp.exp(cum_ref[b, :, BLOCK - 1 :]), (heads, HD))

        def one(h):
            for b, q in enumerate((q0, q1)):
                scale = jnp.exp(cum_ref[b, pl.ds(h, 1), :])
                out_ref[b, h] = (q[h].astype(F32).T * scale).astype(BF16)

        each_head(heads, 4, one)

    return pl.pallas_call(
        kernel,
        in_specs=[NEAR] * 3,
        out_specs=[NEAR] * 2,
        out_shape=[in_vmem(2, heads, HD, BLOCK, kind=BF16), in_vmem(2, heads, HD)],
        compiler_params=params(4),
        cost_estimate=cost(4 * heads * BLOCK * HD, 8 * heads * BLOCK * HD),
        name="scaled_queries",
    )(*near(cum, q0, q1))


def remaining_decay(cum):
    _, heads, _ = cum.shape

    def kernel(cum_ref, out_ref):
        def one(h):
            for b in range(2):
                row = cum_ref[b, pl.ds(h, 1), :]
                out_ref[b, h] = as_columns(jnp.exp(row[:, BLOCK - 1 :] - row))

        each_head(heads, 4, one)

    return pl.pallas_call(
        kernel,
        in_specs=[NEAR],
        out_specs=NEAR,
        out_shape=in_vmem(2, heads, BLOCK, HD),
        compiler_params=params(4),
        cost_estimate=cost(2 * heads * BLOCK * HD, 8 * heads * BLOCK * HD),
        name="remaining_decay",
    )(*near(cum))


def inverse_rms(sums_ref, b):
    at = slice(b * BLOCK, (b + 1) * BLOCK)
    inv = lax.rsqrt(sums_ref[0:1, at] / (HEAD_TOTAL * HD) + 1e-06)
    mean = sums_ref[1:2, at] * inv / (HEAD_TOTAL * HD)
    return inv, mean


def norm_grad(part, ends, gain, sums, scaled, arrays):
    heads, dim = gain.shape
    tok = 2 * BLOCK
    half = heads // 2

    def kernel(ends_ref, gain_ref, sums_ref, queries_ref, o0, o1, att0, att1,
               out_ref, second_ref, g0, g1, scales):
        for b in range(2):
            inv, mean = inverse_rms(sums_ref, b)
            scales[b, 0] = as_columns(inv)
            scales[b, 1] = as_columns(inv * inv * mean)

        def one(i):
            h = part * half + i
            line = gain_ref[pl.ds(h, 1), :]
            starts = []
            for b, (o, att, g) in enumerate(((o0, att0, g0), (o1, att1, g1))):
                grad = line * o[h].astype(F32) * scales[b, 0] - att[i] * scales[b, 1]
                grad = grad.astype(BF16)
                g[i] = grad
                starts.append(dot(queries_ref[b, h], grad))
            second_ref[i] = starts[1]
            out_ref[i] = starts[0] + ends_ref[0, pl.ds(h, 1)] * starts[1]

        each_head(half, 4, one)

    by_head = in_vmem(half, BLOCK, dim, kind=BF16)
    return pl.pallas_call(
        kernel,
        in_specs=[NEAR] * 8,
        out_specs=[NEAR] * 4,
        out_shape=[in_vmem(half, dim, dim), in_vmem(half, dim, dim), by_head, by_head],
        scratch_shapes=[pltpu.VMEM((2, 2, BLOCK, dim), F32)],
        compiler_params=params(4),
        cost_estimate=cost(heads * tok * dim * dim, 7 * heads * tok * dim),
        name=f"norm_grad_{part}",
    )(*near(ends, gain, sums, scaled, *arrays))


def normed_block(b, place_ref, gain_ref, sums_ref, halves, rows, raw):
    inv = as_columns(inverse_rms(sums_ref, b)[0])

    def one(part, i, h):
        rows[b, h] = halves[part][i] * inv * gain_ref[pl.ds(h, 1), :]

    each_half(halves[0].shape[0], 4, one)
    from_heads(raw, rows.at[b], 0, BLOCK, is_upper(place_ref))


def grad_q_kernel(
    place_ref, gain_ref, sums_ref, att_own0, att_own1, att_other0, att_other1,
    ends_ref, keep_ref, recv_ref, first_own, first_send, kh, vh, own0, own1, other0, other1,
    decays0, decays1, columns0, columns1, rows, gs_ref, out_normed, raw, sems,
):
    copies = []
    for b, halves in enumerate(((att_own0, att_other0), (att_own1, att_other1))):
        at = pl.ds(b * BLOCK, BLOCK)
        normed_block(b, place_ref, gain_ref, sums_ref, halves, rows, raw.at[at])
        copies.append(pltpu.make_async_copy(raw.at[at], out_normed.at[at], sems.at[b]))
        copies[-1].start()
    blocks = (((own0, other0), decays0, columns0), ((own1, other1), decays1, columns1))
    for b, (g, decays, columns) in enumerate(blocks):

        def one(part, i, h, b=b, g=g, decays=decays, columns=columns):
            grad = g[part][i]
            scores = causal(dot_rows(grad, vh[b, h]), [decays[h, at] for at in range(3)])
            gs_ref[b, h] = scores
            state = (keep_ref, recv_ref)[part][i]
            if b:
                state = ends_ref[0, pl.ds(h, 1)] * state + (first_own, first_send)[part][i]
            rows[b, h] = dot(scores, kh[b, h]) + columns[h] * times_state_t(grad, state)

        each_half(keep_ref.shape[0], 4, one)
    for copy in copies:
        copy.wait()


def grad_query(place, gain, sums, att, ends, arrays):
    _, heads, dim = ends.shape
    tok = 2 * BLOCK
    return pl.pallas_call(
        grad_q_kernel,
        in_specs=[NEAR] * 22,
        out_specs=[NEAR, NEAR, FAR],
        out_shape=[
            in_vmem(2, heads, BLOCK, dim), in_vmem(2, heads, BLOCK, BLOCK, kind=BF16),
            jax.ShapeDtypeStruct((tok, heads, dim), BF16),
        ],
        scratch_shapes=[
            pltpu.VMEM((tok, heads, dim), BF16),
            pltpu.SemaphoreType.DMA((2,)),
        ],
        compiler_params=params(6),
        cost_estimate=cost(
            4 * heads * tok * dim * (BLOCK + dim), 12 * heads * tok * dim, heads * tok * BLOCK
        ),
        name="grad_query",
    )(*near(place, gain, sums, *att, ends, *arrays))


def grad_kv_kernel(
    place_ref, gs_ref, w0, w1, q0, q1, kh, vh, own0, own1, other0, other1, remaining_ref,
    second_own, second_send, rows, dk, dv, out_q, raw, sems,
):
    upper = is_upper(place_ref)
    copies = []
    for b in range(2):
        for start in range(0, BLOCK, CHUNK):
            at = pl.ds(b * BLOCK + start, CHUNK)
            from_heads(raw.at[at], rows.at[b], start, CHUNK, upper)
            copies.append(pltpu.make_async_copy(raw.at[at], out_q.at[at], sems.at[len(copies)]))
            copies[-1].start()

    def one(part, i, h):
        columns = remaining_ref[0, h]
        state = (second_own, second_send)[part][i]
        g0, g1 = ((own0, own1), (other0, other1))[part]
        dk[0, h] = transposed_dot(gs_ref[0, h], q0[h]) + columns * times_state_t(vh[0, h], state)
        dv[0, h] = transposed_dot(w0[h], g0[i]) + columns * times_state(kh[0, h], state)
        dk[1, h] = transposed_dot(gs_ref[1, h], q1[h])
        dv[1, h] = transposed_dot(w1[h], g1[i])

    each_half(second_own.shape[0], 2, one)
    for copy in copies:
        copy.wait()


def grad_key_value(*arrays):
    _, heads, _, dim = arrays[6].shape
    tok = 2 * BLOCK
    return pl.pallas_call(
        grad_kv_kernel,
        in_specs=[NEAR] * 16,
        out_specs=[NEAR, NEAR, FAR],
        out_shape=[in_vmem(2, heads, BLOCK, dim)] * 2
        + [jax.ShapeDtypeStruct((tok, heads, dim), BF16)],
        scratch_shapes=[
            pltpu.VMEM((tok, heads, dim), BF16),
            pltpu.SemaphoreType.DMA((tok // CHUNK,)),
        ],
        compiler_params=params(6),
        cost_estimate=cost(4 * heads * tok * dim * (BLOCK + dim), 30 * heads * tok * dim),
        name="grad_key_value",
    )(*near(*arrays))


def finish_rows(part, b, ends_ref, state_ref, kh, vh, remaining_ref, dk, dv, rows_k, rows_v):
    half = state_ref.shape[0]

    def one(i):
        h = part * half + i
        columns = remaining_ref[b, h]
        state = state_ref[i]
        if b == 0:
            state = ends_ref[1, pl.ds(h, 1)] * state
        state = state.astype(BF16)
        none = jnp.zeros_like(state)
        both = jnp.concatenate(
            [jnp.concatenate([state.T, none], axis=1), jnp.concatenate([none, state], axis=1)],
            axis=0,
        )
        carried = dot(jnp.concatenate([vh[b, h], kh[b, h]], axis=1), both)
        rows_k[b, h] = dk[b, h] + columns * carried[:, :HD]
        rows_v[b, h] = dv[b, h] + columns * carried[:, HD:]

    each_head(half, 4, one)


def finish_own_kernel(*refs):
    for b in range(2):
        finish_rows(0, b, *refs)


def finish_other_kernel(
    place_ref, old_k, old_v, ends_ref, state_ref, kh, vh, remaining_ref, dk, dv,
    out_k, out_v, rows_k, rows_v, raw_k, raw_v, sems,
):
    upper = is_upper(place_ref)
    copies = []
    for b in range(2):
        finish_rows(1, b, ends_ref, state_ref, kh, vh, remaining_ref, dk, dv, rows_k, rows_v)
        for start in range(0, BLOCK, CHUNK // 2):
            at = pl.ds(b * BLOCK + start, CHUNK // 2)
            for rows, raw, out in ((rows_k, raw_k, out_k), (rows_v, raw_v, out_v)):
                from_heads(raw.at[at], rows.at[b], start, CHUNK // 2, upper)
                copies.append(pltpu.make_async_copy(raw.at[at], out.at[at], sems.at[len(copies)]))
                copies[-1].start()
    for copy in copies:
        copy.wait()


def finish_own(ends, keep, arrays):
    _, heads, dim = ends.shape
    tok = 2 * BLOCK
    return pl.pallas_call(
        finish_own_kernel,
        in_specs=[NEAR] * 7,
        out_specs=[NEAR, NEAR],
        out_shape=[in_vmem(2, heads, BLOCK, dim)] * 2,
        compiler_params=params(4),
        cost_estimate=cost(4 * heads * tok * dim * dim, 8 * heads * tok * dim),
        name="finish_own",
    )(*near(ends, keep, *arrays))


def finish_other(place, rows, ends, recv, arrays):
    _, heads, dim = ends.shape
    tok = 2 * BLOCK
    shape = jax.ShapeDtypeStruct((tok, heads, dim), BF16)
    return pl.pallas_call(
        finish_other_kernel,
        in_specs=[NEAR] * 10,
        out_specs=[FAR, FAR, NEAR, NEAR],
        out_shape=[shape, shape] + [in_vmem(2, heads, BLOCK, dim)] * 2,
        input_output_aliases={1: 2, 2: 3},
        scratch_shapes=[
            pltpu.VMEM((tok, heads, dim), BF16),
            pltpu.VMEM((tok, heads, dim), BF16),
            pltpu.SemaphoreType.DMA((4 * (tok // CHUNK),)),
        ],
        compiler_params=params(8),
        cost_estimate=cost(4 * heads * tok * dim * dim, 8 * heads * tok * dim),
        name="finish_other",
    )(*near(place, *rows, ends, recv, *arrays))[:2]


def follows(value, earlier):
    return lax.optimization_barrier((value, earlier))[0]


def swap(value, axis, bit):
    count = lax.axis_size(axis)
    return lax.ppermute(value, axis, [(i, i ^ bit) for i in range(count)])


def mix(body, backward, place, arrays, shapes, name):
    def kernel(place_ref, *refs):
        bits = [is_set(place_ref, which) != backward for which in (LATE, RIGHT, LOW)]
        body(bits, refs[: len(arrays)], refs[len(arrays) :])

    return pl.pallas_call(
        kernel,
        in_specs=[NEAR] + [NEAR] * len(arrays),
        out_specs=[NEAR] * len(shapes),
        out_shape=[in_vmem(*shape) for shape in shapes],
        compiler_params=params(4),
        cost_estimate=cost(4 * 8 * HD * HD, 16 * 8 * HD * HD),
        name=name,
    )(place, *near(*arrays))


OWN, PARTNER, CHIP, ROW, CORNER = range(5)


def mix_total(bits, own, got, d_own, d_got, first, second):
    late = bits[0]
    quarter = first.shape[0]
    for h in range(2 * quarter):
        total = jnp.where(late, 1.0, d_got(h)) * own[h, :HD] + jnp.where(late, d_own(h), 1.0) * got[h, :HD]
        if h < quarter:
            first[h, :HD] = total
        else:
            second[h - quarter] = total


def mix_total_first(bits, arrays, outputs):
    own, got = arrays
    first, second, chip = outputs
    quarter = first.shape[0]
    d_own = lambda h: own[h, HD : HD + 1]
    d_got = lambda h: got[h, HD : HD + 1]
    mix_total(bits, own, got, d_own, d_got, first, second)
    for h in range(2 * quarter):
        whole = d_own(h) * d_got(h)
        chip[h : h + 1] = whole
        place = HD + (TILE // 2) * (h // quarter)
        first[h % quarter, place : place + TILE // 2] = jnp.broadcast_to(whole, (TILE // 2, HD))


def mix_total_again(bits, arrays, outputs):
    table, own, got = arrays
    decay = lambda which: lambda h: table[which, h : h + 1]
    mix_total(bits, own, got, decay(OWN), decay(PARTNER), *outputs)


def mix_next(bits, decay, totals, gots, outputs):
    _, right, low = bits
    quarter = totals[1].shape[0]
    for i in range(quarter):
        h = i
        scale_total = jnp.where(right, 1.0, decay(ROW, h))
        scale_got = jnp.where(right, decay(CHIP, h), 1.0)
        outputs[0][i] = scale_total * totals[0][i, :HD] + scale_got * gots[0][i, :HD]
        h = quarter + i
        scale_total = jnp.where(low & right, 0.0, 1.0)
        corner = jnp.where(right, 1.0, decay(CHIP, h) * decay(CORNER, h))
        scale_got = jnp.where(low, corner, 0.0)
        outputs[1][i] = scale_total * totals[1][i] + scale_got * gots[1][i]


def mix_next_first(bits, arrays, outputs):
    own, got, chip, corner, first, second, one_a, one_b = arrays
    table = outputs[2]
    quarter = second.shape[0]
    for h in range(2 * quarter):
        place = HD + (TILE // 2) * (h // quarter)
        table[OWN, h : h + 1] = own[h, HD : HD + 1]
        table[PARTNER, h : h + 1] = got[h, HD : HD + 1]
        table[ROW, h : h + 1] = one_a[h % quarter, place : place + 1]
    table[CHIP] = chip[...]
    table[CORNER] = corner[...]
    decay = lambda which, h: table[which, h : h + 1]
    mix_next(bits, decay, (first, second), (one_a, one_b), outputs[:2])


def mix_next_again(bits, arrays, outputs):
    table, first, second, one_a, one_b = arrays
    decay = lambda which, h: table[which, h : h + 1]
    mix_next(bits, decay, (first, second), (one_a, one_b), outputs)


def mix_enter(bits, arrays, outputs):
    table, own, got, one_a, one_b, two_a, two_b = arrays
    kept, sent = outputs
    late, right, low = bits
    quarter = one_b.shape[0]
    decay = lambda which, h: table[which, h : h + 1]
    for h in range(2 * quarter):
        i = h % quarter
        row = jnp.where(right, decay(ROW, h), 1.0)
        if h < quarter:
            one, two = one_a[i, :HD], two_a[i]
            scale_one = jnp.where(right, 1.0, 0.0)
            scale_two = jnp.where(low, row, 0.0)
        else:
            one, two = one_b[i], two_b[i]
            scale_one = jnp.where(low, jnp.where(right, row, decay(CORNER, h)), 0.0)
            scale_two = jnp.where(low | right, 1.0, 0.0)
        enter = scale_one * one + scale_two * two
        after = jnp.where(late, decay(PARTNER, h), decay(OWN, h)) * enter
        after += jnp.where(late, got[h, :HD], own[h, :HD])
        kept[h] = jnp.where(late, after, enter)
        sent[h] = jnp.where(late, enter, after)


def entering_quad(send, own_task, table, place, backward, tasks):
    def work(stage, after, before=()):
        if stage not in tasks:
            return before
        run, outputs = tasks[stage]
        outputs.extend(run(after))
        return lax.optimization_barrier((before, outputs[0]))[0]

    name = "later" if backward else "earlier"
    half = send.shape[0]
    quarter = half // 2
    states, wide = (quarter, HD, HD), (quarter, HD + TILE, HD)
    got = swap(send, "seq", 1)
    own = own_task(send)
    if table is None:
        first, second, chip = mix(
            mix_total_first, backward, place, (own, got), (wide, states, (half, HD)), name + "_total"
        )
    else:
        first, second = mix(
            mix_total_again, backward, place, (table, own, got), (states, states), name + "_total"
        )
    one_a, one_b = swap(first, "seq", 2), swap(second, "seq", 4)
    if table is None:
        corner = swap(chip, "seq", 6)
        one_a, one_b, corner = work(1, second, (one_a, one_b, corner))
        next_a, next_b, table = mix(
            mix_next_first, backward, place, (own, got, chip, corner, first, second, one_a, one_b),
            (states, states, (5, half, HD)), name + "_next",
        )
    else:
        one_a, one_b = work(1, second, (one_a, one_b))
        next_a, next_b = mix(
            mix_next_again, backward, place, (table, first, second, one_a, one_b), (states, states),
            name + "_next",
        )
    two_a, two_b = swap(next_a, "seq", 4), swap(next_b, "seq", 2)
    two_a, two_b = work(2, next_b, (two_a, two_b))
    kept, sent = mix(
        mix_enter, backward, place, (table, own, got, one_a, one_b, two_a, two_b),
        ((half, HD, HD), (half, HD, HD)), name + "_enter",
    )
    received = swap(sent, "seq", 1)
    received = follows(received, tasks[3](follows(kept, sent)))
    return kept, received, table


def entering_any(send, own_task, log_total, backward, tasks):
    own = own_task(send)
    for stage in (1, 2):
        run, outputs = tasks[stage]
        outputs.extend(run(send))
    count, mine = lax.axis_size("seq"), lax.axis_index("seq")
    core = mine % 2
    own, send = own[:, :HD], send[:, :HD]
    half = own.shape[0]
    in_order = jnp.where(
        core == 0, jnp.concatenate([own, send], axis=0), jnp.concatenate([send, own], axis=0)
    )
    states = lax.all_gather(in_order, "seq")
    decays = jnp.exp(lax.all_gather(log_total, "seq"))
    place = mine
    if backward:
        states, decays, place = states[::-1], decays[::-1], count - 1 - mine

    def step(at, total):
        longer = decays[at][:, None, None] * total + states[at]
        return jnp.where(at < place, longer, total)

    total = lax.fori_loop(0, count - 1, step, jnp.zeros_like(in_order))
    kept = lax.dynamic_slice_in_dim(total, core * half, half)
    tasks[3](kept)
    return kept, lax.dynamic_slice_in_dim(total, (1 - core) * half, half)


def add(first, second):
    def kernel(first_ref, second_ref, out_ref):
        out_ref[...] = first_ref[...] + second_ref[...]

    return pl.pallas_call(
        kernel,
        in_specs=[NEAR, NEAR],
        out_specs=NEAR,
        out_shape=in_vmem(*first.shape),
        compiler_params=params(2),
        name="add",
    )(*near(first, second))


def sum_over_heads(value, tasks):
    tasks = list(tasks)
    results = []
    count = lax.axis_size("head")
    reach = 1
    while 2 * reach <= count and count % (2 * reach) == 0:
        got = swap(value, "head", reach)
        if tasks:
            results.append(tasks.pop(0)(value))
            got = follows(got, results[-1])
        value = add(value, got)
        reach *= 2
    results += [task(value) for task in tasks]
    part = value
    for shift in range(1, count // reach):
        value = add(
            value,
            lax.ppermute(part, "head", [(i, (i + shift * reach) % count) for i in range(count)]),
        )
    return value, results


def on_device(query_rows, key_rows, value_rows, output_grad, norm_gain, log_decay):
    mine = lax.axis_index("seq")
    bits = [(mine >> at) % 2 for at in range(3)]
    marks = [1 - bits[0], bits[0], *bits] + [jnp.zeros_like(mine)] * (TILE - 5)
    place = jnp.broadcast_to(jnp.stack(marks).astype(F32)[:, None], (TILE, HD))
    table = [None]

    def entering(send, own_task, backward, tasks):
        if lax.axis_size("seq") != 8:
            log_total = jnp.sum(log_decay, axis=1)
            return entering_any(send, own_task, log_total, backward, tasks)
        kept, received, table[0] = entering_quad(
            send, own_task, table[0], place, backward, tasks
        )
        return kept, received

    send, first_send, kh, vh, cum, _, decay, gain = state_to_send(
        place, norm_gain, log_decay, key_rows, value_rows
    )
    firsts, raws, in_0, in_1, begun = [], [], [], [], []

    def own_task(earlier):
        own, first, *raw = own_state(
            follows(kh, earlier), vh, cum, decay, query_rows, output_grad
        )
        firsts.extend((first, first_send))
        raws.append(raw)
        return own

    def forward_task(index):
        def task(earlier):
            *made, q_next, o_next = [
                *intra(
                    index, place, follows(cum, earlier), kh, vh, *firsts, raws[-1],
                    query_rows, output_grad,
                ),
                *raws[-1] * index,
            ]
            raws.append([q_next, o_next])
            return made

        return task

    def parts():
        q0, o0, _, _, columns0, inner0 = in_0
        q1, o1, _, _, columns1, inner1 = in_1
        return q0, q1, o0, o1, columns0, columns1, inner0, inner1

    def attend_task(kept):
        begun.extend(attend(0, gain, kept, parts()))
        return begun[-1]

    keep, recv = entering(
        send, own_task, False, {1: (forward_task(0), in_0), 2: (forward_task(1), in_1), 3: attend_task}
    )
    q0, o0, w0, decays0, columns0, _ = in_0
    q1, o1, w1, decays1, columns1, _ = in_1
    own_att = begun[:2]
    *other_att, sums = attend(1, gain, recv, parts(), begun[2:])
    sums, ((scaled, ends), remaining) = sum_over_heads(
        sums,
        (
            lambda earlier: scaled_queries(cum, follows(q0, earlier), q1),
            lambda earlier: remaining_decay(follows(cum, earlier)),
        ),
    )
    grad_send, second_send, *other_g = norm_grad(1, ends, gain, sums, scaled, (o0, o1, *other_att))
    own_g, seconds, queries, pairs, rows = [], [], [], [], []

    def own_grad_task(earlier):
        own, second, *grads = norm_grad(
            0, ends, gain, follows(sums, earlier), scaled, (o0, o1, *own_att)
        )
        own_g.extend(grads)
        seconds.extend((second, second_send))
        return own

    def query_task(earlier):
        return grad_query(
            place, gain, sums, (*own_att, *other_att), follows(ends, earlier),
            (keep, recv, *firsts, kh, vh, *own_g, *other_g, decays0, decays1, columns0, columns1),
        )

    def pair_task(earlier):
        return grad_key_value(
            place, queries[1], w0, w1, q0, q1, kh, vh, *own_g, *other_g, remaining,
            follows(seconds[0], earlier), seconds[1], queries[0],
        )

    def finish_task(kept):
        rows.extend(finish_own(ends, kept, (kh, vh, remaining, *pairs[:2])))
        return rows[-1]

    _, grad_recv = entering(
        grad_send, own_grad_task, True,
        {1: (query_task, queries), 2: (pair_task, pairs), 3: finish_task},
    )
    grad_k, grad_v = finish_other(
        place, rows, ends, grad_recv, (kh, vh, remaining, *pairs[:2])
    )
    return queries[2], pairs[2], grad_k, grad_v


def solution(mesh):
    rows = P("seq", "head", None)
    return jax.shard_map(
        on_device,
        mesh=mesh,
        in_specs=(rows, rows, rows, rows, P("head", None), P("head", "seq")),
        out_specs=(rows, rows, rows, rows),
        check_vma=False,
    )
```

```python
import functools

import jax
import jax.numpy as jnp
from jax import lax
from jax.experimental import pallas as pl
from jax.experimental.pallas import tpu as pltpu
from jax.sharding import PartitionSpec as P

HEAD_TOTAL = 64
HD = 128
BLOCK = 256
CHUNK = 128
TILE = 8
F32 = jnp.float32
BF16 = jnp.bfloat16
MIB = 1024 * 1024
NEAR = pl.BlockSpec(memory_space=pltpu.VMEM)
FAR = pl.BlockSpec(memory_space=pl.ANY)
LOWER, UPPER, LATE, RIGHT, LOW = range(5)


def in_vmem(*shape, kind=F32):
    return pltpu.VMEM(shape, kind)


def near(*arrays):
    return [pltpu.with_memory_space_constraint(array, pltpu.VMEM) for array in arrays]


def far(*arrays):
    return [pltpu.with_memory_space_constraint(array, pltpu.HBM) for array in arrays]


def params(mib):
    return pltpu.CompilerParams(vmem_limit_bytes=mib * MIB)


def cost(flops, moved, exps=0):
    return pl.CostEstimate(flops=flops, bytes_accessed=moved, transcendentals=exps)


def block_cum(log_decay):
    size = log_decay.shape[1]
    upper = lax.broadcasted_iota(jnp.int32, (size, size), 0) <= lax.broadcasted_iota(
        jnp.int32, (size, size), 1
    )
    return jnp.dot(
        log_decay,
        jnp.where(upper, 1.0, 0.0).astype(F32),
        precision=lax.Precision.HIGHEST,
        preferred_element_type=F32,
    )


def as_columns(row):
    return jnp.broadcast_to(row, (HD, row.shape[1])).T


def dot(a, b):
    return jnp.dot(a, b, preferred_element_type=F32)


def dot_rows(a, b):
    return lax.dot_general(a, b, (((1,), (1,)), ((), ())), preferred_element_type=F32)


def two_parts(matrix):
    high = matrix.astype(BF16)
    return high, (matrix - high.astype(F32)).astype(BF16)


def times_state(rows, state):
    return dot(jnp.concatenate([rows, rows], axis=1), jnp.concatenate(two_parts(state), axis=0))


def times_state_t(rows, state):
    return dot_rows(
        jnp.concatenate([rows, rows], axis=1), jnp.concatenate(two_parts(state), axis=1)
    )


def decay_quarters(row, columns):
    half = row.shape[1] // 2
    lower = lax.broadcasted_iota(jnp.int32, (half, half), 0) >= lax.broadcasted_iota(
        jnp.int32, (half, half), 1
    )
    quarters = []
    for t, s in ((0, 0), (1, 0), (1, 1)):
        gap = columns[t * half : (t + 1) * half] - row[:, s * half : (s + 1) * half]
        quarters.append(jnp.exp(jnp.where(lower, gap, -jnp.inf) if t == s else gap))
    return quarters


def causal(table, quarters):
    half = table.shape[0] // 2
    first, second, third = (
        (table[t * half : (t + 1) * half, s * half : (s + 1) * half] * quarter).astype(BF16)
        for (t, s), quarter in zip(((0, 0), (1, 0), (1, 1)), quarters)
    )
    top = jnp.concatenate([first, jnp.zeros_like(first)], axis=1)
    return jnp.concatenate([top, jnp.concatenate([second, third], axis=1)], axis=0)


def transposed_dot(a, b):
    return lax.dot_general(a, b, (((0,), (0,)), ((), ())), preferred_element_type=F32)


def each_head(heads, unroll, body):
    def step(h, carry):
        body(h)
        return carry

    lax.fori_loop(0, heads, step, 0, unroll=unroll)


def each_half(half, unroll, body):
    for part in range(2):
        each_head(half, unroll, lambda i, part=part: body(part, i, part * half + i))


def turn_tiles(tiles):
    count = len(tiles)
    at = lax.broadcasted_iota(jnp.int32, tiles[0].shape, 0)
    turned = [tile if i == 0 else pltpu.roll(tile, i, 0) for i, tile in enumerate(tiles)]
    reach = 1
    while reach < count:
        odd = (at & reach) != 0
        turned = [
            jnp.where(odd, turned[(n + reach) % count], turned[n]) for n in range(count)
        ]
        reach *= 2
    picked = [turned[-j % count] for j in range(count)]
    return [tile if j == 0 else pltpu.roll(tile, count - j, 0) for j, tile in enumerate(picked)]


def is_upper(place_ref):
    return jnp.max(place_ref[UPPER : UPPER + 1]) > 0.5


def to_heads(dst, block, upper):
    tok, heads, _ = block.shape

    def step(group, carry):
        at = pl.multiple_of(group * 2 * TILE, 2 * TILE)
        tokens = block[pl.ds(at, 2 * TILE)].astype(F32)
        for first in range(0, heads, TILE):
            halves = [
                turn_tiles([tokens[base + i, first : first + TILE] for i in range(TILE)])
                for base in (0, TILE)
            ]
            local = jnp.where(upper, heads - TILE - first, first)
            for j in range(TILE):
                both = jnp.concatenate([halves[0][j], halves[1][j]], axis=0)
                dst[local + j, pl.ds(at, 2 * TILE)] = both.astype(BF16)
        return carry

    lax.fori_loop(0, tok // (2 * TILE), step, 0, unroll=4)


def from_heads(block, src, start, tok, upper):
    heads = src.shape[0]

    def step(group, carry):
        at = pl.multiple_of(group * TILE, TILE)
        parts = []
        for first in range(0, heads, TILE):
            local = jnp.where(upper, heads - TILE - first, first)
            parts.append(turn_tiles([src[local + i, pl.ds(start + at, TILE)] for i in range(TILE)]))
        for j in range(TILE):
            block[at + j] = jnp.concatenate([part[j] for part in parts], axis=0).astype(BF16)
        return carry

    lax.fori_loop(0, tok // TILE, step, 0, unroll=4)


def is_set(place_ref, which):
    return place_ref[which : which + 1] > 0.5


def in_local_order(place_ref, rows):
    half = rows.shape[0] // 2
    lower, upper = rows[:half], rows[half:]
    mine = jnp.broadcast_to(place_ref[LOWER : LOWER + 1, :1], lower.shape) > 0.5
    return jnp.concatenate(
        [jnp.where(mine, lower, upper), jnp.where(mine, upper, lower)], axis=0
    )


def half_states(part, kh, vh, cum, b, out, first=None):
    half = kh.shape[1] // 2

    def one(i):
        h = part * half + i
        row = cum[b, pl.ds(h, 1), :]
        scale = jnp.exp(row[:, BLOCK - 1 :] - row)
        state = dot((kh[b, h].astype(F32).T * scale).astype(BF16), vh[b, h])
        if first is not None:
            state += jnp.exp(row[:, BLOCK - 1 :]) * first[i]
        out[i, :HD] = state

    each_head(half, 4, one)


def add_decays(out, decay, part):
    half = out.shape[0]
    for i in range(half):
        out[i, HD:] = jnp.broadcast_to(decay[part * half + i : part * half + i + 1], (TILE, HD))


def state_kernel(
    place_ref, gain_hbm, ld_hbm, k_hbm, v_hbm, send_ref, first_ref, kh, vh, cum, ld_ref, decay,
    gain_ref, gain_raw, ld_raw, k_raw, v_raw, sems,
):
    heads, tok = ld_ref.shape
    per_block = BLOCK // CHUNK
    copies = [pltpu.make_async_copy(ld_hbm, ld_raw, sems.at[0])]
    for c in range(tok // CHUNK):
        at = pl.ds(c * CHUNK, CHUNK)
        copies.append(pltpu.make_async_copy(k_hbm.at[at], k_raw.at[at], sems.at[2 * c + 1]))
        copies.append(pltpu.make_async_copy(v_hbm.at[at], v_raw.at[at], sems.at[2 * c + 2]))
    copies.append(pltpu.make_async_copy(gain_hbm, gain_raw, sems.at[len(copies)]))
    for copy in copies:
        copy.start()
    upper = is_upper(place_ref)
    copies[0].wait()
    ld_ref[...] = in_local_order(place_ref, ld_raw[...])
    for b in range(2):
        cum[b] = block_cum(ld_ref[:, b * BLOCK : (b + 1) * BLOCK])
    ends = cum[0, :, BLOCK - 1 :] + cum[1, :, BLOCK - 1 :]
    decay[...] = jnp.broadcast_to(jnp.exp(ends), decay.shape)

    for b in range(2):
        for c in range(per_block):
            at = pl.ds((b * per_block + c) * CHUNK, CHUNK)
            here = pl.ds(c * CHUNK, CHUNK)
            which = 2 * (b * per_block + c) + 1
            copies[which].wait()
            to_heads(kh.at[b, :, here], k_raw.at[at], upper)
            copies[which + 1].wait()
            to_heads(vh.at[b, :, here], v_raw.at[at], upper)
        if b == 0:
            half_states(1, kh, vh, cum, 0, first_ref)
        else:
            half_states(1, kh, vh, cum, 1, send_ref, first_ref)
    add_decays(send_ref, decay, 1)
    copies[-1].wait()
    gain_ref[...] = in_local_order(place_ref, gain_raw[...])


def state_to_send(place, gain, log_decay, key_rows, value_rows):
    tok, heads, dim = key_rows.shape
    half = heads // 2
    by_head = in_vmem(2, heads, BLOCK, dim, kind=BF16)
    return pl.pallas_call(
        state_kernel,
        in_specs=[NEAR, FAR, FAR, FAR, FAR],
        out_specs=[NEAR] * 8,
        out_shape=[
            in_vmem(half, dim + TILE, dim), in_vmem(half, dim, dim), by_head, by_head,
            in_vmem(2, heads, BLOCK), in_vmem(heads, tok), in_vmem(heads, dim), in_vmem(heads, dim),
        ],
        scratch_shapes=[
            pltpu.VMEM((heads, dim), F32),
            pltpu.VMEM((heads, tok), F32),
            pltpu.VMEM((tok, heads, dim), BF16),
            pltpu.VMEM((tok, heads, dim), BF16),
            pltpu.SemaphoreType.DMA((2 * (tok // CHUNK) + 2,)),
        ],
        compiler_params=params(8),
        cost_estimate=cost(tok * heads * dim * dim, 8 * tok * heads * dim),
        name="state_to_send",
    )(place, *far(gain, log_decay, key_rows, value_rows))


def fetch_block(index, arrays, blocks, sems):
    copies = [
        pltpu.make_async_copy(array.at[pl.ds(index * BLOCK, BLOCK)], block, sems.at[at])
        for at, (array, block) in enumerate(zip(arrays, blocks))
    ]
    for copy in copies:
        copy.start()
    return copies


def own_state_kernel(
    kh, vh, cum, decay, q_hbm, o_hbm, own_ref, first_ref, q_raw, o_raw, sems
):
    copies = fetch_block(0, (q_hbm, o_hbm), (q_raw, o_raw), sems)
    half_states(0, kh, vh, cum, 0, first_ref)
    half_states(0, kh, vh, cum, 1, own_ref, first_ref)
    add_decays(own_ref, decay, 0)
    for copy in copies:
        copy.wait()


def own_state(kh, vh, cum, decay, query_rows, output_grad):
    _, heads, tok, dim = kh.shape
    half = heads // 2
    raw = in_vmem(BLOCK, heads, dim, kind=BF16)
    return pl.pallas_call(
        own_state_kernel,
        in_specs=[NEAR] * 4 + [FAR, FAR],
        out_specs=[NEAR] * 4,
        out_shape=[in_vmem(half, dim + TILE, dim), in_vmem(half, dim, dim), raw, raw],
        scratch_shapes=[pltpu.SemaphoreType.DMA((2,))],
        compiler_params=params(4),
        cost_estimate=cost(2 * tok * heads * dim * dim, 4 * tok * heads * dim),
        name="own_state",
    )(*near(kh, vh, cum, decay), *far(query_rows, output_grad))


def intra(index, place, cum, kh, vh, first_own, first_send, raw, query_rows, output_grad):
    tok, heads, dim = query_rows.shape
    ahead = index == 0

    def kernel(place_ref, cum, kh, vh, first_own, first_send, q_raw, o_raw, *refs):
        if ahead:
            q_hbm, o_hbm, *refs = refs
            *refs, q_next, o_next, sems = refs
            copies = fetch_block(1, (q_hbm, o_hbm), (q_next, o_next), sems)
        qh, oh, w_ref, decays_ref, columns_ref, inner_ref = refs
        upper = is_upper(place_ref)
        to_heads(qh, q_raw, upper)
        to_heads(oh, o_raw, upper)

        def one(part, i, h):
            query = qh[h]
            row = cum[index, pl.ds(h, 1), :]
            columns = as_columns(row)
            quarters = decay_quarters(row, columns)
            for at, quarter in enumerate(quarters):
                decays_ref[h, at] = quarter
            weights = causal(dot_rows(query, kh[index, h]), quarters)
            w_ref[h] = weights.T
            inner = dot(weights, vh[index, h])
            columns = jnp.exp(columns)
            columns_ref[h] = columns
            if index:
                inner += columns * times_state(query, (first_own, first_send)[part][i])
            inner_ref[h] = inner

        each_half(heads // 2, 4, one)
        if ahead:
            for copy in copies:
                copy.wait()

    by_head = in_vmem(heads, BLOCK, dim, kind=BF16)
    return pl.pallas_call(
        kernel,
        in_specs=[NEAR] * 8 + [FAR, FAR] * ahead,
        out_specs=[NEAR] * (6 + 2 * ahead),
        out_shape=[
            by_head, by_head, in_vmem(heads, BLOCK, BLOCK, kind=BF16),
            in_vmem(heads, 3, BLOCK // 2, BLOCK // 2), in_vmem(heads, BLOCK, dim),
            in_vmem(heads, BLOCK, dim),
        ]
        + [in_vmem(BLOCK, heads, dim, kind=BF16)] * (2 * ahead),
        scratch_shapes=[pltpu.SemaphoreType.DMA((2,))] * ahead,
        compiler_params=params(4),
        cost_estimate=cost(
            2 * heads * BLOCK * BLOCK * dim * 4, 20 * heads * BLOCK * dim, heads * BLOCK * BLOCK
        ),
        name=f"intra_{index}",
    )(
        *near(place, cum, kh, vh, first_own, first_send, *raw),
        *(far(query_rows, output_grad) if ahead else ()),
    )


def attend_kernel(part, *refs):
    gain_ref, state_ref, q0, q1, o0, o1, columns0, columns1, inner0, inner1 = refs[:10]
    half = state_ref.shape[0]
    if part:
        before, att0, att1, sums_ref, partial = refs[10:]
        partial[...] = before[...]
    else:
        att0, att1, partial = refs[10:]
        partial[...] = jnp.zeros_like(partial)

    def one(i):
        h = part * half + i
        state = state_ref[i]
        gain = gain_ref[pl.ds(h, 1), :]
        blocks = ((q0, o0, columns0, inner0, att0), (q1, o1, columns1, inner1, att1))
        for b, (q, o, columns, inner, att) in enumerate(blocks):
            attended = inner[h] + columns[h] * times_state(q[h], state)
            att[i] = attended
            partial[0, b] += attended * attended
            partial[1, b] += gain * o[h].astype(F32) * attended
            state = columns[h, BLOCK - 1 :] * state

    each_head(half, 4, one)
    if part:
        ones = jnp.ones((8, HD), F32)
        for b in range(2):
            for at in range(2):
                line = lax.dot_general(
                    ones, partial[at, b], (((1,), (1,)), ((), ())),
                    precision=lax.Precision.HIGHEST, preferred_element_type=F32,
                )
                sums_ref[at : at + 1, b * BLOCK : (b + 1) * BLOCK] = line[:1]


def attend(part, gain, state, arrays, before=()):
    heads, dim = gain.shape
    tok = 2 * BLOCK
    half = heads // 2
    by_head = in_vmem(half, BLOCK, dim)
    partial = (2, 2, BLOCK, dim)
    return pl.pallas_call(
        functools.partial(attend_kernel, part),
        in_specs=[NEAR] * (10 + part),
        out_specs=[NEAR] * 3,
        out_shape=[by_head, by_head, in_vmem(2, tok) if part else in_vmem(*partial)],
        scratch_shapes=[pltpu.VMEM(partial, F32)] * part,
        compiler_params=params(6),
        cost_estimate=cost(2 * heads * tok * dim * dim, 8 * heads * tok * dim),
        name=f"attend_{part}",
    )(*near(gain, state, *arrays, *before))


def scaled_queries(cum, q0, q1):
    _, heads, _ = cum.shape

    def kernel(cum_ref, q0, q1, out_ref, ends_ref):
        for b in range(2):
            ends_ref[b] = jnp.broadcast_to(jnp.exp(cum_ref[b, :, BLOCK - 1 :]), (heads, HD))

        def one(h):
            for b, q in enumerate((q0, q1)):
                scale = jnp.exp(cum_ref[b, pl.ds(h, 1), :])
                out_ref[b, h] = (q[h].astype(F32).T * scale).astype(BF16)

        each_head(heads, 4, one)

    return pl.pallas_call(
        kernel,
        in_specs=[NEAR] * 3,
        out_specs=[NEAR] * 2,
        out_shape=[in_vmem(2, heads, HD, BLOCK, kind=BF16), in_vmem(2, heads, HD)],
        compiler_params=params(4),
        cost_estimate=cost(4 * heads * BLOCK * HD, 8 * heads * BLOCK * HD),
        name="scaled_queries",
    )(*near(cum, q0, q1))


def remaining_decay(cum):
    _, heads, _ = cum.shape

    def kernel(cum_ref, out_ref):
        def one(h):
            for b in range(2):
                row = cum_ref[b, pl.ds(h, 1), :]
                out_ref[b, h] = as_columns(jnp.exp(row[:, BLOCK - 1 :] - row))

        each_head(heads, 4, one)

    return pl.pallas_call(
        kernel,
        in_specs=[NEAR],
        out_specs=NEAR,
        out_shape=in_vmem(2, heads, BLOCK, HD),
        compiler_params=params(4),
        cost_estimate=cost(2 * heads * BLOCK * HD, 8 * heads * BLOCK * HD),
        name="remaining_decay",
    )(*near(cum))


def inverse_rms(sums_ref, b):
    at = slice(b * BLOCK, (b + 1) * BLOCK)
    inv = lax.rsqrt(sums_ref[0:1, at] / (HEAD_TOTAL * HD) + 1e-06)
    mean = sums_ref[1:2, at] * inv / (HEAD_TOTAL * HD)
    return inv, mean


def norm_grad(part, ends, gain, sums, scaled, arrays):
    heads, dim = gain.shape
    tok = 2 * BLOCK
    half = heads // 2

    def kernel(ends_ref, gain_ref, sums_ref, queries_ref, o0, o1, att0, att1,
               out_ref, second_ref, g0, g1, scales):
        for b in range(2):
            inv, mean = inverse_rms(sums_ref, b)
            scales[b, 0] = as_columns(inv)
            scales[b, 1] = as_columns(inv * inv * mean)

        def one(i):
            h = part * half + i
            line = gain_ref[pl.ds(h, 1), :]
            starts = []
            for b, (o, att, g) in enumerate(((o0, att0, g0), (o1, att1, g1))):
                grad = line * o[h].astype(F32) * scales[b, 0] - att[i] * scales[b, 1]
                grad = grad.astype(BF16)
                g[i] = grad
                starts.append(dot(queries_ref[b, h], grad))
            second_ref[i] = starts[1]
            out_ref[i] = starts[0] + ends_ref[0, pl.ds(h, 1)] * starts[1]

        each_head(half, 4, one)

    by_head = in_vmem(half, BLOCK, dim, kind=BF16)
    return pl.pallas_call(
        kernel,
        in_specs=[NEAR] * 8,
        out_specs=[NEAR] * 4,
        out_shape=[in_vmem(half, dim, dim), in_vmem(half, dim, dim), by_head, by_head],
        scratch_shapes=[pltpu.VMEM((2, 2, BLOCK, dim), F32)],
        compiler_params=params(4),
        cost_estimate=cost(heads * tok * dim * dim, 7 * heads * tok * dim),
        name=f"norm_grad_{part}",
    )(*near(ends, gain, sums, scaled, *arrays))


def normed_block(b, place_ref, gain_ref, sums_ref, halves, rows, raw):
    inv = as_columns(inverse_rms(sums_ref, b)[0])

    def one(part, i, h):
        rows[b, h] = halves[part][i] * inv * gain_ref[pl.ds(h, 1), :]

    each_half(halves[0].shape[0], 4, one)
    from_heads(raw, rows.at[b], 0, BLOCK, is_upper(place_ref))


def grad_q_kernel(
    place_ref, gain_ref, sums_ref, att_own0, att_own1, att_other0, att_other1,
    ends_ref, keep_ref, recv_ref, first_own, first_send, kh, vh, own0, own1, other0, other1,
    decays0, decays1, columns0, columns1, rows, gs_ref, out_normed, raw, sems,
):
    copies = []
    for b, halves in enumerate(((att_own0, att_other0), (att_own1, att_other1))):
        at = pl.ds(b * BLOCK, BLOCK)
        normed_block(b, place_ref, gain_ref, sums_ref, halves, rows, raw.at[at])
        copies.append(pltpu.make_async_copy(raw.at[at], out_normed.at[at], sems.at[b]))
        copies[-1].start()
    blocks = (((own0, other0), decays0, columns0), ((own1, other1), decays1, columns1))
    for b, (g, decays, columns) in enumerate(blocks):

        def one(part, i, h, b=b, g=g, decays=decays, columns=columns):
            grad = g[part][i]
            scores = causal(dot_rows(grad, vh[b, h]), [decays[h, at] for at in range(3)])
            gs_ref[b, h] = scores
            state = (keep_ref, recv_ref)[part][i]
            if b:
                state = ends_ref[0, pl.ds(h, 1)] * state + (first_own, first_send)[part][i]
            rows[b, h] = dot(scores, kh[b, h]) + columns[h] * times_state_t(grad, state)

        each_half(keep_ref.shape[0], 4, one)
    for copy in copies:
        copy.wait()


def grad_query(place, gain, sums, att, ends, arrays):
    _, heads, dim = ends.shape
    tok = 2 * BLOCK
    return pl.pallas_call(
        grad_q_kernel,
        in_specs=[NEAR] * 22,
        out_specs=[NEAR, NEAR, FAR],
        out_shape=[
            in_vmem(2, heads, BLOCK, dim), in_vmem(2, heads, BLOCK, BLOCK, kind=BF16),
            jax.ShapeDtypeStruct((tok, heads, dim), BF16),
        ],
        scratch_shapes=[
            pltpu.VMEM((tok, heads, dim), BF16),
            pltpu.SemaphoreType.DMA((2,)),
        ],
        compiler_params=params(6),
        cost_estimate=cost(
            4 * heads * tok * dim * (BLOCK + dim), 12 * heads * tok * dim, heads * tok * BLOCK
        ),
        name="grad_query",
    )(*near(place, gain, sums, *att, ends, *arrays))


def grad_kv_kernel(
    place_ref, gs_ref, w0, w1, q0, q1, kh, vh, own0, own1, other0, other1, remaining_ref,
    second_own, second_send, rows, dk, dv, out_q, raw, sems,
):
    upper = is_upper(place_ref)
    copies = []
    for b in range(2):
        for start in range(0, BLOCK, CHUNK):
            at = pl.ds(b * BLOCK + start, CHUNK)
            from_heads(raw.at[at], rows.at[b], start, CHUNK, upper)
            copies.append(pltpu.make_async_copy(raw.at[at], out_q.at[at], sems.at[len(copies)]))
            copies[-1].start()

    def one(part, i, h):
        columns = remaining_ref[0, h]
        state = (second_own, second_send)[part][i]
        g0, g1 = ((own0, own1), (other0, other1))[part]
        dk[0, h] = transposed_dot(gs_ref[0, h], q0[h]) + columns * times_state_t(vh[0, h], state)
        dv[0, h] = dot(w0[h], g0[i]) + columns * times_state(kh[0, h], state)
        dk[1, h] = transposed_dot(gs_ref[1, h], q1[h])
        dv[1, h] = dot(w1[h], g1[i])

    each_half(second_own.shape[0], 2, one)
    for copy in copies:
        copy.wait()


def grad_key_value(*arrays):
    _, heads, _, dim = arrays[6].shape
    tok = 2 * BLOCK
    return pl.pallas_call(
        grad_kv_kernel,
        in_specs=[NEAR] * 16,
        out_specs=[NEAR, NEAR, FAR],
        out_shape=[in_vmem(2, heads, BLOCK, dim)] * 2
        + [jax.ShapeDtypeStruct((tok, heads, dim), BF16)],
        scratch_shapes=[
            pltpu.VMEM((tok, heads, dim), BF16),
            pltpu.SemaphoreType.DMA((tok // CHUNK,)),
        ],
        compiler_params=params(6),
        cost_estimate=cost(4 * heads * tok * dim * (BLOCK + dim), 30 * heads * tok * dim),
        name="grad_key_value",
    )(*near(*arrays))


def finish_rows(part, b, ends_ref, state_ref, kh, vh, remaining_ref, dk, dv, rows_k, rows_v):
    half = state_ref.shape[0]

    def one(i):
        h = part * half + i
        columns = remaining_ref[b, h]
        state = state_ref[i]
        if b == 0:
            state = ends_ref[1, pl.ds(h, 1)] * state
        state = state.astype(BF16)
        none = jnp.zeros_like(state)
        both = jnp.concatenate(
            [jnp.concatenate([state.T, none], axis=1), jnp.concatenate([none, state], axis=1)],
            axis=0,
        )
        carried = dot(jnp.concatenate([vh[b, h], kh[b, h]], axis=1), both)
        rows_k[b, h] = dk[b, h] + columns * carried[:, :HD]
        rows_v[b, h] = dv[b, h] + columns * carried[:, HD:]

    each_head(half, 4, one)


def finish_own_kernel(*refs):
    for b in range(2):
        finish_rows(0, b, *refs)


def finish_other_kernel(
    place_ref, old_k, old_v, ends_ref, state_ref, kh, vh, remaining_ref, dk, dv,
    out_k, out_v, rows_k, rows_v, raw_k, raw_v, sems,
):
    upper = is_upper(place_ref)
    copies = []
    for b in range(2):
        finish_rows(1, b, ends_ref, state_ref, kh, vh, remaining_ref, dk, dv, rows_k, rows_v)
        for start in range(0, BLOCK, CHUNK // 2):
            at = pl.ds(b * BLOCK + start, CHUNK // 2)
            for rows, raw, out in ((rows_k, raw_k, out_k), (rows_v, raw_v, out_v)):
                from_heads(raw.at[at], rows.at[b], start, CHUNK // 2, upper)
                copies.append(pltpu.make_async_copy(raw.at[at], out.at[at], sems.at[len(copies)]))
                copies[-1].start()
    for copy in copies:
        copy.wait()


def finish_own(ends, keep, arrays):
    _, heads, dim = ends.shape
    tok = 2 * BLOCK
    return pl.pallas_call(
        finish_own_kernel,
        in_specs=[NEAR] * 7,
        out_specs=[NEAR, NEAR],
        out_shape=[in_vmem(2, heads, BLOCK, dim)] * 2,
        compiler_params=params(4),
        cost_estimate=cost(4 * heads * tok * dim * dim, 8 * heads * tok * dim),
        name="finish_own",
    )(*near(ends, keep, *arrays))


def finish_other(place, rows, ends, recv, arrays):
    _, heads, dim = ends.shape
    tok = 2 * BLOCK
    shape = jax.ShapeDtypeStruct((tok, heads, dim), BF16)
    return pl.pallas_call(
        finish_other_kernel,
        in_specs=[NEAR] * 10,
        out_specs=[FAR, FAR, NEAR, NEAR],
        out_shape=[shape, shape] + [in_vmem(2, heads, BLOCK, dim)] * 2,
        input_output_aliases={1: 2, 2: 3},
        scratch_shapes=[
            pltpu.VMEM((tok, heads, dim), BF16),
            pltpu.VMEM((tok, heads, dim), BF16),
            pltpu.SemaphoreType.DMA((4 * (tok // CHUNK),)),
        ],
        compiler_params=params(8),
        cost_estimate=cost(4 * heads * tok * dim * dim, 8 * heads * tok * dim),
        name="finish_other",
    )(*near(place, *rows, ends, recv, *arrays))[:2]


def follows(value, earlier):
    return lax.optimization_barrier((value, earlier))[0]


def swap(value, axis, bit):
    count = lax.axis_size(axis)
    return lax.ppermute(value, axis, [(i, i ^ bit) for i in range(count)])


def mix(body, backward, place, arrays, shapes, name):
    def kernel(place_ref, *refs):
        bits = [is_set(place_ref, which) != backward for which in (LATE, RIGHT, LOW)]
        body(bits, refs[: len(arrays)], refs[len(arrays) :])

    return pl.pallas_call(
        kernel,
        in_specs=[NEAR] + [NEAR] * len(arrays),
        out_specs=[NEAR] * len(shapes),
        out_shape=[in_vmem(*shape) for shape in shapes],
        compiler_params=params(4),
        cost_estimate=cost(4 * 8 * HD * HD, 16 * 8 * HD * HD),
        name=name,
    )(place, *near(*arrays))


OWN, PARTNER, CHIP, ROW, CORNER = range(5)


def mix_total(bits, own, got, d_own, d_got, first, second):
    late = bits[0]
    quarter = first.shape[0]
    for h in range(2 * quarter):
        total = jnp.where(late, 1.0, d_got(h)) * own[h, :HD] + jnp.where(late, d_own(h), 1.0) * got[h, :HD]
        if h < quarter:
            first[h, :HD] = total
        else:
            second[h - quarter] = total


def mix_total_first(bits, arrays, outputs):
    own, got = arrays
    first, second, chip = outputs
    quarter = first.shape[0]
    d_own = lambda h: own[h, HD : HD + 1]
    d_got = lambda h: got[h, HD : HD + 1]
    mix_total(bits, own, got, d_own, d_got, first, second)
    for h in range(2 * quarter):
        whole = d_own(h) * d_got(h)
        chip[h : h + 1] = whole
        place = HD + (TILE // 2) * (h // quarter)
        first[h % quarter, place : place + TILE // 2] = jnp.broadcast_to(whole, (TILE // 2, HD))


def mix_total_again(bits, arrays, outputs):
    table, own, got = arrays
    decay = lambda which: lambda h: table[which, h : h + 1]
    mix_total(bits, own, got, decay(OWN), decay(PARTNER), *outputs)


def mix_next_row(bits, chip, row, total, got, out):
    right = bits[1]
    for i in range(out.shape[0]):
        scale_total = jnp.where(right, 1.0, row(i))
        scale_got = jnp.where(right, chip(i), 1.0)
        out[i] = scale_total * total[i, :HD] + scale_got * got[i, :HD]


def mix_next_column(bits, chip, corner, total, got, out):
    _, right, low = bits
    for i in range(out.shape[0]):
        scale_total = jnp.where(low & right, 0.0, 1.0)
        scale_got = jnp.where(low, jnp.where(right, 1.0, chip(i) * corner(i)), 0.0)
        out[i] = scale_total * total[i] + scale_got * got[i]


def lines(ref, first=0):
    return lambda i: ref[first + i : first + i + 1]


def mix_next_row_first(bits, arrays, outputs):
    chip, total, got = arrays
    mix_next_row(bits, lines(chip), lambda i: got[i, HD : HD + 1], total, got, *outputs)


def mix_next_column_first(bits, arrays, outputs):
    own, got, chip, corner, one_a, total, one_b = arrays
    out, table = outputs
    quarter = total.shape[0]
    for h in range(2 * quarter):
        place = HD + (TILE // 2) * (h // quarter)
        table[OWN, h : h + 1] = own[h, HD : HD + 1]
        table[PARTNER, h : h + 1] = got[h, HD : HD + 1]
        table[ROW, h : h + 1] = one_a[h % quarter, place : place + 1]
    table[CHIP] = chip[...]
    table[CORNER] = corner[...]
    mix_next_column(bits, lines(chip, quarter), lines(corner, quarter), total, one_b, out)


def mix_next_row_again(bits, arrays, outputs):
    table, total, got = arrays
    mix_next_row(bits, lines(table.at[CHIP]), lines(table.at[ROW]), total, got, *outputs)


def mix_next_column_again(bits, arrays, outputs):
    table, total, got = arrays
    quarter = total.shape[0]
    chip, corner = (lines(table.at[which], quarter) for which in (CHIP, CORNER))
    mix_next_column(bits, chip, corner, total, got, *outputs)


def mix_enter(bits, arrays, outputs):
    table, own, got, one_a, one_b, two_a, two_b = arrays
    kept, sent = outputs
    late, right, low = bits
    quarter = one_b.shape[0]
    decay = lambda which, h: table[which, h : h + 1]
    for h in range(2 * quarter):
        i = h % quarter
        row = jnp.where(right, decay(ROW, h), 1.0)
        if h < quarter:
            one, two = one_a[i, :HD], two_a[i]
            scale_one = jnp.where(right, 1.0, 0.0)
            scale_two = jnp.where(low, row, 0.0)
        else:
            one, two = one_b[i], two_b[i]
            scale_one = jnp.where(low, jnp.where(right, row, decay(CORNER, h)), 0.0)
            scale_two = jnp.where(low | right, 1.0, 0.0)
        enter = scale_one * one + scale_two * two
        after = jnp.where(late, decay(PARTNER, h), decay(OWN, h)) * enter
        after += jnp.where(late, got[h, :HD], own[h, :HD])
        kept[h] = jnp.where(late, after, enter)
        sent[h] = jnp.where(late, enter, after)


def entering_quad(send, own_task, table, place, backward, tasks):
    def work(stage, after, before=()):
        if stage not in tasks:
            return before
        run, outputs = tasks[stage]
        outputs.extend(run(after))
        return lax.optimization_barrier((before, outputs[0]))[0]

    name = "later" if backward else "earlier"
    half = send.shape[0]
    quarter = half // 2
    states, wide = (quarter, HD, HD), (quarter, HD + TILE, HD)
    got = swap(send, "seq", 1)
    own = own_task(send)
    if table is None:
        first, second, chip = mix(
            mix_total_first, backward, place, (own, got), (wide, states, (half, HD)), name + "_total"
        )
    else:
        first, second = mix(
            mix_total_again, backward, place, (table, own, got), (states, states), name + "_total"
        )
    one_a, one_b = swap(first, "seq", 2), swap(second, "seq", 4)
    if table is None:
        corner = swap(chip, "seq", 6)
        one_a, one_b, corner = work(1, second, (one_a, one_b, corner))
        (next_a,) = mix(
            mix_next_row_first, backward, place, (chip, first, one_a), (states,), name + "_row"
        )
        one_b, corner = follows((one_b, corner), next_a)
        next_b, table = mix(
            mix_next_column_first, backward, place,
            (own, got, chip, corner, one_a, second, one_b), (states, (5, half, HD)),
            name + "_column",
        )
    else:
        one_a, one_b = work(1, second, (one_a, one_b))
        (next_a,) = mix(
            mix_next_row_again, backward, place, (table, first, one_a), (states,), name + "_row"
        )
        (next_b,) = mix(
            mix_next_column_again, backward, place, (table, second, follows(one_b, next_a)),
            (states,), name + "_column",
        )
    two_a, two_b = swap(next_a, "seq", 4), swap(next_b, "seq", 2)
    two_a, two_b = work(2, next_b, (two_a, two_b))
    kept, sent = mix(
        mix_enter, backward, place, (table, own, got, one_a, one_b, two_a, two_b),
        ((half, HD, HD), (half, HD, HD)), name + "_enter",
    )
    received = swap(sent, "seq", 1)
    received = follows(received, tasks[3](follows(kept, sent)))
    return kept, received, table


def entering_any(send, own_task, log_total, backward, tasks):
    own = own_task(send)
    for stage in (1, 2):
        run, outputs = tasks[stage]
        outputs.extend(run(send))
    count, mine = lax.axis_size("seq"), lax.axis_index("seq")
    core = mine % 2
    own, send = own[:, :HD], send[:, :HD]
    half = own.shape[0]
    in_order = jnp.where(
        core == 0, jnp.concatenate([own, send], axis=0), jnp.concatenate([send, own], axis=0)
    )
    states = lax.all_gather(in_order, "seq")
    decays = jnp.exp(lax.all_gather(log_total, "seq"))
    place = mine
    if backward:
        states, decays, place = states[::-1], decays[::-1], count - 1 - mine

    def step(at, total):
        longer = decays[at][:, None, None] * total + states[at]
        return jnp.where(at < place, longer, total)

    total = lax.fori_loop(0, count - 1, step, jnp.zeros_like(in_order))
    kept = lax.dynamic_slice_in_dim(total, core * half, half)
    tasks[3](kept)
    return kept, lax.dynamic_slice_in_dim(total, (1 - core) * half, half)


def add(first, second):
    def kernel(first_ref, second_ref, out_ref):
        out_ref[...] = first_ref[...] + second_ref[...]

    return pl.pallas_call(
        kernel,
        in_specs=[NEAR, NEAR],
        out_specs=NEAR,
        out_shape=in_vmem(*first.shape),
        compiler_params=params(2),
        name="add",
    )(*near(first, second))


def sum_over_heads(value, tasks):
    tasks = list(tasks)
    results = []
    count = lax.axis_size("head")
    reach = 1
    while 2 * reach <= count and count % (2 * reach) == 0:
        got = swap(value, "head", reach)
        if tasks:
            results.append(tasks.pop(0)(value))
            got = follows(got, results[-1])
        value = add(value, got)
        reach *= 2
    results += [task(value) for task in tasks]
    part = value
    for shift in range(1, count // reach):
        value = add(
            value,
            lax.ppermute(part, "head", [(i, (i + shift * reach) % count) for i in range(count)]),
        )
    return value, results


def on_device(query_rows, key_rows, value_rows, output_grad, norm_gain, log_decay):
    mine = lax.axis_index("seq")
    bits = [(mine >> at) % 2 for at in range(3)]
    marks = [1 - bits[0], bits[0], *bits] + [jnp.zeros_like(mine)] * (TILE - 5)
    place = jnp.broadcast_to(jnp.stack(marks).astype(F32)[:, None], (TILE, HD))
    table = [None]

    def entering(send, own_task, backward, tasks):
        if lax.axis_size("seq") != 8:
            log_total = jnp.sum(log_decay, axis=1)
            return entering_any(send, own_task, log_total, backward, tasks)
        kept, received, table[0] = entering_quad(
            send, own_task, table[0], place, backward, tasks
        )
        return kept, received

    send, first_send, kh, vh, cum, _, decay, gain = state_to_send(
        place, norm_gain, log_decay, key_rows, value_rows
    )
    firsts, raws, in_0, in_1, begun = [], [], [], [], []

    def own_task(earlier):
        own, first, *raw = own_state(
            follows(kh, earlier), vh, cum, decay, query_rows, output_grad
        )
        firsts.extend((first, first_send))
        raws.append(raw)
        return own

    def forward_task(index):
        def task(earlier):
            *made, q_next, o_next = [
                *intra(
                    index, place, follows(cum, earlier), kh, vh, *firsts, raws[-1],
                    query_rows, output_grad,
                ),
                *raws[-1] * index,
            ]
            raws.append([q_next, o_next])
            return made

        return task

    def parts():
        q0, o0, _, _, columns0, inner0 = in_0
        q1, o1, _, _, columns1, inner1 = in_1
        return q0, q1, o0, o1, columns0, columns1, inner0, inner1

    def attend_task(kept):
        begun.extend(attend(0, gain, kept, parts()))
        return begun[-1]

    keep, recv = entering(
        send, own_task, False, {1: (forward_task(0), in_0), 2: (forward_task(1), in_1), 3: attend_task}
    )
    q0, o0, w0, decays0, columns0, _ = in_0
    q1, o1, w1, decays1, columns1, _ = in_1
    own_att = begun[:2]
    *other_att, sums = attend(1, gain, recv, parts(), begun[2:])
    sums, ((scaled, ends), remaining) = sum_over_heads(
        sums,
        (
            lambda earlier: scaled_queries(cum, follows(q0, earlier), q1),
            lambda earlier: remaining_decay(follows(cum, earlier)),
        ),
    )
    grad_send, second_send, *other_g = norm_grad(1, ends, gain, sums, scaled, (o0, o1, *other_att))
    own_g, seconds, queries, pairs, rows = [], [], [], [], []

    def own_grad_task(earlier):
        own, second, *grads = norm_grad(
            0, ends, gain, follows(sums, earlier), scaled, (o0, o1, *own_att)
        )
        own_g.extend(grads)
        seconds.extend((second, second_send))
        return own

    def query_task(earlier):
        return grad_query(
            place, gain, sums, (*own_att, *other_att), follows(ends, earlier),
            (keep, recv, *firsts, kh, vh, *own_g, *other_g, decays0, decays1, columns0, columns1),
        )

    def pair_task(earlier):
        return grad_key_value(
            place, queries[1], w0, w1, q0, q1, kh, vh, *own_g, *other_g, remaining,
            follows(seconds[0], earlier), seconds[1], queries[0],
        )

    def finish_task(kept):
        rows.extend(finish_own(ends, kept, (kh, vh, remaining, *pairs[:2])))
        return rows[-1]

    _, grad_recv = entering(
        grad_send, own_grad_task, True,
        {1: (query_task, queries), 2: (pair_task, pairs), 3: finish_task},
    )
    grad_k, grad_v = finish_other(
        place, rows, ends, grad_recv, (kh, vh, remaining, *pairs[:2])
    )
    return queries[2], pairs[2], grad_k, grad_v


def solution(mesh):
    rows = P("seq", "head", None)
    return jax.shard_map(
        on_device,
        mesh=mesh,
        in_specs=(rows, rows, rows, rows, P("head", None), P("head", "seq")),
        out_specs=(rows, rows, rows, rows),
        check_vma=False,
    )
```

```python
import functools

import jax
import jax.numpy as jnp
from jax import lax
from jax.experimental import pallas as pl
from jax.experimental.pallas import tpu as pltpu
from jax.sharding import PartitionSpec as P

HEAD_TOTAL = 64
HD = 128
BLOCK = 256
CHUNK = 128
TILE = 8
F32 = jnp.float32
BF16 = jnp.bfloat16
MIB = 1024 * 1024
NEAR = pl.BlockSpec(memory_space=pltpu.VMEM)
FAR = pl.BlockSpec(memory_space=pl.ANY)
LOWER, UPPER, LATE, RIGHT, LOW = range(5)


def in_vmem(*shape, kind=F32):
    return pltpu.VMEM(shape, kind)


def near(*arrays):
    return [pltpu.with_memory_space_constraint(array, pltpu.VMEM) for array in arrays]


def far(*arrays):
    return [pltpu.with_memory_space_constraint(array, pltpu.HBM) for array in arrays]


def params(mib):
    return pltpu.CompilerParams(vmem_limit_bytes=mib * MIB)


def cost(flops, moved, exps=0):
    return pl.CostEstimate(flops=flops, bytes_accessed=moved, transcendentals=exps)


def block_cum(log_decay):
    size = log_decay.shape[1]
    upper = lax.broadcasted_iota(jnp.int32, (size, size), 0) <= lax.broadcasted_iota(
        jnp.int32, (size, size), 1
    )
    return jnp.dot(
        log_decay,
        jnp.where(upper, 1.0, 0.0).astype(F32),
        precision=lax.Precision.HIGHEST,
        preferred_element_type=F32,
    )


def as_columns(row):
    return jnp.broadcast_to(row, (HD, row.shape[1])).T


def dot(a, b):
    return jnp.dot(a, b, preferred_element_type=F32)


def dot_rows(a, b):
    return lax.dot_general(a, b, (((1,), (1,)), ((), ())), preferred_element_type=F32)


def two_parts(matrix):
    high = matrix.astype(BF16)
    return high, (matrix - high.astype(F32)).astype(BF16)


def times_state(rows, state):
    return dot(jnp.concatenate([rows, rows], axis=1), jnp.concatenate(two_parts(state), axis=0))


def times_state_t(rows, state):
    return dot_rows(
        jnp.concatenate([rows, rows], axis=1), jnp.concatenate(two_parts(state), axis=1)
    )


def decay_quarters(row, columns):
    half = row.shape[1] // 2
    lower = lax.broadcasted_iota(jnp.int32, (half, half), 0) >= lax.broadcasted_iota(
        jnp.int32, (half, half), 1
    )
    quarters = []
    for t, s in ((0, 0), (1, 0), (1, 1)):
        gap = columns[t * half : (t + 1) * half] - row[:, s * half : (s + 1) * half]
        quarters.append(jnp.exp(jnp.where(lower, gap, -jnp.inf) if t == s else gap))
    return quarters


def causal(table, quarters):
    half = table.shape[0] // 2
    first, second, third = (
        (table[t * half : (t + 1) * half, s * half : (s + 1) * half] * quarter).astype(BF16)
        for (t, s), quarter in zip(((0, 0), (1, 0), (1, 1)), quarters)
    )
    top = jnp.concatenate([first, jnp.zeros_like(first)], axis=1)
    return jnp.concatenate([top, jnp.concatenate([second, third], axis=1)], axis=0)


def transposed_dot(a, b):
    return lax.dot_general(a, b, (((0,), (0,)), ((), ())), preferred_element_type=F32)


def each_head(heads, unroll, body):
    def step(h, carry):
        body(h)
        return carry

    lax.fori_loop(0, heads, step, 0, unroll=unroll)


def each_half(half, unroll, body):
    for part in range(2):
        each_head(half, unroll, lambda i, part=part: body(part, i, part * half + i))


def turn_tiles(tiles):
    count = len(tiles)
    at = lax.broadcasted_iota(jnp.int32, tiles[0].shape, 0)
    turned = [tile if i == 0 else pltpu.roll(tile, i, 0) for i, tile in enumerate(tiles)]
    reach = 1
    while reach < count:
        odd = (at & reach) != 0
        turned = [
            jnp.where(odd, turned[(n + reach) % count], turned[n]) for n in range(count)
        ]
        reach *= 2
    picked = [turned[-j % count] for j in range(count)]
    return [tile if j == 0 else pltpu.roll(tile, count - j, 0) for j, tile in enumerate(picked)]


def is_upper(place_ref):
    return jnp.max(place_ref[UPPER : UPPER + 1]) > 0.5


def to_heads(dst, block, upper):
    tok, heads, _ = block.shape

    def step(group, carry):
        at = pl.multiple_of(group * 2 * TILE, 2 * TILE)
        tokens = block[pl.ds(at, 2 * TILE)].astype(F32)
        for first in range(0, heads, TILE):
            halves = [
                turn_tiles([tokens[base + i, first : first + TILE] for i in range(TILE)])
                for base in (0, TILE)
            ]
            local = jnp.where(upper, heads - TILE - first, first)
            for j in range(TILE):
                both = jnp.concatenate([halves[0][j], halves[1][j]], axis=0)
                dst[local + j, pl.ds(at, 2 * TILE)] = both.astype(BF16)
        return carry

    lax.fori_loop(0, tok // (2 * TILE), step, 0, unroll=4)


def from_heads(block, src, start, tok, upper):
    heads = src.shape[0]

    def step(group, carry):
        at = pl.multiple_of(group * TILE, TILE)
        parts = []
        for first in range(0, heads, TILE):
            local = jnp.where(upper, heads - TILE - first, first)
            parts.append(turn_tiles([src[local + i, pl.ds(start + at, TILE)] for i in range(TILE)]))
        for j in range(TILE):
            block[at + j] = jnp.concatenate([part[j] for part in parts], axis=0).astype(BF16)
        return carry

    lax.fori_loop(0, tok // TILE, step, 0, unroll=4)


def is_set(place_ref, which):
    return place_ref[which : which + 1] > 0.5


def in_local_order(place_ref, rows):
    half = rows.shape[0] // 2
    lower, upper = rows[:half], rows[half:]
    mine = jnp.broadcast_to(place_ref[LOWER : LOWER + 1, :1], lower.shape) > 0.5
    return jnp.concatenate(
        [jnp.where(mine, lower, upper), jnp.where(mine, upper, lower)], axis=0
    )


def half_states(part, kh, vh, cum, b, out, first=None):
    half = kh.shape[1] // 2

    def one(i):
        h = part * half + i
        row = cum[b, pl.ds(h, 1), :]
        scale = jnp.exp(row[:, BLOCK - 1 :] - row)
        state = dot((kh[b, h].astype(F32).T * scale).astype(BF16), vh[b, h])
        if first is not None:
            state += jnp.exp(row[:, BLOCK - 1 :]) * first[i]
        out[i, :HD] = state

    each_head(half, 4, one)


def add_decays(out, decay, part):
    half = out.shape[0]
    for i in range(half):
        out[i, HD:] = jnp.broadcast_to(decay[part * half + i : part * half + i + 1], (TILE, HD))


def state_kernel(
    place_ref, gain_hbm, ld_hbm, k_hbm, v_hbm, send_ref, first_ref, kh, vh, cum, ld_ref, decay,
    gain_ref, gain_raw, ld_raw, k_raw, v_raw, sems,
):
    heads, tok = ld_ref.shape
    per_block = BLOCK // CHUNK
    copies = [pltpu.make_async_copy(ld_hbm, ld_raw, sems.at[0])]
    for c in range(tok // CHUNK):
        at = pl.ds(c * CHUNK, CHUNK)
        copies.append(pltpu.make_async_copy(k_hbm.at[at], k_raw.at[at], sems.at[2 * c + 1]))
        copies.append(pltpu.make_async_copy(v_hbm.at[at], v_raw.at[at], sems.at[2 * c + 2]))
    copies.append(pltpu.make_async_copy(gain_hbm, gain_raw, sems.at[len(copies)]))
    early = 1 + 2 * per_block
    for copy in copies[:early]:
        copy.start()
    upper = is_upper(place_ref)
    copies[0].wait()
    ld_ref[...] = in_local_order(place_ref, ld_raw[...])
    for b in range(2):
        cum[b] = block_cum(ld_ref[:, b * BLOCK : (b + 1) * BLOCK])
    ends = cum[0, :, BLOCK - 1 :] + cum[1, :, BLOCK - 1 :]
    decay[...] = jnp.broadcast_to(jnp.exp(ends), decay.shape)

    for b in range(2):
        for c in range(per_block):
            at = pl.ds((b * per_block + c) * CHUNK, CHUNK)
            here = pl.ds(c * CHUNK, CHUNK)
            which = 2 * (b * per_block + c) + 1
            copies[which].wait()
            if which == 1:
                for copy in copies[early:]:
                    copy.start()
            to_heads(kh.at[b, :, here], k_raw.at[at], upper)
            copies[which + 1].wait()
            to_heads(vh.at[b, :, here], v_raw.at[at], upper)
        if b == 0:
            half_states(1, kh, vh, cum, 0, first_ref)
        else:
            half_states(1, kh, vh, cum, 1, send_ref, first_ref)
    add_decays(send_ref, decay, 1)
    copies[-1].wait()
    gain_ref[...] = in_local_order(place_ref, gain_raw[...])


def state_to_send(place, gain, log_decay, key_rows, value_rows):
    tok, heads, dim = key_rows.shape
    half = heads // 2
    by_head = in_vmem(2, heads, BLOCK, dim, kind=BF16)
    return pl.pallas_call(
        state_kernel,
        in_specs=[NEAR, FAR, FAR, FAR, FAR],
        out_specs=[NEAR] * 8,
        out_shape=[
            in_vmem(half, dim + TILE, dim), in_vmem(half, dim, dim), by_head, by_head,
            in_vmem(2, heads, BLOCK), in_vmem(heads, tok), in_vmem(heads, dim), in_vmem(heads, dim),
        ],
        scratch_shapes=[
            pltpu.VMEM((heads, dim), F32),
            pltpu.VMEM((heads, tok), F32),
            pltpu.VMEM((tok, heads, dim), BF16),
            pltpu.VMEM((tok, heads, dim), BF16),
            pltpu.SemaphoreType.DMA((2 * (tok // CHUNK) + 2,)),
        ],
        compiler_params=params(8),
        cost_estimate=cost(tok * heads * dim * dim, 8 * tok * heads * dim),
        name="state_to_send",
    )(place, *far(gain, log_decay, key_rows, value_rows))


def fetch_block(index, arrays, blocks, sems):
    copies = [
        pltpu.make_async_copy(array.at[pl.ds(index * BLOCK, BLOCK)], block, sems.at[at])
        for at, (array, block) in enumerate(zip(arrays, blocks))
    ]
    for copy in copies:
        copy.start()
    return copies


def own_state_kernel(
    kh, vh, cum, decay, q_hbm, o_hbm, own_ref, first_ref, q_raw, o_raw, sems
):
    copies = fetch_block(0, (q_hbm, o_hbm), (q_raw, o_raw), sems)
    half_states(0, kh, vh, cum, 0, first_ref)
    half_states(0, kh, vh, cum, 1, own_ref, first_ref)
    add_decays(own_ref, decay, 0)
    for copy in copies:
        copy.wait()


def own_state(kh, vh, cum, decay, query_rows, output_grad):
    _, heads, tok, dim = kh.shape
    half = heads // 2
    raw = in_vmem(BLOCK, heads, dim, kind=BF16)
    return pl.pallas_call(
        own_state_kernel,
        in_specs=[NEAR] * 4 + [FAR, FAR],
        out_specs=[NEAR] * 4,
        out_shape=[in_vmem(half, dim + TILE, dim), in_vmem(half, dim, dim), raw, raw],
        scratch_shapes=[pltpu.SemaphoreType.DMA((2,))],
        compiler_params=params(4),
        cost_estimate=cost(2 * tok * heads * dim * dim, 4 * tok * heads * dim),
        name="own_state",
    )(*near(kh, vh, cum, decay), *far(query_rows, output_grad))


def intra(index, place, cum, kh, vh, first_own, first_send, raw, query_rows, output_grad):
    tok, heads, dim = query_rows.shape
    ahead = index == 0

    def kernel(place_ref, cum, kh, vh, first_own, first_send, q_raw, o_raw, *refs):
        if ahead:
            q_hbm, o_hbm, *refs = refs
            *refs, q_next, o_next, sems = refs
            copies = fetch_block(1, (q_hbm, o_hbm), (q_next, o_next), sems)
        qh, oh, w_ref, decays_ref, columns_ref, inner_ref = refs
        upper = is_upper(place_ref)
        to_heads(qh, q_raw, upper)
        to_heads(oh, o_raw, upper)

        def one(part, i, h):
            query = qh[h]
            row = cum[index, pl.ds(h, 1), :]
            columns = as_columns(row)
            quarters = decay_quarters(row, columns)
            for at, quarter in enumerate(quarters):
                decays_ref[h, at] = quarter
            weights = causal(dot_rows(query, kh[index, h]), quarters)
            w_ref[h] = weights.T
            inner = dot(weights, vh[index, h])
            columns = jnp.exp(columns)
            columns_ref[h] = columns
            if index:
                inner += columns * times_state(query, (first_own, first_send)[part][i])
            inner_ref[h] = inner

        each_half(heads // 2, 4, one)
        if ahead:
            for copy in copies:
                copy.wait()

    by_head = in_vmem(heads, BLOCK, dim, kind=BF16)
    return pl.pallas_call(
        kernel,
        in_specs=[NEAR] * 8 + [FAR, FAR] * ahead,
        out_specs=[NEAR] * (6 + 2 * ahead),
        out_shape=[
            by_head, by_head, in_vmem(heads, BLOCK, BLOCK, kind=BF16),
            in_vmem(heads, 3, BLOCK // 2, BLOCK // 2), in_vmem(heads, BLOCK, dim),
            in_vmem(heads, BLOCK, dim),
        ]
        + [in_vmem(BLOCK, heads, dim, kind=BF16)] * (2 * ahead),
        scratch_shapes=[pltpu.SemaphoreType.DMA((2,))] * ahead,
        compiler_params=params(4),
        cost_estimate=cost(
            2 * heads * BLOCK * BLOCK * dim * 4, 20 * heads * BLOCK * dim, heads * BLOCK * BLOCK
        ),
        name=f"intra_{index}",
    )(
        *near(place, cum, kh, vh, first_own, first_send, *raw),
        *(far(query_rows, output_grad) if ahead else ()),
    )


def attend_kernel(part, *refs):
    gain_ref, state_ref, q0, q1, o0, o1, columns0, columns1, inner0, inner1 = refs[:10]
    half = state_ref.shape[0]
    if part:
        before, att0, att1, sums_ref, partial = refs[10:]
        partial[...] = before[...]
    else:
        att0, att1, partial = refs[10:]
        partial[...] = jnp.zeros_like(partial)

    def one(i):
        h = part * half + i
        state = state_ref[i]
        gain = gain_ref[pl.ds(h, 1), :]
        blocks = ((q0, o0, columns0, inner0, att0), (q1, o1, columns1, inner1, att1))
        for b, (q, o, columns, inner, att) in enumerate(blocks):
            attended = inner[h] + columns[h] * times_state(q[h], state)
            att[i] = attended
            partial[0, b] += attended * attended
            partial[1, b] += gain * o[h].astype(F32) * attended
            state = columns[h, BLOCK - 1 :] * state

    each_head(half, 4, one)
    if part:
        ones = jnp.ones((8, HD), F32)
        for b in range(2):
            for at in range(2):
                line = lax.dot_general(
                    ones, partial[at, b], (((1,), (1,)), ((), ())),
                    precision=lax.Precision.HIGHEST, preferred_element_type=F32,
                )
                sums_ref[at : at + 1, b * BLOCK : (b + 1) * BLOCK] = line[:1]


def attend(part, gain, state, arrays, before=()):
    heads, dim = gain.shape
    tok = 2 * BLOCK
    half = heads // 2
    by_head = in_vmem(half, BLOCK, dim)
    partial = (2, 2, BLOCK, dim)
    return pl.pallas_call(
        functools.partial(attend_kernel, part),
        in_specs=[NEAR] * (10 + part),
        out_specs=[NEAR] * 3,
        out_shape=[by_head, by_head, in_vmem(2, tok) if part else in_vmem(*partial)],
        scratch_shapes=[pltpu.VMEM(partial, F32)] * part,
        compiler_params=params(6),
        cost_estimate=cost(2 * heads * tok * dim * dim, 8 * heads * tok * dim),
        name=f"attend_{part}",
    )(*near(gain, state, *arrays, *before))


def scaled_queries(cum, q0, q1):
    _, heads, _ = cum.shape

    def kernel(cum_ref, q0, q1, out_ref, ends_ref):
        for b in range(2):
            ends_ref[b] = jnp.broadcast_to(jnp.exp(cum_ref[b, :, BLOCK - 1 :]), (heads, HD))

        def one(h):
            for b, q in enumerate((q0, q1)):
                scale = jnp.exp(cum_ref[b, pl.ds(h, 1), :])
                out_ref[b, h] = (q[h].astype(F32).T * scale).astype(BF16)

        each_head(heads, 4, one)

    return pl.pallas_call(
        kernel,
        in_specs=[NEAR] * 3,
        out_specs=[NEAR] * 2,
        out_shape=[in_vmem(2, heads, HD, BLOCK, kind=BF16), in_vmem(2, heads, HD)],
        compiler_params=params(4),
        cost_estimate=cost(4 * heads * BLOCK * HD, 8 * heads * BLOCK * HD),
        name="scaled_queries",
    )(*near(cum, q0, q1))


def remaining_decay(cum):
    _, heads, _ = cum.shape

    def kernel(cum_ref, out_ref):
        def one(h):
            for b in range(2):
                row = cum_ref[b, pl.ds(h, 1), :]
                out_ref[b, h] = as_columns(jnp.exp(row[:, BLOCK - 1 :] - row))

        each_head(heads, 4, one)

    return pl.pallas_call(
        kernel,
        in_specs=[NEAR],
        out_specs=NEAR,
        out_shape=in_vmem(2, heads, BLOCK, HD),
        compiler_params=params(4),
        cost_estimate=cost(2 * heads * BLOCK * HD, 8 * heads * BLOCK * HD),
        name="remaining_decay",
    )(*near(cum))


def inverse_rms(sums_ref, b):
    at = slice(b * BLOCK, (b + 1) * BLOCK)
    inv = lax.rsqrt(sums_ref[0:1, at] / (HEAD_TOTAL * HD) + 1e-06)
    mean = sums_ref[1:2, at] * inv / (HEAD_TOTAL * HD)
    return inv, mean


def norm_grad(part, ends, gain, sums, scaled, arrays):
    heads, dim = gain.shape
    tok = 2 * BLOCK
    half = heads // 2

    def kernel(ends_ref, gain_ref, sums_ref, queries_ref, o0, o1, att0, att1,
               out_ref, second_ref, g0, g1, scales):
        for b in range(2):
            inv, mean = inverse_rms(sums_ref, b)
            scales[b, 0] = as_columns(inv)
            scales[b, 1] = as_columns(inv * inv * mean)

        def one(i):
            h = part * half + i
            line = gain_ref[pl.ds(h, 1), :]
            starts = []
            for b, (o, att, g) in enumerate(((o0, att0, g0), (o1, att1, g1))):
                grad = line * o[h].astype(F32) * scales[b, 0] - att[i] * scales[b, 1]
                grad = grad.astype(BF16)
                g[i] = grad
                starts.append(dot(queries_ref[b, h], grad))
            second_ref[i] = starts[1]
            out_ref[i] = starts[0] + ends_ref[0, pl.ds(h, 1)] * starts[1]

        each_head(half, 4, one)

    by_head = in_vmem(half, BLOCK, dim, kind=BF16)
    return pl.pallas_call(
        kernel,
        in_specs=[NEAR] * 8,
        out_specs=[NEAR] * 4,
        out_shape=[in_vmem(half, dim, dim), in_vmem(half, dim, dim), by_head, by_head],
        scratch_shapes=[pltpu.VMEM((2, 2, BLOCK, dim), F32)],
        compiler_params=params(4),
        cost_estimate=cost(heads * tok * dim * dim, 7 * heads * tok * dim),
        name=f"norm_grad_{part}",
    )(*near(ends, gain, sums, scaled, *arrays))


def normed_block(b, place_ref, gain_ref, sums_ref, halves, rows, raw):
    inv = as_columns(inverse_rms(sums_ref, b)[0])

    def one(part, i, h):
        rows[b, h] = halves[part][i] * inv * gain_ref[pl.ds(h, 1), :]

    each_half(halves[0].shape[0], 4, one)
    from_heads(raw, rows.at[b], 0, BLOCK, is_upper(place_ref))


def grad_q_kernel(
    place_ref, gain_ref, sums_ref, att_own0, att_own1, att_other0, att_other1,
    ends_ref, keep_ref, recv_ref, first_own, first_send, kh, vh, own0, own1, other0, other1,
    decays0, decays1, columns0, columns1, rows, gs_ref, out_normed, raw, sems,
):
    copies = []
    for b, halves in enumerate(((att_own0, att_other0), (att_own1, att_other1))):
        at = pl.ds(b * BLOCK, BLOCK)
        normed_block(b, place_ref, gain_ref, sums_ref, halves, rows, raw.at[at])
        copies.append(pltpu.make_async_copy(raw.at[at], out_normed.at[at], sems.at[b]))
        copies[-1].start()
    blocks = (((own0, other0), decays0, columns0), ((own1, other1), decays1, columns1))
    for b, (g, decays, columns) in enumerate(blocks):

        def one(part, i, h, b=b, g=g, decays=decays, columns=columns):
            grad = g[part][i]
            scores = causal(dot_rows(grad, vh[b, h]), [decays[h, at] for at in range(3)])
            gs_ref[b, h] = scores
            state = (keep_ref, recv_ref)[part][i]
            if b:
                state = ends_ref[0, pl.ds(h, 1)] * state + (first_own, first_send)[part][i]
            rows[b, h] = dot(scores, kh[b, h]) + columns[h] * times_state_t(grad, state)

        each_half(keep_ref.shape[0], 4, one)
    for copy in copies:
        copy.wait()


def grad_query(place, gain, sums, att, ends, arrays):
    _, heads, dim = ends.shape
    tok = 2 * BLOCK
    return pl.pallas_call(
        grad_q_kernel,
        in_specs=[NEAR] * 22,
        out_specs=[NEAR, NEAR, FAR],
        out_shape=[
            in_vmem(2, heads, BLOCK, dim), in_vmem(2, heads, BLOCK, BLOCK, kind=BF16),
            jax.ShapeDtypeStruct((tok, heads, dim), BF16),
        ],
        scratch_shapes=[
            pltpu.VMEM((tok, heads, dim), BF16),
            pltpu.SemaphoreType.DMA((2,)),
        ],
        compiler_params=params(6),
        cost_estimate=cost(
            4 * heads * tok * dim * (BLOCK + dim), 12 * heads * tok * dim, heads * tok * BLOCK
        ),
        name="grad_query",
    )(*near(place, gain, sums, *att, ends, *arrays))


def grad_kv_kernel(
    place_ref, gs_ref, w0, w1, q0, q1, kh, vh, own0, own1, other0, other1, remaining_ref,
    second_own, second_send, rows, dk, dv, out_q, raw, sems,
):
    upper = is_upper(place_ref)
    copies = []
    for b in range(2):
        for start in range(0, BLOCK, CHUNK):
            at = pl.ds(b * BLOCK + start, CHUNK)
            from_heads(raw.at[at], rows.at[b], start, CHUNK, upper)
            copies.append(pltpu.make_async_copy(raw.at[at], out_q.at[at], sems.at[len(copies)]))
            copies[-1].start()

    def one(part, i, h):
        columns = remaining_ref[0, h]
        state = (second_own, second_send)[part][i]
        g0, g1 = ((own0, own1), (other0, other1))[part]
        dk[0, h] = transposed_dot(gs_ref[0, h], q0[h]) + columns * times_state_t(vh[0, h], state)
        dv[0, h] = dot(w0[h], g0[i]) + columns * times_state(kh[0, h], state)
        dk[1, h] = transposed_dot(gs_ref[1, h], q1[h])
        dv[1, h] = dot(w1[h], g1[i])

    each_half(second_own.shape[0], 2, one)
    for copy in copies:
        copy.wait()


def grad_key_value(*arrays):
    _, heads, _, dim = arrays[6].shape
    tok = 2 * BLOCK
    return pl.pallas_call(
        grad_kv_kernel,
        in_specs=[NEAR] * 16,
        out_specs=[NEAR, NEAR, FAR],
        out_shape=[in_vmem(2, heads, BLOCK, dim)] * 2
        + [jax.ShapeDtypeStruct((tok, heads, dim), BF16)],
        scratch_shapes=[
            pltpu.VMEM((tok, heads, dim), BF16),
            pltpu.SemaphoreType.DMA((tok // CHUNK,)),
        ],
        compiler_params=params(6),
        cost_estimate=cost(4 * heads * tok * dim * (BLOCK + dim), 30 * heads * tok * dim),
        name="grad_key_value",
    )(*near(*arrays))


def finish_rows(part, b, ends_ref, state_ref, kh, vh, remaining_ref, dk, dv, rows_k, rows_v):
    half = state_ref.shape[0]

    def one(i):
        h = part * half + i
        columns = remaining_ref[b, h]
        state = state_ref[i]
        if b == 0:
            state = ends_ref[1, pl.ds(h, 1)] * state
        state = state.astype(BF16)
        none = jnp.zeros_like(state)
        both = jnp.concatenate(
            [jnp.concatenate([state.T, none], axis=1), jnp.concatenate([none, state], axis=1)],
            axis=0,
        )
        carried = dot(jnp.concatenate([vh[b, h], kh[b, h]], axis=1), both)
        rows_k[b, h] = dk[b, h] + columns * carried[:, :HD]
        rows_v[b, h] = dv[b, h] + columns * carried[:, HD:]

    each_head(half, 4, one)


def finish_own_kernel(*refs):
    for b in range(2):
        finish_rows(0, b, *refs)


def finish_other_kernel(
    place_ref, old_k, old_v, ends_ref, state_ref, kh, vh, remaining_ref, dk, dv,
    out_k, out_v, rows_k, rows_v, raw_k, raw_v, sems,
):
    upper = is_upper(place_ref)
    copies = []
    for b in range(2):
        finish_rows(1, b, ends_ref, state_ref, kh, vh, remaining_ref, dk, dv, rows_k, rows_v)
        for start in range(0, BLOCK, CHUNK // 2):
            at = pl.ds(b * BLOCK + start, CHUNK // 2)
            for rows, raw, out in ((rows_k, raw_k, out_k), (rows_v, raw_v, out_v)):
                from_heads(raw.at[at], rows.at[b], start, CHUNK // 2, upper)
                copies.append(pltpu.make_async_copy(raw.at[at], out.at[at], sems.at[len(copies)]))
                copies[-1].start()
    for copy in copies:
        copy.wait()


def finish_own(ends, keep, arrays):
    _, heads, dim = ends.shape
    tok = 2 * BLOCK
    return pl.pallas_call(
        finish_own_kernel,
        in_specs=[NEAR] * 7,
        out_specs=[NEAR, NEAR],
        out_shape=[in_vmem(2, heads, BLOCK, dim)] * 2,
        compiler_params=params(4),
        cost_estimate=cost(4 * heads * tok * dim * dim, 8 * heads * tok * dim),
        name="finish_own",
    )(*near(ends, keep, *arrays))


def finish_other(place, rows, ends, recv, arrays):
    _, heads, dim = ends.shape
    tok = 2 * BLOCK
    shape = jax.ShapeDtypeStruct((tok, heads, dim), BF16)
    return pl.pallas_call(
        finish_other_kernel,
        in_specs=[NEAR] * 10,
        out_specs=[FAR, FAR, NEAR, NEAR],
        out_shape=[shape, shape] + [in_vmem(2, heads, BLOCK, dim)] * 2,
        input_output_aliases={1: 2, 2: 3},
        scratch_shapes=[
            pltpu.VMEM((tok, heads, dim), BF16),
            pltpu.VMEM((tok, heads, dim), BF16),
            pltpu.SemaphoreType.DMA((4 * (tok // CHUNK),)),
        ],
        compiler_params=params(8),
        cost_estimate=cost(4 * heads * tok * dim * dim, 8 * heads * tok * dim),
        name="finish_other",
    )(*near(place, *rows, ends, recv, *arrays))[:2]


def follows(value, earlier):
    return lax.optimization_barrier((value, earlier))[0]


def swap(value, axis, bit):
    count = lax.axis_size(axis)
    return lax.ppermute(value, axis, [(i, i ^ bit) for i in range(count)])


def mix(body, backward, place, arrays, shapes, name):
    def kernel(place_ref, *refs):
        bits = [is_set(place_ref, which) != backward for which in (LATE, RIGHT, LOW)]
        body(bits, refs[: len(arrays)], refs[len(arrays) :])

    return pl.pallas_call(
        kernel,
        in_specs=[NEAR] + [NEAR] * len(arrays),
        out_specs=[NEAR] * len(shapes),
        out_shape=[in_vmem(*shape) for shape in shapes],
        compiler_params=params(4),
        cost_estimate=cost(4 * 8 * HD * HD, 16 * 8 * HD * HD),
        name=name,
    )(place, *near(*arrays))


OWN, PARTNER, CHIP, ROW, CORNER = range(5)


def mix_total(bits, own, got, d_own, d_got, first, second):
    late = bits[0]
    quarter = first.shape[0]
    for h in range(2 * quarter):
        total = jnp.where(late, 1.0, d_got(h)) * own[h, :HD] + jnp.where(late, d_own(h), 1.0) * got[h, :HD]
        if h < quarter:
            first[h, :HD] = total
        else:
            second[h - quarter] = total


def chosen(bits, values, at):
    _, right, low = bits
    upper, lower = (
        jnp.where(right, values[at ^ base ^ 1], values[at ^ base]) for base in (0, 2)
    )
    return jnp.where(low, lower, upper)


PIECE = 32


def mix_blocks(bits, arrays, outputs):
    own, got = arrays
    *blocks, total, table = outputs
    late = bits[0]
    half = total.shape[0]
    heads = half // 4
    for h in range(half):
        d_own, d_got = own[h, HD : HD + 1], got[h, HD : HD + 1]
        scale_own, scale_got = jnp.where(late, 1.0, d_got), jnp.where(late, d_own, 1.0)
        total[h] = scale_own * own[h, :HD] + scale_got * got[h, :HD]
        table[OWN, h : h + 1], table[PARTNER, h : h + 1] = d_own, d_got
        table[CHIP, h : h + 1] = d_own * d_got
    for at, block in enumerate(blocks):
        for i in range(heads):
            for piece in range(0, HD, PIECE):
                rows = pl.ds(piece, PIECE)
                states = [total[heads * chip + i, rows] for chip in range(4)]
                block[i, rows] = chosen(bits, states, at)
            block[i, HD:] = table[CHIP]


def mix_scan(bits, arrays, outputs):
    old, *gots = arrays
    *blocks, table = outputs
    heads = gots[0].shape[0]
    for i in range(heads):
        decays = []
        for got in gots:
            lines = [got[i, HD + heads * chip + i : HD + heads * chip + i + 1] for chip in range(4)]
            decays.append(chosen(bits, lines, 0))
        decays = [chosen(bits, decays, chip) for chip in range(4)]
        for piece in range(0, HD, PIECE):
            rows = pl.ds(piece, PIECE)
            states = [got[i, rows] for got in gots]
            enter = [jnp.zeros((PIECE, HD), F32)]
            for chip in range(3):
                enter.append(decays[chip] * enter[-1] + chosen(bits, states, chip))
            for at, block in enumerate(blocks):
                block[i, rows] = chosen(bits, enter, at)
    for which in (OWN, PARTNER, CHIP):
        table[which] = old[which]
    table[ROW], table[CORNER] = gots[1][0, HD:], gots[3][0, HD:]


def mix_enter_first(bits, arrays, outputs):
    table, own, got, *blocks = arrays
    kept, sent = outputs
    late = bits[0]
    heads = blocks[0].shape[0]
    for h in range(kept.shape[0]):
        scale = jnp.where(late, table[PARTNER, h : h + 1], table[OWN, h : h + 1])
        for piece in range(0, HD, PIECE):
            rows = pl.ds(piece, PIECE)
            enter = chosen(bits, [block[h % heads, rows] for block in blocks], h // heads)
            after = scale * enter + jnp.where(late, got[h, rows], own[h, rows])
            kept[h, rows] = jnp.where(late, after, enter)
            sent[h, rows] = jnp.where(late, enter, after)


def mix_total_again(bits, arrays, outputs):
    table, own, got = arrays
    decay = lambda which: lambda h: table[which, h : h + 1]
    mix_total(bits, own, got, decay(OWN), decay(PARTNER), *outputs)


def mix_next_row(bits, chip, row, total, got, out):
    right = bits[1]
    for i in range(out.shape[0]):
        scale_total = jnp.where(right, 1.0, row(i))
        scale_got = jnp.where(right, chip(i), 1.0)
        out[i] = scale_total * total[i, :HD] + scale_got * got[i, :HD]


def mix_next_column(bits, chip, corner, total, got, out):
    _, right, low = bits
    for i in range(out.shape[0]):
        scale_total = jnp.where(low & right, 0.0, 1.0)
        scale_got = jnp.where(low, jnp.where(right, 1.0, chip(i) * corner(i)), 0.0)
        out[i] = scale_total * total[i] + scale_got * got[i]


def lines(ref, first=0):
    return lambda i: ref[first + i : first + i + 1]


def mix_next_row_again(bits, arrays, outputs):
    table, total, got = arrays
    mix_next_row(bits, lines(table.at[CHIP]), lines(table.at[ROW]), total, got, *outputs)


def mix_next_column_again(bits, arrays, outputs):
    table, total, got = arrays
    quarter = total.shape[0]
    chip, corner = (lines(table.at[which], quarter) for which in (CHIP, CORNER))
    mix_next_column(bits, chip, corner, total, got, *outputs)


def mix_enter(bits, arrays, outputs):
    table, own, got, one_a, one_b, two_a, two_b = arrays
    kept, sent = outputs
    late, right, low = bits
    quarter = one_b.shape[0]
    decay = lambda which, h: table[which, h : h + 1]
    for h in range(2 * quarter):
        i = h % quarter
        row = jnp.where(right, decay(ROW, h), 1.0)
        if h < quarter:
            one, two = one_a[i, :HD], two_a[i]
            scale_one = jnp.where(right, 1.0, 0.0)
            scale_two = jnp.where(low, row, 0.0)
        else:
            one, two = one_b[i], two_b[i]
            scale_one = jnp.where(low, jnp.where(right, row, decay(CORNER, h)), 0.0)
            scale_two = jnp.where(low | right, 1.0, 0.0)
        enter = scale_one * one + scale_two * two
        after = jnp.where(late, decay(PARTNER, h), decay(OWN, h)) * enter
        after += jnp.where(late, got[h, :HD], own[h, :HD])
        kept[h] = jnp.where(late, after, enter)
        sent[h] = jnp.where(late, enter, after)


def entering_quad(send, own_task, table, place, backward, tasks):
    def work(stage, after, before):
        run, outputs = tasks[stage]
        outputs.extend(run(after))
        return follows(before, outputs[0])

    half = send.shape[0]
    whole, part = (half, HD, HD), (half // 2, HD, HD)
    got = swap(send, "seq", 1)
    own = own_task(send)
    run = lambda body, arrays, shapes, name: mix(body, backward, place, arrays, shapes, name)
    if not backward:
        heads = half // 4
        wide, block = (heads, HD + TILE, HD), (heads, HD, HD)
        *blocks, total, table = run(
            mix_blocks, (own, got), [wide] * 4 + [whole, (3, half, HD)], "earlier_blocks"
        )
        gots = [swap(blocks[at], "seq", 2 * at) for at in (1, 2, 3)]
        gots = work(1, total, gots)
        *blocks, table = run(
            mix_scan, (table, blocks[0], *gots), [block] * 4 + [(5, half, HD)], "earlier_scan"
        )
        gots = [swap(blocks[at], "seq", 2 * at) for at in (1, 2, 3)]
        gots = work(2, blocks[0], gots)
        kept, sent = run(
            mix_enter_first, (table, own, got, blocks[0], *gots), [whole] * 2, "earlier_enter"
        )
    else:
        first, second = run(mix_total_again, (table, own, got), [part] * 2, "later_total")
        one_a, one_b = swap(first, "seq", 2), swap(second, "seq", 4)
        one_a, one_b = work(1, second, (one_a, one_b))
        (next_a,) = run(mix_next_row_again, (table, first, one_a), [part], "later_row")
        (next_b,) = run(mix_next_column_again, (table, second, one_b), [part], "later_column")
        two_a, two_b = swap(next_a, "seq", 4), swap(next_b, "seq", 2)
        two_a, two_b = work(2, next_b, (two_a, two_b))
        kept, sent = run(
            mix_enter, (table, own, got, one_a, one_b, two_a, two_b), [whole] * 2, "later_enter"
        )
    received = swap(sent, "seq", 1)
    received = follows(received, tasks[3](follows(kept, sent)))
    return kept, received, table


def entering_any(send, own_task, log_total, backward, tasks):
    own = own_task(send)
    for stage in (1, 2):
        run, outputs = tasks[stage]
        outputs.extend(run(send))
    count, mine = lax.axis_size("seq"), lax.axis_index("seq")
    core = mine % 2
    own, send = own[:, :HD], send[:, :HD]
    half = own.shape[0]
    in_order = jnp.where(
        core == 0, jnp.concatenate([own, send], axis=0), jnp.concatenate([send, own], axis=0)
    )
    states = lax.all_gather(in_order, "seq")
    decays = jnp.exp(lax.all_gather(log_total, "seq"))
    place = mine
    if backward:
        states, decays, place = states[::-1], decays[::-1], count - 1 - mine

    def step(at, total):
        longer = decays[at][:, None, None] * total + states[at]
        return jnp.where(at < place, longer, total)

    total = lax.fori_loop(0, count - 1, step, jnp.zeros_like(in_order))
    kept = lax.dynamic_slice_in_dim(total, core * half, half)
    tasks[3](kept)
    return kept, lax.dynamic_slice_in_dim(total, (1 - core) * half, half)


def add(first, second):
    def kernel(first_ref, second_ref, out_ref):
        out_ref[...] = first_ref[...] + second_ref[...]

    return pl.pallas_call(
        kernel,
        in_specs=[NEAR, NEAR],
        out_specs=NEAR,
        out_shape=in_vmem(*first.shape),
        compiler_params=params(2),
        name="add",
    )(*near(first, second))


def sum_over_heads(value, tasks):
    tasks = list(tasks)
    results = []
    count = lax.axis_size("head")
    reach = 1
    while 2 * reach <= count and count % (2 * reach) == 0:
        got = swap(value, "head", reach)
        if tasks:
            results.append(tasks.pop(0)(value))
            got = follows(got, results[-1])
        value = add(value, got)
        reach *= 2
    results += [task(value) for task in tasks]
    part = value
    for shift in range(1, count // reach):
        value = add(
            value,
            lax.ppermute(part, "head", [(i, (i + shift * reach) % count) for i in range(count)]),
        )
    return value, results


def on_device(query_rows, key_rows, value_rows, output_grad, norm_gain, log_decay):
    mine = lax.axis_index("seq")
    bits = [(mine >> at) % 2 for at in range(3)]
    marks = [1 - bits[0], bits[0], *bits] + [jnp.zeros_like(mine)] * (TILE - 5)
    place = jnp.broadcast_to(jnp.stack(marks).astype(F32)[:, None], (TILE, HD))
    table = [None]

    def entering(send, own_task, backward, tasks):
        if lax.axis_size("seq") != 8:
            log_total = jnp.sum(log_decay, axis=1)
            return entering_any(send, own_task, log_total, backward, tasks)
        kept, received, table[0] = entering_quad(
            send, own_task, table[0], place, backward, tasks
        )
        return kept, received

    send, first_send, kh, vh, cum, _, decay, gain = state_to_send(
        place, norm_gain, log_decay, key_rows, value_rows
    )
    firsts, raws, in_0, in_1, begun = [], [], [], [], []

    def own_task(earlier):
        own, first, *raw = own_state(
            follows(kh, earlier), vh, cum, decay, query_rows, output_grad
        )
        firsts.extend((first, first_send))
        raws.append(raw)
        return own

    def forward_task(index):
        def task(earlier):
            *made, q_next, o_next = [
                *intra(
                    index, place, follows(cum, earlier), kh, vh, *firsts, raws[-1],
                    query_rows, output_grad,
                ),
                *raws[-1] * index,
            ]
            raws.append([q_next, o_next])
            return made

        return task

    def parts():
        q0, o0, _, _, columns0, inner0 = in_0
        q1, o1, _, _, columns1, inner1 = in_1
        return q0, q1, o0, o1, columns0, columns1, inner0, inner1

    def attend_task(kept):
        begun.extend(attend(0, gain, kept, parts()))
        return begun[-1]

    keep, recv = entering(
        send, own_task, False, {1: (forward_task(0), in_0), 2: (forward_task(1), in_1), 3: attend_task}
    )
    q0, o0, w0, decays0, columns0, _ = in_0
    q1, o1, w1, decays1, columns1, _ = in_1
    own_att = begun[:2]
    *other_att, sums = attend(1, gain, recv, parts(), begun[2:])
    sums, ((scaled, ends), remaining) = sum_over_heads(
        sums,
        (
            lambda earlier: scaled_queries(cum, follows(q0, earlier), q1),
            lambda earlier: remaining_decay(follows(cum, earlier)),
        ),
    )
    grad_send, second_send, *other_g = norm_grad(1, ends, gain, sums, scaled, (o0, o1, *other_att))
    own_g, seconds, queries, pairs, rows = [], [], [], [], []

    def own_grad_task(earlier):
        own, second, *grads = norm_grad(
            0, ends, gain, follows(sums, earlier), scaled, (o0, o1, *own_att)
        )
        own_g.extend(grads)
        seconds.extend((second, second_send))
        return own

    def query_task(earlier):
        return grad_query(
            place, gain, sums, (*own_att, *other_att), follows(ends, earlier),
            (keep, recv, *firsts, kh, vh, *own_g, *other_g, decays0, decays1, columns0, columns1),
        )

    def pair_task(earlier):
        return grad_key_value(
            place, queries[1], w0, w1, q0, q1, kh, vh, *own_g, *other_g, remaining,
            follows(seconds[0], earlier), seconds[1], queries[0],
        )

    def finish_task(kept):
        rows.extend(finish_own(ends, kept, (kh, vh, remaining, *pairs[:2])))
        return rows[-1]

    _, grad_recv = entering(
        grad_send, own_grad_task, True,
        {1: (query_task, queries), 2: (pair_task, pairs), 3: finish_task},
    )
    grad_k, grad_v = finish_other(
        place, rows, ends, grad_recv, (kh, vh, remaining, *pairs[:2])
    )
    return queries[2], pairs[2], grad_k, grad_v


def solution(mesh):
    rows = P("seq", "head", None)
    return jax.shard_map(
        on_device,
        mesh=mesh,
        in_specs=(rows, rows, rows, rows, P("head", None), P("head", "seq")),
        out_specs=(rows, rows, rows, rows),
        check_vma=False,
    )
```

```python
import functools

import jax
import jax.numpy as jnp
from jax import lax
from jax.experimental import pallas as pl
from jax.experimental.pallas import tpu as pltpu
from jax.sharding import PartitionSpec as P

HEAD_TOTAL = 64
HD = 128
BLOCK = 256
CHUNK = 128
TILE = 8
F32 = jnp.float32
BF16 = jnp.bfloat16
MIB = 1024 * 1024
NEAR = pl.BlockSpec(memory_space=pltpu.VMEM)
FAR = pl.BlockSpec(memory_space=pl.ANY)
LOWER, UPPER, LATE, RIGHT, LOW = range(5)


def in_vmem(*shape, kind=F32):
    return pltpu.VMEM(shape, kind)


def near(*arrays):
    return [pltpu.with_memory_space_constraint(array, pltpu.VMEM) for array in arrays]


def far(*arrays):
    return [pltpu.with_memory_space_constraint(array, pltpu.HBM) for array in arrays]


def params(mib):
    return pltpu.CompilerParams(vmem_limit_bytes=mib * MIB)


def cost(flops, moved, exps=0):
    return pl.CostEstimate(flops=flops, bytes_accessed=moved, transcendentals=exps)


def block_cum(log_decay):
    size = log_decay.shape[1]
    upper = lax.broadcasted_iota(jnp.int32, (size, size), 0) <= lax.broadcasted_iota(
        jnp.int32, (size, size), 1
    )
    return jnp.dot(
        log_decay,
        jnp.where(upper, 1.0, 0.0).astype(F32),
        precision=lax.Precision.HIGHEST,
        preferred_element_type=F32,
    )


def as_columns(row):
    return jnp.broadcast_to(row, (HD, row.shape[1])).T


def dot(a, b):
    return jnp.dot(a, b, preferred_element_type=F32)


def dot_rows(a, b):
    return lax.dot_general(a, b, (((1,), (1,)), ((), ())), preferred_element_type=F32)


def two_parts(matrix):
    high = matrix.astype(BF16)
    return high, (matrix - high.astype(F32)).astype(BF16)


def times_state(rows, state):
    return dot(jnp.concatenate([rows, rows], axis=1), jnp.concatenate(two_parts(state), axis=0))


def times_state_t(rows, state):
    return dot_rows(
        jnp.concatenate([rows, rows], axis=1), jnp.concatenate(two_parts(state), axis=1)
    )


def decay_quarters(row, columns):
    half = row.shape[1] // 2
    lower = lax.broadcasted_iota(jnp.int32, (half, half), 0) >= lax.broadcasted_iota(
        jnp.int32, (half, half), 1
    )
    quarters = []
    for t, s in ((0, 0), (1, 0), (1, 1)):
        gap = columns[t * half : (t + 1) * half] - row[:, s * half : (s + 1) * half]
        quarters.append(jnp.exp(jnp.where(lower, gap, -jnp.inf) if t == s else gap))
    return quarters


def causal(table, quarters):
    half = table.shape[0] // 2
    first, second, third = (
        (table[t * half : (t + 1) * half, s * half : (s + 1) * half] * quarter).astype(BF16)
        for (t, s), quarter in zip(((0, 0), (1, 0), (1, 1)), quarters)
    )
    top = jnp.concatenate([first, jnp.zeros_like(first)], axis=1)
    return jnp.concatenate([top, jnp.concatenate([second, third], axis=1)], axis=0)


def transposed_dot(a, b):
    return lax.dot_general(a, b, (((0,), (0,)), ((), ())), preferred_element_type=F32)


def each_head(heads, unroll, body):
    def step(h, carry):
        body(h)
        return carry

    lax.fori_loop(0, heads, step, 0, unroll=unroll)


def each_half(half, unroll, body):
    for part in range(2):
        each_head(half, unroll, lambda i, part=part: body(part, i, part * half + i))


def turn_tiles(tiles):
    count = len(tiles)
    at = lax.broadcasted_iota(jnp.int32, tiles[0].shape, 0)
    turned = [tile if i == 0 else pltpu.roll(tile, i, 0) for i, tile in enumerate(tiles)]
    reach = 1
    while reach < count:
        odd = (at & reach) != 0
        turned = [
            jnp.where(odd, turned[(n + reach) % count], turned[n]) for n in range(count)
        ]
        reach *= 2
    picked = [turned[-j % count] for j in range(count)]
    return [tile if j == 0 else pltpu.roll(tile, count - j, 0) for j, tile in enumerate(picked)]


def is_upper(place_ref):
    return jnp.max(place_ref[UPPER : UPPER + 1]) > 0.5


def to_heads(dst, block, upper):
    tok, heads, _ = block.shape

    def step(group, carry):
        at = pl.multiple_of(group * 2 * TILE, 2 * TILE)
        tokens = block[pl.ds(at, 2 * TILE)].astype(F32)
        for first in range(0, heads, TILE):
            halves = [
                turn_tiles([tokens[base + i, first : first + TILE] for i in range(TILE)])
                for base in (0, TILE)
            ]
            local = jnp.where(upper, heads - TILE - first, first)
            for j in range(TILE):
                both = jnp.concatenate([halves[0][j], halves[1][j]], axis=0)
                dst[local + j, pl.ds(at, 2 * TILE)] = both.astype(BF16)
        return carry

    lax.fori_loop(0, tok // (2 * TILE), step, 0, unroll=4)


def from_heads(block, src, start, tok, upper):
    heads = src.shape[0]

    def step(group, carry):
        at = pl.multiple_of(group * TILE, TILE)
        parts = []
        for first in range(0, heads, TILE):
            local = jnp.where(upper, heads - TILE - first, first)
            parts.append(turn_tiles([src[local + i, pl.ds(start + at, TILE)] for i in range(TILE)]))
        for j in range(TILE):
            block[at + j] = jnp.concatenate([part[j] for part in parts], axis=0).astype(BF16)
        return carry

    lax.fori_loop(0, tok // TILE, step, 0, unroll=4)


def is_set(place_ref, which):
    return place_ref[which : which + 1] > 0.5


def in_local_order(place_ref, rows):
    half = rows.shape[0] // 2
    lower, upper = rows[:half], rows[half:]
    mine = jnp.broadcast_to(place_ref[LOWER : LOWER + 1, :1], lower.shape) > 0.5
    return jnp.concatenate(
        [jnp.where(mine, lower, upper), jnp.where(mine, upper, lower)], axis=0
    )


def half_states(part, kh, vh, cum, b, out, first=None):
    half = kh.shape[1] // 2

    def one(i):
        h = part * half + i
        row = cum[b, pl.ds(h, 1), :]
        scale = jnp.exp(row[:, BLOCK - 1 :] - row)
        state = dot((kh[b, h].astype(F32).T * scale).astype(BF16), vh[b, h])
        if first is not None:
            state += jnp.exp(row[:, BLOCK - 1 :]) * first[i]
        out[i, :HD] = state

    each_head(half, 8, one)


def add_decays(out, decay, part):
    half = out.shape[0]
    for i in range(half):
        out[i, HD:] = jnp.broadcast_to(decay[part * half + i : part * half + i + 1], (TILE, HD))


def state_kernel(
    place_ref, gain_hbm, ld_hbm, k_hbm, v_hbm, send_ref, first_ref, kh, vh, cum, ld_ref, decay,
    gain_ref, gain_raw, ld_raw, k_raw, v_raw, sems,
):
    heads, tok = ld_ref.shape
    per_block = BLOCK // CHUNK
    copies = [pltpu.make_async_copy(ld_hbm, ld_raw, sems.at[0])]
    for c in range(tok // CHUNK):
        at = pl.ds(c * CHUNK, CHUNK)
        copies.append(pltpu.make_async_copy(k_hbm.at[at], k_raw.at[at], sems.at[2 * c + 1]))
        copies.append(pltpu.make_async_copy(v_hbm.at[at], v_raw.at[at], sems.at[2 * c + 2]))
    copies.append(pltpu.make_async_copy(gain_hbm, gain_raw, sems.at[len(copies)]))
    for copy in copies:
        copy.start()
    upper = is_upper(place_ref)
    copies[0].wait()
    ld_ref[...] = in_local_order(place_ref, ld_raw[...])
    for b in range(2):
        cum[b] = block_cum(ld_ref[:, b * BLOCK : (b + 1) * BLOCK])
    ends = cum[0, :, BLOCK - 1 :] + cum[1, :, BLOCK - 1 :]
    decay[...] = jnp.broadcast_to(jnp.exp(ends), decay.shape)

    for b in range(2):
        for c in range(per_block):
            at = pl.ds((b * per_block + c) * CHUNK, CHUNK)
            here = pl.ds(c * CHUNK, CHUNK)
            which = 2 * (b * per_block + c) + 1
            copies[which].wait()
            to_heads(kh.at[b, :, here], k_raw.at[at], upper)
            copies[which + 1].wait()
            to_heads(vh.at[b, :, here], v_raw.at[at], upper)
        if b == 0:
            half_states(1, kh, vh, cum, 0, first_ref)
        else:
            half_states(1, kh, vh, cum, 1, send_ref, first_ref)
    add_decays(send_ref, decay, 1)
    copies[-1].wait()
    gain_ref[...] = in_local_order(place_ref, gain_raw[...])


def state_to_send(place, gain, log_decay, key_rows, value_rows):
    tok, heads, dim = key_rows.shape
    half = heads // 2
    by_head = in_vmem(2, heads, BLOCK, dim, kind=BF16)
    return pl.pallas_call(
        state_kernel,
        in_specs=[NEAR, FAR, FAR, FAR, FAR],
        out_specs=[NEAR] * 8,
        out_shape=[
            in_vmem(half, dim + TILE, dim), in_vmem(half, dim, dim), by_head, by_head,
            in_vmem(2, heads, BLOCK), in_vmem(heads, tok), in_vmem(heads, dim), in_vmem(heads, dim),
        ],
        scratch_shapes=[
            pltpu.VMEM((heads, dim), F32),
            pltpu.VMEM((heads, tok), F32),
            pltpu.VMEM((tok, heads, dim), BF16),
            pltpu.VMEM((tok, heads, dim), BF16),
            pltpu.SemaphoreType.DMA((2 * (tok // CHUNK) + 2,)),
        ],
        compiler_params=params(8),
        cost_estimate=cost(tok * heads * dim * dim, 8 * tok * heads * dim),
        name="state_to_send",
    )(place, *far(gain, log_decay, key_rows, value_rows))


def fetch_block(index, arrays, blocks, sems):
    copies = [
        pltpu.make_async_copy(array.at[pl.ds(index * BLOCK, BLOCK)], block, sems.at[at])
        for at, (array, block) in enumerate(zip(arrays, blocks))
    ]
    for copy in copies:
        copy.start()
    return copies


def own_state_kernel(
    kh, vh, cum, decay, q_hbm, o_hbm, own_ref, first_ref, q_raw, o_raw, sems
):
    copies = fetch_block(0, (q_hbm, o_hbm), (q_raw, o_raw), sems)
    half_states(0, kh, vh, cum, 0, first_ref)
    half_states(0, kh, vh, cum, 1, own_ref, first_ref)
    add_decays(own_ref, decay, 0)
    for copy in copies:
        copy.wait()


def own_state(kh, vh, cum, decay, query_rows, output_grad):
    _, heads, tok, dim = kh.shape
    half = heads // 2
    raw = in_vmem(BLOCK, heads, dim, kind=BF16)
    return pl.pallas_call(
        own_state_kernel,
        in_specs=[NEAR] * 4 + [FAR, FAR],
        out_specs=[NEAR] * 4,
        out_shape=[in_vmem(half, dim + TILE, dim), in_vmem(half, dim, dim), raw, raw],
        scratch_shapes=[pltpu.SemaphoreType.DMA((2,))],
        compiler_params=params(4),
        cost_estimate=cost(2 * tok * heads * dim * dim, 4 * tok * heads * dim),
        name="own_state",
    )(*near(kh, vh, cum, decay), *far(query_rows, output_grad))


def intra(index, place, cum, kh, vh, first_own, first_send, raw, query_rows, output_grad):
    tok, heads, dim = query_rows.shape
    ahead = index == 0

    def kernel(place_ref, cum, kh, vh, first_own, first_send, q_raw, o_raw, *refs):
        if ahead:
            q_hbm, o_hbm, *refs = refs
            *refs, q_next, o_next, sems = refs
            copies = fetch_block(1, (q_hbm, o_hbm), (q_next, o_next), sems)
        qh, oh, w_ref, decays_ref, columns_ref, inner_ref = refs
        upper = is_upper(place_ref)
        to_heads(qh, q_raw, upper)
        to_heads(oh, o_raw, upper)

        def one(part, i, h):
            query = qh[h]
            row = cum[index, pl.ds(h, 1), :]
            columns = as_columns(row)
            quarters = decay_quarters(row, columns)
            for at, quarter in enumerate(quarters):
                decays_ref[h, at] = quarter
            weights = causal(dot_rows(query, kh[index, h]), quarters)
            w_ref[h] = weights.T
            inner = dot(weights, vh[index, h])
            columns = jnp.exp(columns)
            columns_ref[h] = columns
            if index:
                inner += columns * times_state(query, (first_own, first_send)[part][i])
            inner_ref[h] = inner

        each_half(heads // 2, 4, one)
        if ahead:
            for copy in copies:
                copy.wait()

    by_head = in_vmem(heads, BLOCK, dim, kind=BF16)
    return pl.pallas_call(
        kernel,
        in_specs=[NEAR] * 8 + [FAR, FAR] * ahead,
        out_specs=[NEAR] * (6 + 2 * ahead),
        out_shape=[
            by_head, by_head, in_vmem(heads, BLOCK, BLOCK, kind=BF16),
            in_vmem(heads, 3, BLOCK // 2, BLOCK // 2), in_vmem(heads, BLOCK, dim),
            in_vmem(heads, BLOCK, dim),
        ]
        + [in_vmem(BLOCK, heads, dim, kind=BF16)] * (2 * ahead),
        scratch_shapes=[pltpu.SemaphoreType.DMA((2,))] * ahead,
        compiler_params=params(4),
        cost_estimate=cost(
            2 * heads * BLOCK * BLOCK * dim * 4, 20 * heads * BLOCK * dim, heads * BLOCK * BLOCK
        ),
        name=f"intra_{index}",
    )(
        *near(place, cum, kh, vh, first_own, first_send, *raw),
        *(far(query_rows, output_grad) if ahead else ()),
    )


def attend_kernel(part, *refs):
    gain_ref, state_ref, q0, q1, o0, o1, columns0, columns1, inner0, inner1 = refs[:10]
    half = state_ref.shape[0]
    if part:
        before, att0, att1, sums_ref, partial = refs[10:]
        partial[...] = before[...]
    else:
        att0, att1, partial = refs[10:]
        partial[...] = jnp.zeros_like(partial)

    def one(i):
        h = part * half + i
        state = state_ref[i]
        gain = gain_ref[pl.ds(h, 1), :]
        blocks = ((q0, o0, columns0, inner0, att0), (q1, o1, columns1, inner1, att1))
        for b, (q, o, columns, inner, att) in enumerate(blocks):
            attended = inner[h] + columns[h] * times_state(q[h], state)
            att[i] = attended
            partial[0, b] += attended * attended
            partial[1, b] += gain * o[h].astype(F32) * attended
            state = columns[h, BLOCK - 1 :] * state

    each_head(half, 8, one)
    if part:
        ones = jnp.ones((8, HD), F32)
        for b in range(2):
            for at in range(2):
                line = lax.dot_general(
                    ones, partial[at, b], (((1,), (1,)), ((), ())),
                    precision=lax.Precision.HIGHEST, preferred_element_type=F32,
                )
                sums_ref[at : at + 1, b * BLOCK : (b + 1) * BLOCK] = line[:1]


def attend(part, gain, state, arrays, before=()):
    heads, dim = gain.shape
    tok = 2 * BLOCK
    half = heads // 2
    by_head = in_vmem(half, BLOCK, dim)
    partial = (2, 2, BLOCK, dim)
    return pl.pallas_call(
        functools.partial(attend_kernel, part),
        in_specs=[NEAR] * (10 + part),
        out_specs=[NEAR] * 3,
        out_shape=[by_head, by_head, in_vmem(2, tok) if part else in_vmem(*partial)],
        scratch_shapes=[pltpu.VMEM(partial, F32)] * part,
        compiler_params=params(6),
        cost_estimate=cost(2 * heads * tok * dim * dim, 8 * heads * tok * dim),
        name=f"attend_{part}",
    )(*near(gain, state, *arrays, *before))


def scaled_queries(cum, q0, q1):
    _, heads, _ = cum.shape

    def kernel(cum_ref, q0, q1, out_ref, ends_ref):
        for b in range(2):
            ends_ref[b] = jnp.broadcast_to(jnp.exp(cum_ref[b, :, BLOCK - 1 :]), (heads, HD))

        def one(h):
            for b, q in enumerate((q0, q1)):
                scale = jnp.exp(cum_ref[b, pl.ds(h, 1), :])
                out_ref[b, h] = (q[h].astype(F32).T * scale).astype(BF16)

        each_head(heads, 4, one)

    return pl.pallas_call(
        kernel,
        in_specs=[NEAR] * 3,
        out_specs=[NEAR] * 2,
        out_shape=[in_vmem(2, heads, HD, BLOCK, kind=BF16), in_vmem(2, heads, HD)],
        compiler_params=params(4),
        cost_estimate=cost(4 * heads * BLOCK * HD, 8 * heads * BLOCK * HD),
        name="scaled_queries",
    )(*near(cum, q0, q1))


def remaining_decay(cum):
    _, heads, _ = cum.shape

    def kernel(cum_ref, out_ref):
        def one(h):
            for b in range(2):
                row = cum_ref[b, pl.ds(h, 1), :]
                out_ref[b, h] = as_columns(jnp.exp(row[:, BLOCK - 1 :] - row))

        each_head(heads, 4, one)

    return pl.pallas_call(
        kernel,
        in_specs=[NEAR],
        out_specs=NEAR,
        out_shape=in_vmem(2, heads, BLOCK, HD),
        compiler_params=params(4),
        cost_estimate=cost(2 * heads * BLOCK * HD, 8 * heads * BLOCK * HD),
        name="remaining_decay",
    )(*near(cum))


def inverse_rms(sums_ref, b):
    at = slice(b * BLOCK, (b + 1) * BLOCK)
    inv = lax.rsqrt(sums_ref[0:1, at] / (HEAD_TOTAL * HD) + 1e-06)
    mean = sums_ref[1:2, at] * inv / (HEAD_TOTAL * HD)
    return inv, mean


def norm_grad(part, ends, gain, sums, scaled, arrays):
    heads, dim = gain.shape
    tok = 2 * BLOCK
    half = heads // 2

    def kernel(ends_ref, gain_ref, sums_ref, queries_ref, o0, o1, att0, att1,
               out_ref, second_ref, g0, g1, scales):
        for b in range(2):
            inv, mean = inverse_rms(sums_ref, b)
            scales[b, 0] = as_columns(inv)
            scales[b, 1] = as_columns(inv * inv * mean)

        def one(i):
            h = part * half + i
            line = gain_ref[pl.ds(h, 1), :]
            starts = []
            for b, (o, att, g) in enumerate(((o0, att0, g0), (o1, att1, g1))):
                grad = line * o[h].astype(F32) * scales[b, 0] - att[i] * scales[b, 1]
                grad = grad.astype(BF16)
                g[i] = grad
                starts.append(dot(queries_ref[b, h], grad))
            second_ref[i] = starts[1]
            out_ref[i] = starts[0] + ends_ref[0, pl.ds(h, 1)] * starts[1]

        each_head(half, 8, one)

    by_head = in_vmem(half, BLOCK, dim, kind=BF16)
    return pl.pallas_call(
        kernel,
        in_specs=[NEAR] * 8,
        out_specs=[NEAR] * 4,
        out_shape=[in_vmem(half, dim, dim), in_vmem(half, dim, dim), by_head, by_head],
        scratch_shapes=[pltpu.VMEM((2, 2, BLOCK, dim), F32)],
        compiler_params=params(4),
        cost_estimate=cost(heads * tok * dim * dim, 7 * heads * tok * dim),
        name=f"norm_grad_{part}",
    )(*near(ends, gain, sums, scaled, *arrays))


def normed_block(b, place_ref, gain_ref, sums_ref, halves, rows, raw):
    inv = as_columns(inverse_rms(sums_ref, b)[0])

    def one(part, i, h):
        rows[b, h] = halves[part][i] * inv * gain_ref[pl.ds(h, 1), :]

    each_half(halves[0].shape[0], 4, one)
    from_heads(raw, rows.at[b], 0, BLOCK, is_upper(place_ref))


def grad_q_kernel(
    place_ref, gain_ref, sums_ref, att_own0, att_own1, att_other0, att_other1,
    ends_ref, keep_ref, recv_ref, first_own, first_send, kh, vh, own0, own1, other0, other1,
    decays0, decays1, columns0, columns1, rows, gs_ref, out_normed, raw, sems,
):
    copies = []
    for b, halves in enumerate(((att_own0, att_other0), (att_own1, att_other1))):
        at = pl.ds(b * BLOCK, BLOCK)
        normed_block(b, place_ref, gain_ref, sums_ref, halves, rows, raw.at[at])
        copies.append(pltpu.make_async_copy(raw.at[at], out_normed.at[at], sems.at[b]))
        copies[-1].start()
    blocks = (((own0, other0), decays0, columns0), ((own1, other1), decays1, columns1))
    for b, (g, decays, columns) in enumerate(blocks):

        def one(part, i, h, b=b, g=g, decays=decays, columns=columns):
            grad = g[part][i]
            scores = causal(dot_rows(grad, vh[b, h]), [decays[h, at] for at in range(3)])
            gs_ref[b, h] = scores
            state = (keep_ref, recv_ref)[part][i]
            if b:
                state = ends_ref[0, pl.ds(h, 1)] * state + (first_own, first_send)[part][i]
            rows[b, h] = dot(scores, kh[b, h]) + columns[h] * times_state_t(grad, state)

        each_half(keep_ref.shape[0], 8, one)
    for copy in copies:
        copy.wait()


def grad_query(place, gain, sums, att, ends, arrays):
    _, heads, dim = ends.shape
    tok = 2 * BLOCK
    return pl.pallas_call(
        grad_q_kernel,
        in_specs=[NEAR] * 22,
        out_specs=[NEAR, NEAR, FAR],
        out_shape=[
            in_vmem(2, heads, BLOCK, dim), in_vmem(2, heads, BLOCK, BLOCK, kind=BF16),
            jax.ShapeDtypeStruct((tok, heads, dim), BF16),
        ],
        scratch_shapes=[
            pltpu.VMEM((tok, heads, dim), BF16),
            pltpu.SemaphoreType.DMA((2,)),
        ],
        compiler_params=params(6),
        cost_estimate=cost(
            4 * heads * tok * dim * (BLOCK + dim), 12 * heads * tok * dim, heads * tok * BLOCK
        ),
        name="grad_query",
    )(*near(place, gain, sums, *att, ends, *arrays))


def grad_kv_kernel(
    place_ref, gs_ref, w0, w1, q0, q1, kh, vh, own0, own1, other0, other1, remaining_ref,
    second_own, second_send, rows, dk, dv, out_q, raw, sems,
):
    upper = is_upper(place_ref)
    copies = []
    for b in range(2):
        for start in range(0, BLOCK, CHUNK):
            at = pl.ds(b * BLOCK + start, CHUNK)
            from_heads(raw.at[at], rows.at[b], start, CHUNK, upper)
            copies.append(pltpu.make_async_copy(raw.at[at], out_q.at[at], sems.at[len(copies)]))
            copies[-1].start()

    def one(part, i, h):
        columns = remaining_ref[0, h]
        state = (second_own, second_send)[part][i]
        g0, g1 = ((own0, own1), (other0, other1))[part]
        dk[0, h] = transposed_dot(gs_ref[0, h], q0[h]) + columns * times_state_t(vh[0, h], state)
        dv[0, h] = dot(w0[h], g0[i]) + columns * times_state(kh[0, h], state)
        dk[1, h] = transposed_dot(gs_ref[1, h], q1[h])
        dv[1, h] = dot(w1[h], g1[i])

    each_half(second_own.shape[0], 4, one)
    for copy in copies:
        copy.wait()


def grad_key_value(*arrays):
    _, heads, _, dim = arrays[6].shape
    tok = 2 * BLOCK
    return pl.pallas_call(
        grad_kv_kernel,
        in_specs=[NEAR] * 16,
        out_specs=[NEAR, NEAR, FAR],
        out_shape=[in_vmem(2, heads, BLOCK, dim)] * 2
        + [jax.ShapeDtypeStruct((tok, heads, dim), BF16)],
        scratch_shapes=[
            pltpu.VMEM((tok, heads, dim), BF16),
            pltpu.SemaphoreType.DMA((tok // CHUNK,)),
        ],
        compiler_params=params(6),
        cost_estimate=cost(4 * heads * tok * dim * (BLOCK + dim), 30 * heads * tok * dim),
        name="grad_key_value",
    )(*near(*arrays))


def finish_rows(part, b, ends_ref, state_ref, kh, vh, remaining_ref, dk, dv, rows_k, rows_v):
    half = state_ref.shape[0]

    def one(i):
        h = part * half + i
        columns = remaining_ref[b, h]
        state = state_ref[i]
        if b == 0:
            state = ends_ref[1, pl.ds(h, 1)] * state
        state = state.astype(BF16)
        none = jnp.zeros_like(state)
        both = jnp.concatenate(
            [jnp.concatenate([state.T, none], axis=1), jnp.concatenate([none, state], axis=1)],
            axis=0,
        )
        carried = dot(jnp.concatenate([vh[b, h], kh[b, h]], axis=1), both)
        rows_k[b, h] = dk[b, h] + columns * carried[:, :HD]
        rows_v[b, h] = dv[b, h] + columns * carried[:, HD:]

    each_head(half, 8, one)


def finish_own_kernel(*refs):
    for b in range(2):
        finish_rows(0, b, *refs)


def finish_other_kernel(
    place_ref, old_k, old_v, ends_ref, state_ref, kh, vh, remaining_ref, dk, dv,
    out_k, out_v, rows_k, rows_v, raw_k, raw_v, sems,
):
    upper = is_upper(place_ref)
    copies = []
    for b in range(2):
        finish_rows(1, b, ends_ref, state_ref, kh, vh, remaining_ref, dk, dv, rows_k, rows_v)
        for start in range(0, BLOCK, CHUNK // 2):
            at = pl.ds(b * BLOCK + start, CHUNK // 2)
            for rows, raw, out in ((rows_k, raw_k, out_k), (rows_v, raw_v, out_v)):
                from_heads(raw.at[at], rows.at[b], start, CHUNK // 2, upper)
                copies.append(pltpu.make_async_copy(raw.at[at], out.at[at], sems.at[len(copies)]))
                copies[-1].start()
    for copy in copies:
        copy.wait()


def finish_own(ends, keep, arrays):
    _, heads, dim = ends.shape
    tok = 2 * BLOCK
    return pl.pallas_call(
        finish_own_kernel,
        in_specs=[NEAR] * 7,
        out_specs=[NEAR, NEAR],
        out_shape=[in_vmem(2, heads, BLOCK, dim)] * 2,
        compiler_params=params(4),
        cost_estimate=cost(4 * heads * tok * dim * dim, 8 * heads * tok * dim),
        name="finish_own",
    )(*near(ends, keep, *arrays))


def finish_other(place, rows, ends, recv, arrays):
    _, heads, dim = ends.shape
    tok = 2 * BLOCK
    shape = jax.ShapeDtypeStruct((tok, heads, dim), BF16)
    return pl.pallas_call(
        finish_other_kernel,
        in_specs=[NEAR] * 10,
        out_specs=[FAR, FAR, NEAR, NEAR],
        out_shape=[shape, shape] + [in_vmem(2, heads, BLOCK, dim)] * 2,
        input_output_aliases={1: 2, 2: 3},
        scratch_shapes=[
            pltpu.VMEM((tok, heads, dim), BF16),
            pltpu.VMEM((tok, heads, dim), BF16),
            pltpu.SemaphoreType.DMA((4 * (tok // CHUNK),)),
        ],
        compiler_params=params(8),
        cost_estimate=cost(4 * heads * tok * dim * dim, 8 * heads * tok * dim),
        name="finish_other",
    )(*near(place, *rows, ends, recv, *arrays))[:2]


def follows(value, earlier):
    return lax.optimization_barrier((value, earlier))[0]


def swap(value, axis, bit):
    count = lax.axis_size(axis)
    return lax.ppermute(value, axis, [(i, i ^ bit) for i in range(count)])


def mix(body, backward, place, arrays, shapes, name):
    def kernel(place_ref, *refs):
        bits = [is_set(place_ref, which) != backward for which in (LATE, RIGHT, LOW)]
        body(bits, refs[: len(arrays)], refs[len(arrays) :])

    return pl.pallas_call(
        kernel,
        in_specs=[NEAR] + [NEAR] * len(arrays),
        out_specs=[NEAR] * len(shapes),
        out_shape=[in_vmem(*shape) for shape in shapes],
        compiler_params=params(4),
        cost_estimate=cost(4 * 8 * HD * HD, 16 * 8 * HD * HD),
        name=name,
    )(place, *near(*arrays))


OWN, PARTNER, CHIP, ROW, CORNER = range(5)


def mix_total(bits, own, got, d_own, d_got, first, second):
    late = bits[0]
    quarter = first.shape[0]
    for h in range(2 * quarter):
        total = jnp.where(late, 1.0, d_got(h)) * own[h, :HD] + jnp.where(late, d_own(h), 1.0) * got[h, :HD]
        if h < quarter:
            first[h, :HD] = total
        else:
            second[h - quarter] = total


def mix_total_first(bits, arrays, outputs):
    own, got = arrays
    first, second, chip = outputs
    quarter = first.shape[0]
    d_own = lambda h: own[h, HD : HD + 1]
    d_got = lambda h: got[h, HD : HD + 1]
    mix_total(bits, own, got, d_own, d_got, first, second)
    for h in range(2 * quarter):
        whole = d_own(h) * d_got(h)
        chip[h : h + 1] = whole
        place = HD + (TILE // 2) * (h // quarter)
        first[h % quarter, place : place + TILE // 2] = jnp.broadcast_to(whole, (TILE // 2, HD))


def mix_total_again(bits, arrays, outputs):
    table, own, got = arrays
    decay = lambda which: lambda h: table[which, h : h + 1]
    mix_total(bits, own, got, decay(OWN), decay(PARTNER), *outputs)


def mix_next_row(bits, chip, row, total, got, out):
    right = bits[1]
    for i in range(out.shape[0]):
        scale_total = jnp.where(right, 1.0, row(i))
        scale_got = jnp.where(right, chip(i), 1.0)
        out[i] = scale_total * total[i, :HD] + scale_got * got[i, :HD]


def mix_next_column(bits, chip, corner, total, got, out):
    _, right, low = bits
    for i in range(out.shape[0]):
        scale_total = jnp.where(low & right, 0.0, 1.0)
        scale_got = jnp.where(low, jnp.where(right, 1.0, chip(i) * corner(i)), 0.0)
        out[i] = scale_total * total[i] + scale_got * got[i]


def lines(ref, first=0):
    return lambda i: ref[first + i : first + i + 1]


def mix_next_row_first(bits, arrays, outputs):
    chip, total, got = arrays
    mix_next_row(bits, lines(chip), lambda i: got[i, HD : HD + 1], total, got, *outputs)


def mix_next_column_first(bits, arrays, outputs):
    own, got, chip, corner, one_a, total, one_b = arrays
    out, table = outputs
    quarter = total.shape[0]
    for h in range(2 * quarter):
        place = HD + (TILE // 2) * (h // quarter)
        table[OWN, h : h + 1] = own[h, HD : HD + 1]
        table[PARTNER, h : h + 1] = got[h, HD : HD + 1]
        table[ROW, h : h + 1] = one_a[h % quarter, place : place + 1]
    table[CHIP] = chip[...]
    table[CORNER] = corner[...]
    mix_next_column(bits, lines(chip, quarter), lines(corner, quarter), total, one_b, out)


def mix_next_row_again(bits, arrays, outputs):
    table, total, got = arrays
    mix_next_row(bits, lines(table.at[CHIP]), lines(table.at[ROW]), total, got, *outputs)


def mix_next_column_again(bits, arrays, outputs):
    table, total, got = arrays
    quarter = total.shape[0]
    chip, corner = (lines(table.at[which], quarter) for which in (CHIP, CORNER))
    mix_next_column(bits, chip, corner, total, got, *outputs)


def mix_enter(bits, arrays, outputs):
    table, own, got, one_a, one_b, two_a, two_b = arrays
    kept, sent = outputs
    late, right, low = bits
    quarter = one_b.shape[0]
    decay = lambda which, h: table[which, h : h + 1]
    for h in range(2 * quarter):
        i = h % quarter
        row = jnp.where(right, decay(ROW, h), 1.0)
        if h < quarter:
            one, two = one_a[i, :HD], two_a[i]
            scale_one = jnp.where(right, 1.0, 0.0)
            scale_two = jnp.where(low, row, 0.0)
        else:
            one, two = one_b[i], two_b[i]
            scale_one = jnp.where(low, jnp.where(right, row, decay(CORNER, h)), 0.0)
            scale_two = jnp.where(low | right, 1.0, 0.0)
        enter = scale_one * one + scale_two * two
        after = jnp.where(late, decay(PARTNER, h), decay(OWN, h)) * enter
        after += jnp.where(late, got[h, :HD], own[h, :HD])
        kept[h] = jnp.where(late, after, enter)
        sent[h] = jnp.where(late, enter, after)


def entering_quad(send, own_task, table, place, backward, tasks):
    def work(stage, after, before=()):
        if stage not in tasks:
            return before
        run, outputs = tasks[stage]
        outputs.extend(run(after))
        return lax.optimization_barrier((before, outputs[0]))[0]

    name = "later" if backward else "earlier"
    half = send.shape[0]
    quarter = half // 2
    states, wide = (quarter, HD, HD), (quarter, HD + TILE, HD)
    got = swap(send, "seq", 1)
    own = own_task(send)
    if table is None:
        first, second, chip = mix(
            mix_total_first, backward, place, (own, got), (wide, states, (half, HD)), name + "_total"
        )
    else:
        first, second = mix(
            mix_total_again, backward, place, (table, own, got), (states, states), name + "_total"
        )
    one_a, one_b = swap(first, "seq", 2), swap(second, "seq", 4)
    if table is None:
        corner = swap(chip, "seq", 6)
        one_a, one_b, corner = work(1, second, (one_a, one_b, corner))
        (next_a,) = mix(
            mix_next_row_first, backward, place, (chip, first, one_a), (states,), name + "_row"
        )
        one_b, corner = follows((one_b, corner), next_a)
        next_b, table = mix(
            mix_next_column_first, backward, place,
            (own, got, chip, corner, one_a, second, one_b), (states, (5, half, HD)),
            name + "_column",
        )
    else:
        one_a, one_b = work(1, second, (one_a, one_b))
        (next_a,) = mix(
            mix_next_row_again, backward, place, (table, first, one_a), (states,), name + "_row"
        )
        (next_b,) = mix(
            mix_next_column_again, backward, place, (table, second, follows(one_b, next_a)),
            (states,), name + "_column",
        )
    two_a, two_b = swap(next_a, "seq", 4), swap(next_b, "seq", 2)
    two_a, two_b = work(2, next_b, (two_a, two_b))
    kept, sent = mix(
        mix_enter, backward, place, (table, own, got, one_a, one_b, two_a, two_b),
        ((half, HD, HD), (half, HD, HD)), name + "_enter",
    )
    received = swap(sent, "seq", 1)
    received = follows(received, tasks[3](follows(kept, sent)))
    return kept, received, table


def entering_any(send, own_task, log_total, backward, tasks):
    own = own_task(send)
    for stage in (1, 2):
        run, outputs = tasks[stage]
        outputs.extend(run(send))
    count, mine = lax.axis_size("seq"), lax.axis_index("seq")
    core = mine % 2
    own, send = own[:, :HD], send[:, :HD]
    half = own.shape[0]
    in_order = jnp.where(
        core == 0, jnp.concatenate([own, send], axis=0), jnp.concatenate([send, own], axis=0)
    )
    states = lax.all_gather(in_order, "seq")
    decays = jnp.exp(lax.all_gather(log_total, "seq"))
    place = mine
    if backward:
        states, decays, place = states[::-1], decays[::-1], count - 1 - mine

    def step(at, total):
        longer = decays[at][:, None, None] * total + states[at]
        return jnp.where(at < place, longer, total)

    total = lax.fori_loop(0, count - 1, step, jnp.zeros_like(in_order))
    kept = lax.dynamic_slice_in_dim(total, core * half, half)
    tasks[3](kept)
    return kept, lax.dynamic_slice_in_dim(total, (1 - core) * half, half)


def add(first, second):
    def kernel(first_ref, second_ref, out_ref):
        out_ref[...] = first_ref[...] + second_ref[...]

    return pl.pallas_call(
        kernel,
        in_specs=[NEAR, NEAR],
        out_specs=NEAR,
        out_shape=in_vmem(*first.shape),
        compiler_params=params(2),
        name="add",
    )(*near(first, second))


def sum_over_heads(value, tasks):
    tasks = list(tasks)
    results = []
    count = lax.axis_size("head")
    reach = 1
    while 2 * reach <= count and count % (2 * reach) == 0:
        got = swap(value, "head", reach)
        if tasks:
            results.append(tasks.pop(0)(value))
            got = follows(got, results[-1])
        value = add(value, got)
        reach *= 2
    results += [task(value) for task in tasks]
    part = value
    for shift in range(1, count // reach):
        value = add(
            value,
            lax.ppermute(part, "head", [(i, (i + shift * reach) % count) for i in range(count)]),
        )
    return value, results


def on_device(query_rows, key_rows, value_rows, output_grad, norm_gain, log_decay):
    mine = lax.axis_index("seq")
    bits = [(mine >> at) % 2 for at in range(3)]
    marks = [1 - bits[0], bits[0], *bits] + [jnp.zeros_like(mine)] * (TILE - 5)
    place = jnp.broadcast_to(jnp.stack(marks).astype(F32)[:, None], (TILE, HD))
    table = [None]

    def entering(send, own_task, backward, tasks):
        if lax.axis_size("seq") != 8:
            log_total = jnp.sum(log_decay, axis=1)
            return entering_any(send, own_task, log_total, backward, tasks)
        kept, received, table[0] = entering_quad(
            send, own_task, table[0], place, backward, tasks
        )
        return kept, received

    send, first_send, kh, vh, cum, _, decay, gain = state_to_send(
        place, norm_gain, log_decay, key_rows, value_rows
    )
    firsts, raws, in_0, in_1, begun = [], [], [], [], []

    def own_task(earlier):
        own, first, *raw = own_state(
            follows(kh, earlier), vh, cum, decay, query_rows, output_grad
        )
        firsts.extend((first, first_send))
        raws.append(raw)
        return own

    def forward_task(index):
        def task(earlier):
            *made, q_next, o_next = [
                *intra(
                    index, place, follows(cum, earlier), kh, vh, *firsts, raws[-1],
                    query_rows, output_grad,
                ),
                *raws[-1] * index,
            ]
            raws.append([q_next, o_next])
            return made

        return task

    def parts():
        q0, o0, _, _, columns0, inner0 = in_0
        q1, o1, _, _, columns1, inner1 = in_1
        return q0, q1, o0, o1, columns0, columns1, inner0, inner1

    def attend_task(kept):
        begun.extend(attend(0, gain, kept, parts()))
        return begun[-1]

    keep, recv = entering(
        send, own_task, False, {1: (forward_task(0), in_0), 2: (forward_task(1), in_1), 3: attend_task}
    )
    q0, o0, w0, decays0, columns0, _ = in_0
    q1, o1, w1, decays1, columns1, _ = in_1
    own_att = begun[:2]
    *other_att, sums = attend(1, gain, recv, parts(), begun[2:])
    sums, ((scaled, ends), remaining) = sum_over_heads(
        sums,
        (
            lambda earlier: scaled_queries(cum, follows(q0, earlier), q1),
            lambda earlier: remaining_decay(follows(cum, earlier)),
        ),
    )
    grad_send, second_send, *other_g = norm_grad(1, ends, gain, sums, scaled, (o0, o1, *other_att))
    own_g, seconds, queries, pairs, rows = [], [], [], [], []

    def own_grad_task(earlier):
        own, second, *grads = norm_grad(
            0, ends, gain, follows(sums, earlier), scaled, (o0, o1, *own_att)
        )
        own_g.extend(grads)
        seconds.extend((second, second_send))
        return own

    def query_task(earlier):
        return grad_query(
            place, gain, sums, (*own_att, *other_att), follows(ends, earlier),
            (keep, recv, *firsts, kh, vh, *own_g, *other_g, decays0, decays1, columns0, columns1),
        )

    def pair_task(earlier):
        return grad_key_value(
            place, queries[1], w0, w1, q0, q1, kh, vh, *own_g, *other_g, remaining,
            follows(seconds[0], earlier), seconds[1], queries[0],
        )

    def finish_task(kept):
        rows.extend(finish_own(ends, kept, (kh, vh, remaining, *pairs[:2])))
        return rows[-1]

    _, grad_recv = entering(
        grad_send, own_grad_task, True,
        {1: (query_task, queries), 2: (pair_task, pairs), 3: finish_task},
    )
    grad_k, grad_v = finish_other(
        place, rows, ends, grad_recv, (kh, vh, remaining, *pairs[:2])
    )
    return queries[2], pairs[2], grad_k, grad_v


def solution(mesh):
    rows = P("seq", "head", None)
    return jax.shard_map(
        on_device,
        mesh=mesh,
        in_specs=(rows, rows, rows, rows, P("head", None), P("head", "seq")),
        out_specs=(rows, rows, rows, rows),
        check_vma=False,
    )
```

```python
import functools

import jax
import jax.numpy as jnp
from jax import lax
from jax.experimental import pallas as pl
from jax.experimental.pallas import tpu as pltpu
from jax.sharding import PartitionSpec as P

HEAD_TOTAL = 64
HD = 128
BLOCK = 256
CHUNK = 128
TILE = 8
F32 = jnp.float32
BF16 = jnp.bfloat16
MIB = 1024 * 1024
NEAR = pl.BlockSpec(memory_space=pltpu.VMEM)
FAR = pl.BlockSpec(memory_space=pl.ANY)
LOWER, UPPER, LATE, RIGHT, LOW = range(5)


def in_vmem(*shape, kind=F32):
    return pltpu.VMEM(shape, kind)


def near(*arrays):
    return [pltpu.with_memory_space_constraint(array, pltpu.VMEM) for array in arrays]


def far(*arrays):
    return [pltpu.with_memory_space_constraint(array, pltpu.HBM) for array in arrays]


def params(mib):
    return pltpu.CompilerParams(vmem_limit_bytes=mib * MIB)


def cost(flops, moved, exps=0):
    return pl.CostEstimate(flops=flops, bytes_accessed=moved, transcendentals=exps)


def block_cum(log_decay):
    size = log_decay.shape[1]
    upper = lax.broadcasted_iota(jnp.int32, (size, size), 0) <= lax.broadcasted_iota(
        jnp.int32, (size, size), 1
    )
    return jnp.dot(
        log_decay,
        jnp.where(upper, 1.0, 0.0).astype(F32),
        precision=lax.Precision.HIGHEST,
        preferred_element_type=F32,
    )


def as_columns(row):
    return jnp.broadcast_to(row, (HD, row.shape[1])).T


def dot(a, b):
    return jnp.dot(a, b, preferred_element_type=F32)


def dot_rows(a, b):
    return lax.dot_general(a, b, (((1,), (1,)), ((), ())), preferred_element_type=F32)


def two_parts(matrix):
    high = matrix.astype(BF16)
    return high, (matrix - high.astype(F32)).astype(BF16)


def times_state(rows, state):
    return dot(jnp.concatenate([rows, rows], axis=1), jnp.concatenate(two_parts(state), axis=0))


def times_state_t(rows, state):
    return dot_rows(
        jnp.concatenate([rows, rows], axis=1), jnp.concatenate(two_parts(state), axis=1)
    )


def decay_quarters(row, columns):
    half = row.shape[1] // 2
    lower = lax.broadcasted_iota(jnp.int32, (half, half), 0) >= lax.broadcasted_iota(
        jnp.int32, (half, half), 1
    )
    quarters = []
    for t, s in ((0, 0), (1, 0), (1, 1)):
        gap = columns[t * half : (t + 1) * half] - row[:, s * half : (s + 1) * half]
        quarters.append(jnp.exp(jnp.where(lower, gap, -jnp.inf) if t == s else gap))
    return quarters


def causal(table, quarters):
    half = table.shape[0] // 2
    first, second, third = (
        (table[t * half : (t + 1) * half, s * half : (s + 1) * half] * quarter).astype(BF16)
        for (t, s), quarter in zip(((0, 0), (1, 0), (1, 1)), quarters)
    )
    top = jnp.concatenate([first, jnp.zeros_like(first)], axis=1)
    return jnp.concatenate([top, jnp.concatenate([second, third], axis=1)], axis=0)


def transposed_dot(a, b):
    return lax.dot_general(a, b, (((0,), (0,)), ((), ())), preferred_element_type=F32)


def each_head(heads, unroll, body):
    def step(h, carry):
        body(h)
        return carry

    lax.fori_loop(0, heads, step, 0, unroll=unroll)


def each_half(half, unroll, body):
    for part in range(2):
        each_head(half, unroll, lambda i, part=part: body(part, i, part * half + i))


def turn_tiles(tiles):
    count = len(tiles)
    at = lax.broadcasted_iota(jnp.int32, tiles[0].shape, 0)
    turned = [tile if i == 0 else pltpu.roll(tile, i, 0) for i, tile in enumerate(tiles)]
    reach = 1
    while reach < count:
        odd = (at & reach) != 0
        turned = [
            jnp.where(odd, turned[(n + reach) % count], turned[n]) for n in range(count)
        ]
        reach *= 2
    picked = [turned[-j % count] for j in range(count)]
    return [tile if j == 0 else pltpu.roll(tile, count - j, 0) for j, tile in enumerate(picked)]


def is_upper(place_ref):
    return jnp.max(place_ref[UPPER : UPPER + 1]) > 0.5


def to_heads(dst, block, upper):
    tok, heads, _ = block.shape

    def step(group, carry):
        at = pl.multiple_of(group * 2 * TILE, 2 * TILE)
        tokens = block[pl.ds(at, 2 * TILE)].astype(F32)
        for first in range(0, heads, TILE):
            halves = [
                turn_tiles([tokens[base + i, first : first + TILE] for i in range(TILE)])
                for base in (0, TILE)
            ]
            local = jnp.where(upper, heads - TILE - first, first)
            for j in range(TILE):
                both = jnp.concatenate([halves[0][j], halves[1][j]], axis=0)
                dst[local + j, pl.ds(at, 2 * TILE)] = both.astype(BF16)
        return carry

    lax.fori_loop(0, tok // (2 * TILE), step, 0, unroll=4)


def from_heads(block, src, start, tok, upper):
    heads = src.shape[0]

    def step(group, carry):
        at = pl.multiple_of(group * TILE, TILE)
        parts = []
        for first in range(0, heads, TILE):
            local = jnp.where(upper, heads - TILE - first, first)
            parts.append(turn_tiles([src[local + i, pl.ds(start + at, TILE)] for i in range(TILE)]))
        for j in range(TILE):
            block[at + j] = jnp.concatenate([part[j] for part in parts], axis=0).astype(BF16)
        return carry

    lax.fori_loop(0, tok // TILE, step, 0, unroll=4)


def is_set(place_ref, which):
    return place_ref[which : which + 1] > 0.5


def in_local_order(place_ref, rows):
    half = rows.shape[0] // 2
    lower, upper = rows[:half], rows[half:]
    mine = jnp.broadcast_to(place_ref[LOWER : LOWER + 1, :1], lower.shape) > 0.5
    return jnp.concatenate(
        [jnp.where(mine, lower, upper), jnp.where(mine, upper, lower)], axis=0
    )


def half_states(part, kh, vh, cum, b, out, first=None, unroll=8):
    half = kh.shape[1] // 2

    def one(i):
        h = part * half + i
        row = cum[b, pl.ds(h, 1), :]
        scale = jnp.exp(row[:, BLOCK - 1 :] - row)
        state = dot((kh[b, h].astype(F32).T * scale).astype(BF16), vh[b, h])
        if first is not None:
            state += jnp.exp(row[:, BLOCK - 1 :]) * first[i]
        out[i, :HD] = state

    each_head(half, unroll, one)


def add_decays(out, decay, part):
    half = out.shape[0]
    for i in range(half):
        out[i, HD:] = jnp.broadcast_to(decay[part * half + i : part * half + i + 1], (TILE, HD))


def state_kernel(
    place_ref, gain_hbm, ld_hbm, k_hbm, v_hbm, send_ref, first_ref, kh, vh, cum, ld_ref, decay,
    gain_ref, gain_raw, ld_raw, k_raw, v_raw, sems,
):
    heads, tok = ld_ref.shape
    per_block = BLOCK // CHUNK
    copies = [pltpu.make_async_copy(ld_hbm, ld_raw, sems.at[0])]
    for c in range(tok // CHUNK):
        at = pl.ds(c * CHUNK, CHUNK)
        copies.append(pltpu.make_async_copy(k_hbm.at[at], k_raw.at[at], sems.at[2 * c + 1]))
        copies.append(pltpu.make_async_copy(v_hbm.at[at], v_raw.at[at], sems.at[2 * c + 2]))
    copies.append(pltpu.make_async_copy(gain_hbm, gain_raw, sems.at[len(copies)]))
    for copy in copies:
        copy.start()
    upper = is_upper(place_ref)
    copies[0].wait()
    ld_ref[...] = in_local_order(place_ref, ld_raw[...])
    for b in range(2):
        cum[b] = block_cum(ld_ref[:, b * BLOCK : (b + 1) * BLOCK])
    ends = cum[0, :, BLOCK - 1 :] + cum[1, :, BLOCK - 1 :]
    decay[...] = jnp.broadcast_to(jnp.exp(ends), decay.shape)

    for b in range(2):
        for c in range(per_block):
            at = pl.ds((b * per_block + c) * CHUNK, CHUNK)
            here = pl.ds(c * CHUNK, CHUNK)
            which = 2 * (b * per_block + c) + 1
            copies[which].wait()
            to_heads(kh.at[b, :, here], k_raw.at[at], upper)
            copies[which + 1].wait()
            to_heads(vh.at[b, :, here], v_raw.at[at], upper)
        if b == 0:
            half_states(1, kh, vh, cum, 0, first_ref)
        else:
            half_states(1, kh, vh, cum, 1, send_ref, first_ref)
    add_decays(send_ref, decay, 1)
    copies[-1].wait()
    gain_ref[...] = in_local_order(place_ref, gain_raw[...])


def state_to_send(place, gain, log_decay, key_rows, value_rows):
    tok, heads, dim = key_rows.shape
    half = heads // 2
    by_head = in_vmem(2, heads, BLOCK, dim, kind=BF16)
    return pl.pallas_call(
        state_kernel,
        in_specs=[NEAR, FAR, FAR, FAR, FAR],
        out_specs=[NEAR] * 8,
        out_shape=[
            in_vmem(half, dim + TILE, dim), in_vmem(half, dim, dim), by_head, by_head,
            in_vmem(2, heads, BLOCK), in_vmem(heads, tok), in_vmem(heads, dim), in_vmem(heads, dim),
        ],
        scratch_shapes=[
            pltpu.VMEM((heads, dim), F32),
            pltpu.VMEM((heads, tok), F32),
            pltpu.VMEM((tok, heads, dim), BF16),
            pltpu.VMEM((tok, heads, dim), BF16),
            pltpu.SemaphoreType.DMA((2 * (tok // CHUNK) + 2,)),
        ],
        compiler_params=params(8),
        cost_estimate=cost(tok * heads * dim * dim, 8 * tok * heads * dim),
        name="state_to_send",
    )(place, *far(gain, log_decay, key_rows, value_rows))


def fetch_block(index, arrays, blocks, sems):
    copies = [
        pltpu.make_async_copy(array.at[pl.ds(index * BLOCK, BLOCK)], block, sems.at[at])
        for at, (array, block) in enumerate(zip(arrays, blocks))
    ]
    for copy in copies:
        copy.start()
    return copies


def own_state_kernel(
    kh, vh, cum, decay, q_hbm, o_hbm, own_ref, first_ref, q_raw, o_raw, sems
):
    copies = fetch_block(0, (q_hbm, o_hbm), (q_raw, o_raw), sems)
    half_states(0, kh, vh, cum, 0, first_ref, unroll=4)
    half_states(0, kh, vh, cum, 1, own_ref, first_ref, unroll=4)
    add_decays(own_ref, decay, 0)
    for copy in copies:
        copy.wait()


def own_state(kh, vh, cum, decay, query_rows, output_grad):
    _, heads, tok, dim = kh.shape
    half = heads // 2
    raw = in_vmem(BLOCK, heads, dim, kind=BF16)
    return pl.pallas_call(
        own_state_kernel,
        in_specs=[NEAR] * 4 + [FAR, FAR],
        out_specs=[NEAR] * 4,
        out_shape=[in_vmem(half, dim + TILE, dim), in_vmem(half, dim, dim), raw, raw],
        scratch_shapes=[pltpu.SemaphoreType.DMA((2,))],
        compiler_params=params(4),
        cost_estimate=cost(2 * tok * heads * dim * dim, 4 * tok * heads * dim),
        name="own_state",
    )(*near(kh, vh, cum, decay), *far(query_rows, output_grad))


def intra(index, place, cum, kh, vh, first_own, first_send, raw, query_rows, output_grad):
    tok, heads, dim = query_rows.shape
    ahead = index == 0

    def kernel(place_ref, cum, kh, vh, first_own, first_send, q_raw, o_raw, *refs):
        if ahead:
            q_hbm, o_hbm, *refs = refs
            *refs, q_next, o_next, sems = refs
            copies = fetch_block(1, (q_hbm, o_hbm), (q_next, o_next), sems)
        qh, oh, w_ref, decays_ref, columns_ref, inner_ref = refs
        upper = is_upper(place_ref)
        to_heads(qh, q_raw, upper)
        to_heads(oh, o_raw, upper)

        def one(part, i, h):
            query = qh[h]
            row = cum[index, pl.ds(h, 1), :]
            columns = as_columns(row)
            quarters = decay_quarters(row, columns)
            for at, quarter in enumerate(quarters):
                decays_ref[h, at] = quarter
            weights = causal(dot_rows(query, kh[index, h]), quarters)
            w_ref[h] = weights.T
            inner = dot(weights, vh[index, h])
            columns = jnp.exp(columns)
            columns_ref[h] = columns
            if index:
                inner += columns * times_state(query, (first_own, first_send)[part][i])
            inner_ref[h] = inner

        each_half(heads // 2, 4, one)
        if ahead:
            for copy in copies:
                copy.wait()

    by_head = in_vmem(heads, BLOCK, dim, kind=BF16)
    return pl.pallas_call(
        kernel,
        in_specs=[NEAR] * 8 + [FAR, FAR] * ahead,
        out_specs=[NEAR] * (6 + 2 * ahead),
        out_shape=[
            by_head, by_head, in_vmem(heads, BLOCK, BLOCK, kind=BF16),
            in_vmem(heads, 3, BLOCK // 2, BLOCK // 2), in_vmem(heads, BLOCK, dim),
            in_vmem(heads, BLOCK, dim),
        ]
        + [in_vmem(BLOCK, heads, dim, kind=BF16)] * (2 * ahead),
        scratch_shapes=[pltpu.SemaphoreType.DMA((2,))] * ahead,
        compiler_params=params(4),
        cost_estimate=cost(
            2 * heads * BLOCK * BLOCK * dim * 4, 20 * heads * BLOCK * dim, heads * BLOCK * BLOCK
        ),
        name=f"intra_{index}",
    )(
        *near(place, cum, kh, vh, first_own, first_send, *raw),
        *(far(query_rows, output_grad) if ahead else ()),
    )


def attend_kernel(part, *refs):
    gain_ref, state_ref, q0, q1, o0, o1, columns0, columns1, inner0, inner1 = refs[:10]
    half = state_ref.shape[0]
    if part:
        before, att0, att1, sums_ref, partial = refs[10:]
        partial[...] = before[...]
    else:
        att0, att1, partial = refs[10:]
        partial[...] = jnp.zeros_like(partial)

    def one(i):
        h = part * half + i
        state = state_ref[i]
        gain = gain_ref[pl.ds(h, 1), :]
        blocks = ((q0, o0, columns0, inner0, att0), (q1, o1, columns1, inner1, att1))
        for b, (q, o, columns, inner, att) in enumerate(blocks):
            attended = inner[h] + columns[h] * times_state(q[h], state)
            att[i] = attended
            partial[0, b] += attended * attended
            partial[1, b] += gain * o[h].astype(F32) * attended
            state = columns[h, BLOCK - 1 :] * state

    each_head(half, 8, one)
    if part:
        ones = jnp.ones((8, HD), F32)
        for b in range(2):
            for at in range(2):
                line = lax.dot_general(
                    ones, partial[at, b], (((1,), (1,)), ((), ())),
                    precision=lax.Precision.HIGHEST, preferred_element_type=F32,
                )
                sums_ref[at : at + 1, b * BLOCK : (b + 1) * BLOCK] = line[:1]


def attend(part, gain, state, arrays, before=()):
    heads, dim = gain.shape
    tok = 2 * BLOCK
    half = heads // 2
    by_head = in_vmem(half, BLOCK, dim)
    partial = (2, 2, BLOCK, dim)
    return pl.pallas_call(
        functools.partial(attend_kernel, part),
        in_specs=[NEAR] * (10 + part),
        out_specs=[NEAR] * 3,
        out_shape=[by_head, by_head, in_vmem(2, tok) if part else in_vmem(*partial)],
        scratch_shapes=[pltpu.VMEM(partial, F32)] * part,
        compiler_params=params(6),
        cost_estimate=cost(2 * heads * tok * dim * dim, 8 * heads * tok * dim),
        name=f"attend_{part}",
    )(*near(gain, state, *arrays, *before))


def scaled_queries(cum, q0, q1):
    _, heads, _ = cum.shape

    def kernel(cum_ref, q0, q1, out_ref, ends_ref):
        for b in range(2):
            ends_ref[b] = jnp.broadcast_to(jnp.exp(cum_ref[b, :, BLOCK - 1 :]), (heads, HD))

        def one(h):
            for b, q in enumerate((q0, q1)):
                scale = jnp.exp(cum_ref[b, pl.ds(h, 1), :])
                out_ref[b, h] = (q[h].astype(F32).T * scale).astype(BF16)

        each_head(heads, 4, one)

    return pl.pallas_call(
        kernel,
        in_specs=[NEAR] * 3,
        out_specs=[NEAR] * 2,
        out_shape=[in_vmem(2, heads, HD, BLOCK, kind=BF16), in_vmem(2, heads, HD)],
        compiler_params=params(4),
        cost_estimate=cost(4 * heads * BLOCK * HD, 8 * heads * BLOCK * HD),
        name="scaled_queries",
    )(*near(cum, q0, q1))


def remaining_decay(cum):
    _, heads, _ = cum.shape

    def kernel(cum_ref, out_ref):
        def one(h):
            for b in range(2):
                row = cum_ref[b, pl.ds(h, 1), :]
                out_ref[b, h] = as_columns(jnp.exp(row[:, BLOCK - 1 :] - row))

        each_head(heads, 4, one)

    return pl.pallas_call(
        kernel,
        in_specs=[NEAR],
        out_specs=NEAR,
        out_shape=in_vmem(2, heads, BLOCK, HD),
        compiler_params=params(4),
        cost_estimate=cost(2 * heads * BLOCK * HD, 8 * heads * BLOCK * HD),
        name="remaining_decay",
    )(*near(cum))


def inverse_rms(sums_ref, b):
    at = slice(b * BLOCK, (b + 1) * BLOCK)
    inv = lax.rsqrt(sums_ref[0:1, at] / (HEAD_TOTAL * HD) + 1e-06)
    mean = sums_ref[1:2, at] * inv / (HEAD_TOTAL * HD)
    return inv, mean


def norm_grad(part, ends, gain, sums, scaled, arrays):
    heads, dim = gain.shape
    tok = 2 * BLOCK
    half = heads // 2

    def kernel(ends_ref, gain_ref, sums_ref, queries_ref, o0, o1, att0, att1,
               out_ref, second_ref, g0, g1, scales):
        for b in range(2):
            inv, mean = inverse_rms(sums_ref, b)
            scales[b, 0] = as_columns(inv)
            scales[b, 1] = as_columns(inv * inv * mean)

        def one(i):
            h = part * half + i
            line = gain_ref[pl.ds(h, 1), :]
            starts = []
            for b, (o, att, g) in enumerate(((o0, att0, g0), (o1, att1, g1))):
                grad = line * o[h].astype(F32) * scales[b, 0] - att[i] * scales[b, 1]
                grad = grad.astype(BF16)
                g[i] = grad
                starts.append(dot(queries_ref[b, h], grad))
            second_ref[i] = starts[1]
            out_ref[i] = starts[0] + ends_ref[0, pl.ds(h, 1)] * starts[1]

        each_head(half, 8, one)

    by_head = in_vmem(half, BLOCK, dim, kind=BF16)
    return pl.pallas_call(
        kernel,
        in_specs=[NEAR] * 8,
        out_specs=[NEAR] * 4,
        out_shape=[in_vmem(half, dim, dim), in_vmem(half, dim, dim), by_head, by_head],
        scratch_shapes=[pltpu.VMEM((2, 2, BLOCK, dim), F32)],
        compiler_params=params(4),
        cost_estimate=cost(heads * tok * dim * dim, 7 * heads * tok * dim),
        name=f"norm_grad_{part}",
    )(*near(ends, gain, sums, scaled, *arrays))


def normed_block(b, place_ref, gain_ref, sums_ref, halves, rows, raw):
    inv = as_columns(inverse_rms(sums_ref, b)[0])

    def one(part, i, h):
        rows[b, h] = halves[part][i] * inv * gain_ref[pl.ds(h, 1), :]

    each_half(halves[0].shape[0], 4, one)
    from_heads(raw, rows.at[b], 0, BLOCK, is_upper(place_ref))


def grad_q_kernel(
    ends_ref, keep_ref, recv_ref, first_own, first_send, kh, vh, own0, own1, other0, other1,
    decays0, decays1, columns0, columns1, rows, gs_ref,
):
    blocks = (((own0, other0), decays0, columns0), ((own1, other1), decays1, columns1))
    for b, (g, decays, columns) in enumerate(blocks):

        def one(part, i, h, b=b, g=g, decays=decays, columns=columns):
            grad = g[part][i]
            scores = causal(dot_rows(grad, vh[b, h]), [decays[h, at] for at in range(3)])
            gs_ref[b, h] = scores
            state = (keep_ref, recv_ref)[part][i]
            if b:
                state = ends_ref[0, pl.ds(h, 1)] * state + (first_own, first_send)[part][i]
            rows[b, h] = dot(scores, kh[b, h]) + columns[h] * times_state_t(grad, state)

        each_half(keep_ref.shape[0], 8, one)


def grad_query(ends, arrays):
    _, heads, dim = ends.shape
    tok = 2 * BLOCK
    return pl.pallas_call(
        grad_q_kernel,
        in_specs=[NEAR] * 15,
        out_specs=[NEAR, NEAR],
        out_shape=[
            in_vmem(2, heads, BLOCK, dim), in_vmem(2, heads, BLOCK, BLOCK, kind=BF16),
        ],
        compiler_params=params(4),
        cost_estimate=cost(
            4 * heads * tok * dim * (BLOCK + dim), 12 * heads * tok * dim, heads * tok * BLOCK
        ),
        name="grad_query",
    )(*near(ends, *arrays))


def grad_kv_kernel(
    place_ref, gain_ref, sums_ref, att_own0, att_own1, att_other0, att_other1,
    gs_ref, w0, w1, q0, q1, kh, vh, own0, own1, other0, other1, remaining_ref,
    second_own, second_send, dk, dv, out_normed, raw, sems,
):
    copies = []
    for b, halves in enumerate(((att_own0, att_other0), (att_own1, att_other1))):
        at = pl.ds(b * BLOCK, BLOCK)
        normed_block(b, place_ref, gain_ref, sums_ref, halves, dk, raw.at[at])
        copies.append(pltpu.make_async_copy(raw.at[at], out_normed.at[at], sems.at[b]))
        copies[-1].start()

    def one(part, i, h):
        columns = remaining_ref[0, h]
        state = (second_own, second_send)[part][i]
        g0, g1 = ((own0, own1), (other0, other1))[part]
        dk[0, h] = transposed_dot(gs_ref[0, h], q0[h]) + columns * times_state_t(vh[0, h], state)
        dv[0, h] = dot(w0[h], g0[i]) + columns * times_state(kh[0, h], state)
        dk[1, h] = transposed_dot(gs_ref[1, h], q1[h])
        dv[1, h] = dot(w1[h], g1[i])

    each_half(second_own.shape[0], 4, one)
    for copy in copies:
        copy.wait()


def grad_key_value(place, gain, sums, att, arrays):
    heads, dim = gain.shape
    tok = 2 * BLOCK
    return pl.pallas_call(
        grad_kv_kernel,
        in_specs=[NEAR] * 21,
        out_specs=[NEAR, NEAR, FAR],
        out_shape=[in_vmem(2, heads, BLOCK, dim)] * 2
        + [jax.ShapeDtypeStruct((tok, heads, dim), BF16)],
        scratch_shapes=[
            pltpu.VMEM((tok, heads, dim), BF16),
            pltpu.SemaphoreType.DMA((2,)),
        ],
        compiler_params=params(6),
        cost_estimate=cost(4 * heads * tok * dim * (BLOCK + dim), 30 * heads * tok * dim),
        name="grad_key_value",
    )(*near(place, gain, sums, *att, *arrays))


def finish_rows(part, b, ends_ref, state_ref, kh, vh, remaining_ref, dk, dv, rows_k, rows_v):
    half = state_ref.shape[0]

    def one(i):
        h = part * half + i
        columns = remaining_ref[b, h]
        state = state_ref[i]
        if b == 0:
            state = ends_ref[1, pl.ds(h, 1)] * state
        state = state.astype(BF16)
        none = jnp.zeros_like(state)
        both = jnp.concatenate(
            [jnp.concatenate([state.T, none], axis=1), jnp.concatenate([none, state], axis=1)],
            axis=0,
        )
        carried = dot(jnp.concatenate([vh[b, h], kh[b, h]], axis=1), both)
        rows_k[b, h] = dk[b, h] + columns * carried[:, :HD]
        rows_v[b, h] = dv[b, h] + columns * carried[:, HD:]

    each_head(half, 8, one)


def finish_own_kernel(place_ref, query_rows, *refs):
    *refs, out_q, raw, sems = refs
    upper = is_upper(place_ref)
    copies = []
    for b in range(2):
        for start in range(0, BLOCK, CHUNK):
            at = pl.ds(b * BLOCK + start, CHUNK)
            from_heads(raw.at[at], query_rows.at[b], start, CHUNK, upper)
            copies.append(pltpu.make_async_copy(raw.at[at], out_q.at[at], sems.at[len(copies)]))
            copies[-1].start()
    for b in range(2):
        finish_rows(0, b, *refs)
    for copy in copies:
        copy.wait()


def finish_other_kernel(
    place_ref, old_k, old_v, ends_ref, state_ref, kh, vh, remaining_ref, dk, dv,
    out_k, out_v, rows_k, rows_v, raw_k, raw_v, sems,
):
    upper = is_upper(place_ref)
    copies = []
    for b in range(2):
        finish_rows(1, b, ends_ref, state_ref, kh, vh, remaining_ref, dk, dv, rows_k, rows_v)
        for start in range(0, BLOCK, CHUNK // 2):
            at = pl.ds(b * BLOCK + start, CHUNK // 2)
            for rows, raw, out in ((rows_k, raw_k, out_k), (rows_v, raw_v, out_v)):
                from_heads(raw.at[at], rows.at[b], start, CHUNK // 2, upper)
                copies.append(pltpu.make_async_copy(raw.at[at], out.at[at], sems.at[len(copies)]))
                copies[-1].start()
    for copy in copies:
        copy.wait()


def finish_own(place, query_rows, ends, keep, arrays):
    _, heads, dim = ends.shape
    tok = 2 * BLOCK
    return pl.pallas_call(
        finish_own_kernel,
        in_specs=[NEAR] * 9,
        out_specs=[NEAR, NEAR, FAR],
        out_shape=[in_vmem(2, heads, BLOCK, dim)] * 2
        + [jax.ShapeDtypeStruct((tok, heads, dim), BF16)],
        scratch_shapes=[
            pltpu.VMEM((tok, heads, dim), BF16),
            pltpu.SemaphoreType.DMA((tok // CHUNK,)),
        ],
        compiler_params=params(6),
        cost_estimate=cost(4 * heads * tok * dim * dim, 8 * heads * tok * dim),
        name="finish_own",
    )(*near(place, query_rows, ends, keep, *arrays))


def finish_other(place, rows, ends, recv, arrays):
    _, heads, dim = ends.shape
    tok = 2 * BLOCK
    shape = jax.ShapeDtypeStruct((tok, heads, dim), BF16)
    return pl.pallas_call(
        finish_other_kernel,
        in_specs=[NEAR] * 10,
        out_specs=[FAR, FAR, NEAR, NEAR],
        out_shape=[shape, shape] + [in_vmem(2, heads, BLOCK, dim)] * 2,
        input_output_aliases={1: 2, 2: 3},
        scratch_shapes=[
            pltpu.VMEM((tok, heads, dim), BF16),
            pltpu.VMEM((tok, heads, dim), BF16),
            pltpu.SemaphoreType.DMA((4 * (tok // CHUNK),)),
        ],
        compiler_params=params(8),
        cost_estimate=cost(4 * heads * tok * dim * dim, 8 * heads * tok * dim),
        name="finish_other",
    )(*near(place, *rows, ends, recv, *arrays))[:2]


def follows(value, earlier):
    return lax.optimization_barrier((value, earlier))[0]


def swap(value, axis, bit):
    count = lax.axis_size(axis)
    return lax.ppermute(value, axis, [(i, i ^ bit) for i in range(count)])


def mix(body, backward, place, arrays, shapes, name):
    def kernel(place_ref, *refs):
        bits = [is_set(place_ref, which) != backward for which in (LATE, RIGHT, LOW)]
        body(bits, refs[: len(arrays)], refs[len(arrays) :])

    return pl.pallas_call(
        kernel,
        in_specs=[NEAR] + [NEAR] * len(arrays),
        out_specs=[NEAR] * len(shapes),
        out_shape=[in_vmem(*shape) for shape in shapes],
        compiler_params=params(4),
        cost_estimate=cost(4 * 8 * HD * HD, 16 * 8 * HD * HD),
        name=name,
    )(place, *near(*arrays))


OWN, PARTNER, CHIP, ROW, CORNER = range(5)


def mix_total(bits, own, got, d_own, d_got, first, second):
    late = bits[0]
    quarter = first.shape[0]
    for h in range(2 * quarter):
        total = jnp.where(late, 1.0, d_got(h)) * own[h, :HD] + jnp.where(late, d_own(h), 1.0) * got[h, :HD]
        if h < quarter:
            first[h, :HD] = total
        else:
            second[h - quarter] = total


def mix_total_first(bits, arrays, outputs):
    own, got = arrays
    first, second, chip = outputs
    quarter = first.shape[0]
    d_own = lambda h: own[h, HD : HD + 1]
    d_got = lambda h: got[h, HD : HD + 1]
    mix_total(bits, own, got, d_own, d_got, first, second)
    for h in range(2 * quarter):
        whole = d_own(h) * d_got(h)
        chip[h : h + 1] = whole
        place = HD + (TILE // 2) * (h // quarter)
        first[h % quarter, place : place + TILE // 2] = jnp.broadcast_to(whole, (TILE // 2, HD))


def mix_total_again(bits, arrays, outputs):
    table, own, got = arrays
    decay = lambda which: lambda h: table[which, h : h + 1]
    mix_total(bits, own, got, decay(OWN), decay(PARTNER), *outputs)


def mix_next_row(bits, chip, row, total, got, out):
    right = bits[1]
    for i in range(out.shape[0]):
        scale_total = jnp.where(right, 1.0, row(i))
        scale_got = jnp.where(right, chip(i), 1.0)
        out[i] = scale_total * total[i, :HD] + scale_got * got[i, :HD]


def mix_next_column(bits, chip, corner, total, got, out):
    _, right, low = bits
    for i in range(out.shape[0]):
        scale_total = jnp.where(low & right, 0.0, 1.0)
        scale_got = jnp.where(low, jnp.where(right, 1.0, chip(i) * corner(i)), 0.0)
        out[i] = scale_total * total[i] + scale_got * got[i]


def lines(ref, first=0):
    return lambda i: ref[first + i : first + i + 1]


def mix_next_row_first(bits, arrays, outputs):
    chip, total, got = arrays
    mix_next_row(bits, lines(chip), lambda i: got[i, HD : HD + 1], total, got, *outputs)


def mix_next_column_first(bits, arrays, outputs):
    own, got, chip, corner, one_a, total, one_b = arrays
    out, table = outputs
    quarter = total.shape[0]
    for h in range(2 * quarter):
        place = HD + (TILE // 2) * (h // quarter)
        table[OWN, h : h + 1] = own[h, HD : HD + 1]
        table[PARTNER, h : h + 1] = got[h, HD : HD + 1]
        table[ROW, h : h + 1] = one_a[h % quarter, place : place + 1]
    table[CHIP] = chip[...]
    table[CORNER] = corner[...]
    mix_next_column(bits, lines(chip, quarter), lines(corner, quarter), total, one_b, out)


def mix_next_row_again(bits, arrays, outputs):
    table, total, got = arrays
    mix_next_row(bits, lines(table.at[CHIP]), lines(table.at[ROW]), total, got, *outputs)


def mix_next_column_again(bits, arrays, outputs):
    table, total, got = arrays
    quarter = total.shape[0]
    chip, corner = (lines(table.at[which], quarter) for which in (CHIP, CORNER))
    mix_next_column(bits, chip, corner, total, got, *outputs)


def mix_enter(bits, arrays, outputs):
    table, own, got, one_a, one_b, two_a, two_b = arrays
    kept, sent = outputs
    late, right, low = bits
    quarter = one_b.shape[0]
    decay = lambda which, h: table[which, h : h + 1]
    for h in range(2 * quarter):
        i = h % quarter
        row = jnp.where(right, decay(ROW, h), 1.0)
        if h < quarter:
            one, two = one_a[i, :HD], two_a[i]
            scale_one = jnp.where(right, 1.0, 0.0)
            scale_two = jnp.where(low, row, 0.0)
        else:
            one, two = one_b[i], two_b[i]
            scale_one = jnp.where(low, jnp.where(right, row, decay(CORNER, h)), 0.0)
            scale_two = jnp.where(low | right, 1.0, 0.0)
        enter = scale_one * one + scale_two * two
        after = jnp.where(late, decay(PARTNER, h), decay(OWN, h)) * enter
        after += jnp.where(late, got[h, :HD], own[h, :HD])
        kept[h] = jnp.where(late, after, enter)
        sent[h] = jnp.where(late, enter, after)


def entering_quad(send, own_task, table, place, backward, tasks):
    def work(stage, after, before=()):
        if stage not in tasks:
            return before
        run, outputs = tasks[stage]
        outputs.extend(run(after))
        return lax.optimization_barrier((before, outputs[0]))[0]

    name = "later" if backward else "earlier"
    half = send.shape[0]
    quarter = half // 2
    states, wide = (quarter, HD, HD), (quarter, HD + TILE, HD)
    got = swap(send, "seq", 1)
    own = own_task(send)
    if table is None:
        first, second, chip = mix(
            mix_total_first, backward, place, (own, got), (wide, states, (half, HD)), name + "_total"
        )
    else:
        first, second = mix(
            mix_total_again, backward, place, (table, own, got), (states, states), name + "_total"
        )
    one_a, one_b = swap(first, "seq", 2), swap(second, "seq", 4)
    if table is None:
        corner = swap(chip, "seq", 6)
        one_a, one_b, corner = work(1, second, (one_a, one_b, corner))
        (next_a,) = mix(
            mix_next_row_first, backward, place, (chip, first, one_a), (states,), name + "_row"
        )
        one_b, corner = follows((one_b, corner), next_a)
        next_b, table = mix(
            mix_next_column_first, backward, place,
            (own, got, chip, corner, one_a, second, one_b), (states, (5, half, HD)),
            name + "_column",
        )
    else:
        one_a, one_b = work(1, second, (one_a, one_b))
        (next_a,) = mix(
            mix_next_row_again, backward, place, (table, first, one_a), (states,), name + "_row"
        )
        (next_b,) = mix(
            mix_next_column_again, backward, place, (table, second, follows(one_b, next_a)),
            (states,), name + "_column",
        )
    two_a, two_b = swap(next_a, "seq", 4), swap(next_b, "seq", 2)
    two_a, two_b = work(2, next_b, (two_a, two_b))
    kept, sent = mix(
        mix_enter, backward, place, (table, own, got, one_a, one_b, two_a, two_b),
        ((half, HD, HD), (half, HD, HD)), name + "_enter",
    )
    received = swap(sent, "seq", 1)
    received = follows(received, tasks[3](follows(kept, sent)))
    return kept, received, table


def entering_any(send, own_task, log_total, backward, tasks):
    own = own_task(send)
    for stage in (1, 2):
        run, outputs = tasks[stage]
        outputs.extend(run(send))
    count, mine = lax.axis_size("seq"), lax.axis_index("seq")
    core = mine % 2
    own, send = own[:, :HD], send[:, :HD]
    half = own.shape[0]
    in_order = jnp.where(
        core == 0, jnp.concatenate([own, send], axis=0), jnp.concatenate([send, own], axis=0)
    )
    states = lax.all_gather(in_order, "seq")
    decays = jnp.exp(lax.all_gather(log_total, "seq"))
    place = mine
    if backward:
        states, decays, place = states[::-1], decays[::-1], count - 1 - mine

    def step(at, total):
        longer = decays[at][:, None, None] * total + states[at]
        return jnp.where(at < place, longer, total)

    total = lax.fori_loop(0, count - 1, step, jnp.zeros_like(in_order))
    kept = lax.dynamic_slice_in_dim(total, core * half, half)
    tasks[3](kept)
    return kept, lax.dynamic_slice_in_dim(total, (1 - core) * half, half)


def add(first, second):
    def kernel(first_ref, second_ref, out_ref):
        out_ref[...] = first_ref[...] + second_ref[...]

    return pl.pallas_call(
        kernel,
        in_specs=[NEAR, NEAR],
        out_specs=NEAR,
        out_shape=in_vmem(*first.shape),
        compiler_params=params(2),
        name="add",
    )(*near(first, second))


def sum_over_heads(value, tasks):
    tasks = list(tasks)
    results = []
    count = lax.axis_size("head")
    reach = 1
    while 2 * reach <= count and count % (2 * reach) == 0:
        got = swap(value, "head", reach)
        if tasks:
            results.append(tasks.pop(0)(value))
            got = follows(got, results[-1])
        value = add(value, got)
        reach *= 2
    results += [task(value) for task in tasks]
    part = value
    for shift in range(1, count // reach):
        value = add(
            value,
            lax.ppermute(part, "head", [(i, (i + shift * reach) % count) for i in range(count)]),
        )
    return value, results


def on_device(query_rows, key_rows, value_rows, output_grad, norm_gain, log_decay):
    mine = lax.axis_index("seq")
    bits = [(mine >> at) % 2 for at in range(3)]
    marks = [1 - bits[0], bits[0], *bits] + [jnp.zeros_like(mine)] * (TILE - 5)
    place = jnp.broadcast_to(jnp.stack(marks).astype(F32)[:, None], (TILE, HD))
    table = [None]

    def entering(send, own_task, backward, tasks):
        if lax.axis_size("seq") != 8:
            log_total = jnp.sum(log_decay, axis=1)
            return entering_any(send, own_task, log_total, backward, tasks)
        kept, received, table[0] = entering_quad(
            send, own_task, table[0], place, backward, tasks
        )
        return kept, received

    send, first_send, kh, vh, cum, _, decay, gain = state_to_send(
        place, norm_gain, log_decay, key_rows, value_rows
    )
    firsts, raws, in_0, in_1, begun = [], [], [], [], []

    def own_task(earlier):
        own, first, *raw = own_state(
            follows(kh, earlier), vh, cum, decay, query_rows, output_grad
        )
        firsts.extend((first, first_send))
        raws.append(raw)
        return own

    def forward_task(index):
        def task(earlier):
            *made, q_next, o_next = [
                *intra(
                    index, place, follows(cum, earlier), kh, vh, *firsts, raws[-1],
                    query_rows, output_grad,
                ),
                *raws[-1] * index,
            ]
            raws.append([q_next, o_next])
            return made

        return task

    def parts():
        q0, o0, _, _, columns0, inner0 = in_0
        q1, o1, _, _, columns1, inner1 = in_1
        return q0, q1, o0, o1, columns0, columns1, inner0, inner1

    def attend_task(kept):
        begun.extend(attend(0, gain, kept, parts()))
        return begun[-1]

    keep, recv = entering(
        send, own_task, False, {1: (forward_task(0), in_0), 2: (forward_task(1), in_1), 3: attend_task}
    )
    q0, o0, w0, decays0, columns0, _ = in_0
    q1, o1, w1, decays1, columns1, _ = in_1
    own_att = begun[:2]
    *other_att, sums = attend(1, gain, recv, parts(), begun[2:])
    sums, ((scaled, ends), remaining) = sum_over_heads(
        sums,
        (
            lambda earlier: scaled_queries(cum, follows(q0, earlier), q1),
            lambda earlier: remaining_decay(follows(cum, earlier)),
        ),
    )
    grad_send, second_send, *other_g = norm_grad(1, ends, gain, sums, scaled, (o0, o1, *other_att))
    own_g, seconds, queries, pairs, rows = [], [], [], [], []

    def own_grad_task(earlier):
        own, second, *grads = norm_grad(
            0, ends, gain, follows(sums, earlier), scaled, (o0, o1, *own_att)
        )
        own_g.extend(grads)
        seconds.extend((second, second_send))
        return own

    def query_task(earlier):
        return grad_query(
            follows(ends, earlier),
            (keep, recv, *firsts, kh, vh, *own_g, *other_g, decays0, decays1, columns0, columns1),
        )

    def pair_task(earlier):
        return grad_key_value(
            place, gain, sums, (*own_att, *other_att),
            (
                queries[1], w0, w1, q0, q1, kh, vh, *own_g, *other_g, remaining,
                follows(seconds[0], earlier), seconds[1],
            ),
        )

    def finish_task(kept):
        rows.extend(finish_own(place, queries[0], ends, kept, (kh, vh, remaining, *pairs[:2])))
        return rows[0]

    _, grad_recv = entering(
        grad_send, own_grad_task, True,
        {1: (query_task, queries), 2: (pair_task, pairs), 3: finish_task},
    )
    grad_k, grad_v = finish_other(
        place, rows[:2], ends, grad_recv, (kh, vh, remaining, *pairs[:2])
    )
    return pairs[2], rows[2], grad_k, grad_v


def solution(mesh):
    rows = P("seq", "head", None)
    return jax.shard_map(
        on_device,
        mesh=mesh,
        in_specs=(rows, rows, rows, rows, P("head", None), P("head", "seq")),
        out_specs=(rows, rows, rows, rows),
        check_vma=False,
    )
```

```python
import functools

import jax
import jax.numpy as jnp
from jax import lax
from jax.experimental import pallas as pl
from jax.experimental.pallas import tpu as pltpu
from jax.sharding import PartitionSpec as P

HEAD_TOTAL = 64
HD = 128
BLOCK = 256
CHUNK = 128
TILE = 8
F32 = jnp.float32
BF16 = jnp.bfloat16
MIB = 1024 * 1024
NEAR = pl.BlockSpec(memory_space=pltpu.VMEM)
FAR = pl.BlockSpec(memory_space=pl.ANY)
LOWER, UPPER, LATE, RIGHT, LOW = range(5)


def in_vmem(*shape, kind=F32):
    return pltpu.VMEM(shape, kind)


def near(*arrays):
    return [pltpu.with_memory_space_constraint(array, pltpu.VMEM) for array in arrays]


def far(*arrays):
    return [pltpu.with_memory_space_constraint(array, pltpu.HBM) for array in arrays]


def params(mib):
    return pltpu.CompilerParams(vmem_limit_bytes=mib * MIB)


def cost(flops, moved, exps=0):
    return pl.CostEstimate(flops=flops, bytes_accessed=moved, transcendentals=exps)


def block_cum(log_decay):
    size = log_decay.shape[1]
    upper = lax.broadcasted_iota(jnp.int32, (size, size), 0) <= lax.broadcasted_iota(
        jnp.int32, (size, size), 1
    )
    return jnp.dot(
        log_decay,
        jnp.where(upper, 1.0, 0.0).astype(F32),
        precision=lax.Precision.HIGHEST,
        preferred_element_type=F32,
    )


def as_columns(row):
    return jnp.broadcast_to(row, (HD, row.shape[1])).T


def dot(a, b):
    return jnp.dot(a, b, preferred_element_type=F32)


def dot_rows(a, b):
    return lax.dot_general(a, b, (((1,), (1,)), ((), ())), preferred_element_type=F32)


def two_parts(matrix):
    high = matrix.astype(BF16)
    return high, (matrix - high.astype(F32)).astype(BF16)


def times_state(rows, state):
    return dot(jnp.concatenate([rows, rows], axis=1), jnp.concatenate(two_parts(state), axis=0))


def times_state_t(rows, state):
    return dot_rows(
        jnp.concatenate([rows, rows], axis=1), jnp.concatenate(two_parts(state), axis=1)
    )


def decay_quarters(row, columns):
    half = row.shape[1] // 2
    lower = lax.broadcasted_iota(jnp.int32, (half, half), 0) >= lax.broadcasted_iota(
        jnp.int32, (half, half), 1
    )
    quarters = []
    for t, s in ((0, 0), (1, 0), (1, 1)):
        gap = columns[t * half : (t + 1) * half] - row[:, s * half : (s + 1) * half]
        quarters.append(jnp.exp(jnp.where(lower, gap, -jnp.inf) if t == s else gap))
    return quarters


def causal(table, quarters):
    half = table.shape[0] // 2
    first, second, third = (
        (table[t * half : (t + 1) * half, s * half : (s + 1) * half] * quarter).astype(BF16)
        for (t, s), quarter in zip(((0, 0), (1, 0), (1, 1)), quarters)
    )
    top = jnp.concatenate([first, jnp.zeros_like(first)], axis=1)
    return jnp.concatenate([top, jnp.concatenate([second, third], axis=1)], axis=0)


def transposed_dot(a, b):
    return lax.dot_general(a, b, (((0,), (0,)), ((), ())), preferred_element_type=F32)


def each_head(heads, unroll, body):
    def step(h, carry):
        body(h)
        return carry

    lax.fori_loop(0, heads, step, 0, unroll=unroll)


def each_half(half, unroll, body):
    for part in range(2):
        each_head(half, unroll, lambda i, part=part: body(part, i, part * half + i))


def turn_tiles(tiles):
    count = len(tiles)
    at = lax.broadcasted_iota(jnp.int32, tiles[0].shape, 0)
    turned = [tile if i == 0 else pltpu.roll(tile, i, 0) for i, tile in enumerate(tiles)]
    reach = 1
    while reach < count:
        odd = (at & reach) != 0
        turned = [
            jnp.where(odd, turned[(n + reach) % count], turned[n]) for n in range(count)
        ]
        reach *= 2
    picked = [turned[-j % count] for j in range(count)]
    return [tile if j == 0 else pltpu.roll(tile, count - j, 0) for j, tile in enumerate(picked)]


def is_upper(place_ref):
    return jnp.max(place_ref[UPPER : UPPER + 1]) > 0.5


def to_heads(dst, block, upper):
    tok, heads, _ = block.shape

    def step(group, carry):
        at = pl.multiple_of(group * 2 * TILE, 2 * TILE)
        tokens = block[pl.ds(at, 2 * TILE)].astype(F32)
        for first in range(0, heads, TILE):
            halves = [
                turn_tiles([tokens[base + i, first : first + TILE] for i in range(TILE)])
                for base in (0, TILE)
            ]
            local = jnp.where(upper, heads - TILE - first, first)
            for j in range(TILE):
                both = jnp.concatenate([halves[0][j], halves[1][j]], axis=0)
                dst[local + j, pl.ds(at, 2 * TILE)] = both.astype(BF16)
        return carry

    lax.fori_loop(0, tok // (2 * TILE), step, 0, unroll=4)


def from_heads(block, src, start, tok, upper):
    heads = src.shape[0]

    def step(group, carry):
        at = pl.multiple_of(group * TILE, TILE)
        parts = []
        for first in range(0, heads, TILE):
            local = jnp.where(upper, heads - TILE - first, first)
            parts.append(turn_tiles([src[local + i, pl.ds(start + at, TILE)] for i in range(TILE)]))
        for j in range(TILE):
            block[at + j] = jnp.concatenate([part[j] for part in parts], axis=0).astype(BF16)
        return carry

    lax.fori_loop(0, tok // TILE, step, 0, unroll=4)


def is_set(place_ref, which):
    return place_ref[which : which + 1] > 0.5


def in_local_order(place_ref, rows):
    half = rows.shape[0] // 2
    lower, upper = rows[:half], rows[half:]
    mine = jnp.broadcast_to(place_ref[LOWER : LOWER + 1, :1], lower.shape) > 0.5
    return jnp.concatenate(
        [jnp.where(mine, lower, upper), jnp.where(mine, upper, lower)], axis=0
    )


def half_states(part, kh, vh, cum, b, out, first=None, unroll=8):
    half = kh.shape[1] // 2

    def one(i):
        h = part * half + i
        row = cum[b, pl.ds(h, 1), :]
        scale = jnp.exp(row[:, BLOCK - 1 :] - row)
        state = dot((kh[b, h].astype(F32).T * scale).astype(BF16), vh[b, h])
        if first is not None:
            state += jnp.exp(row[:, BLOCK - 1 :]) * first[i]
        out[i, :HD] = state

    each_head(half, unroll, one)


def add_decays(out, decay, part):
    half = out.shape[0]
    for i in range(half):
        out[i, HD:] = jnp.broadcast_to(decay[part * half + i : part * half + i + 1], (TILE, HD))


def state_kernel(
    place_ref, gain_hbm, ld_hbm, k_hbm, v_hbm, send_ref, first_ref, kh, vh, cum, ld_ref, decay,
    gain_ref, gain_raw, ld_raw, k_raw, v_raw, sems,
):
    heads, tok = ld_ref.shape
    per_block = BLOCK // CHUNK
    copies = [pltpu.make_async_copy(ld_hbm, ld_raw, sems.at[0])]
    for c in range(tok // CHUNK):
        at = pl.ds(c * CHUNK, CHUNK)
        copies.append(pltpu.make_async_copy(k_hbm.at[at], k_raw.at[at], sems.at[2 * c + 1]))
        copies.append(pltpu.make_async_copy(v_hbm.at[at], v_raw.at[at], sems.at[2 * c + 2]))
    copies.append(pltpu.make_async_copy(gain_hbm, gain_raw, sems.at[len(copies)]))
    for copy in copies:
        copy.start()
    upper = is_upper(place_ref)
    copies[0].wait()
    ld_ref[...] = in_local_order(place_ref, ld_raw[...])
    for b in range(2):
        cum[b] = block_cum(ld_ref[:, b * BLOCK : (b + 1) * BLOCK])
    ends = cum[0, :, BLOCK - 1 :] + cum[1, :, BLOCK - 1 :]
    decay[...] = jnp.broadcast_to(jnp.exp(ends), decay.shape)

    for b in range(2):
        for c in range(per_block):
            at = pl.ds((b * per_block + c) * CHUNK, CHUNK)
            here = pl.ds(c * CHUNK, CHUNK)
            which = 2 * (b * per_block + c) + 1
            copies[which].wait()
            to_heads(kh.at[b, :, here], k_raw.at[at], upper)
            copies[which + 1].wait()
            to_heads(vh.at[b, :, here], v_raw.at[at], upper)
        if b == 0:
            half_states(1, kh, vh, cum, 0, first_ref)
        else:
            half_states(1, kh, vh, cum, 1, send_ref, first_ref)
    add_decays(send_ref, decay, 1)
    copies[-1].wait()
    gain_ref[...] = in_local_order(place_ref, gain_raw[...])


def state_to_send(place, gain, log_decay, key_rows, value_rows):
    tok, heads, dim = key_rows.shape
    half = heads // 2
    by_head = in_vmem(2, heads, BLOCK, dim, kind=BF16)
    return pl.pallas_call(
        state_kernel,
        in_specs=[NEAR, FAR, FAR, FAR, FAR],
        out_specs=[NEAR] * 8,
        out_shape=[
            in_vmem(half, dim + TILE, dim), in_vmem(half, dim, dim), by_head, by_head,
            in_vmem(2, heads, BLOCK), in_vmem(heads, tok), in_vmem(heads, dim), in_vmem(heads, dim),
        ],
        scratch_shapes=[
            pltpu.VMEM((heads, dim), F32),
            pltpu.VMEM((heads, tok), F32),
            pltpu.VMEM((tok, heads, dim), BF16),
            pltpu.VMEM((tok, heads, dim), BF16),
            pltpu.SemaphoreType.DMA((2 * (tok // CHUNK) + 2,)),
        ],
        compiler_params=params(8),
        cost_estimate=cost(tok * heads * dim * dim, 8 * tok * heads * dim),
        name="state_to_send",
    )(place, *far(gain, log_decay, key_rows, value_rows))


def fetch_block(index, arrays, blocks, sems):
    copies = [
        pltpu.make_async_copy(array.at[pl.ds(index * BLOCK, BLOCK)], block, sems.at[at])
        for at, (array, block) in enumerate(zip(arrays, blocks))
    ]
    for copy in copies:
        copy.start()
    return copies


def own_state_kernel(
    kh, vh, cum, decay, q_hbm, o_hbm, own_ref, first_ref, q_raw, o_raw, sems
):
    copies = fetch_block(0, (q_hbm, o_hbm), (q_raw, o_raw), sems)
    half_states(0, kh, vh, cum, 0, first_ref, unroll=4)
    half_states(0, kh, vh, cum, 1, own_ref, first_ref, unroll=4)
    add_decays(own_ref, decay, 0)
    for copy in copies:
        copy.wait()


def own_state(kh, vh, cum, decay, query_rows, output_grad):
    _, heads, tok, dim = kh.shape
    half = heads // 2
    raw = in_vmem(BLOCK, heads, dim, kind=BF16)
    return pl.pallas_call(
        own_state_kernel,
        in_specs=[NEAR] * 4 + [FAR, FAR],
        out_specs=[NEAR] * 4,
        out_shape=[in_vmem(half, dim + TILE, dim), in_vmem(half, dim, dim), raw, raw],
        scratch_shapes=[pltpu.SemaphoreType.DMA((2,))],
        compiler_params=params(4),
        cost_estimate=cost(2 * tok * heads * dim * dim, 4 * tok * heads * dim),
        name="own_state",
    )(*near(kh, vh, cum, decay), *far(query_rows, output_grad))


def intra(index, place, cum, kh, vh, first_own, first_send, raw, query_rows, output_grad):
    tok, heads, dim = query_rows.shape
    ahead = index == 0

    def kernel(place_ref, cum, kh, vh, first_own, first_send, q_raw, o_raw, *refs):
        if ahead:
            q_hbm, o_hbm, *refs = refs
            *refs, q_next, o_next, sems = refs
            copies = fetch_block(1, (q_hbm, o_hbm), (q_next, o_next), sems)
        qh, oh, w_ref, decays_ref, columns_ref, inner_ref = refs
        upper = is_upper(place_ref)
        to_heads(qh, q_raw, upper)
        to_heads(oh, o_raw, upper)

        def one(part, i, h):
            query = qh[h]
            row = cum[index, pl.ds(h, 1), :]
            columns = as_columns(row)
            quarters = decay_quarters(row, columns)
            for at, quarter in enumerate(quarters):
                decays_ref[h, at] = quarter
            weights = causal(dot_rows(query, kh[index, h]), quarters)
            w_ref[h] = weights.T
            inner = dot(weights, vh[index, h])
            columns = jnp.exp(columns)
            columns_ref[h] = columns
            if index:
                inner += columns * times_state(query, (first_own, first_send)[part][i])
            inner_ref[h] = inner

        each_half(heads // 2, 4, one)
        if ahead:
            for copy in copies:
                copy.wait()

    by_head = in_vmem(heads, BLOCK, dim, kind=BF16)
    return pl.pallas_call(
        kernel,
        in_specs=[NEAR] * 8 + [FAR, FAR] * ahead,
        out_specs=[NEAR] * (6 + 2 * ahead),
        out_shape=[
            by_head, by_head, in_vmem(heads, BLOCK, BLOCK, kind=BF16),
            in_vmem(heads, 3, BLOCK // 2, BLOCK // 2), in_vmem(heads, BLOCK, dim),
            in_vmem(heads, BLOCK, dim),
        ]
        + [in_vmem(BLOCK, heads, dim, kind=BF16)] * (2 * ahead),
        scratch_shapes=[pltpu.SemaphoreType.DMA((2,))] * ahead,
        compiler_params=params(4),
        cost_estimate=cost(
            2 * heads * BLOCK * BLOCK * dim * 4, 20 * heads * BLOCK * dim, heads * BLOCK * BLOCK
        ),
        name=f"intra_{index}",
    )(
        *near(place, cum, kh, vh, first_own, first_send, *raw),
        *(far(query_rows, output_grad) if ahead else ()),
    )


def attend_kernel(part, *refs):
    gain_ref, state_ref, q0, q1, o0, o1, columns0, columns1, inner0, inner1 = refs[:10]
    half = state_ref.shape[0]
    if part:
        before, att0, att1, sums_ref, partial = refs[10:]
        partial[...] = before[...]
    else:
        att0, att1, partial = refs[10:]
        partial[...] = jnp.zeros_like(partial)

    def one(i):
        h = part * half + i
        state = state_ref[i]
        gain = gain_ref[pl.ds(h, 1), :]
        blocks = ((q0, o0, columns0, inner0, att0), (q1, o1, columns1, inner1, att1))
        for b, (q, o, columns, inner, att) in enumerate(blocks):
            attended = inner[h] + columns[h] * times_state(q[h], state)
            att[i] = attended
            partial[0, b] += attended * attended
            partial[1, b] += gain * o[h].astype(F32) * attended
            state = columns[h, BLOCK - 1 :] * state

    each_head(half, 8, one)
    if part:
        ones = jnp.ones((8, HD), F32)
        for b in range(2):
            for at in range(2):
                line = lax.dot_general(
                    ones, partial[at, b], (((1,), (1,)), ((), ())),
                    precision=lax.Precision.HIGHEST, preferred_element_type=F32,
                )
                sums_ref[at : at + 1, b * BLOCK : (b + 1) * BLOCK] = line[:1]


def attend(part, gain, state, arrays, before=()):
    heads, dim = gain.shape
    tok = 2 * BLOCK
    half = heads // 2
    by_head = in_vmem(half, BLOCK, dim)
    partial = (2, 2, BLOCK, dim)
    return pl.pallas_call(
        functools.partial(attend_kernel, part),
        in_specs=[NEAR] * (10 + part),
        out_specs=[NEAR] * 3,
        out_shape=[by_head, by_head, in_vmem(2, tok) if part else in_vmem(*partial)],
        scratch_shapes=[pltpu.VMEM(partial, F32)] * part,
        compiler_params=params(6),
        cost_estimate=cost(2 * heads * tok * dim * dim, 8 * heads * tok * dim),
        name=f"attend_{part}",
    )(*near(gain, state, *arrays, *before))


def scaled_queries(cum, q0, q1):
    _, heads, _ = cum.shape

    def kernel(cum_ref, q0, q1, out_ref, ends_ref):
        for b in range(2):
            ends_ref[b] = jnp.broadcast_to(jnp.exp(cum_ref[b, :, BLOCK - 1 :]), (heads, HD))

        def one(h):
            for b, q in enumerate((q0, q1)):
                scale = jnp.exp(cum_ref[b, pl.ds(h, 1), :])
                out_ref[b, h] = (q[h].astype(F32).T * scale).astype(BF16)

        each_head(heads, 4, one)

    return pl.pallas_call(
        kernel,
        in_specs=[NEAR] * 3,
        out_specs=[NEAR] * 2,
        out_shape=[in_vmem(2, heads, HD, BLOCK, kind=BF16), in_vmem(2, heads, HD)],
        compiler_params=params(4),
        cost_estimate=cost(4 * heads * BLOCK * HD, 8 * heads * BLOCK * HD),
        name="scaled_queries",
    )(*near(cum, q0, q1))


def remaining_decay(cum):
    _, heads, _ = cum.shape

    def kernel(cum_ref, out_ref):
        def one(h):
            for b in range(2):
                row = cum_ref[b, pl.ds(h, 1), :]
                out_ref[b, h] = as_columns(jnp.exp(row[:, BLOCK - 1 :] - row))

        each_head(heads, 4, one)

    return pl.pallas_call(
        kernel,
        in_specs=[NEAR],
        out_specs=NEAR,
        out_shape=in_vmem(2, heads, BLOCK, HD),
        compiler_params=params(4),
        cost_estimate=cost(2 * heads * BLOCK * HD, 8 * heads * BLOCK * HD),
        name="remaining_decay",
    )(*near(cum))


def inverse_rms(sums_ref, b):
    at = slice(b * BLOCK, (b + 1) * BLOCK)
    inv = lax.rsqrt(sums_ref[0:1, at] / (HEAD_TOTAL * HD) + 1e-06)
    mean = sums_ref[1:2, at] * inv / (HEAD_TOTAL * HD)
    return inv, mean


def norm_grad(part, ends, gain, sums, scaled, arrays):
    heads, dim = gain.shape
    tok = 2 * BLOCK
    half = heads // 2

    def kernel(ends_ref, gain_ref, sums_ref, queries_ref, o0, o1, att0, att1,
               out_ref, second_ref, g0, g1, scales):
        for b in range(2):
            inv, mean = inverse_rms(sums_ref, b)
            scales[b, 0] = as_columns(inv)
            scales[b, 1] = as_columns(inv * inv * mean)

        def one(i):
            h = part * half + i
            line = gain_ref[pl.ds(h, 1), :]
            starts = []
            for b, (o, att, g) in enumerate(((o0, att0, g0), (o1, att1, g1))):
                grad = line * o[h].astype(F32) * scales[b, 0] - att[i] * scales[b, 1]
                grad = grad.astype(BF16)
                g[i] = grad
                starts.append(dot(queries_ref[b, h], grad))
            second_ref[i] = starts[1]
            out_ref[i] = starts[0] + ends_ref[0, pl.ds(h, 1)] * starts[1]

        each_head(half, 8, one)

    by_head = in_vmem(half, BLOCK, dim, kind=BF16)
    return pl.pallas_call(
        kernel,
        in_specs=[NEAR] * 8,
        out_specs=[NEAR] * 4,
        out_shape=[in_vmem(half, dim, dim), in_vmem(half, dim, dim), by_head, by_head],
        scratch_shapes=[pltpu.VMEM((2, 2, BLOCK, dim), F32)],
        compiler_params=params(4),
        cost_estimate=cost(heads * tok * dim * dim, 7 * heads * tok * dim),
        name=f"norm_grad_{part}",
    )(*near(ends, gain, sums, scaled, *arrays))


def normed_block(b, place_ref, gain_ref, sums_ref, halves, rows, raw):
    inv = as_columns(inverse_rms(sums_ref, b)[0])

    def one(part, i, h):
        rows[b, h] = halves[part][i] * inv * gain_ref[pl.ds(h, 1), :]

    each_half(halves[0].shape[0], 4, one)
    from_heads(raw, rows.at[b], 0, BLOCK, is_upper(place_ref))


def grad_q_kernel(
    place_ref, ends_ref, keep_ref, recv_ref, first_own, first_send, kh, vh, own0, own1, other0,
    other1, decays0, decays1, columns0, columns1, gs_ref, out_q, rows, raw, sems,
):
    upper = is_upper(place_ref)
    copies = []
    blocks = (((own0, other0), decays0, columns0), ((own1, other1), decays1, columns1))
    for b, (g, decays, columns) in enumerate(blocks):

        def one(part, i, h, b=b, g=g, decays=decays, columns=columns):
            grad = g[part][i]
            scores = causal(dot_rows(grad, vh[b, h]), [decays[h, at] for at in range(3)])
            gs_ref[b, h] = scores
            state = (keep_ref, recv_ref)[part][i]
            if b:
                state = ends_ref[0, pl.ds(h, 1)] * state + (first_own, first_send)[part][i]
            rows[h] = dot(scores, kh[b, h]) + columns[h] * times_state_t(grad, state)

        each_half(keep_ref.shape[0], 8, one)
        for start in range(0, BLOCK, CHUNK):
            at = pl.ds(b * BLOCK + start, CHUNK)
            from_heads(raw.at[at], rows, start, CHUNK, upper)
            copies.append(pltpu.make_async_copy(raw.at[at], out_q.at[at], sems.at[len(copies)]))
            copies[-1].start()
    for copy in copies:
        copy.wait()


def grad_query(place, ends, arrays):
    _, heads, dim = ends.shape
    tok = 2 * BLOCK
    return pl.pallas_call(
        grad_q_kernel,
        in_specs=[NEAR] * 16,
        out_specs=[NEAR, FAR],
        out_shape=[
            in_vmem(2, heads, BLOCK, BLOCK, kind=BF16),
            jax.ShapeDtypeStruct((tok, heads, dim), BF16),
        ],
        scratch_shapes=[
            pltpu.VMEM((heads, BLOCK, dim), F32),
            pltpu.VMEM((tok, heads, dim), BF16),
            pltpu.SemaphoreType.DMA((tok // CHUNK,)),
        ],
        compiler_params=params(8),
        cost_estimate=cost(
            4 * heads * tok * dim * (BLOCK + dim), 12 * heads * tok * dim, heads * tok * BLOCK
        ),
        name="grad_query",
    )(*near(place, ends, *arrays))


def grad_kv_kernel(
    place_ref, gain_ref, sums_ref, att_own0, att_own1, att_other0, att_other1,
    gs_ref, w0, w1, q0, q1, kh, vh, own0, own1, other0, other1, remaining_ref,
    second_own, second_send, dk, dv, out_normed, raw, sems,
):
    copies = []
    for b, halves in enumerate(((att_own0, att_other0), (att_own1, att_other1))):
        at = pl.ds(b * BLOCK, BLOCK)
        normed_block(b, place_ref, gain_ref, sums_ref, halves, dk, raw.at[at])
        copies.append(pltpu.make_async_copy(raw.at[at], out_normed.at[at], sems.at[b]))
        copies[-1].start()

    def one(part, i, h):
        columns = remaining_ref[0, h]
        state = (second_own, second_send)[part][i]
        g0, g1 = ((own0, own1), (other0, other1))[part]
        dk[0, h] = transposed_dot(gs_ref[0, h], q0[h]) + columns * times_state_t(vh[0, h], state)
        dv[0, h] = dot(w0[h], g0[i]) + columns * times_state(kh[0, h], state)
        dk[1, h] = transposed_dot(gs_ref[1, h], q1[h])
        dv[1, h] = dot(w1[h], g1[i])

    each_half(second_own.shape[0], 4, one)
    for copy in copies:
        copy.wait()


def grad_key_value(place, gain, sums, att, arrays):
    heads, dim = gain.shape
    tok = 2 * BLOCK
    return pl.pallas_call(
        grad_kv_kernel,
        in_specs=[NEAR] * 21,
        out_specs=[NEAR, NEAR, FAR],
        out_shape=[in_vmem(2, heads, BLOCK, dim)] * 2
        + [jax.ShapeDtypeStruct((tok, heads, dim), BF16)],
        scratch_shapes=[
            pltpu.VMEM((tok, heads, dim), BF16),
            pltpu.SemaphoreType.DMA((2,)),
        ],
        compiler_params=params(6),
        cost_estimate=cost(4 * heads * tok * dim * (BLOCK + dim), 30 * heads * tok * dim),
        name="grad_key_value",
    )(*near(place, gain, sums, *att, *arrays))


def finish_rows(part, b, ends_ref, state_ref, kh, vh, remaining_ref, dk, dv, rows_k, rows_v):
    half = state_ref.shape[0]

    def one(i):
        h = part * half + i
        columns = remaining_ref[b, h]
        state = state_ref[i]
        if b == 0:
            state = ends_ref[1, pl.ds(h, 1)] * state
        state = state.astype(BF16)
        none = jnp.zeros_like(state)
        both = jnp.concatenate(
            [jnp.concatenate([state.T, none], axis=1), jnp.concatenate([none, state], axis=1)],
            axis=0,
        )
        carried = dot(jnp.concatenate([vh[b, h], kh[b, h]], axis=1), both)
        rows_k[b, h] = dk[b, h] + columns * carried[:, :HD]
        rows_v[b, h] = dv[b, h] + columns * carried[:, HD:]

    each_head(half, 8, one)


def finish_own_kernel(*refs):
    for b in range(2):
        finish_rows(0, b, *refs)


def finish_other_kernel(
    place_ref, old_k, old_v, ends_ref, state_ref, kh, vh, remaining_ref, dk, dv,
    out_k, out_v, rows_k, rows_v, raw_k, raw_v, sems,
):
    upper = is_upper(place_ref)
    copies = []
    for b in range(2):
        finish_rows(1, b, ends_ref, state_ref, kh, vh, remaining_ref, dk, dv, rows_k, rows_v)
        for start in range(0, BLOCK, CHUNK // 2):
            at = pl.ds(b * BLOCK + start, CHUNK // 2)
            for rows, raw, out in ((rows_k, raw_k, out_k), (rows_v, raw_v, out_v)):
                from_heads(raw.at[at], rows.at[b], start, CHUNK // 2, upper)
                copies.append(pltpu.make_async_copy(raw.at[at], out.at[at], sems.at[len(copies)]))
                copies[-1].start()
    for copy in copies:
        copy.wait()


def finish_own(ends, keep, arrays):
    _, heads, dim = ends.shape
    tok = 2 * BLOCK
    return pl.pallas_call(
        finish_own_kernel,
        in_specs=[NEAR] * 7,
        out_specs=[NEAR, NEAR],
        out_shape=[in_vmem(2, heads, BLOCK, dim)] * 2,
        compiler_params=params(4),
        cost_estimate=cost(4 * heads * tok * dim * dim, 8 * heads * tok * dim),
        name="finish_own",
    )(*near(ends, keep, *arrays))


def finish_other(place, rows, ends, recv, arrays):
    _, heads, dim = ends.shape
    tok = 2 * BLOCK
    shape = jax.ShapeDtypeStruct((tok, heads, dim), BF16)
    return pl.pallas_call(
        finish_other_kernel,
        in_specs=[NEAR] * 10,
        out_specs=[FAR, FAR, NEAR, NEAR],
        out_shape=[shape, shape] + [in_vmem(2, heads, BLOCK, dim)] * 2,
        input_output_aliases={1: 2, 2: 3},
        scratch_shapes=[
            pltpu.VMEM((tok, heads, dim), BF16),
            pltpu.VMEM((tok, heads, dim), BF16),
            pltpu.SemaphoreType.DMA((4 * (tok // CHUNK),)),
        ],
        compiler_params=params(8),
        cost_estimate=cost(4 * heads * tok * dim * dim, 8 * heads * tok * dim),
        name="finish_other",
    )(*near(place, *rows, ends, recv, *arrays))[:2]


def follows(value, earlier):
    return lax.optimization_barrier((value, earlier))[0]


def swap(value, axis, bit):
    count = lax.axis_size(axis)
    return lax.ppermute(value, axis, [(i, i ^ bit) for i in range(count)])


def mix(body, backward, place, arrays, shapes, name):
    def kernel(place_ref, *refs):
        bits = [is_set(place_ref, which) != backward for which in (LATE, RIGHT, LOW)]
        body(bits, refs[: len(arrays)], refs[len(arrays) :])

    return pl.pallas_call(
        kernel,
        in_specs=[NEAR] + [NEAR] * len(arrays),
        out_specs=[NEAR] * len(shapes),
        out_shape=[in_vmem(*shape) for shape in shapes],
        compiler_params=params(4),
        cost_estimate=cost(4 * 8 * HD * HD, 16 * 8 * HD * HD),
        name=name,
    )(place, *near(*arrays))


OWN, PARTNER, CHIP, ROW, CORNER = range(5)


def mix_total(bits, own, got, d_own, d_got, first, second):
    late = bits[0]
    quarter = first.shape[0]
    for h in range(2 * quarter):
        total = jnp.where(late, 1.0, d_got(h)) * own[h, :HD] + jnp.where(late, d_own(h), 1.0) * got[h, :HD]
        if h < quarter:
            first[h, :HD] = total
        else:
            second[h - quarter] = total


def mix_total_first(bits, arrays, outputs):
    own, got = arrays
    first, second, chip = outputs
    quarter = first.shape[0]
    d_own = lambda h: own[h, HD : HD + 1]
    d_got = lambda h: got[h, HD : HD + 1]
    mix_total(bits, own, got, d_own, d_got, first, second)
    for h in range(2 * quarter):
        whole = d_own(h) * d_got(h)
        chip[h : h + 1] = whole
        place = HD + (TILE // 2) * (h // quarter)
        first[h % quarter, place : place + TILE // 2] = jnp.broadcast_to(whole, (TILE // 2, HD))


def mix_total_again(bits, arrays, outputs):
    table, own, got = arrays
    decay = lambda which: lambda h: table[which, h : h + 1]
    mix_total(bits, own, got, decay(OWN), decay(PARTNER), *outputs)


def mix_next_row(bits, chip, row, total, got, out):
    right = bits[1]
    for i in range(out.shape[0]):
        scale_total = jnp.where(right, 1.0, row(i))
        scale_got = jnp.where(right, chip(i), 1.0)
        out[i] = scale_total * total[i, :HD] + scale_got * got[i, :HD]


def mix_next_column(bits, chip, corner, total, got, out):
    _, right, low = bits
    for i in range(out.shape[0]):
        scale_total = jnp.where(low & right, 0.0, 1.0)
        scale_got = jnp.where(low, jnp.where(right, 1.0, chip(i) * corner(i)), 0.0)
        out[i] = scale_total * total[i] + scale_got * got[i]


def lines(ref, first=0):
    return lambda i: ref[first + i : first + i + 1]


def mix_next_row_first(bits, arrays, outputs):
    chip, total, got = arrays
    mix_next_row(bits, lines(chip), lambda i: got[i, HD : HD + 1], total, got, *outputs)


def mix_next_column_first(bits, arrays, outputs):
    own, got, chip, corner, one_a, total, one_b = arrays
    out, table = outputs
    quarter = total.shape[0]
    for h in range(2 * quarter):
        place = HD + (TILE // 2) * (h // quarter)
        table[OWN, h : h + 1] = own[h, HD : HD + 1]
        table[PARTNER, h : h + 1] = got[h, HD : HD + 1]
        table[ROW, h : h + 1] = one_a[h % quarter, place : place + 1]
    table[CHIP] = chip[...]
    table[CORNER] = corner[...]
    mix_next_column(bits, lines(chip, quarter), lines(corner, quarter), total, one_b, out)


def mix_next_row_again(bits, arrays, outputs):
    table, total, got = arrays
    mix_next_row(bits, lines(table.at[CHIP]), lines(table.at[ROW]), total, got, *outputs)


def mix_next_column_again(bits, arrays, outputs):
    table, total, got = arrays
    quarter = total.shape[0]
    chip, corner = (lines(table.at[which], quarter) for which in (CHIP, CORNER))
    mix_next_column(bits, chip, corner, total, got, *outputs)


def mix_enter(bits, arrays, outputs):
    table, own, got, one_a, one_b, two_a, two_b = arrays
    kept, sent = outputs
    late, right, low = bits
    quarter = one_b.shape[0]
    decay = lambda which, h: table[which, h : h + 1]
    for h in range(2 * quarter):
        i = h % quarter
        row = jnp.where(right, decay(ROW, h), 1.0)
        if h < quarter:
            one, two = one_a[i, :HD], two_a[i]
            scale_one = jnp.where(right, 1.0, 0.0)
            scale_two = jnp.where(low, row, 0.0)
        else:
            one, two = one_b[i], two_b[i]
            scale_one = jnp.where(low, jnp.where(right, row, decay(CORNER, h)), 0.0)
            scale_two = jnp.where(low | right, 1.0, 0.0)
        enter = scale_one * one + scale_two * two
        after = jnp.where(late, decay(PARTNER, h), decay(OWN, h)) * enter
        after += jnp.where(late, got[h, :HD], own[h, :HD])
        kept[h] = jnp.where(late, after, enter)
        sent[h] = jnp.where(late, enter, after)


def entering_quad(send, own_task, table, place, backward, tasks):
    def work(stage, after, before=()):
        if stage not in tasks:
            return before
        run, outputs = tasks[stage]
        outputs.extend(run(after))
        return lax.optimization_barrier((before, outputs[0]))[0]

    name = "later" if backward else "earlier"
    half = send.shape[0]
    quarter = half // 2
    states, wide = (quarter, HD, HD), (quarter, HD + TILE, HD)
    got = swap(send, "seq", 1)
    own = own_task(send)
    if table is None:
        first, second, chip = mix(
            mix_total_first, backward, place, (own, got), (wide, states, (half, HD)), name + "_total"
        )
    else:
        first, second = mix(
            mix_total_again, backward, place, (table, own, got), (states, states), name + "_total"
        )
    one_a, one_b = swap(first, "seq", 2), swap(second, "seq", 4)
    if table is None:
        corner = swap(chip, "seq", 6)
        one_a, one_b, corner = work(1, second, (one_a, one_b, corner))
        (next_a,) = mix(
            mix_next_row_first, backward, place, (chip, first, one_a), (states,), name + "_row"
        )
        one_b, corner = follows((one_b, corner), next_a)
        next_b, table = mix(
            mix_next_column_first, backward, place,
            (own, got, chip, corner, one_a, second, one_b), (states, (5, half, HD)),
            name + "_column",
        )
    else:
        one_a, one_b = work(1, second, (one_a, one_b))
        (next_a,) = mix(
            mix_next_row_again, backward, place, (table, first, one_a), (states,), name + "_row"
        )
        (next_b,) = mix(
            mix_next_column_again, backward, place, (table, second, follows(one_b, next_a)),
            (states,), name + "_column",
        )
    two_a, two_b = swap(next_a, "seq", 4), swap(next_b, "seq", 2)
    two_a, two_b = work(2, next_b, (two_a, two_b))
    kept, sent = mix(
        mix_enter, backward, place, (table, own, got, one_a, one_b, two_a, two_b),
        ((half, HD, HD), (half, HD, HD)), name + "_enter",
    )
    received = swap(sent, "seq", 1)
    received = follows(received, tasks[3](follows(kept, sent)))
    return kept, received, table


def entering_any(send, own_task, log_total, backward, tasks):
    own = own_task(send)
    for stage in (1, 2):
        run, outputs = tasks[stage]
        outputs.extend(run(send))
    count, mine = lax.axis_size("seq"), lax.axis_index("seq")
    core = mine % 2
    own, send = own[:, :HD], send[:, :HD]
    half = own.shape[0]
    in_order = jnp.where(
        core == 0, jnp.concatenate([own, send], axis=0), jnp.concatenate([send, own], axis=0)
    )
    states = lax.all_gather(in_order, "seq")
    decays = jnp.exp(lax.all_gather(log_total, "seq"))
    place = mine
    if backward:
        states, decays, place = states[::-1], decays[::-1], count - 1 - mine

    def step(at, total):
        longer = decays[at][:, None, None] * total + states[at]
        return jnp.where(at < place, longer, total)

    total = lax.fori_loop(0, count - 1, step, jnp.zeros_like(in_order))
    kept = lax.dynamic_slice_in_dim(total, core * half, half)
    tasks[3](kept)
    return kept, lax.dynamic_slice_in_dim(total, (1 - core) * half, half)


def add(first, second):
    def kernel(first_ref, second_ref, out_ref):
        out_ref[...] = first_ref[...] + second_ref[...]

    return pl.pallas_call(
        kernel,
        in_specs=[NEAR, NEAR],
        out_specs=NEAR,
        out_shape=in_vmem(*first.shape),
        compiler_params=params(2),
        name="add",
    )(*near(first, second))


def sum_over_heads(value, tasks):
    tasks = list(tasks)
    results = []
    count = lax.axis_size("head")
    reach = 1
    while 2 * reach <= count and count % (2 * reach) == 0:
        got = swap(value, "head", reach)
        if tasks:
            results.append(tasks.pop(0)(value))
            got = follows(got, results[-1])
        value = add(value, got)
        reach *= 2
    results += [task(value) for task in tasks]
    part = value
    for shift in range(1, count // reach):
        value = add(
            value,
            lax.ppermute(part, "head", [(i, (i + shift * reach) % count) for i in range(count)]),
        )
    return value, results


def on_device(query_rows, key_rows, value_rows, output_grad, norm_gain, log_decay):
    mine = lax.axis_index("seq")
    bits = [(mine >> at) % 2 for at in range(3)]
    marks = [1 - bits[0], bits[0], *bits] + [jnp.zeros_like(mine)] * (TILE - 5)
    place = jnp.broadcast_to(jnp.stack(marks).astype(F32)[:, None], (TILE, HD))
    table = [None]

    def entering(send, own_task, backward, tasks):
        if lax.axis_size("seq") != 8:
            log_total = jnp.sum(log_decay, axis=1)
            return entering_any(send, own_task, log_total, backward, tasks)
        kept, received, table[0] = entering_quad(
            send, own_task, table[0], place, backward, tasks
        )
        return kept, received

    send, first_send, kh, vh, cum, _, decay, gain = state_to_send(
        place, norm_gain, log_decay, key_rows, value_rows
    )
    firsts, raws, in_0, in_1, begun = [], [], [], [], []

    def own_task(earlier):
        own, first, *raw = own_state(
            follows(kh, earlier), vh, cum, decay, query_rows, output_grad
        )
        firsts.extend((first, first_send))
        raws.append(raw)
        return own

    def forward_task(index):
        def task(earlier):
            *made, q_next, o_next = [
                *intra(
                    index, place, follows(cum, earlier), kh, vh, *firsts, raws[-1],
                    query_rows, output_grad,
                ),
                *raws[-1] * index,
            ]
            raws.append([q_next, o_next])
            return made

        return task

    def parts():
        q0, o0, _, _, columns0, inner0 = in_0
        q1, o1, _, _, columns1, inner1 = in_1
        return q0, q1, o0, o1, columns0, columns1, inner0, inner1

    def attend_task(kept):
        begun.extend(attend(0, gain, kept, parts()))
        return begun[-1]

    keep, recv = entering(
        send, own_task, False, {1: (forward_task(0), in_0), 2: (forward_task(1), in_1), 3: attend_task}
    )
    q0, o0, w0, decays0, columns0, _ = in_0
    q1, o1, w1, decays1, columns1, _ = in_1
    own_att = begun[:2]
    *other_att, sums = attend(1, gain, recv, parts(), begun[2:])
    sums, ((scaled, ends), remaining) = sum_over_heads(
        sums,
        (
            lambda earlier: scaled_queries(cum, follows(q0, earlier), q1),
            lambda earlier: remaining_decay(follows(cum, earlier)),
        ),
    )
    grad_send, second_send, *other_g = norm_grad(1, ends, gain, sums, scaled, (o0, o1, *other_att))
    own_g, seconds, queries, pairs, rows = [], [], [], [], []

    def own_grad_task(earlier):
        own, second, *grads = norm_grad(
            0, ends, gain, follows(sums, earlier), scaled, (o0, o1, *own_att)
        )
        own_g.extend(grads)
        seconds.extend((second, second_send))
        return own

    def query_task(earlier):
        return grad_query(
            place, follows(ends, earlier),
            (keep, recv, *firsts, kh, vh, *own_g, *other_g, decays0, decays1, columns0, columns1),
        )

    def pair_task(earlier):
        return grad_key_value(
            place, gain, sums, (*own_att, *other_att),
            (
                queries[0], w0, w1, q0, q1, kh, vh, *own_g, *other_g, remaining,
                follows(seconds[0], earlier), seconds[1],
            ),
        )

    def finish_task(kept):
        rows.extend(finish_own(ends, kept, (kh, vh, remaining, *pairs[:2])))
        return rows[0]

    _, grad_recv = entering(
        grad_send, own_grad_task, True,
        {1: (query_task, queries), 2: (pair_task, pairs), 3: finish_task},
    )
    grad_k, grad_v = finish_other(
        place, rows, ends, grad_recv, (kh, vh, remaining, *pairs[:2])
    )
    return pairs[2], queries[1], grad_k, grad_v


def solution(mesh):
    rows = P("seq", "head", None)
    return jax.shard_map(
        on_device,
        mesh=mesh,
        in_specs=(rows, rows, rows, rows, P("head", None), P("head", "seq")),
        out_specs=(rows, rows, rows, rows),
        check_vma=False,
    )
```

```python
import functools

import jax
import jax.numpy as jnp
from jax import lax
from jax.experimental import pallas as pl
from jax.experimental.pallas import tpu as pltpu
from jax.sharding import PartitionSpec as P

HEAD_TOTAL = 64
HD = 128
BLOCK = 256
CHUNK = 128
TILE = 8
F32 = jnp.float32
BF16 = jnp.bfloat16
MIB = 1024 * 1024
NEAR = pl.BlockSpec(memory_space=pltpu.VMEM)
FAR = pl.BlockSpec(memory_space=pl.ANY)
LOWER, UPPER, LATE, RIGHT, LOW = range(5)


def in_vmem(*shape, kind=F32):
    return pltpu.VMEM(shape, kind)


def near(*arrays):
    return [pltpu.with_memory_space_constraint(array, pltpu.VMEM) for array in arrays]


def far(*arrays):
    return [pltpu.with_memory_space_constraint(array, pltpu.HBM) for array in arrays]


def params(mib):
    return pltpu.CompilerParams(vmem_limit_bytes=mib * MIB)


def cost(flops, moved, exps=0):
    return pl.CostEstimate(flops=flops, bytes_accessed=moved, transcendentals=exps)


def block_cum(log_decay):
    size = log_decay.shape[1]
    upper = lax.broadcasted_iota(jnp.int32, (size, size), 0) <= lax.broadcasted_iota(
        jnp.int32, (size, size), 1
    )
    return jnp.dot(
        log_decay,
        jnp.where(upper, 1.0, 0.0).astype(F32),
        precision=lax.Precision.HIGHEST,
        preferred_element_type=F32,
    )


def as_columns(row):
    return jnp.broadcast_to(row, (HD, row.shape[1])).T


def dot(a, b):
    return jnp.dot(a, b, preferred_element_type=F32)


def dot_rows(a, b):
    return lax.dot_general(a, b, (((1,), (1,)), ((), ())), preferred_element_type=F32)


def two_parts(matrix):
    high = matrix.astype(BF16)
    return high, (matrix - high.astype(F32)).astype(BF16)


def times_state(rows, state):
    return dot(jnp.concatenate([rows, rows], axis=1), jnp.concatenate(two_parts(state), axis=0))


def times_state_t(rows, state):
    return dot_rows(
        jnp.concatenate([rows, rows], axis=1), jnp.concatenate(two_parts(state), axis=1)
    )


def decay_quarters(row, columns):
    half = row.shape[1] // 2
    lower = lax.broadcasted_iota(jnp.int32, (half, half), 0) >= lax.broadcasted_iota(
        jnp.int32, (half, half), 1
    )
    quarters = []
    for t, s in ((0, 0), (1, 0), (1, 1)):
        gap = columns[t * half : (t + 1) * half] - row[:, s * half : (s + 1) * half]
        quarters.append(jnp.exp(jnp.where(lower, gap, -jnp.inf) if t == s else gap))
    return quarters


def causal(table, quarters):
    half = table.shape[0] // 2
    first, second, third = (
        (table[t * half : (t + 1) * half, s * half : (s + 1) * half] * quarter).astype(BF16)
        for (t, s), quarter in zip(((0, 0), (1, 0), (1, 1)), quarters)
    )
    top = jnp.concatenate([first, jnp.zeros_like(first)], axis=1)
    return jnp.concatenate([top, jnp.concatenate([second, third], axis=1)], axis=0)


def transposed_dot(a, b):
    return lax.dot_general(a, b, (((0,), (0,)), ((), ())), preferred_element_type=F32)


def each_head(heads, unroll, body):
    def step(h, carry):
        body(h)
        return carry

    lax.fori_loop(0, heads, step, 0, unroll=unroll)


def each_half(half, unroll, body):
    for part in range(2):
        each_head(half, unroll, lambda i, part=part: body(part, i, part * half + i))


def turn_tiles(tiles):
    count = len(tiles)
    at = lax.broadcasted_iota(jnp.int32, tiles[0].shape, 0)
    turned = [tile if i == 0 else pltpu.roll(tile, i, 0) for i, tile in enumerate(tiles)]
    reach = 1
    while reach < count:
        odd = (at & reach) != 0
        turned = [
            jnp.where(odd, turned[(n + reach) % count], turned[n]) for n in range(count)
        ]
        reach *= 2
    picked = [turned[-j % count] for j in range(count)]
    return [tile if j == 0 else pltpu.roll(tile, count - j, 0) for j, tile in enumerate(picked)]


def is_upper(place_ref):
    return jnp.max(place_ref[UPPER : UPPER + 1]) > 0.5


def to_heads(dst, block, upper):
    tok, heads, _ = block.shape

    def step(group, carry):
        at = pl.multiple_of(group * 2 * TILE, 2 * TILE)
        tokens = block[pl.ds(at, 2 * TILE)].astype(F32)
        for first in range(0, heads, TILE):
            halves = [
                turn_tiles([tokens[base + i, first : first + TILE] for i in range(TILE)])
                for base in (0, TILE)
            ]
            local = jnp.where(upper, heads - TILE - first, first)
            for j in range(TILE):
                both = jnp.concatenate([halves[0][j], halves[1][j]], axis=0)
                dst[local + j, pl.ds(at, 2 * TILE)] = both.astype(BF16)
        return carry

    lax.fori_loop(0, tok // (2 * TILE), step, 0, unroll=4)


def from_heads(block, src, start, tok, upper):
    heads = src.shape[0]

    def step(group, carry):
        at = pl.multiple_of(group * TILE, TILE)
        parts = []
        for first in range(0, heads, TILE):
            local = jnp.where(upper, heads - TILE - first, first)
            parts.append(turn_tiles([src[local + i, pl.ds(start + at, TILE)] for i in range(TILE)]))
        for j in range(TILE):
            block[at + j] = jnp.concatenate([part[j] for part in parts], axis=0).astype(BF16)
        return carry

    lax.fori_loop(0, tok // TILE, step, 0, unroll=4)


def is_set(place_ref, which):
    return place_ref[which : which + 1] > 0.5


def in_local_order(place_ref, rows):
    half = rows.shape[0] // 2
    lower, upper = rows[:half], rows[half:]
    mine = jnp.broadcast_to(place_ref[LOWER : LOWER + 1, :1], lower.shape) > 0.5
    return jnp.concatenate(
        [jnp.where(mine, lower, upper), jnp.where(mine, upper, lower)], axis=0
    )


def half_states(part, kh, vh, cum, b, out, first=None, unroll=8):
    half = kh.shape[1] // 2

    def one(i):
        h = part * half + i
        row = cum[b, pl.ds(h, 1), :]
        scale = jnp.exp(row[:, BLOCK - 1 :] - row)
        state = dot((kh[b, h].astype(F32).T * scale).astype(BF16), vh[b, h])
        if first is not None:
            state += jnp.exp(row[:, BLOCK - 1 :]) * first[i]
        out[i, :HD] = state

    each_head(half, unroll, one)


def add_decays(out, decay, part):
    half = out.shape[0]
    for i in range(half):
        out[i, HD:] = jnp.broadcast_to(decay[part * half + i : part * half + i + 1], (TILE, HD))


def state_kernel(
    place_ref, gain_hbm, ld_hbm, k_hbm, v_hbm, send_ref, first_ref, kh, vh, cum, ld_ref, decay,
    gain_ref, gain_raw, ld_raw, k_raw, v_raw, sems,
):
    heads, tok = ld_ref.shape
    per_block = BLOCK // CHUNK
    copies = [pltpu.make_async_copy(ld_hbm, ld_raw, sems.at[0])]
    for c in range(tok // CHUNK):
        at = pl.ds(c * CHUNK, CHUNK)
        copies.append(pltpu.make_async_copy(k_hbm.at[at], k_raw.at[at], sems.at[2 * c + 1]))
        copies.append(pltpu.make_async_copy(v_hbm.at[at], v_raw.at[at], sems.at[2 * c + 2]))
    copies.append(pltpu.make_async_copy(gain_hbm, gain_raw, sems.at[len(copies)]))
    for copy in copies:
        copy.start()
    upper = is_upper(place_ref)
    copies[0].wait()
    ld_ref[...] = in_local_order(place_ref, ld_raw[...])
    for b in range(2):
        cum[b] = block_cum(ld_ref[:, b * BLOCK : (b + 1) * BLOCK])
    ends = cum[0, :, BLOCK - 1 :] + cum[1, :, BLOCK - 1 :]
    decay[...] = jnp.broadcast_to(jnp.exp(ends), decay.shape)

    for b in range(2):
        for c in range(per_block):
            at = pl.ds((b * per_block + c) * CHUNK, CHUNK)
            here = pl.ds(c * CHUNK, CHUNK)
            which = 2 * (b * per_block + c) + 1
            copies[which].wait()
            to_heads(kh.at[b, :, here], k_raw.at[at], upper)
            copies[which + 1].wait()
            to_heads(vh.at[b, :, here], v_raw.at[at], upper)
        if b == 0:
            half_states(1, kh, vh, cum, 0, first_ref)
        else:
            half_states(1, kh, vh, cum, 1, send_ref, first_ref)
    add_decays(send_ref, decay, 1)
    copies[-1].wait()
    gain_ref[...] = in_local_order(place_ref, gain_raw[...])


def state_to_send(place, gain, log_decay, key_rows, value_rows):
    tok, heads, dim = key_rows.shape
    half = heads // 2
    by_head = in_vmem(2, heads, BLOCK, dim, kind=BF16)
    return pl.pallas_call(
        state_kernel,
        in_specs=[NEAR, FAR, FAR, FAR, FAR],
        out_specs=[NEAR] * 8,
        out_shape=[
            in_vmem(half, dim + TILE, dim), in_vmem(half, dim, dim), by_head, by_head,
            in_vmem(2, heads, BLOCK), in_vmem(heads, tok), in_vmem(heads, dim), in_vmem(heads, dim),
        ],
        scratch_shapes=[
            pltpu.VMEM((heads, dim), F32),
            pltpu.VMEM((heads, tok), F32),
            pltpu.VMEM((tok, heads, dim), BF16),
            pltpu.VMEM((tok, heads, dim), BF16),
            pltpu.SemaphoreType.DMA((2 * (tok // CHUNK) + 2,)),
        ],
        compiler_params=params(8),
        cost_estimate=cost(tok * heads * dim * dim, 8 * tok * heads * dim),
        name="state_to_send",
    )(place, *far(gain, log_decay, key_rows, value_rows))


def fetch_block(index, arrays, blocks, sems):
    copies = [
        pltpu.make_async_copy(array.at[pl.ds(index * BLOCK, BLOCK)], block, sems.at[at])
        for at, (array, block) in enumerate(zip(arrays, blocks))
    ]
    for copy in copies:
        copy.start()
    return copies


def own_state_kernel(
    kh, vh, cum, decay, q_hbm, o_hbm, own_ref, first_ref, q_raw, o_raw, sems
):
    copies = fetch_block(0, (q_hbm, o_hbm), (q_raw, o_raw), sems)
    half_states(0, kh, vh, cum, 0, first_ref, unroll=4)
    half_states(0, kh, vh, cum, 1, own_ref, first_ref, unroll=4)
    add_decays(own_ref, decay, 0)
    for copy in copies:
        copy.wait()


def own_state(kh, vh, cum, decay, query_rows, output_grad):
    _, heads, tok, dim = kh.shape
    half = heads // 2
    raw = in_vmem(BLOCK, heads, dim, kind=BF16)
    return pl.pallas_call(
        own_state_kernel,
        in_specs=[NEAR] * 4 + [FAR, FAR],
        out_specs=[NEAR] * 4,
        out_shape=[in_vmem(half, dim + TILE, dim), in_vmem(half, dim, dim), raw, raw],
        scratch_shapes=[pltpu.SemaphoreType.DMA((2,))],
        compiler_params=params(4),
        cost_estimate=cost(2 * tok * heads * dim * dim, 4 * tok * heads * dim),
        name="own_state",
    )(*near(kh, vh, cum, decay), *far(query_rows, output_grad))


def intra(index, place, cum, kh, vh, first_own, first_send, raw, query_rows, output_grad):
    tok, heads, dim = query_rows.shape
    ahead = index == 0

    def kernel(place_ref, cum, kh, vh, first_own, first_send, q_raw, o_raw, *refs):
        if ahead:
            q_hbm, o_hbm, *refs = refs
            *refs, q_next, o_next, sems = refs
            copies = fetch_block(1, (q_hbm, o_hbm), (q_next, o_next), sems)
        qh, oh, w_ref, decays_ref, columns_ref, inner_ref = refs
        upper = is_upper(place_ref)
        to_heads(qh, q_raw, upper)
        to_heads(oh, o_raw, upper)

        def one(part, i, h):
            query = qh[h]
            row = cum[index, pl.ds(h, 1), :]
            columns = as_columns(row)
            quarters = decay_quarters(row, columns)
            for at, quarter in enumerate(quarters):
                decays_ref[h, at] = quarter
            weights = causal(dot_rows(query, kh[index, h]), quarters)
            w_ref[h] = weights.T
            inner = dot(weights, vh[index, h])
            columns = jnp.exp(columns)
            columns_ref[h] = columns
            if index:
                inner += columns * times_state(query, (first_own, first_send)[part][i])
            inner_ref[h] = inner

        each_half(heads // 2, 4, one)
        if ahead:
            for copy in copies:
                copy.wait()

    by_head = in_vmem(heads, BLOCK, dim, kind=BF16)
    return pl.pallas_call(
        kernel,
        in_specs=[NEAR] * 8 + [FAR, FAR] * ahead,
        out_specs=[NEAR] * (6 + 2 * ahead),
        out_shape=[
            by_head, by_head, in_vmem(heads, BLOCK, BLOCK, kind=BF16),
            in_vmem(heads, 3, BLOCK // 2, BLOCK // 2), in_vmem(heads, BLOCK, dim),
            in_vmem(heads, BLOCK, dim),
        ]
        + [in_vmem(BLOCK, heads, dim, kind=BF16)] * (2 * ahead),
        scratch_shapes=[pltpu.SemaphoreType.DMA((2,))] * ahead,
        compiler_params=params(4),
        cost_estimate=cost(
            2 * heads * BLOCK * BLOCK * dim * 4, 20 * heads * BLOCK * dim, heads * BLOCK * BLOCK
        ),
        name=f"intra_{index}",
    )(
        *near(place, cum, kh, vh, first_own, first_send, *raw),
        *(far(query_rows, output_grad) if ahead else ()),
    )


def attend_kernel(part, *refs):
    gain_ref, state_ref, q0, q1, o0, o1, columns0, columns1, inner0, inner1 = refs[:10]
    half = state_ref.shape[0]
    if part:
        before, att0, att1, sums_ref, partial = refs[10:]
        partial[...] = before[...]
    else:
        att0, att1, partial = refs[10:]
        partial[...] = jnp.zeros_like(partial)

    def one(i):
        h = part * half + i
        state = state_ref[i]
        gain = gain_ref[pl.ds(h, 1), :]
        blocks = ((q0, o0, columns0, inner0, att0), (q1, o1, columns1, inner1, att1))
        for b, (q, o, columns, inner, att) in enumerate(blocks):
            attended = inner[h] + columns[h] * times_state(q[h], state)
            att[i] = attended
            partial[0, b] += attended * attended
            partial[1, b] += gain * o[h].astype(F32) * attended
            state = columns[h, BLOCK - 1 :] * state

    each_head(half, 8, one)
    if part:
        totals = partial[...].reshape(4 * BLOCK, HD)
        high, rest = two_parts(totals)
        low = (totals - high.astype(F32) - rest.astype(F32)).astype(BF16)
        parts = jnp.concatenate([high, rest, low], axis=1)
        line = dot_rows(jnp.ones((2 * TILE, 3 * HD), BF16), parts)
        for at in range(2):
            sums_ref[at : at + 1] = line[:1, at * 2 * BLOCK : (at + 1) * 2 * BLOCK]


def attend(part, gain, state, arrays, before=()):
    heads, dim = gain.shape
    tok = 2 * BLOCK
    half = heads // 2
    by_head = in_vmem(half, BLOCK, dim)
    partial = (2, 2, BLOCK, dim)
    return pl.pallas_call(
        functools.partial(attend_kernel, part),
        in_specs=[NEAR] * (10 + part),
        out_specs=[NEAR] * 3,
        out_shape=[by_head, by_head, in_vmem(2, tok) if part else in_vmem(*partial)],
        scratch_shapes=[pltpu.VMEM(partial, F32)] * part,
        compiler_params=params(6),
        cost_estimate=cost(2 * heads * tok * dim * dim, 8 * heads * tok * dim),
        name=f"attend_{part}",
    )(*near(gain, state, *arrays, *before))


def scaled_queries(cum, q0, q1):
    _, heads, _ = cum.shape

    def kernel(cum_ref, q0, q1, out_ref, ends_ref):
        for b in range(2):
            ends_ref[b] = jnp.broadcast_to(jnp.exp(cum_ref[b, :, BLOCK - 1 :]), (heads, HD))

        def one(h):
            for b, q in enumerate((q0, q1)):
                scale = jnp.exp(cum_ref[b, pl.ds(h, 1), :])
                out_ref[b, h] = (q[h].astype(F32).T * scale).astype(BF16)

        each_head(heads, 4, one)

    return pl.pallas_call(
        kernel,
        in_specs=[NEAR] * 3,
        out_specs=[NEAR] * 2,
        out_shape=[in_vmem(2, heads, HD, BLOCK, kind=BF16), in_vmem(2, heads, HD)],
        compiler_params=params(4),
        cost_estimate=cost(4 * heads * BLOCK * HD, 8 * heads * BLOCK * HD),
        name="scaled_queries",
    )(*near(cum, q0, q1))


def remaining_decay(cum):
    _, heads, _ = cum.shape

    def kernel(cum_ref, out_ref):
        def one(h):
            for b in range(2):
                row = cum_ref[b, pl.ds(h, 1), :]
                out_ref[b, h] = as_columns(jnp.exp(row[:, BLOCK - 1 :] - row))

        each_head(heads, 4, one)

    return pl.pallas_call(
        kernel,
        in_specs=[NEAR],
        out_specs=NEAR,
        out_shape=in_vmem(2, heads, BLOCK, HD),
        compiler_params=params(4),
        cost_estimate=cost(2 * heads * BLOCK * HD, 8 * heads * BLOCK * HD),
        name="remaining_decay",
    )(*near(cum))


def inverse_rms(sums_ref, b):
    at = slice(b * BLOCK, (b + 1) * BLOCK)
    inv = lax.rsqrt(sums_ref[0:1, at] / (HEAD_TOTAL * HD) + 1e-06)
    mean = sums_ref[1:2, at] * inv / (HEAD_TOTAL * HD)
    return inv, mean


def norm_grad(part, ends, gain, sums, scaled, arrays):
    heads, dim = gain.shape
    tok = 2 * BLOCK
    half = heads // 2

    def kernel(ends_ref, gain_ref, sums_ref, queries_ref, o0, o1, att0, att1,
               out_ref, second_ref, g0, g1, scales):
        for b in range(2):
            inv, mean = inverse_rms(sums_ref, b)
            scales[b, 0] = as_columns(inv)
            scales[b, 1] = as_columns(inv * inv * mean)

        def one(i):
            h = part * half + i
            line = gain_ref[pl.ds(h, 1), :]
            starts = []
            for b, (o, att, g) in enumerate(((o0, att0, g0), (o1, att1, g1))):
                grad = line * o[h].astype(F32) * scales[b, 0] - att[i] * scales[b, 1]
                grad = grad.astype(BF16)
                g[i] = grad
                starts.append(dot(queries_ref[b, h], grad))
            second_ref[i] = starts[1]
            out_ref[i] = starts[0] + ends_ref[0, pl.ds(h, 1)] * starts[1]

        each_head(half, 8, one)

    by_head = in_vmem(half, BLOCK, dim, kind=BF16)
    return pl.pallas_call(
        kernel,
        in_specs=[NEAR] * 8,
        out_specs=[NEAR] * 4,
        out_shape=[in_vmem(half, dim, dim), in_vmem(half, dim, dim), by_head, by_head],
        scratch_shapes=[pltpu.VMEM((2, 2, BLOCK, dim), F32)],
        compiler_params=params(4),
        cost_estimate=cost(heads * tok * dim * dim, 7 * heads * tok * dim),
        name=f"norm_grad_{part}",
    )(*near(ends, gain, sums, scaled, *arrays))


def normed_block(b, place_ref, gain_ref, sums_ref, halves, rows, raw):
    inv = as_columns(inverse_rms(sums_ref, b)[0])

    def one(part, i, h):
        rows[b, h] = halves[part][i] * inv * gain_ref[pl.ds(h, 1), :]

    each_half(halves[0].shape[0], 4, one)
    from_heads(raw, rows.at[b], 0, BLOCK, is_upper(place_ref))


def grad_q_kernel(
    place_ref, ends_ref, keep_ref, recv_ref, first_own, first_send, kh, vh, own0, own1, other0,
    other1, decays0, decays1, columns0, columns1, gs_ref, out_q, rows, raw, sems,
):
    upper = is_upper(place_ref)
    copies = []
    blocks = (((own0, other0), decays0, columns0), ((own1, other1), decays1, columns1))
    for b, (g, decays, columns) in enumerate(blocks):

        def one(part, i, h, b=b, g=g, decays=decays, columns=columns):
            grad = g[part][i]
            scores = causal(dot_rows(grad, vh[b, h]), [decays[h, at] for at in range(3)])
            gs_ref[b, h] = scores
            state = (keep_ref, recv_ref)[part][i]
            if b:
                state = ends_ref[0, pl.ds(h, 1)] * state + (first_own, first_send)[part][i]
            rows[h] = dot(scores, kh[b, h]) + columns[h] * times_state_t(grad, state)

        each_half(keep_ref.shape[0], 8, one)
        for start in range(0, BLOCK, CHUNK):
            at = pl.ds(b * BLOCK + start, CHUNK)
            from_heads(raw.at[at], rows, start, CHUNK, upper)
            copies.append(pltpu.make_async_copy(raw.at[at], out_q.at[at], sems.at[len(copies)]))
            copies[-1].start()
    for copy in copies:
        copy.wait()


def grad_query(place, ends, arrays):
    _, heads, dim = ends.shape
    tok = 2 * BLOCK
    return pl.pallas_call(
        grad_q_kernel,
        in_specs=[NEAR] * 16,
        out_specs=[NEAR, FAR],
        out_shape=[
            in_vmem(2, heads, BLOCK, BLOCK, kind=BF16),
            jax.ShapeDtypeStruct((tok, heads, dim), BF16),
        ],
        scratch_shapes=[
            pltpu.VMEM((heads, BLOCK, dim), F32),
            pltpu.VMEM((tok, heads, dim), BF16),
            pltpu.SemaphoreType.DMA((tok // CHUNK,)),
        ],
        compiler_params=params(8),
        cost_estimate=cost(
            4 * heads * tok * dim * (BLOCK + dim), 12 * heads * tok * dim, heads * tok * BLOCK
        ),
        name="grad_query",
    )(*near(place, ends, *arrays))


def grad_kv_kernel(
    place_ref, gain_ref, sums_ref, att_own0, att_own1, att_other0, att_other1,
    gs_ref, w0, w1, q0, q1, kh, vh, own0, own1, other0, other1, remaining_ref,
    second_own, second_send, dk, dv, out_normed, raw, sems,
):
    copies = []
    for b, halves in enumerate(((att_own0, att_other0), (att_own1, att_other1))):
        at = pl.ds(b * BLOCK, BLOCK)
        normed_block(b, place_ref, gain_ref, sums_ref, halves, dk, raw.at[at])
        copies.append(pltpu.make_async_copy(raw.at[at], out_normed.at[at], sems.at[b]))
        copies[-1].start()

    def one(part, i, h):
        columns = remaining_ref[0, h]
        state = (second_own, second_send)[part][i]
        g0, g1 = ((own0, own1), (other0, other1))[part]
        dk[0, h] = transposed_dot(gs_ref[0, h], q0[h]) + columns * times_state_t(vh[0, h], state)
        dv[0, h] = dot(w0[h], g0[i]) + columns * times_state(kh[0, h], state)
        dk[1, h] = transposed_dot(gs_ref[1, h], q1[h])
        dv[1, h] = dot(w1[h], g1[i])

    each_half(second_own.shape[0], 4, one)
    for copy in copies:
        copy.wait()


def grad_key_value(place, gain, sums, att, arrays):
    heads, dim = gain.shape
    tok = 2 * BLOCK
    return pl.pallas_call(
        grad_kv_kernel,
        in_specs=[NEAR] * 21,
        out_specs=[NEAR, NEAR, FAR],
        out_shape=[in_vmem(2, heads, BLOCK, dim)] * 2
        + [jax.ShapeDtypeStruct((tok, heads, dim), BF16)],
        scratch_shapes=[
            pltpu.VMEM((tok, heads, dim), BF16),
            pltpu.SemaphoreType.DMA((2,)),
        ],
        compiler_params=params(6),
        cost_estimate=cost(4 * heads * tok * dim * (BLOCK + dim), 30 * heads * tok * dim),
        name="grad_key_value",
    )(*near(place, gain, sums, *att, *arrays))


def finish_rows(part, b, ends_ref, state_ref, kh, vh, remaining_ref, dk, dv, rows_k, rows_v):
    half = state_ref.shape[0]

    def one(i):
        h = part * half + i
        columns = remaining_ref[b, h]
        state = state_ref[i]
        if b == 0:
            state = ends_ref[1, pl.ds(h, 1)] * state
        state = state.astype(BF16)
        none = jnp.zeros_like(state)
        both = jnp.concatenate(
            [jnp.concatenate([state.T, none], axis=1), jnp.concatenate([none, state], axis=1)],
            axis=0,
        )
        carried = dot(jnp.concatenate([vh[b, h], kh[b, h]], axis=1), both)
        rows_k[b, h] = dk[b, h] + columns * carried[:, :HD]
        rows_v[b, h] = dv[b, h] + columns * carried[:, HD:]

    each_head(half, 8, one)


def finish_own_kernel(*refs):
    for b in range(2):
        finish_rows(0, b, *refs)


def finish_other_kernel(
    place_ref, old_k, old_v, ends_ref, state_ref, kh, vh, remaining_ref, dk, dv,
    out_k, out_v, rows_k, rows_v, raw_k, raw_v, sems,
):
    upper = is_upper(place_ref)
    copies = []
    for b in range(2):
        finish_rows(1, b, ends_ref, state_ref, kh, vh, remaining_ref, dk, dv, rows_k, rows_v)
        for start in range(0, BLOCK, CHUNK // 2):
            at = pl.ds(b * BLOCK + start, CHUNK // 2)
            for rows, raw, out in ((rows_k, raw_k, out_k), (rows_v, raw_v, out_v)):
                from_heads(raw.at[at], rows.at[b], start, CHUNK // 2, upper)
                copies.append(pltpu.make_async_copy(raw.at[at], out.at[at], sems.at[len(copies)]))
                copies[-1].start()
    for copy in copies:
        copy.wait()


def finish_own(ends, keep, arrays):
    _, heads, dim = ends.shape
    tok = 2 * BLOCK
    return pl.pallas_call(
        finish_own_kernel,
        in_specs=[NEAR] * 7,
        out_specs=[NEAR, NEAR],
        out_shape=[in_vmem(2, heads, BLOCK, dim)] * 2,
        compiler_params=params(4),
        cost_estimate=cost(4 * heads * tok * dim * dim, 8 * heads * tok * dim),
        name="finish_own",
    )(*near(ends, keep, *arrays))


def finish_other(place, rows, ends, recv, arrays):
    _, heads, dim = ends.shape
    tok = 2 * BLOCK
    shape = jax.ShapeDtypeStruct((tok, heads, dim), BF16)
    return pl.pallas_call(
        finish_other_kernel,
        in_specs=[NEAR] * 10,
        out_specs=[FAR, FAR, NEAR, NEAR],
        out_shape=[shape, shape] + [in_vmem(2, heads, BLOCK, dim)] * 2,
        input_output_aliases={1: 2, 2: 3},
        scratch_shapes=[
            pltpu.VMEM((tok, heads, dim), BF16),
            pltpu.VMEM((tok, heads, dim), BF16),
            pltpu.SemaphoreType.DMA((4 * (tok // CHUNK),)),
        ],
        compiler_params=params(8),
        cost_estimate=cost(4 * heads * tok * dim * dim, 8 * heads * tok * dim),
        name="finish_other",
    )(*near(place, *rows, ends, recv, *arrays))[:2]


def follows(value, earlier):
    return lax.optimization_barrier((value, earlier))[0]


def swap(value, axis, bit):
    count = lax.axis_size(axis)
    return lax.ppermute(value, axis, [(i, i ^ bit) for i in range(count)])


def mix(body, backward, place, arrays, shapes, name):
    def kernel(place_ref, *refs):
        bits = [is_set(place_ref, which) != backward for which in (LATE, RIGHT, LOW)]
        body(bits, refs[: len(arrays)], refs[len(arrays) :])

    return pl.pallas_call(
        kernel,
        in_specs=[NEAR] + [NEAR] * len(arrays),
        out_specs=[NEAR] * len(shapes),
        out_shape=[in_vmem(*shape) for shape in shapes],
        compiler_params=params(4),
        cost_estimate=cost(4 * 8 * HD * HD, 16 * 8 * HD * HD),
        name=name,
    )(place, *near(*arrays))


OWN, PARTNER, CHIP, ROW, CORNER = range(5)


def mix_total(bits, own, got, d_own, d_got, first, second):
    late = bits[0]
    quarter = first.shape[0]
    for h in range(2 * quarter):
        total = jnp.where(late, 1.0, d_got(h)) * own[h, :HD] + jnp.where(late, d_own(h), 1.0) * got[h, :HD]
        if h < quarter:
            first[h, :HD] = total
        else:
            second[h - quarter] = total


def mix_total_first(bits, arrays, outputs):
    own, got = arrays
    first, second, chip = outputs
    quarter = first.shape[0]
    d_own = lambda h: own[h, HD : HD + 1]
    d_got = lambda h: got[h, HD : HD + 1]
    mix_total(bits, own, got, d_own, d_got, first, second)
    for h in range(2 * quarter):
        whole = d_own(h) * d_got(h)
        chip[h : h + 1] = whole
        place = HD + (TILE // 2) * (h // quarter)
        first[h % quarter, place : place + TILE // 2] = jnp.broadcast_to(whole, (TILE // 2, HD))


def mix_total_again(bits, arrays, outputs):
    table, own, got = arrays
    decay = lambda which: lambda h: table[which, h : h + 1]
    mix_total(bits, own, got, decay(OWN), decay(PARTNER), *outputs)


def mix_next_row(bits, chip, row, total, got, out):
    right = bits[1]
    for i in range(out.shape[0]):
        scale_total = jnp.where(right, 1.0, row(i))
        scale_got = jnp.where(right, chip(i), 1.0)
        out[i] = scale_total * total[i, :HD] + scale_got * got[i, :HD]


def mix_next_column(bits, chip, corner, total, got, out):
    _, right, low = bits
    for i in range(out.shape[0]):
        scale_total = jnp.where(low & right, 0.0, 1.0)
        scale_got = jnp.where(low, jnp.where(right, 1.0, chip(i) * corner(i)), 0.0)
        out[i] = scale_total * total[i] + scale_got * got[i]


def lines(ref, first=0):
    return lambda i: ref[first + i : first + i + 1]


def mix_next_row_first(bits, arrays, outputs):
    chip, total, got = arrays
    mix_next_row(bits, lines(chip), lambda i: got[i, HD : HD + 1], total, got, *outputs)


def mix_next_column_first(bits, arrays, outputs):
    own, got, chip, corner, one_a, total, one_b = arrays
    out, table = outputs
    quarter = total.shape[0]
    for h in range(2 * quarter):
        place = HD + (TILE // 2) * (h // quarter)
        table[OWN, h : h + 1] = own[h, HD : HD + 1]
        table[PARTNER, h : h + 1] = got[h, HD : HD + 1]
        table[ROW, h : h + 1] = one_a[h % quarter, place : place + 1]
    table[CHIP] = chip[...]
    table[CORNER] = corner[...]
    mix_next_column(bits, lines(chip, quarter), lines(corner, quarter), total, one_b, out)


def mix_next_row_again(bits, arrays, outputs):
    table, total, got = arrays
    mix_next_row(bits, lines(table.at[CHIP]), lines(table.at[ROW]), total, got, *outputs)


def mix_next_column_again(bits, arrays, outputs):
    table, total, got = arrays
    quarter = total.shape[0]
    chip, corner = (lines(table.at[which], quarter) for which in (CHIP, CORNER))
    mix_next_column(bits, chip, corner, total, got, *outputs)


def mix_enter(bits, arrays, outputs):
    table, own, got, one_a, one_b, two_a, two_b = arrays
    kept, sent = outputs
    late, right, low = bits
    quarter = one_b.shape[0]
    decay = lambda which, h: table[which, h : h + 1]
    for h in range(2 * quarter):
        i = h % quarter
        row = jnp.where(right, decay(ROW, h), 1.0)
        if h < quarter:
            one, two = one_a[i, :HD], two_a[i]
            scale_one = jnp.where(right, 1.0, 0.0)
            scale_two = jnp.where(low, row, 0.0)
        else:
            one, two = one_b[i], two_b[i]
            scale_one = jnp.where(low, jnp.where(right, row, decay(CORNER, h)), 0.0)
            scale_two = jnp.where(low | right, 1.0, 0.0)
        enter = scale_one * one + scale_two * two
        after = jnp.where(late, decay(PARTNER, h), decay(OWN, h)) * enter
        after += jnp.where(late, got[h, :HD], own[h, :HD])
        kept[h] = jnp.where(late, after, enter)
        sent[h] = jnp.where(late, enter, after)


def entering_quad(send, own_task, table, place, backward, tasks):
    def work(stage, after, before=()):
        if stage not in tasks:
            return before
        run, outputs = tasks[stage]
        outputs.extend(run(after))
        return lax.optimization_barrier((before, outputs[0]))[0]

    name = "later" if backward else "earlier"
    half = send.shape[0]
    quarter = half // 2
    states, wide = (quarter, HD, HD), (quarter, HD + TILE, HD)
    got = swap(send, "seq", 1)
    own = own_task(send)
    if table is None:
        first, second, chip = mix(
            mix_total_first, backward, place, (own, got), (wide, states, (half, HD)), name + "_total"
        )
    else:
        first, second = mix(
            mix_total_again, backward, place, (table, own, got), (states, states), name + "_total"
        )
    one_a, one_b = swap(first, "seq", 2), swap(second, "seq", 4)
    if table is None:
        corner = swap(chip, "seq", 6)
        one_a, one_b, corner = work(1, second, (one_a, one_b, corner))
        (next_a,) = mix(
            mix_next_row_first, backward, place, (chip, first, one_a), (states,), name + "_row"
        )
        one_b, corner = follows((one_b, corner), next_a)
        next_b, table = mix(
            mix_next_column_first, backward, place,
            (own, got, chip, corner, one_a, second, one_b), (states, (5, half, HD)),
            name + "_column",
        )
    else:
        one_a, one_b = work(1, second, (one_a, one_b))
        (next_a,) = mix(
            mix_next_row_again, backward, place, (table, first, one_a), (states,), name + "_row"
        )
        (next_b,) = mix(
            mix_next_column_again, backward, place, (table, second, follows(one_b, next_a)),
            (states,), name + "_column",
        )
    two_a, two_b = swap(next_a, "seq", 4), swap(next_b, "seq", 2)
    two_a, two_b = work(2, next_b, (two_a, two_b))
    kept, sent = mix(
        mix_enter, backward, place, (table, own, got, one_a, one_b, two_a, two_b),
        ((half, HD, HD), (half, HD, HD)), name + "_enter",
    )
    received = swap(sent, "seq", 1)
    received = follows(received, tasks[3](follows(kept, sent)))
    return kept, received, table


def entering_any(send, own_task, log_total, backward, tasks):
    own = own_task(send)
    for stage in (1, 2):
        run, outputs = tasks[stage]
        outputs.extend(run(send))
    count, mine = lax.axis_size("seq"), lax.axis_index("seq")
    core = mine % 2
    own, send = own[:, :HD], send[:, :HD]
    half = own.shape[0]
    in_order = jnp.where(
        core == 0, jnp.concatenate([own, send], axis=0), jnp.concatenate([send, own], axis=0)
    )
    states = lax.all_gather(in_order, "seq")
    decays = jnp.exp(lax.all_gather(log_total, "seq"))
    place = mine
    if backward:
        states, decays, place = states[::-1], decays[::-1], count - 1 - mine

    def step(at, total):
        longer = decays[at][:, None, None] * total + states[at]
        return jnp.where(at < place, longer, total)

    total = lax.fori_loop(0, count - 1, step, jnp.zeros_like(in_order))
    kept = lax.dynamic_slice_in_dim(total, core * half, half)
    tasks[3](kept)
    return kept, lax.dynamic_slice_in_dim(total, (1 - core) * half, half)


def add(first, second):
    def kernel(first_ref, second_ref, out_ref):
        out_ref[...] = first_ref[...] + second_ref[...]

    return pl.pallas_call(
        kernel,
        in_specs=[NEAR, NEAR],
        out_specs=NEAR,
        out_shape=in_vmem(*first.shape),
        compiler_params=params(2),
        name="add",
    )(*near(first, second))


def sum_over_heads(value, tasks):
    tasks = list(tasks)
    results = []
    count = lax.axis_size("head")
    reach = 1
    while 2 * reach <= count and count % (2 * reach) == 0:
        got = swap(value, "head", reach)
        if tasks:
            results.append(tasks.pop(0)(value))
            got = follows(got, results[-1])
        value = add(value, got)
        reach *= 2
    results += [task(value) for task in tasks]
    part = value
    for shift in range(1, count // reach):
        value = add(
            value,
            lax.ppermute(part, "head", [(i, (i + shift * reach) % count) for i in range(count)]),
        )
    return value, results


def on_device(query_rows, key_rows, value_rows, output_grad, norm_gain, log_decay):
    mine = lax.axis_index("seq")
    bits = [(mine >> at) % 2 for at in range(3)]
    marks = [1 - bits[0], bits[0], *bits] + [jnp.zeros_like(mine)] * (TILE - 5)
    place = jnp.broadcast_to(jnp.stack(marks).astype(F32)[:, None], (TILE, HD))
    table = [None]

    def entering(send, own_task, backward, tasks):
        if lax.axis_size("seq") != 8:
            log_total = jnp.sum(log_decay, axis=1)
            return entering_any(send, own_task, log_total, backward, tasks)
        kept, received, table[0] = entering_quad(
            send, own_task, table[0], place, backward, tasks
        )
        return kept, received

    send, first_send, kh, vh, cum, _, decay, gain = state_to_send(
        place, norm_gain, log_decay, key_rows, value_rows
    )
    firsts, raws, in_0, in_1, begun = [], [], [], [], []

    def own_task(earlier):
        own, first, *raw = own_state(
            follows(kh, earlier), vh, cum, decay, query_rows, output_grad
        )
        firsts.extend((first, first_send))
        raws.append(raw)
        return own

    def forward_task(index):
        def task(earlier):
            *made, q_next, o_next = [
                *intra(
                    index, place, follows(cum, earlier), kh, vh, *firsts, raws[-1],
                    query_rows, output_grad,
                ),
                *raws[-1] * index,
            ]
            raws.append([q_next, o_next])
            return made

        return task

    def parts():
        q0, o0, _, _, columns0, inner0 = in_0
        q1, o1, _, _, columns1, inner1 = in_1
        return q0, q1, o0, o1, columns0, columns1, inner0, inner1

    def attend_task(kept):
        begun.extend(attend(0, gain, kept, parts()))
        return begun[-1]

    keep, recv = entering(
        send, own_task, False, {1: (forward_task(0), in_0), 2: (forward_task(1), in_1), 3: attend_task}
    )
    q0, o0, w0, decays0, columns0, _ = in_0
    q1, o1, w1, decays1, columns1, _ = in_1
    own_att = begun[:2]
    *other_att, sums = attend(1, gain, recv, parts(), begun[2:])
    sums, ((scaled, ends), remaining) = sum_over_heads(
        sums,
        (
            lambda earlier: scaled_queries(cum, follows(q0, earlier), q1),
            lambda earlier: remaining_decay(follows(cum, earlier)),
        ),
    )
    grad_send, second_send, *other_g = norm_grad(1, ends, gain, sums, scaled, (o0, o1, *other_att))
    own_g, seconds, queries, pairs, rows = [], [], [], [], []

    def own_grad_task(earlier):
        own, second, *grads = norm_grad(
            0, ends, gain, follows(sums, earlier), scaled, (o0, o1, *own_att)
        )
        own_g.extend(grads)
        seconds.extend((second, second_send))
        return own

    def query_task(earlier):
        return grad_query(
            place, follows(ends, earlier),
            (keep, recv, *firsts, kh, vh, *own_g, *other_g, decays0, decays1, columns0, columns1),
        )

    def pair_task(earlier):
        return grad_key_value(
            place, gain, sums, (*own_att, *other_att),
            (
                queries[0], w0, w1, q0, q1, kh, vh, *own_g, *other_g, remaining,
                follows(seconds[0], earlier), seconds[1],
            ),
        )

    def finish_task(kept):
        rows.extend(finish_own(ends, kept, (kh, vh, remaining, *pairs[:2])))
        return rows[0]

    _, grad_recv = entering(
        grad_send, own_grad_task, True,
        {1: (query_task, queries), 2: (pair_task, pairs), 3: finish_task},
    )
    grad_k, grad_v = finish_other(
        place, rows, ends, grad_recv, (kh, vh, remaining, *pairs[:2])
    )
    return pairs[2], queries[1], grad_k, grad_v


def solution(mesh):
    rows = P("seq", "head", None)
    return jax.shard_map(
        on_device,
        mesh=mesh,
        in_specs=(rows, rows, rows, rows, P("head", None), P("head", "seq")),
        out_specs=(rows, rows, rows, rows),
        check_vma=False,
    )
```

```python
import functools

import jax
import jax.numpy as jnp
from jax import lax
from jax.experimental import pallas as pl
from jax.experimental.pallas import tpu as pltpu
from jax.sharding import PartitionSpec as P

HEAD_TOTAL = 64
HD = 128
BLOCK = 256
CHUNK = 128
TILE = 8
F32 = jnp.float32
BF16 = jnp.bfloat16
MIB = 1024 * 1024
NEAR = pl.BlockSpec(memory_space=pltpu.VMEM)
FAR = pl.BlockSpec(memory_space=pl.ANY)
LOWER, UPPER, LATE, RIGHT, LOW = range(5)


def in_vmem(*shape, kind=F32):
    return pltpu.VMEM(shape, kind)


def near(*arrays):
    return [pltpu.with_memory_space_constraint(array, pltpu.VMEM) for array in arrays]


def far(*arrays):
    return [pltpu.with_memory_space_constraint(array, pltpu.HBM) for array in arrays]


def params(mib):
    return pltpu.CompilerParams(vmem_limit_bytes=mib * MIB)


def cost(flops, moved, exps=0):
    return pl.CostEstimate(flops=flops, bytes_accessed=moved, transcendentals=exps)


def block_cum(log_decay):
    size = log_decay.shape[1]
    upper = lax.broadcasted_iota(jnp.int32, (size, size), 0) <= lax.broadcasted_iota(
        jnp.int32, (size, size), 1
    )
    high, rest = two_parts(log_decay)
    low = (log_decay - high.astype(F32) - rest.astype(F32)).astype(BF16)
    ones = jnp.where(upper, 1.0, 0.0).astype(BF16)
    return dot(jnp.concatenate([high, rest, low], axis=1), jnp.concatenate([ones] * 3, axis=0))


def as_columns(row):
    return jnp.broadcast_to(row, (HD, row.shape[1])).T


def dot(a, b):
    return jnp.dot(a, b, preferred_element_type=F32)


def dot_rows(a, b):
    return lax.dot_general(a, b, (((1,), (1,)), ((), ())), preferred_element_type=F32)


def two_parts(matrix):
    high = matrix.astype(BF16)
    return high, (matrix - high.astype(F32)).astype(BF16)


def times_state(rows, state):
    return dot(jnp.concatenate([rows, rows], axis=1), jnp.concatenate(two_parts(state), axis=0))


def times_state_t(rows, state):
    return dot_rows(
        jnp.concatenate([rows, rows], axis=1), jnp.concatenate(two_parts(state), axis=1)
    )


def decay_quarters(row, columns):
    half = row.shape[1] // 2
    lower = lax.broadcasted_iota(jnp.int32, (half, half), 0) >= lax.broadcasted_iota(
        jnp.int32, (half, half), 1
    )
    quarters = []
    for t, s in ((0, 0), (1, 0), (1, 1)):
        gap = columns[t * half : (t + 1) * half] - row[:, s * half : (s + 1) * half]
        quarters.append(jnp.exp(jnp.where(lower, gap, -jnp.inf) if t == s else gap))
    return quarters


def causal(table, quarters):
    half = table.shape[0] // 2
    first, second, third = (
        (table[t * half : (t + 1) * half, s * half : (s + 1) * half] * quarter).astype(BF16)
        for (t, s), quarter in zip(((0, 0), (1, 0), (1, 1)), quarters)
    )
    top = jnp.concatenate([first, jnp.zeros_like(first)], axis=1)
    return jnp.concatenate([top, jnp.concatenate([second, third], axis=1)], axis=0)


def transposed_dot(a, b):
    return lax.dot_general(a, b, (((0,), (0,)), ((), ())), preferred_element_type=F32)


def each_head(heads, unroll, body):
    def step(h, carry):
        body(h)
        return carry

    lax.fori_loop(0, heads, step, 0, unroll=unroll)


def each_half(half, unroll, body):
    for part in range(2):
        each_head(half, unroll, lambda i, part=part: body(part, i, part * half + i))


def turn_tiles(tiles):
    count = len(tiles)
    at = lax.broadcasted_iota(jnp.int32, tiles[0].shape, 0)
    turned = [tile if i == 0 else pltpu.roll(tile, i, 0) for i, tile in enumerate(tiles)]
    reach = 1
    while reach < count:
        odd = (at & reach) != 0
        turned = [
            jnp.where(odd, turned[(n + reach) % count], turned[n]) for n in range(count)
        ]
        reach *= 2
    picked = [turned[-j % count] for j in range(count)]
    return [tile if j == 0 else pltpu.roll(tile, count - j, 0) for j, tile in enumerate(picked)]


def is_upper(place_ref):
    return jnp.max(place_ref[UPPER : UPPER + 1]) > 0.5


def to_heads(dst, block, upper):
    tok, heads, _ = block.shape

    def step(group, carry):
        at = pl.multiple_of(group * 2 * TILE, 2 * TILE)
        tokens = block[pl.ds(at, 2 * TILE)].astype(F32)
        for first in range(0, heads, TILE):
            halves = [
                turn_tiles([tokens[base + i, first : first + TILE] for i in range(TILE)])
                for base in (0, TILE)
            ]
            local = jnp.where(upper, heads - TILE - first, first)
            for j in range(TILE):
                both = jnp.concatenate([halves[0][j], halves[1][j]], axis=0)
                dst[local + j, pl.ds(at, 2 * TILE)] = both.astype(BF16)
        return carry

    lax.fori_loop(0, tok // (2 * TILE), step, 0, unroll=4)


def from_heads(block, src, start, tok, upper):
    heads = src.shape[0]

    def step(group, carry):
        at = pl.multiple_of(group * TILE, TILE)
        parts = []
        for first in range(0, heads, TILE):
            local = jnp.where(upper, heads - TILE - first, first)
            parts.append(turn_tiles([src[local + i, pl.ds(start + at, TILE)] for i in range(TILE)]))
        for j in range(TILE):
            block[at + j] = jnp.concatenate([part[j] for part in parts], axis=0).astype(BF16)
        return carry

    lax.fori_loop(0, tok // TILE, step, 0, unroll=4)


def is_set(place_ref, which):
    return place_ref[which : which + 1] > 0.5


def in_local_order(place_ref, rows):
    half = rows.shape[0] // 2
    lower, upper = rows[:half], rows[half:]
    mine = jnp.broadcast_to(place_ref[LOWER : LOWER + 1, :1], lower.shape) > 0.5
    return jnp.concatenate(
        [jnp.where(mine, lower, upper), jnp.where(mine, upper, lower)], axis=0
    )


def half_states(part, kh, vh, cum, b, out, first=None, unroll=8):
    half = kh.shape[1] // 2

    def one(i):
        h = part * half + i
        row = cum[b, pl.ds(h, 1), :]
        scale = jnp.exp(row[:, BLOCK - 1 :] - row)
        state = dot((kh[b, h].astype(F32).T * scale).astype(BF16), vh[b, h])
        if first is not None:
            state += jnp.exp(row[:, BLOCK - 1 :]) * first[i]
        out[i, :HD] = state

    each_head(half, unroll, one)


def add_decays(out, decay, part):
    half = out.shape[0]
    for i in range(half):
        out[i, HD:] = jnp.broadcast_to(decay[part * half + i : part * half + i + 1], (TILE, HD))


def state_kernel(
    place_ref, gain_hbm, ld_hbm, k_hbm, v_hbm, send_ref, first_ref, kh, vh, cum, ld_ref, decay,
    gain_ref, gain_raw, ld_raw, k_raw, v_raw, sems,
):
    heads, tok = ld_ref.shape
    per_block = BLOCK // CHUNK
    copies = [pltpu.make_async_copy(ld_hbm, ld_raw, sems.at[0])]
    for c in range(tok // CHUNK):
        at = pl.ds(c * CHUNK, CHUNK)
        copies.append(pltpu.make_async_copy(k_hbm.at[at], k_raw.at[at], sems.at[2 * c + 1]))
        copies.append(pltpu.make_async_copy(v_hbm.at[at], v_raw.at[at], sems.at[2 * c + 2]))
    copies.append(pltpu.make_async_copy(gain_hbm, gain_raw, sems.at[len(copies)]))
    for copy in copies:
        copy.start()
    upper = is_upper(place_ref)
    copies[0].wait()
    ld_ref[...] = in_local_order(place_ref, ld_raw[...])
    for b in range(2):
        cum[b] = block_cum(ld_ref[:, b * BLOCK : (b + 1) * BLOCK])
    ends = cum[0, :, BLOCK - 1 :] + cum[1, :, BLOCK - 1 :]
    decay[...] = jnp.broadcast_to(jnp.exp(ends), decay.shape)

    for b in range(2):
        for c in range(per_block):
            at = pl.ds((b * per_block + c) * CHUNK, CHUNK)
            here = pl.ds(c * CHUNK, CHUNK)
            which = 2 * (b * per_block + c) + 1
            copies[which].wait()
            to_heads(kh.at[b, :, here], k_raw.at[at], upper)
            copies[which + 1].wait()
            to_heads(vh.at[b, :, here], v_raw.at[at], upper)
        if b == 0:
            half_states(1, kh, vh, cum, 0, first_ref)
        else:
            half_states(1, kh, vh, cum, 1, send_ref, first_ref)
    add_decays(send_ref, decay, 1)
    copies[-1].wait()
    gain_ref[...] = in_local_order(place_ref, gain_raw[...])


def state_to_send(place, gain, log_decay, key_rows, value_rows):
    tok, heads, dim = key_rows.shape
    half = heads // 2
    by_head = in_vmem(2, heads, BLOCK, dim, kind=BF16)
    return pl.pallas_call(
        state_kernel,
        in_specs=[NEAR, FAR, FAR, FAR, FAR],
        out_specs=[NEAR] * 8,
        out_shape=[
            in_vmem(half, dim + TILE, dim), in_vmem(half, dim, dim), by_head, by_head,
            in_vmem(2, heads, BLOCK), in_vmem(heads, tok), in_vmem(heads, dim), in_vmem(heads, dim),
        ],
        scratch_shapes=[
            pltpu.VMEM((heads, dim), F32),
            pltpu.VMEM((heads, tok), F32),
            pltpu.VMEM((tok, heads, dim), BF16),
            pltpu.VMEM((tok, heads, dim), BF16),
            pltpu.SemaphoreType.DMA((2 * (tok // CHUNK) + 2,)),
        ],
        compiler_params=params(8),
        cost_estimate=cost(tok * heads * dim * dim, 8 * tok * heads * dim),
        name="state_to_send",
    )(place, *far(gain, log_decay, key_rows, value_rows))


def fetch_block(index, arrays, blocks, sems):
    copies = [
        pltpu.make_async_copy(array.at[pl.ds(index * BLOCK, BLOCK)], block, sems.at[at])
        for at, (array, block) in enumerate(zip(arrays, blocks))
    ]
    for copy in copies:
        copy.start()
    return copies


def own_state_kernel(
    kh, vh, cum, decay, q_hbm, o_hbm, own_ref, first_ref, q_raw, o_raw, sems
):
    copies = fetch_block(0, (q_hbm, o_hbm), (q_raw, o_raw), sems)
    half_states(0, kh, vh, cum, 0, first_ref, unroll=4)
    half_states(0, kh, vh, cum, 1, own_ref, first_ref, unroll=4)
    add_decays(own_ref, decay, 0)
    for copy in copies:
        copy.wait()


def own_state(kh, vh, cum, decay, query_rows, output_grad):
    _, heads, tok, dim = kh.shape
    half = heads // 2
    raw = in_vmem(BLOCK, heads, dim, kind=BF16)
    return pl.pallas_call(
        own_state_kernel,
        in_specs=[NEAR] * 4 + [FAR, FAR],
        out_specs=[NEAR] * 4,
        out_shape=[in_vmem(half, dim + TILE, dim), in_vmem(half, dim, dim), raw, raw],
        scratch_shapes=[pltpu.SemaphoreType.DMA((2,))],
        compiler_params=params(4),
        cost_estimate=cost(2 * tok * heads * dim * dim, 4 * tok * heads * dim),
        name="own_state",
    )(*near(kh, vh, cum, decay), *far(query_rows, output_grad))


def intra(index, place, cum, kh, vh, first_own, first_send, raw, query_rows, output_grad):
    tok, heads, dim = query_rows.shape
    ahead = index == 0

    def kernel(place_ref, cum, kh, vh, first_own, first_send, q_raw, o_raw, *refs):
        if ahead:
            q_hbm, o_hbm, *refs = refs
            *refs, q_next, o_next, sems = refs
            copies = fetch_block(1, (q_hbm, o_hbm), (q_next, o_next), sems)
        qh, oh, w_ref, decays_ref, columns_ref, inner_ref = refs
        upper = is_upper(place_ref)
        to_heads(qh, q_raw, upper)
        to_heads(oh, o_raw, upper)

        def one(part, i, h):
            query = qh[h]
            row = cum[index, pl.ds(h, 1), :]
            columns = as_columns(row)
            quarters = decay_quarters(row, columns)
            for at, quarter in enumerate(quarters):
                decays_ref[h, at] = quarter
            weights = causal(dot_rows(query, kh[index, h]), quarters)
            w_ref[h] = weights.T
            inner = dot(weights, vh[index, h])
            columns = jnp.exp(columns)
            columns_ref[h] = columns
            if index:
                inner += columns * times_state(query, (first_own, first_send)[part][i])
            inner_ref[h] = inner

        each_half(heads // 2, 4, one)
        if ahead:
            for copy in copies:
                copy.wait()

    by_head = in_vmem(heads, BLOCK, dim, kind=BF16)
    return pl.pallas_call(
        kernel,
        in_specs=[NEAR] * 8 + [FAR, FAR] * ahead,
        out_specs=[NEAR] * (6 + 2 * ahead),
        out_shape=[
            by_head, by_head, in_vmem(heads, BLOCK, BLOCK, kind=BF16),
            in_vmem(heads, 3, BLOCK // 2, BLOCK // 2), in_vmem(heads, BLOCK, dim),
            in_vmem(heads, BLOCK, dim),
        ]
        + [in_vmem(BLOCK, heads, dim, kind=BF16)] * (2 * ahead),
        scratch_shapes=[pltpu.SemaphoreType.DMA((2,))] * ahead,
        compiler_params=params(4),
        cost_estimate=cost(
            2 * heads * BLOCK * BLOCK * dim * 4, 20 * heads * BLOCK * dim, heads * BLOCK * BLOCK
        ),
        name=f"intra_{index}",
    )(
        *near(place, cum, kh, vh, first_own, first_send, *raw),
        *(far(query_rows, output_grad) if ahead else ()),
    )


def attend_kernel(part, *refs):
    gain_ref, state_ref, q0, q1, o0, o1, columns0, columns1, inner0, inner1 = refs[:10]
    half = state_ref.shape[0]
    if part:
        before, att0, att1, sums_ref, partial = refs[10:]
        partial[...] = before[...]
    else:
        att0, att1, partial = refs[10:]
        partial[...] = jnp.zeros_like(partial)

    def one(i):
        h = part * half + i
        state = state_ref[i]
        gain = gain_ref[pl.ds(h, 1), :]
        blocks = ((q0, o0, columns0, inner0, att0), (q1, o1, columns1, inner1, att1))
        for b, (q, o, columns, inner, att) in enumerate(blocks):
            attended = inner[h] + columns[h] * times_state(q[h], state)
            att[i] = attended
            partial[0, b] += attended * attended
            partial[1, b] += gain * o[h].astype(F32) * attended
            state = columns[h, BLOCK - 1 :] * state

    each_head(half, 8, one)
    if part:
        totals = partial[...].reshape(4 * BLOCK, HD)
        high, rest = two_parts(totals)
        low = (totals - high.astype(F32) - rest.astype(F32)).astype(BF16)
        parts = jnp.concatenate([high, rest, low], axis=1)
        line = dot_rows(jnp.ones((2 * TILE, 3 * HD), BF16), parts)
        for at in range(2):
            sums_ref[at : at + 1] = line[:1, at * 2 * BLOCK : (at + 1) * 2 * BLOCK]


def attend(part, gain, state, arrays, before=()):
    heads, dim = gain.shape
    tok = 2 * BLOCK
    half = heads // 2
    by_head = in_vmem(half, BLOCK, dim)
    partial = (2, 2, BLOCK, dim)
    return pl.pallas_call(
        functools.partial(attend_kernel, part),
        in_specs=[NEAR] * (10 + part),
        out_specs=[NEAR] * 3,
        out_shape=[by_head, by_head, in_vmem(2, tok) if part else in_vmem(*partial)],
        scratch_shapes=[pltpu.VMEM(partial, F32)] * part,
        compiler_params=params(6),
        cost_estimate=cost(2 * heads * tok * dim * dim, 8 * heads * tok * dim),
        name=f"attend_{part}",
    )(*near(gain, state, *arrays, *before))


def scaled_queries(cum, q0, q1):
    _, heads, _ = cum.shape

    def kernel(cum_ref, q0, q1, out_ref, ends_ref):
        for b in range(2):
            ends_ref[b] = jnp.broadcast_to(jnp.exp(cum_ref[b, :, BLOCK - 1 :]), (heads, HD))

        def one(h):
            for b, q in enumerate((q0, q1)):
                scale = jnp.exp(cum_ref[b, pl.ds(h, 1), :])
                out_ref[b, h] = (q[h].astype(F32).T * scale).astype(BF16)

        each_head(heads, 4, one)

    return pl.pallas_call(
        kernel,
        in_specs=[NEAR] * 3,
        out_specs=[NEAR] * 2,
        out_shape=[in_vmem(2, heads, HD, BLOCK, kind=BF16), in_vmem(2, heads, HD)],
        compiler_params=params(4),
        cost_estimate=cost(4 * heads * BLOCK * HD, 8 * heads * BLOCK * HD),
        name="scaled_queries",
    )(*near(cum, q0, q1))


def remaining_decay(cum):
    _, heads, _ = cum.shape

    def kernel(cum_ref, out_ref):
        def one(h):
            for b in range(2):
                row = cum_ref[b, pl.ds(h, 1), :]
                out_ref[b, h] = as_columns(jnp.exp(row[:, BLOCK - 1 :] - row))

        each_head(heads, 4, one)

    return pl.pallas_call(
        kernel,
        in_specs=[NEAR],
        out_specs=NEAR,
        out_shape=in_vmem(2, heads, BLOCK, HD),
        compiler_params=params(4),
        cost_estimate=cost(2 * heads * BLOCK * HD, 8 * heads * BLOCK * HD),
        name="remaining_decay",
    )(*near(cum))


def inverse_rms(sums_ref, b):
    at = slice(b * BLOCK, (b + 1) * BLOCK)
    inv = lax.rsqrt(sums_ref[0:1, at] / (HEAD_TOTAL * HD) + 1e-06)
    mean = sums_ref[1:2, at] * inv / (HEAD_TOTAL * HD)
    return inv, mean


def norm_grad(part, ends, gain, sums, scaled, arrays):
    heads, dim = gain.shape
    tok = 2 * BLOCK
    half = heads // 2

    def kernel(ends_ref, gain_ref, sums_ref, queries_ref, o0, o1, att0, att1,
               out_ref, second_ref, g0, g1, scales):
        for b in range(2):
            inv, mean = inverse_rms(sums_ref, b)
            scales[b, 0] = as_columns(inv)
            scales[b, 1] = as_columns(inv * inv * mean)

        def one(i):
            h = part * half + i
            line = gain_ref[pl.ds(h, 1), :]
            starts = []
            for b, (o, att, g) in enumerate(((o0, att0, g0), (o1, att1, g1))):
                grad = line * o[h].astype(F32) * scales[b, 0] - att[i] * scales[b, 1]
                grad = grad.astype(BF16)
                g[i] = grad
                starts.append(dot(queries_ref[b, h], grad))
            second_ref[i] = starts[1]
            out_ref[i] = starts[0] + ends_ref[0, pl.ds(h, 1)] * starts[1]

        each_head(half, 8, one)

    by_head = in_vmem(half, BLOCK, dim, kind=BF16)
    return pl.pallas_call(
        kernel,
        in_specs=[NEAR] * 8,
        out_specs=[NEAR] * 4,
        out_shape=[in_vmem(half, dim, dim), in_vmem(half, dim, dim), by_head, by_head],
        scratch_shapes=[pltpu.VMEM((2, 2, BLOCK, dim), F32)],
        compiler_params=params(4),
        cost_estimate=cost(heads * tok * dim * dim, 7 * heads * tok * dim),
        name=f"norm_grad_{part}",
    )(*near(ends, gain, sums, scaled, *arrays))


def normed_block(b, place_ref, gain_ref, sums_ref, halves, rows, raw):
    inv = as_columns(inverse_rms(sums_ref, b)[0])

    def one(part, i, h):
        rows[b, h] = halves[part][i] * inv * gain_ref[pl.ds(h, 1), :]

    each_half(halves[0].shape[0], 4, one)
    from_heads(raw, rows.at[b], 0, BLOCK, is_upper(place_ref))


def grad_q_kernel(
    place_ref, ends_ref, keep_ref, recv_ref, first_own, first_send, kh, vh, own0, own1, other0,
    other1, decays0, decays1, columns0, columns1, gs_ref, out_q, rows, raw, sems,
):
    upper = is_upper(place_ref)
    copies = []
    blocks = (((own0, other0), decays0, columns0), ((own1, other1), decays1, columns1))
    for b, (g, decays, columns) in enumerate(blocks):

        def one(part, i, h, b=b, g=g, decays=decays, columns=columns):
            grad = g[part][i]
            scores = causal(dot_rows(grad, vh[b, h]), [decays[h, at] for at in range(3)])
            gs_ref[b, h] = scores
            state = (keep_ref, recv_ref)[part][i]
            if b:
                state = ends_ref[0, pl.ds(h, 1)] * state + (first_own, first_send)[part][i]
            rows[h] = dot(scores, kh[b, h]) + columns[h] * times_state_t(grad, state)

        each_half(keep_ref.shape[0], 8, one)
        for start in range(0, BLOCK, CHUNK):
            at = pl.ds(b * BLOCK + start, CHUNK)
            from_heads(raw.at[at], rows, start, CHUNK, upper)
            copies.append(pltpu.make_async_copy(raw.at[at], out_q.at[at], sems.at[len(copies)]))
            copies[-1].start()
    for copy in copies:
        copy.wait()


def grad_query(place, ends, arrays):
    _, heads, dim = ends.shape
    tok = 2 * BLOCK
    return pl.pallas_call(
        grad_q_kernel,
        in_specs=[NEAR] * 16,
        out_specs=[NEAR, FAR],
        out_shape=[
            in_vmem(2, heads, BLOCK, BLOCK, kind=BF16),
            jax.ShapeDtypeStruct((tok, heads, dim), BF16),
        ],
        scratch_shapes=[
            pltpu.VMEM((heads, BLOCK, dim), F32),
            pltpu.VMEM((tok, heads, dim), BF16),
            pltpu.SemaphoreType.DMA((tok // CHUNK,)),
        ],
        compiler_params=params(8),
        cost_estimate=cost(
            4 * heads * tok * dim * (BLOCK + dim), 12 * heads * tok * dim, heads * tok * BLOCK
        ),
        name="grad_query",
    )(*near(place, ends, *arrays))


def grad_kv_kernel(
    place_ref, gain_ref, sums_ref, att_own0, att_own1, att_other0, att_other1,
    gs_ref, w0, w1, q0, q1, kh, vh, own0, own1, other0, other1, remaining_ref,
    second_own, second_send, dk, dv, out_normed, raw, sems,
):
    copies = []
    for b, halves in enumerate(((att_own0, att_other0), (att_own1, att_other1))):
        at = pl.ds(b * BLOCK, BLOCK)
        normed_block(b, place_ref, gain_ref, sums_ref, halves, dk, raw.at[at])
        copies.append(pltpu.make_async_copy(raw.at[at], out_normed.at[at], sems.at[b]))
        copies[-1].start()

    def one(part, i, h):
        columns = remaining_ref[0, h]
        state = (second_own, second_send)[part][i]
        g0, g1 = ((own0, own1), (other0, other1))[part]
        dk[0, h] = transposed_dot(gs_ref[0, h], q0[h]) + columns * times_state_t(vh[0, h], state)
        dv[0, h] = dot(w0[h], g0[i]) + columns * times_state(kh[0, h], state)
        dk[1, h] = transposed_dot(gs_ref[1, h], q1[h])
        dv[1, h] = dot(w1[h], g1[i])

    each_half(second_own.shape[0], 4, one)
    for copy in copies:
        copy.wait()


def grad_key_value(place, gain, sums, att, arrays):
    heads, dim = gain.shape
    tok = 2 * BLOCK
    return pl.pallas_call(
        grad_kv_kernel,
        in_specs=[NEAR] * 21,
        out_specs=[NEAR, NEAR, FAR],
        out_shape=[in_vmem(2, heads, BLOCK, dim)] * 2
        + [jax.ShapeDtypeStruct((tok, heads, dim), BF16)],
        scratch_shapes=[
            pltpu.VMEM((tok, heads, dim), BF16),
            pltpu.SemaphoreType.DMA((2,)),
        ],
        compiler_params=params(6),
        cost_estimate=cost(4 * heads * tok * dim * (BLOCK + dim), 30 * heads * tok * dim),
        name="grad_key_value",
    )(*near(place, gain, sums, *att, *arrays))


def finish_rows(part, b, ends_ref, state_ref, kh, vh, remaining_ref, dk, dv, rows_k, rows_v):
    half = state_ref.shape[0]

    def one(i):
        h = part * half + i
        columns = remaining_ref[b, h]
        state = state_ref[i]
        if b == 0:
            state = ends_ref[1, pl.ds(h, 1)] * state
        state = state.astype(BF16)
        none = jnp.zeros_like(state)
        both = jnp.concatenate(
            [jnp.concatenate([state.T, none], axis=1), jnp.concatenate([none, state], axis=1)],
            axis=0,
        )
        carried = dot(jnp.concatenate([vh[b, h], kh[b, h]], axis=1), both)
        rows_k[b, h] = dk[b, h] + columns * carried[:, :HD]
        rows_v[b, h] = dv[b, h] + columns * carried[:, HD:]

    each_head(half, 8, one)


def finish_own_kernel(*refs):
    for b in range(2):
        finish_rows(0, b, *refs)


def finish_other_kernel(
    place_ref, old_k, old_v, ends_ref, state_ref, kh, vh, remaining_ref, dk, dv,
    out_k, out_v, rows_k, rows_v, raw_k, raw_v, sems,
):
    upper = is_upper(place_ref)
    copies = []
    for b in range(2):
        finish_rows(1, b, ends_ref, state_ref, kh, vh, remaining_ref, dk, dv, rows_k, rows_v)
        for start in range(0, BLOCK, CHUNK // 2):
            at = pl.ds(b * BLOCK + start, CHUNK // 2)
            for rows, raw, out in ((rows_k, raw_k, out_k), (rows_v, raw_v, out_v)):
                from_heads(raw.at[at], rows.at[b], start, CHUNK // 2, upper)
                copies.append(pltpu.make_async_copy(raw.at[at], out.at[at], sems.at[len(copies)]))
                copies[-1].start()
    for copy in copies:
        copy.wait()


def finish_own(ends, keep, arrays):
    _, heads, dim = ends.shape
    tok = 2 * BLOCK
    return pl.pallas_call(
        finish_own_kernel,
        in_specs=[NEAR] * 7,
        out_specs=[NEAR, NEAR],
        out_shape=[in_vmem(2, heads, BLOCK, dim)] * 2,
        compiler_params=params(4),
        cost_estimate=cost(4 * heads * tok * dim * dim, 8 * heads * tok * dim),
        name="finish_own",
    )(*near(ends, keep, *arrays))


def finish_other(place, rows, ends, recv, arrays):
    _, heads, dim = ends.shape
    tok = 2 * BLOCK
    shape = jax.ShapeDtypeStruct((tok, heads, dim), BF16)
    return pl.pallas_call(
        finish_other_kernel,
        in_specs=[NEAR] * 10,
        out_specs=[FAR, FAR, NEAR, NEAR],
        out_shape=[shape, shape] + [in_vmem(2, heads, BLOCK, dim)] * 2,
        input_output_aliases={1: 2, 2: 3},
        scratch_shapes=[
            pltpu.VMEM((tok, heads, dim), BF16),
            pltpu.VMEM((tok, heads, dim), BF16),
            pltpu.SemaphoreType.DMA((4 * (tok // CHUNK),)),
        ],
        compiler_params=params(8),
        cost_estimate=cost(4 * heads * tok * dim * dim, 8 * heads * tok * dim),
        name="finish_other",
    )(*near(place, *rows, ends, recv, *arrays))[:2]


def follows(value, earlier):
    return lax.optimization_barrier((value, earlier))[0]


def swap(value, axis, bit):
    count = lax.axis_size(axis)
    return lax.ppermute(value, axis, [(i, i ^ bit) for i in range(count)])


def mix(body, backward, place, arrays, shapes, name):
    def kernel(place_ref, *refs):
        bits = [is_set(place_ref, which) != backward for which in (LATE, RIGHT, LOW)]
        body(bits, refs[: len(arrays)], refs[len(arrays) :])

    return pl.pallas_call(
        kernel,
        in_specs=[NEAR] + [NEAR] * len(arrays),
        out_specs=[NEAR] * len(shapes),
        out_shape=[in_vmem(*shape) for shape in shapes],
        compiler_params=params(4),
        cost_estimate=cost(4 * 8 * HD * HD, 16 * 8 * HD * HD),
        name=name,
    )(place, *near(*arrays))


OWN, PARTNER, CHIP, ROW, CORNER = range(5)


def mix_total(bits, own, got, d_own, d_got, first, second):
    late = bits[0]
    quarter = first.shape[0]
    for h in range(2 * quarter):
        total = jnp.where(late, 1.0, d_got(h)) * own[h, :HD] + jnp.where(late, d_own(h), 1.0) * got[h, :HD]
        if h < quarter:
            first[h, :HD] = total
        else:
            second[h - quarter] = total


def mix_total_first(bits, arrays, outputs):
    own, got = arrays
    first, second, chip = outputs
    quarter = first.shape[0]
    d_own = lambda h: own[h, HD : HD + 1]
    d_got = lambda h: got[h, HD : HD + 1]
    mix_total(bits, own, got, d_own, d_got, first, second)
    for h in range(2 * quarter):
        whole = d_own(h) * d_got(h)
        chip[h : h + 1] = whole
        place = HD + (TILE // 2) * (h // quarter)
        first[h % quarter, place : place + TILE // 2] = jnp.broadcast_to(whole, (TILE // 2, HD))


def mix_total_again(bits, arrays, outputs):
    table, own, got = arrays
    decay = lambda which: lambda h: table[which, h : h + 1]
    mix_total(bits, own, got, decay(OWN), decay(PARTNER), *outputs)


def mix_next_row(bits, chip, row, total, got, out):
    right = bits[1]
    for i in range(out.shape[0]):
        scale_total = jnp.where(right, 1.0, row(i))
        scale_got = jnp.where(right, chip(i), 1.0)
        out[i] = scale_total * total[i, :HD] + scale_got * got[i, :HD]


def mix_next_column(bits, chip, corner, total, got, out):
    _, right, low = bits
    for i in range(out.shape[0]):
        scale_total = jnp.where(low & right, 0.0, 1.0)
        scale_got = jnp.where(low, jnp.where(right, 1.0, chip(i) * corner(i)), 0.0)
        out[i] = scale_total * total[i] + scale_got * got[i]


def lines(ref, first=0):
    return lambda i: ref[first + i : first + i + 1]


def mix_next_row_first(bits, arrays, outputs):
    chip, total, got = arrays
    mix_next_row(bits, lines(chip), lambda i: got[i, HD : HD + 1], total, got, *outputs)


def mix_next_column_first(bits, arrays, outputs):
    own, got, chip, corner, one_a, total, one_b = arrays
    out, table = outputs
    quarter = total.shape[0]
    for h in range(2 * quarter):
        place = HD + (TILE // 2) * (h // quarter)
        table[OWN, h : h + 1] = own[h, HD : HD + 1]
        table[PARTNER, h : h + 1] = got[h, HD : HD + 1]
        table[ROW, h : h + 1] = one_a[h % quarter, place : place + 1]
    table[CHIP] = chip[...]
    table[CORNER] = corner[...]
    mix_next_column(bits, lines(chip, quarter), lines(corner, quarter), total, one_b, out)


def mix_next_row_again(bits, arrays, outputs):
    table, total, got = arrays
    mix_next_row(bits, lines(table.at[CHIP]), lines(table.at[ROW]), total, got, *outputs)


def mix_next_column_again(bits, arrays, outputs):
    table, total, got = arrays
    quarter = total.shape[0]
    chip, corner = (lines(table.at[which], quarter) for which in (CHIP, CORNER))
    mix_next_column(bits, chip, corner, total, got, *outputs)


def mix_enter(bits, arrays, outputs):
    table, own, got, one_a, one_b, two_a, two_b = arrays
    kept, sent = outputs
    late, right, low = bits
    quarter = one_b.shape[0]
    decay = lambda which, h: table[which, h : h + 1]
    for h in range(2 * quarter):
        i = h % quarter
        row = jnp.where(right, decay(ROW, h), 1.0)
        if h < quarter:
            one, two = one_a[i, :HD], two_a[i]
            scale_one = jnp.where(right, 1.0, 0.0)
            scale_two = jnp.where(low, row, 0.0)
        else:
            one, two = one_b[i], two_b[i]
            scale_one = jnp.where(low, jnp.where(right, row, decay(CORNER, h)), 0.0)
            scale_two = jnp.where(low | right, 1.0, 0.0)
        enter = scale_one * one + scale_two * two
        after = jnp.where(late, decay(PARTNER, h), decay(OWN, h)) * enter
        after += jnp.where(late, got[h, :HD], own[h, :HD])
        kept[h] = jnp.where(late, after, enter)
        sent[h] = jnp.where(late, enter, after)


def entering_quad(send, own_task, table, place, backward, tasks):
    def work(stage, after, before=()):
        if stage not in tasks:
            return before
        run, outputs = tasks[stage]
        outputs.extend(run(after))
        return lax.optimization_barrier((before, outputs[0]))[0]

    name = "later" if backward else "earlier"
    half = send.shape[0]
    quarter = half // 2
    states, wide = (quarter, HD, HD), (quarter, HD + TILE, HD)
    got = swap(send, "seq", 1)
    own = own_task(send)
    if table is None:
        first, second, chip = mix(
            mix_total_first, backward, place, (own, got), (wide, states, (half, HD)), name + "_total"
        )
    else:
        first, second = mix(
            mix_total_again, backward, place, (table, own, got), (states, states), name + "_total"
        )
    one_a, one_b = swap(first, "seq", 2), swap(second, "seq", 4)
    if table is None:
        corner = swap(chip, "seq", 6)
        one_a, one_b, corner = work(1, second, (one_a, one_b, corner))
        (next_a,) = mix(
            mix_next_row_first, backward, place, (chip, first, one_a), (states,), name + "_row"
        )
        one_b, corner = follows((one_b, corner), next_a)
        next_b, table = mix(
            mix_next_column_first, backward, place,
            (own, got, chip, corner, one_a, second, one_b), (states, (5, half, HD)),
            name + "_column",
        )
    else:
        one_a, one_b = work(1, second, (one_a, one_b))
        (next_a,) = mix(
            mix_next_row_again, backward, place, (table, first, one_a), (states,), name + "_row"
        )
        (next_b,) = mix(
            mix_next_column_again, backward, place, (table, second, follows(one_b, next_a)),
            (states,), name + "_column",
        )
    two_a, two_b = swap(next_a, "seq", 4), swap(next_b, "seq", 2)
    two_a, two_b = work(2, next_b, (two_a, two_b))
    kept, sent = mix(
        mix_enter, backward, place, (table, own, got, one_a, one_b, two_a, two_b),
        ((half, HD, HD), (half, HD, HD)), name + "_enter",
    )
    received = swap(sent, "seq", 1)
    received = follows(received, tasks[3](follows(kept, sent)))
    return kept, received, table


def entering_any(send, own_task, log_total, backward, tasks):
    own = own_task(send)
    for stage in (1, 2):
        run, outputs = tasks[stage]
        outputs.extend(run(send))
    count, mine = lax.axis_size("seq"), lax.axis_index("seq")
    core = mine % 2
    own, send = own[:, :HD], send[:, :HD]
    half = own.shape[0]
    in_order = jnp.where(
        core == 0, jnp.concatenate([own, send], axis=0), jnp.concatenate([send, own], axis=0)
    )
    states = lax.all_gather(in_order, "seq")
    decays = jnp.exp(lax.all_gather(log_total, "seq"))
    place = mine
    if backward:
        states, decays, place = states[::-1], decays[::-1], count - 1 - mine

    def step(at, total):
        longer = decays[at][:, None, None] * total + states[at]
        return jnp.where(at < place, longer, total)

    total = lax.fori_loop(0, count - 1, step, jnp.zeros_like(in_order))
    kept = lax.dynamic_slice_in_dim(total, core * half, half)
    tasks[3](kept)
    return kept, lax.dynamic_slice_in_dim(total, (1 - core) * half, half)


def add(first, second):
    def kernel(first_ref, second_ref, out_ref):
        out_ref[...] = first_ref[...] + second_ref[...]

    return pl.pallas_call(
        kernel,
        in_specs=[NEAR, NEAR],
        out_specs=NEAR,
        out_shape=in_vmem(*first.shape),
        compiler_params=params(2),
        name="add",
    )(*near(first, second))


def sum_over_heads(value, tasks):
    tasks = list(tasks)
    results = []
    count = lax.axis_size("head")
    reach = 1
    while 2 * reach <= count and count % (2 * reach) == 0:
        got = swap(value, "head", reach)
        if tasks:
            results.append(tasks.pop(0)(value))
            got = follows(got, results[-1])
        value = add(value, got)
        reach *= 2
    results += [task(value) for task in tasks]
    part = value
    for shift in range(1, count // reach):
        value = add(
            value,
            lax.ppermute(part, "head", [(i, (i + shift * reach) % count) for i in range(count)]),
        )
    return value, results


def on_device(query_rows, key_rows, value_rows, output_grad, norm_gain, log_decay):
    mine = lax.axis_index("seq")
    bits = [(mine >> at) % 2 for at in range(3)]
    marks = [1 - bits[0], bits[0], *bits] + [jnp.zeros_like(mine)] * (TILE - 5)
    place = jnp.broadcast_to(jnp.stack(marks).astype(F32)[:, None], (TILE, HD))
    table = [None]

    def entering(send, own_task, backward, tasks):
        if lax.axis_size("seq") != 8:
            log_total = jnp.sum(log_decay, axis=1)
            return entering_any(send, own_task, log_total, backward, tasks)
        kept, received, table[0] = entering_quad(
            send, own_task, table[0], place, backward, tasks
        )
        return kept, received

    send, first_send, kh, vh, cum, _, decay, gain = state_to_send(
        place, norm_gain, log_decay, key_rows, value_rows
    )
    firsts, raws, in_0, in_1, begun = [], [], [], [], []

    def own_task(earlier):
        own, first, *raw = own_state(
            follows(kh, earlier), vh, cum, decay, query_rows, output_grad
        )
        firsts.extend((first, first_send))
        raws.append(raw)
        return own

    def forward_task(index):
        def task(earlier):
            *made, q_next, o_next = [
                *intra(
                    index, place, follows(cum, earlier), kh, vh, *firsts, raws[-1],
                    query_rows, output_grad,
                ),
                *raws[-1] * index,
            ]
            raws.append([q_next, o_next])
            return made

        return task

    def parts():
        q0, o0, _, _, columns0, inner0 = in_0
        q1, o1, _, _, columns1, inner1 = in_1
        return q0, q1, o0, o1, columns0, columns1, inner0, inner1

    def attend_task(kept):
        begun.extend(attend(0, gain, kept, parts()))
        return begun[-1]

    keep, recv = entering(
        send, own_task, False, {1: (forward_task(0), in_0), 2: (forward_task(1), in_1), 3: attend_task}
    )
    q0, o0, w0, decays0, columns0, _ = in_0
    q1, o1, w1, decays1, columns1, _ = in_1
    own_att = begun[:2]
    *other_att, sums = attend(1, gain, recv, parts(), begun[2:])
    sums, ((scaled, ends), remaining) = sum_over_heads(
        sums,
        (
            lambda earlier: scaled_queries(cum, follows(q0, earlier), q1),
            lambda earlier: remaining_decay(follows(cum, earlier)),
        ),
    )
    grad_send, second_send, *other_g = norm_grad(1, ends, gain, sums, scaled, (o0, o1, *other_att))
    own_g, seconds, queries, pairs, rows = [], [], [], [], []

    def own_grad_task(earlier):
        own, second, *grads = norm_grad(
            0, ends, gain, follows(sums, earlier), scaled, (o0, o1, *own_att)
        )
        own_g.extend(grads)
        seconds.extend((second, second_send))
        return own

    def query_task(earlier):
        return grad_query(
            place, follows(ends, earlier),
            (keep, recv, *firsts, kh, vh, *own_g, *other_g, decays0, decays1, columns0, columns1),
        )

    def pair_task(earlier):
        return grad_key_value(
            place, gain, sums, (*own_att, *other_att),
            (
                queries[0], w0, w1, q0, q1, kh, vh, *own_g, *other_g, remaining,
                follows(seconds[0], earlier), seconds[1],
            ),
        )

    def finish_task(kept):
        rows.extend(finish_own(ends, kept, (kh, vh, remaining, *pairs[:2])))
        return rows[0]

    _, grad_recv = entering(
        grad_send, own_grad_task, True,
        {1: (query_task, queries), 2: (pair_task, pairs), 3: finish_task},
    )
    grad_k, grad_v = finish_other(
        place, rows, ends, grad_recv, (kh, vh, remaining, *pairs[:2])
    )
    return pairs[2], queries[1], grad_k, grad_v


def solution(mesh):
    rows = P("seq", "head", None)
    return jax.shard_map(
        on_device,
        mesh=mesh,
        in_specs=(rows, rows, rows, rows, P("head", None), P("head", "seq")),
        out_specs=(rows, rows, rows, rows),
        check_vma=False,
    )
```
